32 devices in a mesh: groups: 2 (over y), dom: 4 (over z), sample: 2 (over x), sub: 2 (over core).
Axes of the slice: x: 2, y: 2, z: 4, core: 2. Of those that a mesh axis runs over, the one named last changes fastest.
Arguments:
- node_in: bfloat16 [4, 8192, 128], P(('groups', 'sample'), ('dom', 'sub')), parts along dimension 0, may hold values from -6 to 6
- edge_in: bfloat16 [4, 24576, 128], P(('groups', 'sample'), ('dom', 'sub')), parts along dimension 0, may hold values from -6 to 6
- senders: int32 [24576], P(('dom', 'sub')), may hold values from 0 to 1023
- receivers: int32 [24576], P(('dom', 'sub')), may hold values from 0 to 1279, as said below
- send_list: int32 [8, 2, 128], P(('dom', 'sub')), may hold values from 0 to 1023, as said below
- w_edge_first: bfloat16 [384, 128], replicated, may hold values from -0.3125 to 0.3125
- b_edge_first: float32 [128], replicated, may hold values from -3 to 3
- w_edge_second: bfloat16 [128, 128], replicated, may hold values from -0.5 to 0.5
- b_edge_second: float32 [128], replicated, may hold values from -3 to 3
- edge_gain: float32 [128], replicated, may hold values from 0.5 to 1.5
- edge_shift: float32 [128], replicated, may hold values from -3 to 3
- w_node_first: bfloat16 [256, 128], replicated, may hold values from -0.375 to 0.375
- b_node_first: float32 [128], replicated, may hold values from -3 to 3
- w_node_second: bfloat16 [128, 128], replicated, may hold values from -0.5 to 0.5
- b_node_second: float32 [128], replicated, may hold values from -3 to 3
- node_gain: float32 [128], replicated, may hold values from 0.5 to 1.5
- node_shift: float32 [128], replicated, may hold values from -3 to 3
- node_cotangent: bfloat16 [4, 8192, 128], P(('groups', 'sample'), ('dom', 'sub')), parts along dimension 0, may hold values from -6 to 6
- edge_cotangent: bfloat16 [4, 24576, 128], P(('groups', 'sample'), ('dom', 'sub')), parts along dimension 0, may hold values from -6 to 6
Outputs:
- node_out: bfloat16 [4, 8192, 128], P(('groups', 'sample'), ('dom', 'sub')), parts along dimension 0
- edge_out: bfloat16 [4, 24576, 128], P(('groups', 'sample'), ('dom', 'sub')), parts along dimension 0
- node_grad: bfloat16 [4, 8192, 128], P(('groups', 'sample'), ('dom', 'sub')), parts along dimension 0
- edge_grad: bfloat16 [4, 24576, 128], P(('groups', 'sample'), ('dom', 'sub')), parts along dimension 0
- g_edge_first: float32 [768, 128], P('groups'), parts along dimension 0
- g_b_edge_first: float32 [256], P('groups'), parts along dimension 0
- g_edge_second: float32 [256, 128], P('groups'), parts along dimension 0
- g_b_edge_second: float32 [256], P('groups'), parts along dimension 0
- g_edge_gain: float32 [256], P('groups'), parts along dimension 0
- g_edge_shift: float32 [256], P('groups'), parts along dimension 0
- g_node_first: float32 [512, 128], P('groups'), parts along dimension 0
- g_b_node_first: float32 [256], P('groups'), parts along dimension 0
- g_node_second: float32 [256, 128], P('groups'), parts along dimension 0
- g_b_node_second: float32 [256], P('groups'), parts along dimension 0
- g_node_gain: float32 [256], P('groups'), parts along dimension 0
- g_node_shift: float32 [256], P('groups'), parts along dimension 0
The draws below stay inside these ranges and needn't reach their ends.
There are 2 independent parts, one for each index of `groups`. The reference program is written for one: setup_inputs(seed, part) draws one part's arguments, and reference() takes and returns one part's arrays. A program takes and returns all parts, laid end to end along the dimension named above; an argument that names none is the same for every part. Nothing has to cross between parts.
Inputs may be any that keep to these rules, and one draw needn't show every extreme that they name: Values of 1024 and above name halo slots: slot k below 128 is the left neighbour's send_list row 1, entry k; the rest are the right neighbour's row 0. The first partition has no left slots and the last none on the right. In every other partition exactly 512 edges have halo receivers and every slot receives at least one edge. `send_list`: each row holds 128 distinct nodes of the partition.
All inputs are finite; a program needn't handle non-finite values.
Results may differ from the reference program's by a relative error of at most 0.0078.
Values may be sent and summed in bfloat16 or wider, within the bound.
No kernel may reach another device: no remote copies, remote signals or barrier semaphores. Data moves between devices by JAX's collectives and lax.ppermute only.
A program may use at most 64 MiB of HBM per device.

```python
import jax
import jax.numpy as jnp
from jax import lax

D = 128
HID = 128
NODE_DEV = 1024
EDGE_DEV = 3072
BND = 128
PARTS_SIZE = 8
SAMPLES = 2
NODES = 8192
EDGES = 24576


def draw_receivers(key, part):
    key = jax.random.fold_in(key, 11)
    local_key, remote_key, fix_key, order_key = jax.random.split(key, 4)
    local_ids = jax.random.randint(local_key, (PARTS_SIZE, EDGE_DEV - 4 * BND), 0, NODE_DEV)
    covered = jnp.broadcast_to(jnp.arange(2 * BND, dtype=jnp.int32), (PARTS_SIZE, 2 * BND))
    extra = jax.random.randint(remote_key, (PARTS_SIZE, 2 * BND), 0, 2 * BND)
    remote_ids = NODE_DEV + jnp.concatenate([covered, extra], axis=1)
    partition = lax.broadcasted_iota(jnp.int32, (PARTS_SIZE, 4 * BND), 0)
    missing = (partition == 0) & (remote_ids < NODE_DEV + BND) | (partition == PARTS_SIZE - 1) & (remote_ids >= NODE_DEV + BND)
    replacement = jax.random.randint(fix_key, (PARTS_SIZE, 4 * BND), 0, NODE_DEV)
    remote_ids = jnp.where(missing, replacement, remote_ids)
    joined = jnp.concatenate([local_ids, remote_ids], axis=1)
    shuffled = jax.random.permutation(order_key, joined, axis=1, independent=True)
    return shuffled.reshape(EDGES).astype(jnp.int32)


def draw_send_list(key, part):
    key = jax.random.fold_in(key, 23)
    ordered = jnp.broadcast_to(jnp.arange(NODE_DEV, dtype=jnp.int32), (PARTS_SIZE, 2, NODE_DEV))
    shuffled = jax.random.permutation(key, ordered, axis=2, independent=True)
    return shuffled[:, :, :BND].astype(jnp.int32)


def with_ends(values, own_key, low, top_value):
    index_at = [jax.random.randint(jax.random.fold_in(own_key, axis), (), 0, length) for axis, length in enumerate(values.shape)]
    widest = values.shape.index(max(values.shape))
    neighbour = index_at[:widest] + [(index_at[widest] + 1) % values.shape[widest]] + index_at[widest + 1:]
    return values.at[tuple(index_at)].set(low).at[tuple(neighbour)].set(top_value)


def levels(stream_key, extent, cuts, smallest, high):
    level = 1.0
    for position, shards_of in cuts:
        steps = jax.random.uniform(jax.random.fold_in(jax.random.fold_in(stream_key, 6), position), (shards_of,), jnp.float32, smallest / len(cuts), high / len(cuts))
        level = level * jnp.repeat(jnp.exp(steps), extent[position] // shards_of).reshape((-1,) + (1,) * (len(extent) - 1 - position))
    return level


def centred(stream_key, shape, spread, bound, cuts=(), kind=jnp.bfloat16):
    drawn = jax.random.normal(stream_key, shape, jnp.float32) * spread
    if len(cuts) > 0:
        drawn = levels(stream_key, shape, cuts, -0.22, 0.18) * drawn
    return jnp.clip(drawn, min=-bound, max=bound).astype(kind)


def setup_inputs(seed: int = 0, part: int = 0) -> dict:
    seeds = jax.random.split(jax.random.key(seed), 20)
    own_keys = jax.random.split(jax.random.fold_in(seeds[19], part), 20)
    return {
        "node_in": centred(own_keys[0], (SAMPLES, NODES, D), 1.0, 6.0, ((0, 2), (1, 8))),
        "edge_in": centred(own_keys[1], (SAMPLES, EDGES, D), 1.0, 6.0, ((0, 2), (1, 8))),
        "senders": with_ends(jax.random.randint(seeds[2], (EDGES,), 0, NODE_DEV), jax.random.fold_in(seeds[2], 1), 0, NODE_DEV - 1).astype(jnp.int32),
        "receivers": draw_receivers(jax.random.fold_in(seeds[19], 71), part),
        "send_list": draw_send_list(jax.random.fold_in(seeds[19], 71), part),
        "w_edge_first": centred(seeds[5], (3 * D, HID), (3 * D) ** -0.5, 0.3125),
        "b_edge_first": centred(seeds[6], (HID,), 0.5, 3.0, (), jnp.float32),
        "w_edge_second": centred(seeds[7], (HID, D), HID ** -0.5, 0.5),
        "b_edge_second": centred(seeds[8], (D,), 0.5, 3.0, (), jnp.float32),
        "edge_gain": jnp.clip(1.0 + 0.1 * jax.random.normal(seeds[9], (D,), jnp.float32), 0.5, 1.5),
        "edge_shift": centred(seeds[10], (D,), 0.5, 3.0, (), jnp.float32),
        "w_node_first": centred(seeds[11], (2 * D, HID), (2 * D) ** -0.5, 0.375),
        "b_node_first": centred(seeds[12], (HID,), 0.5, 3.0, (), jnp.float32),
        "w_node_second": centred(seeds[13], (HID, D), HID ** -0.5, 0.5),
        "b_node_second": centred(seeds[14], (D,), 0.5, 3.0, (), jnp.float32),
        "node_gain": jnp.clip(1.0 + 0.1 * jax.random.normal(seeds[15], (D,), jnp.float32), 0.5, 1.5),
        "node_shift": centred(seeds[16], (D,), 0.5, 3.0, (), jnp.float32),
        "node_cotangent": centred(own_keys[17], (SAMPLES, NODES, D), 1.0, 6.0, ((0, 2), (1, 8))),
        "edge_cotangent": centred(own_keys[18], (SAMPLES, EDGES, D), 1.0, 6.0, ((0, 2), (1, 8))),
    }


epsilon = 1e-05
plain_dims = (((1,), (0,)), ((), ()))
rows_dims = (((0,), (0,)), ((), ()))
back_dims = (((1,), (1,)), ((), ()))

def product(left_side, right_side, dims):
    return lax.dot_general(left_side.astype(jnp.float32), right_side.astype(jnp.float32), dims, precision=lax.Precision.HIGHEST)

def block_forward(inputs, w_first, b_first, w_second, b_second, gain, shift):
    hidden_pre = product(inputs, w_first, plain_dims) + b_first
    hidden_act = jax.nn.silu(hidden_pre).astype(jnp.bfloat16)
    second = product(hidden_act, w_second, plain_dims) + b_second
    center = second - lax.optimization_barrier(jnp.mean(second, axis=-1, keepdims=True))
    scale_inv = lax.rsqrt(lax.optimization_barrier(jnp.mean(center * center, axis=-1, keepdims=True)) + epsilon)
    normed = center * scale_inv
    return (normed * gain + shift, (hidden_pre, hidden_act, normed, scale_inv))

def block_backward(inputs, saved, w_first, w_second, gain, upstream):
    hidden_pre, hidden_act, normed, scale_inv = saved
    d_gain = lax.optimization_barrier(jnp.sum(upstream * normed, axis=0))
    d_shift = lax.optimization_barrier(jnp.sum(upstream, axis=0))
    d_normed = upstream * gain
    d_second = scale_inv * (d_normed - lax.optimization_barrier(jnp.mean(d_normed, axis=-1, keepdims=True)) - normed * lax.optimization_barrier(jnp.mean(d_normed * normed, axis=-1, keepdims=True)))
    d_second_b = d_second.astype(jnp.bfloat16)
    g_second = product(hidden_act, d_second_b, rows_dims)
    g_bias_second = lax.optimization_barrier(jnp.sum(d_second, axis=0))
    d_act = product(d_second_b, w_second, back_dims)
    sigmoid_value = jax.nn.sigmoid(hidden_pre)
    d_pre = d_act * sigmoid_value * (1.0 + hidden_pre * (1.0 - sigmoid_value))
    d_pre_b = d_pre.astype(jnp.bfloat16)
    g_first = product(inputs, d_pre_b, rows_dims)
    g_bias_first = lax.optimization_barrier(jnp.sum(d_pre, axis=0))
    d_inputs = product(d_pre_b, w_first, back_dims)
    return (d_inputs, (g_first, g_bias_first, g_second, g_bias_second, d_gain, d_shift))

def global_ids(senders, receivers, send_list):
    part_index = jnp.arange(EDGES, dtype=jnp.int32) // EDGE_DEV
    slot = receivers - NODE_DEV
    left_part = jnp.clip(part_index - 1, 0, PARTS_SIZE - 1).astype(jnp.int32)
    right_part = jnp.clip(part_index + 1, 0, PARTS_SIZE - 1).astype(jnp.int32)
    left_slot = jnp.clip(slot, 0, BND - 1).astype(jnp.int32)
    right_slot = jnp.clip(slot - BND, 0, BND - 1).astype(jnp.int32)
    from_left = left_part * NODE_DEV + send_list[left_part, 1, left_slot]
    from_right = right_part * NODE_DEV + send_list[right_part, 0, right_slot]
    global_rcv = jnp.where(receivers < NODE_DEV, part_index * NODE_DEV + receivers, jnp.where(slot < BND, from_left, from_right))
    global_snd = part_index * NODE_DEV + senders
    return (global_snd.astype(jnp.int32), global_rcv.astype(jnp.int32))

def reference(node_in, edge_in, senders, receivers, send_list, w_edge_first, b_edge_first, w_edge_second, b_edge_second, edge_gain, edge_shift, w_node_first, b_node_first, w_node_second, b_node_second, node_gain, node_shift, node_cotangent, edge_cotangent):
    global_snd, global_rcv = global_ids(senders, receivers, send_list)
    node_outs, edge_outs, node_grads, edge_grads = ([], [], [], [])
    totals = None
    for sample_index in range(SAMPLES):
        node_rows = node_in[sample_index]
        edge_rows = edge_in[sample_index]
        edge_inputs = jnp.concatenate([edge_rows, node_rows[global_snd], node_rows[global_rcv]], axis=1)
        edge_update, edge_saved = block_forward(edge_inputs, w_edge_first, b_edge_first, w_edge_second, b_edge_second, edge_gain, edge_shift)
        edge_outs.append((edge_rows.astype(jnp.float32) + edge_update).astype(jnp.bfloat16))
        messages = edge_update.astype(jnp.bfloat16)
        aggregate = jax.ops.segment_sum(messages.astype(jnp.float32), global_rcv, num_segments=NODES)
        node_inputs = jnp.concatenate([node_rows, aggregate.astype(jnp.bfloat16)], axis=1)
        node_update, node_saved = block_forward(node_inputs, w_node_first, b_node_first, w_node_second, b_node_second, node_gain, node_shift)
        node_outs.append((node_rows.astype(jnp.float32) + node_update).astype(jnp.bfloat16))
        node_upstream = node_cotangent[sample_index].astype(jnp.float32)
        node_back, node_terms = block_backward(node_inputs, node_saved, w_node_first, w_node_second, node_gain, node_upstream)
        aggregate_grad = node_back[:, D:].astype(jnp.bfloat16)
        edge_upstream = edge_cotangent[sample_index].astype(jnp.float32) + aggregate_grad[global_rcv].astype(jnp.float32)
        edge_back, edge_terms = block_backward(edge_inputs, edge_saved, w_edge_first, w_edge_second, edge_gain, edge_upstream)
        edge_grads.append((edge_cotangent[sample_index].astype(jnp.float32) + edge_back[:, :D]).astype(jnp.bfloat16))
        sender_grad = edge_back[:, D:2 * D].astype(jnp.bfloat16).astype(jnp.float32)
        receiver_grad = edge_back[:, 2 * D:].astype(jnp.bfloat16).astype(jnp.float32)
        sender_sum = jax.ops.segment_sum(sender_grad, global_snd, num_segments=NODES)
        receiver_sum = jax.ops.segment_sum(receiver_grad, global_rcv, num_segments=NODES)
        node_grads.append((node_upstream + node_back[:, :D] + sender_sum + receiver_sum).astype(jnp.bfloat16))
        terms = edge_terms + node_terms
        totals = terms if totals is None else tuple((old + new for old, new in zip(totals, terms)))
    return (jnp.stack(node_outs), jnp.stack(edge_outs), jnp.stack(node_grads), jnp.stack(edge_grads), totals[0], totals[1], totals[2], totals[3], totals[4], totals[5], totals[6], totals[7], totals[8], totals[9], totals[10], totals[11])
```

```python
import jax
import jax.numpy as jnp
from jax import lax
from jax.experimental import pallas as pl
from jax.experimental.pallas import tpu as pltpu
from jax.sharding import PartitionSpec as P

epsilon = 1e-05
rows_dims = (((0,), (0,)), ((), ()))
back_dims = (((1,), (1,)), ((), ()))
f32 = jnp.float32
bf16 = jnp.bfloat16
lane = 128
edge_tile = 512
vmem_limit = 32 * 1024 * 1024
sum_rows = 16


def dot(left, right):
    return jnp.dot(left, right, preferred_element_type=f32)


def dot_rows(left, right):
    return lax.dot_general(left, right, rows_dims, preferred_element_type=f32)


def dot_back(left, right):
    return lax.dot_general(left, right, back_dims, preferred_element_type=f32)


def column_of(row):
    return jnp.broadcast_to(row, (lane, lane)).T


def hot_columns(ids, width):
    targets = lax.broadcasted_iota(jnp.int32, ids.shape, 1)
    parts = [
        jnp.where(ids == targets + at, 1.0, 0.0).astype(bf16) for at in range(0, width, lane)
    ]
    return jnp.concatenate(parts, axis=1)


def hot_rows(row, height):
    targets = lax.broadcasted_iota(jnp.int32, (height, lane), 0)
    return jnp.where(row == targets, 1.0, 0.0).astype(bf16)


def fold(ids, half):
    upper = ids >= half
    return upper, jnp.where(upper, ids - half, ids)


def side_by_side(rows):
    half = rows.shape[0] // 2
    return jnp.concatenate([rows[:half], rows[half:]], axis=1)


def pick(ids, table):
    half = table.shape[0]
    upper, low = fold(ids, half)
    both = dot(hot_columns(low, half), table)
    return jnp.where(upper, both[:, lane:], both[:, :lane])


def spread(ids_ref, first, count, half, ids, values):
    upper, unused = fold(ids, half)
    paired = jnp.concatenate(
        [jnp.where(upper, 0.0, values).astype(bf16), jnp.where(upper, values, 0.0).astype(bf16)],
        axis=1,
    )
    parts = []
    for k in range(count):
        row = ids_ref[pl.ds(first + k, 1), :]
        unused, low = fold(row, half)
        parts.append(hot_rows(low, half))
    return dot(jnp.concatenate(parts, axis=1), paired)


def sigmoid(z):
    return 0.5 * jnp.tanh(0.5 * z) + 0.5


def centred_second(w_ref, b_ref):
    w = w_ref[...].astype(f32)
    w = w - jnp.mean(w, axis=1, keepdims=True)
    high = w.astype(bf16)
    low = (w - high.astype(f32)).astype(bf16)
    b = b_ref[...]
    return jnp.concatenate([high, low], axis=1), b - jnp.mean(b, axis=1, keepdims=True)


def normed_of(act, w_pair, b_centred):
    both = dot(act, w_pair)
    center = both[:, :lane] + both[:, lane:] + b_centred
    scale_inv = lax.rsqrt(jnp.mean(center * center, axis=1, keepdims=True) + epsilon)
    return center * scale_inv, scale_inv


def back_norm(upstream, normed, scale_inv, gain):
    d_normed = upstream * gain
    return scale_inv * (
        d_normed
        - jnp.mean(d_normed, axis=1, keepdims=True)
        - normed * jnp.mean(d_normed * normed, axis=1, keepdims=True)
    )


def column_sum(values):
    return jnp.sum(values, axis=0, keepdims=True)


def fill_columns(ids_ref, out_ref):
    for k in range(ids_ref.shape[0]):
        out_ref[k * lane : (k + 1) * lane, :] = column_of(ids_ref[k : k + 1, :])


def rim_kernel(node_ref, list_ref, low_ref, high_ref):
    node = node_ref[...]
    for side, out_ref in ((0, low_ref), (1, high_ref)):
        hot = hot_columns(column_of(list_ref[side : side + 1, :]), node.shape[0])
        out_ref[...] = dot(hot, node).astype(bf16)


def edge_forward_kernel(
    node_ref,
    low_ref,
    high_ref,
    edge_ref,
    snd_ref,
    rcv_ref,
    w1_ref,
    b1_ref,
    w2_ref,
    b2_ref,
    gain_ref,
    shift_ref,
    out_ref,
    z_ref,
    agg_ref,
    agg_low_ref,
    agg_high_ref,
    snd_table,
    rcv_table,
    snd_column,
    rcv_column,
    w2_pair,
    total,
):
    nodes = node_ref.shape[0]
    rim = low_ref.shape[0]
    half = rcv_table.shape[0]
    w1_edge = w1_ref[:lane]
    b1 = b1_ref[...]
    gain = gain_ref[...]
    shift = shift_ref[...]
    snd_table[...] = side_by_side(dot(node_ref[...], w1_ref[lane : 2 * lane]).astype(bf16))
    extended = jnp.concatenate([node_ref[...], low_ref[...], high_ref[...]], axis=0)
    rcv_table[...] = side_by_side(dot(extended, w1_ref[2 * lane :]).astype(bf16))
    pair, b2 = centred_second(w2_ref, b2_ref)
    w2_pair[...] = pair
    fill_columns(snd_ref, snd_column)
    fill_columns(rcv_ref, rcv_column)
    total[...] = jnp.zeros_like(total)

    def tile(i, carry):
        rows = pl.ds(pl.multiple_of(i * edge_tile, edge_tile), edge_tile)
        x = edge_ref[rows, :]
        rcv = rcv_column[rows, :]
        z = dot(x, w1_edge) + b1
        z = z + pick(snd_column[rows, :], snd_table[...])
        z = z + pick(rcv, rcv_table[...])
        z_ref[rows, :] = z
        act = (z * sigmoid(z)).astype(bf16)
        normed, unused = normed_of(act, w2_pair[...], b2)
        update = normed * gain + shift
        out_ref[rows, :] = (x.astype(f32) + update).astype(bf16)
        total[...] += spread(rcv_ref, i * (edge_tile // lane), edge_tile // lane, half, rcv, update)
        return carry

    lax.fori_loop(0, edge_ref.shape[0] // edge_tile, tile, 0)
    agg_ref[:half, :] = total[:, :lane]
    agg_ref[half:, :] = total[: nodes - half, lane:]
    agg_low_ref[...] = total[nodes - half : nodes - half + rim, lane:].astype(bf16)
    agg_high_ref[...] = total[nodes - half + rim :, lane:].astype(bf16)


def node_kernel(
    node_ref,
    agg_ref,
    low_ref,
    high_ref,
    list_ref,
    w1_ref,
    b1_ref,
    w2_ref,
    b2_ref,
    gain_ref,
    shift_ref,
    cot_ref,
    out_ref,
    base_ref,
    dagg_ref,
    rim_low_ref,
    rim_high_ref,
    grads_ref,
):
    nodes = node_ref.shape[0]
    node = node_ref[...]
    hot = jnp.concatenate(
        [hot_rows(list_ref[0:1, :], nodes), hot_rows(list_ref[1:2, :], nodes)], axis=1
    )
    returned = jnp.concatenate([low_ref[...], high_ref[...]], axis=0)
    agg = (agg_ref[...] + dot(hot, returned)).astype(bf16)
    x = jnp.concatenate([node, agg], axis=1)
    w1 = w1_ref[...]
    z = dot(x, w1) + b1_ref[...]
    sig = sigmoid(z)
    act = (z * sig).astype(bf16)
    pair, b2 = centred_second(w2_ref, b2_ref)
    normed, scale_inv = normed_of(act, pair, b2)
    gain = gain_ref[...]
    out_ref[...] = (node.astype(f32) + normed * gain + shift_ref[...]).astype(bf16)
    upstream = cot_ref[...].astype(f32)
    dz2 = back_norm(upstream, normed, scale_inv, gain)
    dz2b = dz2.astype(bf16)
    da = dot_back(dz2b, w2_ref[...])
    dz1 = da * sig * (1.0 + z * (1.0 - sig))
    dz1b = dz1.astype(bf16)
    dx = dot_back(dz1b, w1)
    base_ref[...] = upstream + dx[:, :lane]
    dagg = dx[:, lane:].astype(bf16)
    dagg_ref[...] = dagg
    for side, rim_ref in ((0, rim_low_ref), (1, rim_high_ref)):
        picked = hot_columns(column_of(list_ref[side : side + 1, :]), nodes)
        rim_ref[...] = dot(picked, dagg).astype(bf16)
    first = 2 * lane
    second = first + lane
    grads_ref[:first, :] = dot_rows(x, dz1b).astype(bf16)
    grads_ref[first:second, :] = dot_rows(act, dz2b).astype(bf16)
    sums = [column_sum(dz1), column_sum(dz2), column_sum(upstream * normed), column_sum(upstream)]
    sums.append(jnp.zeros((sum_rows - len(sums), lane), f32))
    grads_ref[second:, :] = jnp.concatenate(sums, axis=0).astype(bf16)


def edge_backward_kernel(
    z_ref,
    cot_ref,
    edge_ref,
    snd_ref,
    rcv_ref,
    node_ref,
    low_ref,
    high_ref,
    dagg_ref,
    dagg_low_ref,
    dagg_high_ref,
    base_ref,
    w1_ref,
    w2_ref,
    b2_ref,
    gain_ref,
    node_grads_ref,
    grad_ref,
    acc_ref,
    back_low_ref,
    back_high_ref,
    grads_ref,
    table,
    snd_column,
    rcv_column,
    w2_pair,
    snd_total,
    rcv_total,
    squares,
    sums,
):
    nodes = node_ref.shape[0]
    rim = low_ref.shape[0]
    snd_half = snd_total.shape[0]
    rcv_half = rcv_total.shape[0]
    w1_edge = w1_ref[:lane]
    w2 = w2_ref[...]
    gain = gain_ref[...]
    table[...] = side_by_side(
        jnp.concatenate([dagg_ref[...], dagg_low_ref[...], dagg_high_ref[...]], axis=0)
    )
    pair, b2 = centred_second(w2_ref, b2_ref)
    w2_pair[...] = pair
    fill_columns(snd_ref, snd_column)
    fill_columns(rcv_ref, rcv_column)
    snd_total[...] = jnp.zeros_like(snd_total)
    rcv_total[...] = jnp.zeros_like(rcv_total)
    squares[...] = jnp.zeros_like(squares)
    sums[...] = jnp.zeros_like(sums)

    def tile(i, carry):
        rows = pl.ds(pl.multiple_of(i * edge_tile, edge_tile), edge_tile)
        chunk = edge_tile // lane
        rcv = rcv_column[rows, :]
        snd = snd_column[rows, :]
        x = edge_ref[rows, :]
        z = z_ref[rows, :]
        cot = cot_ref[rows, :].astype(f32)
        upstream = cot + pick(rcv, table[...])
        sig = sigmoid(z)
        act = (z * sig).astype(bf16)
        normed, scale_inv = normed_of(act, w2_pair[...], b2)
        dz2 = back_norm(upstream, normed, scale_inv, gain)
        dz2b = dz2.astype(bf16)
        da = dot_back(dz2b, w2)
        dz1 = da * sig * (1.0 + z * (1.0 - sig))
        dz1b = dz1.astype(bf16)
        grad_ref[rows, :] = (cot + dot_back(dz1b, w1_edge)).astype(bf16)
        squares[:lane, :] += dot_rows(x, dz1b)
        squares[lane:, :] += dot_rows(act, dz2b)
        sums[0:1, :] += column_sum(dz1)
        sums[1:2, :] += column_sum(dz2)
        sums[2:3, :] += column_sum(upstream * normed)
        sums[3:4, :] += column_sum(upstream)
        snd_total[...] += spread(snd_ref, i * chunk, chunk, snd_half, snd, dz1)
        rcv_total[...] += spread(rcv_ref, i * chunk, chunk, rcv_half, rcv, dz1)
        return carry

    lax.fori_loop(0, edge_ref.shape[0] // edge_tile, tile, 0)
    snd_sum = jnp.concatenate([snd_total[:, :lane], snd_total[:, lane:]], axis=0).astype(bf16)
    rcv_sum = jnp.concatenate([rcv_total[:, :lane], rcv_total[:, lane:]], axis=0).astype(bf16)
    w1_snd = w1_ref[lane : 2 * lane]
    w1_rcv = w1_ref[2 * lane :]
    acc_ref[...] = base_ref[...] + dot_back(snd_sum, w1_snd) + dot_back(rcv_sum[:nodes], w1_rcv)
    back = dot_back(rcv_sum[nodes:], w1_rcv).astype(bf16)
    back_low_ref[...] = back[:rim]
    back_high_ref[...] = back[rim:]
    extended = jnp.concatenate([node_ref[...], low_ref[...], high_ref[...]], axis=0)
    grads_ref[:lane, :] = squares[:lane, :].astype(bf16)
    grads_ref[lane : 2 * lane, :] = dot_rows(node_ref[...], snd_sum).astype(bf16)
    grads_ref[2 * lane : 3 * lane, :] = dot_rows(extended, rcv_sum).astype(bf16)
    grads_ref[3 * lane : 4 * lane, :] = squares[lane:, :].astype(bf16)
    node_rows = node_grads_ref.shape[0] - sum_rows
    grads_ref[4 * lane : 4 * lane + node_rows, :] = node_grads_ref[:node_rows, :]
    node_sums = node_grads_ref[node_rows:, :].astype(f32)
    grads_ref[4 * lane + node_rows :, :] = jnp.concatenate(
        [sums[0:4, :], node_sums[0:4, :], jnp.zeros((sum_rows - 8, lane), f32)], axis=0
    ).astype(bf16)


def node_grad_kernel(acc_ref, low_ref, high_ref, list_ref, out_ref):
    nodes = acc_ref.shape[0]
    hot = jnp.concatenate(
        [hot_rows(list_ref[0:1, :], nodes), hot_rows(list_ref[1:2, :], nodes)], axis=1
    )
    returned = jnp.concatenate([low_ref[...], high_ref[...]], axis=0)
    out_ref[...] = (acc_ref[...] + dot(hot, returned)).astype(bf16)


def finish_kernel(own_ref, other_ref, *out_refs):
    total = own_ref[...].astype(f32) + other_ref[...].astype(f32)
    at = 0
    for out_ref in out_refs[:4]:
        out_ref[...] = total[at : at + out_ref.shape[0]]
        at += out_ref.shape[0]
    for k, out_ref in enumerate(out_refs[4:]):
        out_ref[...] = total[at + k : at + k + 1]


def call(kernel, outs, scratch, *operands, flops=0):
    held = sum(x.size * x.dtype.itemsize for x in operands)
    return pl.pallas_call(
        kernel,
        out_shape=[jax.ShapeDtypeStruct(shape, dtype) for shape, dtype in outs],
        in_specs=[pl.BlockSpec(memory_space=pltpu.VMEM)] * len(operands),
        out_specs=[pl.BlockSpec(memory_space=pltpu.VMEM)] * len(outs),
        scratch_shapes=[pltpu.VMEM(shape, dtype) for shape, dtype in scratch],
        compiler_params=pltpu.CompilerParams(vmem_limit_bytes=vmem_limit),
        cost_estimate=pl.CostEstimate(flops=flops, bytes_accessed=held, transcendentals=0),
    )(*operands)


def neighbours(low, high):
    axis = ("dom", "sub")
    count = lax.axis_size("dom") * lax.axis_size("sub")
    forward = [(i, i + 1) for i in range(count - 1)]
    backward = [(target, source) for source, target in forward]
    return lax.ppermute(high, axis, forward), lax.ppermute(low, axis, backward)


def sum_rounds():
    for axis in ("sub", "sample", "dom"):
        count = lax.axis_size(axis)
        step = 1
        while step < count:
            yield axis, [(i, i ^ step) for i in range(count)]
            step *= 2


def on_device(
    node_in,
    edge_in,
    senders,
    receivers,
    send_list,
    w_edge_first,
    b_edge_first,
    w_edge_second,
    b_edge_second,
    edge_gain,
    edge_shift,
    w_node_first,
    b_node_first,
    w_node_second,
    b_node_second,
    node_gain,
    node_shift,
    node_cotangent,
    edge_cotangent,
):
    node = node_in[0]
    edge = edge_in[0]
    lists = send_list[0]
    nodes = node.shape[0]
    edges = edge.shape[0]
    rim = lists.shape[1]
    snd = senders.reshape(edges // lane, lane)
    rcv = receivers.reshape(edges // lane, lane)
    row = lambda vector: vector.reshape(1, vector.shape[0])
    rim_shape = ((rim, lane), bf16)
    snd_half = nodes // 2
    rcv_half = (nodes + 2 * rim) // 2

    rim_low, rim_high = call(rim_kernel, [rim_shape] * 2, [], node, lists)
    low, high = neighbours(rim_low, rim_high)
    edge_out, z, agg, agg_low, agg_high = call(
        edge_forward_kernel,
        [((edges, lane), bf16), ((edges, lane), f32), ((nodes, lane), f32), rim_shape, rim_shape],
        [
            ((snd_half, 2 * lane), bf16),
            ((rcv_half, 2 * lane), bf16),
            ((edges, lane), jnp.int32),
            ((edges, lane), jnp.int32),
            ((lane, 2 * lane), bf16),
            ((rcv_half, 2 * lane), f32),
        ],
        node,
        low,
        high,
        edge,
        snd,
        rcv,
        w_edge_first,
        row(b_edge_first),
        w_edge_second,
        row(b_edge_second),
        row(edge_gain),
        row(edge_shift),
    )
    back_low, back_high = neighbours(agg_low, agg_high)
    node_out, base, dagg, dagg_rim_low, dagg_rim_high, node_grads = call(
        node_kernel,
        [
            ((nodes, lane), bf16),
            ((nodes, lane), f32),
            ((nodes, lane), bf16),
            rim_shape,
            rim_shape,
            ((3 * lane + sum_rows, lane), bf16),
        ],
        [],
        node,
        agg,
        back_low,
        back_high,
        lists,
        w_node_first,
        row(b_node_first),
        w_node_second,
        row(b_node_second),
        row(node_gain),
        row(node_shift),
        node_cotangent[0],
    )
    dagg_low, dagg_high = neighbours(dagg_rim_low, dagg_rim_high)
    edge_grad, acc, grad_low, grad_high, grads = call(
        edge_backward_kernel,
        [
            ((edges, lane), bf16),
            ((nodes, lane), f32),
            rim_shape,
            rim_shape,
            ((7 * lane + sum_rows, lane), bf16),
        ],
        [
            ((rcv_half, 2 * lane), bf16),
            ((edges, lane), jnp.int32),
            ((edges, lane), jnp.int32),
            ((lane, 2 * lane), bf16),
            ((snd_half, 2 * lane), f32),
            ((rcv_half, 2 * lane), f32),
            ((2 * lane, lane), f32),
            ((8, lane), f32),
        ],
        z,
        edge_cotangent[0],
        edge,
        snd,
        rcv,
        node,
        low,
        high,
        dagg,
        dagg_low,
        dagg_high,
        base,
        w_edge_first,
        w_edge_second,
        row(b_edge_second),
        row(edge_gain),
        node_grads,
    )
    returned_low, returned_high = neighbours(grad_low, grad_high)
    (node_grad,) = call(
        node_grad_kernel, [((nodes, lane), bf16)], [], acc, returned_low, returned_high, lists
    )
    rounds = list(sum_rounds())
    for axis, pairs in rounds[:-1]:
        other = lax.ppermute(grads, axis, pairs)
        grads = (grads.astype(f32) + other.astype(f32)).astype(bf16)
    axis, pairs = rounds[-1]
    other = lax.ppermute(grads, axis, pairs)
    matrices = [3 * lane, lane, 2 * lane, lane]
    totals = call(
        finish_kernel,
        [((height, lane), f32) for height in matrices] + [((1, lane), f32)] * 8,
        [],
        grads,
        other,
    )
    flat = [total.reshape(lane) for total in totals[4:]]
    return (
        node_out[None],
        edge_out[None],
        node_grad[None],
        edge_grad[None],
        totals[0],
        flat[0],
        totals[1],
        flat[1],
        flat[2],
        flat[3],
        totals[2],
        flat[4],
        totals[3],
        flat[5],
        flat[6],
        flat[7],
    )


def solution(mesh):
    node_spec = P(("groups", "sample"), ("dom", "sub"), None)
    ids_spec = P(("dom", "sub"))
    return jax.shard_map(
        on_device,
        mesh=mesh,
        in_specs=(
            (node_spec, node_spec, ids_spec, ids_spec, P(("dom", "sub"), None, None))
            + (P(),) * 12
            + (node_spec, node_spec)
        ),
        out_specs=(
            (node_spec,) * 4
            + (P("groups", None), P("groups"), P("groups", None), P("groups"), P("groups"), P("groups"))
            * 2
        ),
        check_vma=False,
    )
```

```python
import functools
import math

import jax
import jax.numpy as jnp
from jax import lax
from jax.experimental import pallas as pl
from jax.experimental.pallas import tpu as pltpu
from jax.sharding import PartitionSpec as P

epsilon = 1e-05
rows_dims = (((0,), (0,)), ((), ()))
back_dims = (((1,), (1,)), ((), ()))
f32 = jnp.float32
bf16 = jnp.bfloat16
lane = 128
edge_tile = 512
vmem_limit = 32 * 1024 * 1024
sum_rows = 16
chain = ("dom", "sub")


def dot(left, right):
    return jnp.dot(left, right, preferred_element_type=f32)


def dot_rows(left, right):
    return lax.dot_general(left, right, rows_dims, preferred_element_type=f32)


def dot_back(left, right):
    return lax.dot_general(left, right, back_dims, preferred_element_type=f32)


def column_of(row):
    return jnp.broadcast_to(row, (lane, lane)).T


def hot_columns(ids, width):
    targets = lax.broadcasted_iota(jnp.int32, ids.shape, 1)
    parts = [
        jnp.where(ids == targets + at, 1.0, 0.0).astype(bf16) for at in range(0, width, lane)
    ]
    return jnp.concatenate(parts, axis=1)


def hot_rows(row, height):
    targets = lax.broadcasted_iota(jnp.int32, (height, lane), 0)
    return jnp.where(row == targets, 1.0, 0.0).astype(bf16)


def fold(ids, half):
    upper = ids >= half
    return upper, jnp.where(upper, ids - half, ids)


def side_by_side(rows):
    half = rows.shape[0] // 2
    return jnp.concatenate([rows[:half], rows[half:]], axis=1)


def pick(ids, table):
    half = table.shape[0]
    upper, low = fold(ids, half)
    both = dot(hot_columns(low, half), table)
    return jnp.where(upper, both[:, lane:], both[:, :lane])


def spread(ids_ref, first, count, half, ids, values):
    upper, unused = fold(ids, half)
    paired = jnp.concatenate(
        [jnp.where(upper, 0.0, values).astype(bf16), jnp.where(upper, values, 0.0).astype(bf16)],
        axis=1,
    )
    parts = []
    for k in range(count):
        row = ids_ref[pl.ds(first + k, 1), :]
        unused, low = fold(row, half)
        parts.append(hot_rows(low, half))
    return dot(jnp.concatenate(parts, axis=1), paired)


def sigmoid(z):
    return 0.5 * jnp.tanh(0.5 * z) + 0.5


def vector(vectors_ref, k):
    return vectors_ref[k : k + 1, :]


def centred_second(w, b):
    w = w.astype(f32)
    w = w - jnp.mean(w, axis=1, keepdims=True)
    high = w.astype(bf16)
    low = (w - high.astype(f32)).astype(bf16)
    return jnp.concatenate([high, low], axis=1), b - jnp.mean(b, axis=1, keepdims=True)


def normed_of(act, w_pair, b_centred):
    both = dot(act, w_pair)
    center = both[:, :lane] + both[:, lane:] + b_centred
    scale_inv = lax.rsqrt(jnp.mean(center * center, axis=1, keepdims=True) + epsilon)
    return center * scale_inv, scale_inv


def back_norm(upstream, normed, scale_inv, gain):
    d_normed = upstream * gain
    return scale_inv * (
        d_normed
        - jnp.mean(d_normed, axis=1, keepdims=True)
        - normed * jnp.mean(d_normed * normed, axis=1, keepdims=True)
    )


def column_sum(values):
    return jnp.sum(values, axis=0, keepdims=True)


def parity_of_place():
    return lax.axis_index(chain) % 2


def rim_kernel(node_ref, ids_ref, near_ref, far_ref):
    parity = parity_of_place()
    node = node_ref[...]
    first = ids_ref.shape[0] - 2
    for side, out_ref in ((1 - parity, near_ref), (parity, far_ref)):
        hot = hot_columns(column_of(ids_ref[pl.ds(first + side, 1), :]), node.shape[0])
        out_ref[...] = dot(hot, node).astype(bf16)


def prepare_kernel(
    ids_ref,
    node_ref,
    weights_ref,
    edge_ref,
    edge_cot_ref,
    node_cot_ref,
    edge_out,
    edge_cot_out,
    node_cot_out,
    snd_column,
    rcv_column,
    snd_table,
    rcv_local,
    sems,
):
    copies = [
        pltpu.make_async_copy(source, target, sems.at[k])
        for k, (source, target) in enumerate(
            ((edge_ref, edge_out), (edge_cot_ref, edge_cot_out), (node_cot_ref, node_cot_out))
        )
    ]
    for copy in copies:
        copy.start()
    chunks = snd_column.shape[0] // lane
    for k in range(chunks):
        at = slice(k * lane, (k + 1) * lane)
        snd_column[at, :] = column_of(ids_ref[k : k + 1, :])
        rcv_column[at, :] = column_of(ids_ref[chunks + k : chunks + k + 1, :])
    node = node_ref[...]
    snd_table[...] = side_by_side(dot(node, weights_ref[lane : 2 * lane]).astype(bf16))
    rcv_local[...] = dot(node, weights_ref[2 * lane : 3 * lane]).astype(bf16)
    for copy in copies:
        copy.wait()


def edge_forward_kernel(
    near_ref,
    far_ref,
    edge_ref,
    ids_ref,
    weights_ref,
    vectors_ref,
    snd_column,
    rcv_column,
    snd_table,
    rcv_local,
    out_ref,
    z_ref,
    agg_ref,
    agg_near_ref,
    agg_far_ref,
    halo,
    rcv_table,
    w2_pair,
    total,
):
    nodes = rcv_local.shape[0]
    rim = near_ref.shape[0]
    half = rcv_table.shape[0]
    parity = parity_of_place()
    near_at = pl.multiple_of((1 - parity) * rim, rim)
    far_at = pl.multiple_of(parity * rim, rim)
    w1_edge = weights_ref[:lane]
    w1_rcv = weights_ref[2 * lane : 3 * lane]
    b1, gain, shift = vector(vectors_ref, 0), vector(vectors_ref, 2), vector(vectors_ref, 3)
    halo[pl.ds(near_at, rim), :] = dot(near_ref[...], w1_rcv).astype(bf16)
    halo[pl.ds(far_at, rim), :] = dot(far_ref[...], w1_rcv).astype(bf16)
    rcv_table[:, :lane] = rcv_local[:half, :]
    rcv_table[: nodes - half, lane:] = rcv_local[half:, :]
    rcv_table[nodes - half :, lane:] = halo[...]
    pair, b2 = centred_second(weights_ref[3 * lane : 4 * lane], vector(vectors_ref, 1))
    w2_pair[...] = pair
    total[...] = jnp.zeros_like(total)

    def tile(i, carry):
        rows = pl.ds(pl.multiple_of(i * edge_tile, edge_tile), edge_tile)
        x = edge_ref[rows, :]
        rcv = rcv_column[rows, :]
        z = dot(x, w1_edge) + b1
        z = z + pick(snd_column[rows, :], snd_table[...])
        z = z + pick(rcv, rcv_table[...])
        z_ref[rows, :] = z
        act = (z * sigmoid(z)).astype(bf16)
        normed, unused = normed_of(act, w2_pair[...], b2)
        update = normed * gain + shift
        out_ref[rows, :] = (x.astype(f32) + update).astype(bf16)
        first = (rcv_column.shape[0] + i * edge_tile) // lane
        total[...] += spread(ids_ref, first, edge_tile // lane, half, rcv, update)
        return carry

    lax.fori_loop(0, edge_ref.shape[0] // edge_tile, tile, 0)
    agg_ref[:half, :] = total[:, :lane]
    agg_ref[half:, :] = total[: nodes - half, lane:]
    agg_near_ref[...] = total[pl.ds(nodes - half + near_at, rim), lane:].astype(bf16)
    agg_far_ref[...] = total[pl.ds(nodes - half + far_at, rim), lane:].astype(bf16)


def hot_lists(ids_ref, nodes):
    parity = parity_of_place()
    first = ids_ref.shape[0] - 2
    near = ids_ref[pl.ds(first + 1 - parity, 1), :]
    far = ids_ref[pl.ds(first + parity, 1), :]
    return jnp.concatenate([hot_rows(near, nodes), hot_rows(far, nodes)], axis=1)


def node_kernel(
    node_ref,
    agg_ref,
    near_ref,
    far_ref,
    ids_ref,
    weights_ref,
    vectors_ref,
    cot_ref,
    out_ref,
    base_ref,
    dagg_ref,
    rim_near_ref,
    rim_far_ref,
    grads_ref,
):
    nodes = node_ref.shape[0]
    node = node_ref[...]
    returned = jnp.concatenate([near_ref[...], far_ref[...]], axis=0)
    agg = (agg_ref[...] + dot(hot_lists(ids_ref, nodes), returned)).astype(bf16)
    x = jnp.concatenate([node, agg], axis=1)
    w1 = weights_ref[4 * lane : 6 * lane]
    w2 = weights_ref[6 * lane :]
    z = dot(x, w1) + vector(vectors_ref, 4)
    sig = sigmoid(z)
    act = (z * sig).astype(bf16)
    pair, b2 = centred_second(w2, vector(vectors_ref, 5))
    normed, scale_inv = normed_of(act, pair, b2)
    gain = vector(vectors_ref, 6)
    out_ref[...] = (node.astype(f32) + normed * gain + vector(vectors_ref, 7)).astype(bf16)
    upstream = cot_ref[...].astype(f32)
    dz2 = back_norm(upstream, normed, scale_inv, gain)
    dz2b = dz2.astype(bf16)
    da = dot_back(dz2b, w2)
    dz1 = da * sig * (1.0 + z * (1.0 - sig))
    dz1b = dz1.astype(bf16)
    dx = dot_back(dz1b, w1)
    base_ref[...] = upstream + dx[:, :lane]
    dagg = dx[:, lane:].astype(bf16)
    dagg_ref[...] = dagg
    parity = parity_of_place()
    first = ids_ref.shape[0] - 2
    for side, rim_ref in ((1 - parity, rim_near_ref), (parity, rim_far_ref)):
        picked = hot_columns(column_of(ids_ref[pl.ds(first + side, 1), :]), nodes)
        rim_ref[...] = dot(picked, dagg).astype(bf16)
    first = 2 * lane
    second = first + lane
    grads_ref[:first, :] = dot_rows(x, dz1b).astype(bf16)
    grads_ref[first:second, :] = dot_rows(act, dz2b).astype(bf16)
    sums = [column_sum(dz1), column_sum(dz2), column_sum(upstream * normed), column_sum(upstream)]
    sums.append(jnp.zeros((sum_rows - len(sums), lane), f32))
    grads_ref[second:, :] = jnp.concatenate(sums, axis=0).astype(bf16)


def edge_backward_kernel(
    z_ref,
    cot_ref,
    edge_ref,
    ids_ref,
    node_ref,
    near_ref,
    far_ref,
    dagg_ref,
    dagg_near_ref,
    dagg_far_ref,
    base_ref,
    weights_ref,
    vectors_ref,
    node_grads_ref,
    snd_column,
    rcv_column,
    grad_ref,
    acc_ref,
    back_near_ref,
    back_far_ref,
    grads_ref,
    halo,
    table,
    w2_pair,
    snd_total,
    rcv_total,
    squares,
    sums,
):
    nodes = node_ref.shape[0]
    rim = near_ref.shape[0]
    snd_half = snd_total.shape[0]
    rcv_half = rcv_total.shape[0]
    parity = parity_of_place()
    near_at = pl.multiple_of((1 - parity) * rim, rim)
    far_at = pl.multiple_of(parity * rim, rim)
    w1_edge = weights_ref[:lane]
    w2 = weights_ref[3 * lane : 4 * lane]
    gain = vector(vectors_ref, 2)
    table[:, :lane] = dagg_ref[:rcv_half, :]
    table[: nodes - rcv_half, lane:] = dagg_ref[rcv_half:, :]
    table[pl.ds(nodes - rcv_half + near_at, rim), lane:] = dagg_near_ref[...]
    table[pl.ds(nodes - rcv_half + far_at, rim), lane:] = dagg_far_ref[...]
    halo[pl.ds(near_at, rim), :] = near_ref[...]
    halo[pl.ds(far_at, rim), :] = far_ref[...]
    pair, b2 = centred_second(w2, vector(vectors_ref, 1))
    w2_pair[...] = pair
    snd_total[...] = jnp.zeros_like(snd_total)
    rcv_total[...] = jnp.zeros_like(rcv_total)
    squares[...] = jnp.zeros_like(squares)
    sums[...] = jnp.zeros_like(sums)

    def tile(i, carry):
        rows = pl.ds(pl.multiple_of(i * edge_tile, edge_tile), edge_tile)
        chunk = edge_tile // lane
        rcv = rcv_column[rows, :]
        snd = snd_column[rows, :]
        x = edge_ref[rows, :]
        z = z_ref[rows, :]
        cot = cot_ref[rows, :].astype(f32)
        upstream = cot + pick(rcv, table[...])
        sig = sigmoid(z)
        act = (z * sig).astype(bf16)
        normed, scale_inv = normed_of(act, w2_pair[...], b2)
        dz2 = back_norm(upstream, normed, scale_inv, gain)
        dz2b = dz2.astype(bf16)
        da = dot_back(dz2b, w2)
        dz1 = da * sig * (1.0 + z * (1.0 - sig))
        dz1b = dz1.astype(bf16)
        grad_ref[rows, :] = (cot + dot_back(dz1b, w1_edge)).astype(bf16)
        squares[:lane, :] += dot_rows(x, dz1b)
        squares[lane:, :] += dot_rows(act, dz2b)
        sums[0:1, :] += column_sum(dz1)
        sums[1:2, :] += column_sum(dz2)
        sums[2:3, :] += column_sum(upstream * normed)
        sums[3:4, :] += column_sum(upstream)
        first = rcv_column.shape[0] // lane + i * chunk
        snd_total[...] += spread(ids_ref, i * chunk, chunk, snd_half, snd, dz1)
        rcv_total[...] += spread(ids_ref, first, chunk, rcv_half, rcv, dz1)
        return carry

    lax.fori_loop(0, edge_ref.shape[0] // edge_tile, tile, 0)
    snd_sum = jnp.concatenate([snd_total[:, :lane], snd_total[:, lane:]], axis=0).astype(bf16)
    rcv_sum = jnp.concatenate([rcv_total[:, :lane], rcv_total[:, lane:]], axis=0).astype(bf16)
    w1_snd = weights_ref[lane : 2 * lane]
    w1_rcv = weights_ref[2 * lane : 3 * lane]
    acc_ref[...] = base_ref[...] + dot_back(snd_sum, w1_snd) + dot_back(rcv_sum[:nodes], w1_rcv)
    for at, back_ref in ((near_at, back_near_ref), (far_at, back_far_ref)):
        returned = rcv_total[pl.ds(nodes - rcv_half + at, rim), lane:].astype(bf16)
        back_ref[...] = dot_back(returned, w1_rcv).astype(bf16)
    extended = jnp.concatenate([node_ref[...], halo[...]], axis=0)
    grads_ref[:lane, :] = squares[:lane, :].astype(bf16)
    grads_ref[lane : 2 * lane, :] = dot_rows(node_ref[...], snd_sum).astype(bf16)
    grads_ref[2 * lane : 3 * lane, :] = dot_rows(extended, rcv_sum).astype(bf16)
    grads_ref[3 * lane : 4 * lane, :] = squares[lane:, :].astype(bf16)
    node_rows = node_grads_ref.shape[0] - sum_rows
    grads_ref[4 * lane : 4 * lane + node_rows, :] = node_grads_ref[:node_rows, :]
    node_sums = node_grads_ref[node_rows:, :].astype(f32)
    last = 4 * lane + node_rows
    grads_ref[last : last + sum_rows, :] = jnp.concatenate(
        [sums[0:4, :], node_sums[0:4, :], jnp.zeros((sum_rows - 8, lane), f32)], axis=0
    ).astype(bf16)
    if last + sum_rows < grads_ref.shape[0]:
        grads_ref[last + sum_rows :, :] = jnp.zeros(
            (grads_ref.shape[0] - last - sum_rows, lane), bf16
        )


def node_grad_kernel(acc_ref, near_ref, far_ref, ids_ref, out_ref):
    returned = jnp.concatenate([near_ref[...], far_ref[...]], axis=0)
    hot = hot_lists(ids_ref, acc_ref.shape[0])
    out_ref[...] = (acc_ref[...] + dot(hot, returned)).astype(bf16)


def share_kernel(parts_ref, out_ref):
    count = parts_ref.shape[0]
    total = parts_ref[0].astype(f32)
    for k in range(1, count):
        total = total + parts_ref[k].astype(f32)
    total = total.astype(bf16)
    for k in range(count):
        out_ref[k] = total


def finish_kernel(total_ref, *out_refs):
    at = 0
    for out_ref in out_refs[:4]:
        out_ref[...] = total_ref[at : at + out_ref.shape[0], :].astype(f32)
        at += out_ref.shape[0]
    last = total_ref[at : at + sum_rows, :].astype(f32)
    for k, out_ref in enumerate(out_refs[4:]):
        out_ref[...] = last[k : k + 1]


def call(kernel, outs, scratch, *operands, anywhere=0, sems=0):
    moved = sum(x.size * x.dtype.itemsize for x in operands)
    inside = [pl.BlockSpec(memory_space=pltpu.VMEM)] * (len(operands) - anywhere)
    outside = [pl.BlockSpec(memory_space=pl.ANY)] * anywhere
    scratch_shapes = [pltpu.VMEM(shape, dtype) for shape, dtype in scratch]
    if sems:
        scratch_shapes.append(pltpu.SemaphoreType.DMA((sems,)))
    return pl.pallas_call(
        kernel,
        out_shape=[jax.ShapeDtypeStruct(shape, dtype) for shape, dtype in outs],
        in_specs=inside + outside,
        out_specs=[pl.BlockSpec(memory_space=pltpu.VMEM)] * len(outs),
        scratch_shapes=scratch_shapes,
        compiler_params=pltpu.CompilerParams(vmem_limit_bytes=vmem_limit),
        cost_estimate=pl.CostEstimate(flops=0, bytes_accessed=moved, transcendentals=0),
    )(*operands)


def swap(near, far):
    count = lax.axis_size("dom") * lax.axis_size("sub")
    outer = [(i, i + 1) for i in range(1, count - 1, 2)]
    inner = [(i, i + 1) for i in range(0, count - 1, 2)]
    outer += [(target, source) for source, target in outer]
    inner += [(target, source) for source, target in inner]
    far = lax.ppermute(far, chain, outer)
    return lax.ppermute(near, chain, inner), far


def on_device(
    node_in,
    edge_in,
    senders,
    receivers,
    send_list,
    w_edge_first,
    b_edge_first,
    w_edge_second,
    b_edge_second,
    edge_gain,
    edge_shift,
    w_node_first,
    b_node_first,
    w_node_second,
    b_node_second,
    node_gain,
    node_shift,
    node_cotangent,
    edge_cotangent,
):
    node = node_in[0]
    edge = edge_in[0]
    nodes = node.shape[0]
    edges = edge.shape[0]
    rim = send_list.shape[2]
    rim_shape = ((rim, lane), bf16)
    snd_half = nodes // 2
    rcv_half = (nodes + 2 * rim) // 2
    members = ("dom", "sample", "sub")
    sharers = math.prod(lax.axis_size(axis) for axis in members)
    grad_rows = 7 * lane + sum_rows
    share = -(-grad_rows // (sharers * sum_rows)) * sum_rows
    ids = jnp.concatenate([senders, receivers, send_list.reshape(2 * rim)]).reshape(-1, lane)
    weights = jnp.concatenate([w_edge_first, w_edge_second, w_node_first, w_node_second], axis=0)
    vectors = jnp.stack(
        [
            b_edge_first,
            b_edge_second,
            edge_gain,
            edge_shift,
            b_node_first,
            b_node_second,
            node_gain,
            node_shift,
        ]
    )

    rim_near, rim_far = call(rim_kernel, [rim_shape, rim_shape], [], node, ids)
    near, far = swap(rim_near, rim_far)
    edge, edge_cot, node_cot, snd_column, rcv_column, snd_table, rcv_local = call(
        prepare_kernel,
        [
            ((edges, lane), bf16),
            ((edges, lane), bf16),
            ((nodes, lane), bf16),
            ((edges, lane), jnp.int32),
            ((edges, lane), jnp.int32),
            ((snd_half, 2 * lane), bf16),
            ((nodes, lane), bf16),
        ],
        [],
        ids,
        node,
        weights,
        edge,
        edge_cotangent[0],
        node_cotangent[0],
        anywhere=3,
        sems=3,
    )
    edge_out, z, agg, agg_near, agg_far = call(
        edge_forward_kernel,
        [((edges, lane), bf16), ((edges, lane), f32), ((nodes, lane), f32), rim_shape, rim_shape],
        [
            ((2 * rim, lane), bf16),
            ((rcv_half, 2 * lane), bf16),
            ((lane, 2 * lane), bf16),
            ((rcv_half, 2 * lane), f32),
        ],
        near,
        far,
        edge,
        ids,
        weights,
        vectors,
        snd_column,
        rcv_column,
        snd_table,
        rcv_local,
    )
    back_near, back_far = swap(agg_near, agg_far)
    node_out, base, dagg, dagg_rim_near, dagg_rim_far, node_grads = call(
        node_kernel,
        [
            ((nodes, lane), bf16),
            ((nodes, lane), f32),
            ((nodes, lane), bf16),
            rim_shape,
            rim_shape,
            ((3 * lane + sum_rows, lane), bf16),
        ],
        [],
        node,
        agg,
        back_near,
        back_far,
        ids,
        weights,
        vectors,
        node_cot,
    )
    dagg_near, dagg_far = swap(dagg_rim_near, dagg_rim_far)
    edge_grad, acc, grad_near, grad_far, grads = call(
        edge_backward_kernel,
        [
            ((edges, lane), bf16),
            ((nodes, lane), f32),
            rim_shape,
            rim_shape,
            ((sharers * share, lane), bf16),
        ],
        [
            ((2 * rim, lane), bf16),
            ((rcv_half, 2 * lane), bf16),
            ((lane, 2 * lane), bf16),
            ((snd_half, 2 * lane), f32),
            ((rcv_half, 2 * lane), f32),
            ((2 * lane, lane), f32),
            ((8, lane), f32),
        ],
        z,
        edge_cot,
        edge,
        ids,
        node,
        near,
        far,
        dagg,
        dagg_near,
        dagg_far,
        base,
        weights,
        vectors,
        node_grads,
        snd_column,
        rcv_column,
    )
    returned_near, returned_far = swap(grad_near, grad_far)
    (node_grad,) = call(
        node_grad_kernel, [((nodes, lane), bf16)], [], acc, returned_near, returned_far, ids
    )
    parts = lax.all_to_all(grads.reshape(sharers, share, lane), members, 0, 0, tiled=True)
    (shares,) = call(share_kernel, [(parts.shape, bf16)], [], parts)
    shares = lax.all_to_all(shares, members, 0, 0, tiled=True)
    matrices = [3 * lane, lane, 2 * lane, lane]
    totals = call(
        finish_kernel,
        [((height, lane), f32) for height in matrices] + [((1, lane), f32)] * 8,
        [],
        shares.reshape(sharers * share, lane),
    )
    flat = [total.reshape(lane) for total in totals[4:]]
    return (
        node_out[None],
        edge_out[None],
        node_grad[None],
        edge_grad[None],
        totals[0],
        flat[0],
        totals[1],
        flat[1],
        flat[2],
        flat[3],
        totals[2],
        flat[4],
        totals[3],
        flat[5],
        flat[6],
        flat[7],
    )


def solution(mesh):
    node_spec = P(("groups", "sample"), ("dom", "sub"), None)
    ids_spec = P(("dom", "sub"))
    return jax.shard_map(
        on_device,
        mesh=mesh,
        in_specs=(
            (node_spec, node_spec, ids_spec, ids_spec, P(("dom", "sub"), None, None))
            + (P(),) * 12
            + (node_spec, node_spec)
        ),
        out_specs=(
            (node_spec,) * 4
            + (P("groups", None), P("groups"), P("groups", None), P("groups"), P("groups"), P("groups"))
            * 2
        ),
        check_vma=False,
    )
```

```python
import functools
import math

import jax
import jax.numpy as jnp
from jax import lax
from jax.experimental import pallas as pl
from jax.experimental.pallas import tpu as pltpu
from jax.sharding import PartitionSpec as P

epsilon = 1e-05
rows_dims = (((0,), (0,)), ((), ()))
back_dims = (((1,), (1,)), ((), ()))
f32 = jnp.float32
bf16 = jnp.bfloat16
lane = 128
edge_tile = 512
vmem_limit = 32 * 1024 * 1024
sum_rows = 16
chain = ("dom", "sub")


def dot(left, right):
    return jnp.dot(left, right, preferred_element_type=f32)


def dot_rows(left, right):
    return lax.dot_general(left, right, rows_dims, preferred_element_type=f32)


def dot_back(left, right):
    return lax.dot_general(left, right, back_dims, preferred_element_type=f32)


def column_of(row):
    return jnp.broadcast_to(row, (lane, lane)).T


def hot_columns(ids, width):
    targets = lax.broadcasted_iota(jnp.int32, ids.shape, 1)
    parts = [
        jnp.where(ids == targets + at, 1.0, 0.0).astype(bf16) for at in range(0, width, lane)
    ]
    return jnp.concatenate(parts, axis=1)


def hot_rows(row, height):
    targets = lax.broadcasted_iota(jnp.int32, (height, lane), 0)
    return jnp.where(row == targets, 1.0, 0.0).astype(bf16)


def fold(ids, half):
    upper = ids >= half
    return upper, jnp.where(upper, ids - half, ids)


def side_by_side(rows):
    half = rows.shape[0] // 2
    return jnp.concatenate([rows[:half], rows[half:]], axis=1)


def pick(ids, table):
    half = table.shape[0]
    upper, low = fold(ids, half)
    both = dot(hot_columns(low, half), table)
    return jnp.where(upper, both[:, lane:], both[:, :lane])


def spread(ids_ref, first, count, half, ids, values):
    upper, unused = fold(ids, half)
    paired = jnp.concatenate(
        [jnp.where(upper, 0.0, values).astype(bf16), jnp.where(upper, values, 0.0).astype(bf16)],
        axis=1,
    )
    parts = []
    for k in range(count):
        row = ids_ref[pl.ds(first + k, 1), :]
        unused, low = fold(row, half)
        parts.append(hot_rows(low, half))
    return dot(jnp.concatenate(parts, axis=1), paired)


def sigmoid(z):
    return 0.5 * jnp.tanh(0.5 * z) + 0.5


def vector(vectors_ref, k):
    return vectors_ref[k : k + 1, :]


def centred_second(w, b):
    w = w.astype(f32)
    w = w - jnp.mean(w, axis=1, keepdims=True)
    high = w.astype(bf16)
    low = (w - high.astype(f32)).astype(bf16)
    return jnp.concatenate([high, low], axis=1), b - jnp.mean(b, axis=1, keepdims=True)


def normed_of(act, w_pair, b_centred):
    both = dot(act, w_pair)
    center = both[:, :lane] + both[:, lane:] + b_centred
    scale_inv = lax.rsqrt(jnp.mean(center * center, axis=1, keepdims=True) + epsilon)
    return center * scale_inv, scale_inv


def back_norm(upstream, normed, scale_inv, gain):
    d_normed = upstream * gain
    return scale_inv * (
        d_normed
        - jnp.mean(d_normed, axis=1, keepdims=True)
        - normed * jnp.mean(d_normed * normed, axis=1, keepdims=True)
    )


def column_sum(values):
    return jnp.sum(values, axis=0, keepdims=True)


def parity_of_place():
    return lax.axis_index(chain) % 2


def first_kernel(
    node_hbm,
    snd_hbm,
    rcv_hbm,
    list_hbm,
    edge_hbm,
    edge_cot_hbm,
    node_cot_hbm,
    *refs,
):
    small = refs[:12]
    node_ref, ids_ref, edge_ref, edge_cot_ref, node_cot_ref, weights_ref, vectors_ref = refs[12:19]
    near_ref, far_ref, sems = refs[19:]
    chunks = snd_hbm.shape[0]
    moves = [
        (node_hbm, node_ref),
        (list_hbm, ids_ref.at[2 * chunks : 2 * chunks + 2]),
        (snd_hbm, ids_ref.at[:chunks]),
        (rcv_hbm, ids_ref.at[chunks : 2 * chunks]),
    ]
    at = 0
    for source in small[:4]:
        moves.append((source, weights_ref.at[at : at + source.shape[0]]))
        at += source.shape[0]
    for k, source in enumerate(small[4:]):
        moves.append((source, vectors_ref.at[k : k + 1]))
    moves += [(edge_hbm, edge_ref), (edge_cot_hbm, edge_cot_ref), (node_cot_hbm, node_cot_ref)]
    copies = [
        pltpu.make_async_copy(source, target, sems.at[k])
        for k, (source, target) in enumerate(moves)
    ]
    for copy in copies:
        copy.start()
    for copy in copies[:2]:
        copy.wait()
    parity = parity_of_place()
    node = node_ref[...]
    for side, out_ref in ((1 - parity, near_ref), (parity, far_ref)):
        hot = hot_columns(column_of(ids_ref[pl.ds(2 * chunks + side, 1), :]), node.shape[0])
        out_ref[...] = dot(hot, node).astype(bf16)
    for copy in copies[2:]:
        copy.wait()


def prepare_kernel(
    ids_ref,
    node_ref,
    weights_ref,
    vectors_ref,
    edge_ref,
    snd_column,
    rcv_column,
    z_ref,
    rcv_local,
    snd_table,
):
    chunks = snd_column.shape[0] // lane
    for k in range(chunks):
        at = slice(k * lane, (k + 1) * lane)
        snd_column[at, :] = column_of(ids_ref[k : k + 1, :])
        rcv_column[at, :] = column_of(ids_ref[chunks + k : chunks + k + 1, :])
    node = node_ref[...]
    snd_table[...] = side_by_side(dot(node, weights_ref[lane : 2 * lane]).astype(bf16))
    rcv_local[...] = dot(node, weights_ref[2 * lane : 3 * lane]).astype(bf16)
    w1_edge = weights_ref[:lane]
    b1 = vector(vectors_ref, 0)

    def tile(i, carry):
        rows = pl.ds(pl.multiple_of(i * edge_tile, edge_tile), edge_tile)
        z = dot(edge_ref[rows, :], w1_edge) + b1
        z_ref[rows, :] = z + pick(snd_column[rows, :], snd_table[...])
        return carry

    lax.fori_loop(0, edge_ref.shape[0] // edge_tile, tile, 0)


def edge_forward_kernel(
    near_ref,
    far_ref,
    edge_ref,
    ids_ref,
    weights_ref,
    vectors_ref,
    rcv_column,
    z_sent,
    rcv_local,
    out_ref,
    z_ref,
    agg_ref,
    agg_near_ref,
    agg_far_ref,
    halo,
    rcv_table,
    w2_pair,
    total,
):
    nodes = rcv_local.shape[0]
    rim = near_ref.shape[0]
    half = rcv_table.shape[0]
    parity = parity_of_place()
    near_at = pl.multiple_of((1 - parity) * rim, rim)
    far_at = pl.multiple_of(parity * rim, rim)
    w1_rcv = weights_ref[2 * lane : 3 * lane]
    gain, shift = vector(vectors_ref, 2), vector(vectors_ref, 3)
    halo[pl.ds(near_at, rim), :] = dot(near_ref[...], w1_rcv).astype(bf16)
    halo[pl.ds(far_at, rim), :] = dot(far_ref[...], w1_rcv).astype(bf16)
    rcv_table[:, :lane] = rcv_local[:half, :]
    rcv_table[: nodes - half, lane:] = rcv_local[half:, :]
    rcv_table[nodes - half :, lane:] = halo[...]
    pair, b2 = centred_second(weights_ref[3 * lane : 4 * lane], vector(vectors_ref, 1))
    w2_pair[...] = pair
    total[...] = jnp.zeros_like(total)

    def tile(i, carry):
        rows = pl.ds(pl.multiple_of(i * edge_tile, edge_tile), edge_tile)
        x = edge_ref[rows, :]
        rcv = rcv_column[rows, :]
        z = z_sent[rows, :] + pick(rcv, rcv_table[...])
        z_ref[rows, :] = z
        act = (z * sigmoid(z)).astype(bf16)
        normed, unused = normed_of(act, w2_pair[...], b2)
        update = normed * gain + shift
        out_ref[rows, :] = (x.astype(f32) + update).astype(bf16)
        first = (rcv_column.shape[0] + i * edge_tile) // lane
        total[...] += spread(ids_ref, first, edge_tile // lane, half, rcv, update)
        return carry

    lax.fori_loop(0, edge_ref.shape[0] // edge_tile, tile, 0)
    agg_ref[:half, :] = total[:, :lane]
    agg_ref[half:, :] = total[: nodes - half, lane:]
    agg_near_ref[...] = total[pl.ds(nodes - half + near_at, rim), lane:].astype(bf16)
    agg_far_ref[...] = total[pl.ds(nodes - half + far_at, rim), lane:].astype(bf16)


def hot_lists(ids_ref, nodes):
    parity = parity_of_place()
    first = ids_ref.shape[0] - 2
    near = ids_ref[pl.ds(first + 1 - parity, 1), :]
    far = ids_ref[pl.ds(first + parity, 1), :]
    return jnp.concatenate([hot_rows(near, nodes), hot_rows(far, nodes)], axis=1)


def node_kernel(
    node_ref,
    agg_ref,
    near_ref,
    far_ref,
    ids_ref,
    weights_ref,
    vectors_ref,
    cot_ref,
    out_ref,
    base_ref,
    dagg_ref,
    rim_near_ref,
    rim_far_ref,
    grads_ref,
):
    nodes = node_ref.shape[0]
    node = node_ref[...]
    returned = jnp.concatenate([near_ref[...], far_ref[...]], axis=0)
    agg = (agg_ref[...] + dot(hot_lists(ids_ref, nodes), returned)).astype(bf16)
    x = jnp.concatenate([node, agg], axis=1)
    w1 = weights_ref[4 * lane : 6 * lane]
    w2 = weights_ref[6 * lane :]
    z = dot(x, w1) + vector(vectors_ref, 4)
    sig = sigmoid(z)
    act = (z * sig).astype(bf16)
    pair, b2 = centred_second(w2, vector(vectors_ref, 5))
    normed, scale_inv = normed_of(act, pair, b2)
    gain = vector(vectors_ref, 6)
    out_ref[...] = (node.astype(f32) + normed * gain + vector(vectors_ref, 7)).astype(bf16)
    upstream = cot_ref[...].astype(f32)
    dz2 = back_norm(upstream, normed, scale_inv, gain)
    dz2b = dz2.astype(bf16)
    da = dot_back(dz2b, w2)
    dz1 = da * sig * (1.0 + z * (1.0 - sig))
    dz1b = dz1.astype(bf16)
    dx = dot_back(dz1b, w1)
    base_ref[...] = upstream + dx[:, :lane]
    dagg = dx[:, lane:].astype(bf16)
    dagg_ref[...] = dagg
    parity = parity_of_place()
    first = ids_ref.shape[0] - 2
    for side, rim_ref in ((1 - parity, rim_near_ref), (parity, rim_far_ref)):
        picked = hot_columns(column_of(ids_ref[pl.ds(first + side, 1), :]), nodes)
        rim_ref[...] = dot(picked, dagg).astype(bf16)
    first = 2 * lane
    second = first + lane
    grads_ref[:first, :] = dot_rows(x, dz1b)
    grads_ref[first:second, :] = dot_rows(act, dz2b)
    sums = [column_sum(dz1), column_sum(dz2), column_sum(upstream * normed), column_sum(upstream)]
    sums.append(jnp.zeros((sum_rows - len(sums), lane), f32))
    grads_ref[second:, :] = jnp.concatenate(sums, axis=0)


def edge_backward_kernel(
    z_ref,
    cot_ref,
    edge_ref,
    ids_ref,
    node_ref,
    near_ref,
    far_ref,
    dagg_ref,
    dagg_near_ref,
    dagg_far_ref,
    base_ref,
    weights_ref,
    vectors_ref,
    node_grads_ref,
    snd_column,
    rcv_column,
    grad_ref,
    acc_ref,
    far_back_ref,
    kept_ref,
    sent_ref,
    halo,
    grads_ref,
    table,
    w2_pair,
    snd_total,
    rcv_total,
    squares,
    sums,
):
    nodes = node_ref.shape[0]
    rim = near_ref.shape[0]
    snd_half = snd_total.shape[0]
    rcv_half = rcv_total.shape[0]
    parity = parity_of_place()
    near_at = pl.multiple_of((1 - parity) * rim, rim)
    far_at = pl.multiple_of(parity * rim, rim)
    w1_edge = weights_ref[:lane]
    w2 = weights_ref[3 * lane : 4 * lane]
    gain = vector(vectors_ref, 2)
    table[:, :lane] = dagg_ref[:rcv_half, :]
    table[: nodes - rcv_half, lane:] = dagg_ref[rcv_half:, :]
    table[pl.ds(nodes - rcv_half + near_at, rim), lane:] = dagg_near_ref[...]
    table[pl.ds(nodes - rcv_half + far_at, rim), lane:] = dagg_far_ref[...]
    halo[pl.ds(near_at, rim), :] = near_ref[...]
    halo[pl.ds(far_at, rim), :] = far_ref[...]
    pair, b2 = centred_second(w2, vector(vectors_ref, 1))
    w2_pair[...] = pair
    snd_total[...] = jnp.zeros_like(snd_total)
    rcv_total[...] = jnp.zeros_like(rcv_total)
    squares[...] = jnp.zeros_like(squares)
    sums[...] = jnp.zeros_like(sums)

    def tile(i, carry):
        rows = pl.ds(pl.multiple_of(i * edge_tile, edge_tile), edge_tile)
        chunk = edge_tile // lane
        rcv = rcv_column[rows, :]
        snd = snd_column[rows, :]
        x = edge_ref[rows, :]
        z = z_ref[rows, :]
        cot = cot_ref[rows, :].astype(f32)
        upstream = cot + pick(rcv, table[...])
        sig = sigmoid(z)
        act = (z * sig).astype(bf16)
        normed, scale_inv = normed_of(act, w2_pair[...], b2)
        dz2 = back_norm(upstream, normed, scale_inv, gain)
        dz2b = dz2.astype(bf16)
        da = dot_back(dz2b, w2)
        dz1 = da * sig * (1.0 + z * (1.0 - sig))
        dz1b = dz1.astype(bf16)
        grad_ref[rows, :] = (cot + dot_back(dz1b, w1_edge)).astype(bf16)
        squares[:lane, :] += dot_rows(x, dz1b)
        squares[lane:, :] += dot_rows(act, dz2b)
        sums[0:1, :] += column_sum(dz1)
        sums[1:2, :] += column_sum(dz2)
        sums[2:3, :] += column_sum(upstream * normed)
        sums[3:4, :] += column_sum(upstream)
        first = rcv_column.shape[0] // lane + i * chunk
        snd_total[...] += spread(ids_ref, i * chunk, chunk, snd_half, snd, dz1)
        rcv_total[...] += spread(ids_ref, first, chunk, rcv_half, rcv, dz1)
        return carry

    lax.fori_loop(0, edge_ref.shape[0] // edge_tile, tile, 0)
    snd_sum = jnp.concatenate([snd_total[:, :lane], snd_total[:, lane:]], axis=0).astype(bf16)
    rcv_sum = jnp.concatenate([rcv_total[:, :lane], rcv_total[:, lane:]], axis=0).astype(bf16)
    w1_snd = weights_ref[lane : 2 * lane]
    w1_rcv = weights_ref[2 * lane : 3 * lane]
    acc_ref[...] = base_ref[...] + dot_back(snd_sum, w1_snd) + dot_back(rcv_sum[:nodes], w1_rcv)
    kept = kept_ref.shape[0]
    for at, back_ref in ((near_at, sent_ref.at[kept:]), (far_at, far_back_ref)):
        returned = rcv_total[pl.ds(nodes - rcv_half + at, rim), lane:].astype(bf16)
        back_ref[...] = dot_back(returned, w1_rcv).astype(bf16)
    extended = jnp.concatenate([node_ref[...], halo[...]], axis=0)
    grads_ref[:lane, :] = squares[:lane, :]
    grads_ref[lane : 2 * lane, :] = dot_rows(node_ref[...], snd_sum)
    grads_ref[2 * lane : 3 * lane, :] = dot_rows(extended, rcv_sum)
    grads_ref[3 * lane : 4 * lane, :] = squares[lane:, :]
    node_rows = node_grads_ref.shape[0] - sum_rows
    last = 4 * lane + node_rows
    grads_ref[4 * lane : last, :] = node_grads_ref[:node_rows, :]
    grads_ref[last : last + sum_rows, :] = jnp.concatenate(
        [sums[0:4, :], node_grads_ref[node_rows : node_rows + 4, :], jnp.zeros((8, lane), f32)],
        axis=0,
    )
    if last + sum_rows < grads_ref.shape[0]:
        grads_ref[last + sum_rows :, :] = jnp.zeros(
            (grads_ref.shape[0] - last - sum_rows, lane), f32
        )
    own = lax.axis_index("sub")
    kept_ref[...] = grads_ref[pl.ds(pl.multiple_of(own * kept, kept), kept), :]
    other = pl.multiple_of((1 - own) * kept, kept)
    sent_ref[:kept, :] = grads_ref[pl.ds(other, kept), :].astype(bf16)


def node_grad_kernel(acc_ref, near_ref, far_ref, ids_ref, out_ref):
    rim = far_ref.shape[0]
    returned = jnp.concatenate([near_ref[near_ref.shape[0] - rim :, :], far_ref[...]], axis=0)
    hot = hot_lists(ids_ref, acc_ref.shape[0])
    out_ref[...] = (acc_ref[...] + dot(hot, returned)).astype(bf16)


def halves_kernel(kept_ref, other_ref, out_ref):
    kept = kept_ref.shape[0]
    out_ref[...] = (kept_ref[...] + other_ref[:kept, :].astype(f32)).astype(bf16)


def share_kernel(parts_ref, out_ref):
    count = parts_ref.shape[0]
    total = parts_ref[0].astype(f32)
    for k in range(1, count):
        total = total + parts_ref[k].astype(f32)
    total = total.astype(bf16)
    for k in range(count):
        out_ref[k] = total


def finish_kernel(own_ref, other_ref, *refs):
    out_refs, total_ref = refs[:-1], refs[-1]
    kept = own_ref.shape[0]
    own = lax.axis_index("sub")
    total_ref[pl.ds(pl.multiple_of(own * kept, kept), kept), :] = own_ref[...].astype(f32)
    other = pl.multiple_of((1 - own) * kept, kept)
    total_ref[pl.ds(other, kept), :] = other_ref[...].astype(f32)
    at = 0
    for out_ref in out_refs[:4]:
        out_ref[...] = total_ref[at : at + out_ref.shape[0], :]
        at += out_ref.shape[0]
    for k, out_ref in enumerate(out_refs[4:]):
        out_ref[...] = total_ref[at + k : at + k + 1, :]


def call(kernel, outs, scratch, *operands, anywhere=0, sems=0):
    moved = sum(x.size * x.dtype.itemsize for x in operands)
    held = operands[len(operands) - anywhere :]
    operands = operands[: len(operands) - anywhere]
    operands += tuple(pltpu.with_memory_space_constraint(x, pltpu.HBM) for x in held)
    inside = [pl.BlockSpec(memory_space=pltpu.VMEM)] * (len(operands) - anywhere)
    outside = [pl.BlockSpec(memory_space=pl.ANY)] * anywhere
    scratch_shapes = [pltpu.VMEM(shape, dtype) for shape, dtype in scratch]
    if sems:
        scratch_shapes.append(pltpu.SemaphoreType.DMA((sems,)))
    return pl.pallas_call(
        kernel,
        out_shape=[jax.ShapeDtypeStruct(shape, dtype) for shape, dtype in outs],
        in_specs=inside + outside,
        out_specs=[pl.BlockSpec(memory_space=pltpu.VMEM)] * len(outs),
        scratch_shapes=scratch_shapes,
        compiler_params=pltpu.CompilerParams(vmem_limit_bytes=vmem_limit),
        cost_estimate=pl.CostEstimate(flops=0, bytes_accessed=moved, transcendentals=0),
    )(*operands)


def swap(near, far):
    count = lax.axis_size("dom") * lax.axis_size("sub")
    outer = [(i, i + 1) for i in range(1, count - 1, 2)]
    inner = [(i, i + 1) for i in range(0, count - 1, 2)]
    outer += [(target, source) for source, target in outer]
    inner += [(target, source) for source, target in inner]
    far = lax.ppermute(far, chain, outer)
    return lax.ppermute(near, chain, inner), far


def on_device(
    node_in,
    edge_in,
    senders,
    receivers,
    send_list,
    w_edge_first,
    b_edge_first,
    w_edge_second,
    b_edge_second,
    edge_gain,
    edge_shift,
    w_node_first,
    b_node_first,
    w_node_second,
    b_node_second,
    node_gain,
    node_shift,
    node_cotangent,
    edge_cotangent,
):
    node = node_in[0]
    edge = edge_in[0]
    nodes = node.shape[0]
    edges = edge.shape[0]
    rim = send_list.shape[2]
    rim_shape = ((rim, lane), bf16)
    snd_half = nodes // 2
    rcv_half = (nodes + 2 * rim) // 2
    members = ("dom", "sample")
    sharers = math.prod(lax.axis_size(axis) for axis in members)
    grad_rows = 7 * lane + sum_rows
    share = -(-grad_rows // (2 * sharers * sum_rows)) * sum_rows
    kept = sharers * share
    row = lambda x: x.reshape(1, lane)
    small = [w_edge_first, w_edge_second, w_node_first, w_node_second]
    small += [row(b_edge_first), row(b_edge_second), row(edge_gain), row(edge_shift)]
    small += [row(b_node_first), row(b_node_second), row(node_gain), row(node_shift)]
    chunks = edges // lane
    sources = [
        node,
        senders.reshape(chunks, lane),
        receivers.reshape(chunks, lane),
        send_list[0],
        edge,
        edge_cotangent[0],
        node_cotangent[0],
    ] + small
    node, ids, edge, edge_cot, node_cot, weights, vectors, rim_near, rim_far = call(
        first_kernel,
        [
            ((nodes, lane), bf16),
            ((2 * chunks + 2, lane), jnp.int32),
            ((edges, lane), bf16),
            ((edges, lane), bf16),
            ((nodes, lane), bf16),
            ((7 * lane, lane), bf16),
            ((8, lane), f32),
            rim_shape,
            rim_shape,
        ],
        [],
        *sources,
        anywhere=len(sources),
        sems=len(sources),
    )
    near, far = swap(rim_near, rim_far)
    snd_column, rcv_column, z_sent, rcv_local = call(
        prepare_kernel,
        [
            ((edges, lane), jnp.int32),
            ((edges, lane), jnp.int32),
            ((edges, lane), f32),
            ((nodes, lane), bf16),
        ],
        [((snd_half, 2 * lane), bf16)],
        ids,
        node,
        weights,
        vectors,
        edge,
    )
    edge_out, z, agg, agg_near, agg_far = call(
        edge_forward_kernel,
        [((edges, lane), bf16), ((edges, lane), f32), ((nodes, lane), f32), rim_shape, rim_shape],
        [
            ((2 * rim, lane), bf16),
            ((rcv_half, 2 * lane), bf16),
            ((lane, 2 * lane), bf16),
            ((rcv_half, 2 * lane), f32),
        ],
        near,
        far,
        edge,
        ids,
        weights,
        vectors,
        rcv_column,
        z_sent,
        rcv_local,
    )
    back_near, back_far = swap(agg_near, agg_far)
    node_out, base, dagg, dagg_rim_near, dagg_rim_far, node_grads = call(
        node_kernel,
        [
            ((nodes, lane), bf16),
            ((nodes, lane), f32),
            ((nodes, lane), bf16),
            rim_shape,
            rim_shape,
            ((3 * lane + sum_rows, lane), f32),
        ],
        [],
        node,
        agg,
        back_near,
        back_far,
        ids,
        weights,
        vectors,
        node_cot,
    )
    dagg_near, dagg_far = swap(dagg_rim_near, dagg_rim_far)
    edge_grad, acc, grad_far, grads_kept, grads_sent = call(
        edge_backward_kernel,
        [
            ((edges, lane), bf16),
            ((nodes, lane), f32),
            rim_shape,
            ((kept, lane), f32),
            ((kept + rim, lane), bf16),
        ],
        [
            ((2 * rim, lane), bf16),
            ((2 * kept, lane), f32),
            ((rcv_half, 2 * lane), bf16),
            ((lane, 2 * lane), bf16),
            ((snd_half, 2 * lane), f32),
            ((rcv_half, 2 * lane), f32),
            ((2 * lane, lane), f32),
            ((8, lane), f32),
        ],
        z,
        edge_cot,
        edge,
        ids,
        node,
        near,
        far,
        dagg,
        dagg_near,
        dagg_far,
        base,
        weights,
        vectors,
        node_grads,
        snd_column,
        rcv_column,
    )
    returned_near, returned_far = swap(grads_sent, grad_far)
    (halves,) = call(halves_kernel, [((kept, lane), bf16)], [], grads_kept, returned_near)
    parts = lax.all_to_all(halves.reshape(sharers, share, lane), members, 0, 0, tiled=True)
    (shares,) = call(share_kernel, [(parts.shape, bf16)], [], parts)
    shares = lax.all_to_all(shares, members, 0, 0, tiled=True).reshape(kept, lane)
    (node_grad,) = call(
        node_grad_kernel, [((nodes, lane), bf16)], [], acc, returned_near, returned_far, ids
    )
    others = lax.ppermute(shares, "sub", [(0, 1), (1, 0)])
    matrices = [3 * lane, lane, 2 * lane, lane]
    totals = call(
        finish_kernel,
        [((height, lane), f32) for height in matrices] + [((1, lane), f32)] * 8,
        [((2 * kept, lane), f32)],
        shares,
        others,
    )
    flat = [total.reshape(lane) for total in totals[4:]]
    return (
        node_out[None],
        edge_out[None],
        node_grad[None],
        edge_grad[None],
        totals[0],
        flat[0],
        totals[1],
        flat[1],
        flat[2],
        flat[3],
        totals[2],
        flat[4],
        totals[3],
        flat[5],
        flat[6],
        flat[7],
    )


def solution(mesh):
    node_spec = P(("groups", "sample"), ("dom", "sub"), None)
    ids_spec = P(("dom", "sub"))
    return jax.shard_map(
        on_device,
        mesh=mesh,
        in_specs=(
            (node_spec, node_spec, ids_spec, ids_spec, P(("dom", "sub"), None, None))
            + (P(),) * 12
            + (node_spec, node_spec)
        ),
        out_specs=(
            (node_spec,) * 4
            + (P("groups", None), P("groups"), P("groups", None), P("groups"), P("groups"), P("groups"))
            * 2
        ),
        check_vma=False,
    )
```

```python
import jax
import jax.numpy as jnp
from jax import lax
from jax.experimental import pallas as pl
from jax.experimental.pallas import tpu as pltpu
from jax.sharding import PartitionSpec as P

epsilon = 1e-05
rows_dims = (((0,), (0,)), ((), ()))
back_dims = (((1,), (1,)), ((), ()))
f32 = jnp.float32
bf16 = jnp.bfloat16
lane = 128
edge_tile = 512
vmem_limit = 32 * 1024 * 1024
sum_rows = 16
chain = ("dom", "sub")


def dot(left, right):
    return jnp.dot(left, right, preferred_element_type=f32)


def dot_rows(left, right):
    return lax.dot_general(left, right, rows_dims, preferred_element_type=f32)


def dot_back(left, right):
    return lax.dot_general(left, right, back_dims, preferred_element_type=f32)


def column_of(row):
    return jnp.broadcast_to(row, (lane, lane)).T


def hot_columns(ids, width):
    targets = lax.broadcasted_iota(jnp.int32, ids.shape, 1)
    parts = [
        jnp.where(ids == targets + at, 1.0, 0.0).astype(bf16) for at in range(0, width, lane)
    ]
    return jnp.concatenate(parts, axis=1)


def hot_rows(row, height):
    targets = lax.broadcasted_iota(jnp.int32, (height, lane), 0)
    return jnp.where(row == targets, 1.0, 0.0).astype(bf16)


def fold(ids, half):
    upper = ids >= half
    return upper, jnp.where(upper, ids - half, ids)


def side_by_side(rows):
    half = rows.shape[0] // 2
    return jnp.concatenate([rows[:half], rows[half:]], axis=1)


def pick(ids, table):
    half = table.shape[0]
    upper, low = fold(ids, half)
    both = dot(hot_columns(low, half), table)
    return jnp.where(upper, both[:, lane:], both[:, :lane])


def spread(ids_ref, first, count, half, ids, values):
    upper, unused = fold(ids, half)
    paired = jnp.concatenate(
        [jnp.where(upper, 0.0, values).astype(bf16), jnp.where(upper, values, 0.0).astype(bf16)],
        axis=1,
    )
    parts = []
    for k in range(count):
        row = ids_ref[pl.ds(first + k, 1), :]
        unused, low = fold(row, half)
        parts.append(hot_rows(low, half))
    return dot(jnp.concatenate(parts, axis=1), paired)


def sigmoid(z):
    return 0.5 * jnp.tanh(0.5 * z) + 0.5


def vector(vectors_ref, k):
    return vectors_ref[k : k + 1, :]


def centred_second(w, b):
    w = w.astype(f32)
    w = w - jnp.mean(w, axis=1, keepdims=True)
    high = w.astype(bf16)
    low = (w - high.astype(f32)).astype(bf16)
    return jnp.concatenate([high, low], axis=1), b - jnp.mean(b, axis=1, keepdims=True)


def normed_of(act, w_pair, b_centred):
    both = dot(act, w_pair)
    center = both[:, :lane] + both[:, lane:] + b_centred
    scale_inv = lax.rsqrt(jnp.mean(center * center, axis=1, keepdims=True) + epsilon)
    return center * scale_inv, scale_inv


def back_norm(upstream, normed, scale_inv, gain):
    d_normed = upstream * gain
    return scale_inv * (
        d_normed
        - jnp.mean(d_normed, axis=1, keepdims=True)
        - normed * jnp.mean(d_normed * normed, axis=1, keepdims=True)
    )


def column_sum(values):
    return jnp.sum(values, axis=0, keepdims=True)


def parity_of_place():
    return lax.axis_index(chain) % 2


def first_kernel(
    node_hbm,
    snd_hbm,
    rcv_hbm,
    list_hbm,
    edge_hbm,
    edge_cot_hbm,
    node_cot_hbm,
    *refs,
):
    small = refs[:12]
    node_ref, ids_ref, edge_ref, edge_cot_ref, node_cot_ref, weights_ref, vectors_ref = refs[12:19]
    near_ref, far_ref, sems = refs[19:]
    chunks = snd_hbm.shape[0]
    moves = [
        (node_hbm, node_ref),
        (list_hbm, ids_ref.at[2 * chunks : 2 * chunks + 2]),
        (snd_hbm, ids_ref.at[:chunks]),
        (rcv_hbm, ids_ref.at[chunks : 2 * chunks]),
    ]
    at = 0
    for source in small[:4]:
        moves.append((source, weights_ref.at[at : at + source.shape[0]]))
        at += source.shape[0]
    for k, source in enumerate(small[4:]):
        moves.append((source, vectors_ref.at[k : k + 1]))
    moves += [(edge_hbm, edge_ref), (edge_cot_hbm, edge_cot_ref), (node_cot_hbm, node_cot_ref)]
    copies = [
        pltpu.make_async_copy(source, target, sems.at[k])
        for k, (source, target) in enumerate(moves)
    ]
    for copy in copies:
        copy.start()
    for copy in copies[:2]:
        copy.wait()
    parity = parity_of_place()
    node = node_ref[...]
    for side, out_ref in ((1 - parity, near_ref), (parity, far_ref)):
        hot = hot_columns(column_of(ids_ref[pl.ds(2 * chunks + side, 1), :]), node.shape[0])
        out_ref[...] = dot(hot, node).astype(bf16)
    for copy in copies[2:]:
        copy.wait()


def prepare_kernel(
    ids_ref,
    node_ref,
    weights_ref,
    vectors_ref,
    edge_ref,
    snd_column,
    rcv_column,
    z_ref,
    rcv_local,
    snd_table,
):
    chunks = snd_column.shape[0] // lane
    for k in range(chunks):
        at = slice(k * lane, (k + 1) * lane)
        snd_column[at, :] = column_of(ids_ref[k : k + 1, :])
        rcv_column[at, :] = column_of(ids_ref[chunks + k : chunks + k + 1, :])
    node = node_ref[...]
    snd_table[...] = side_by_side(dot(node, weights_ref[lane : 2 * lane]).astype(bf16))
    rcv_local[...] = dot(node, weights_ref[2 * lane : 3 * lane]).astype(bf16)
    w1_edge = weights_ref[:lane]
    b1 = vector(vectors_ref, 0)

    def tile(i, carry):
        rows = pl.ds(pl.multiple_of(i * edge_tile, edge_tile), edge_tile)
        z = dot(edge_ref[rows, :], w1_edge) + b1
        z_ref[rows, :] = z + pick(snd_column[rows, :], snd_table[...])
        return carry

    lax.fori_loop(0, edge_ref.shape[0] // edge_tile, tile, 0)


def edge_forward_kernel(
    near_ref,
    far_ref,
    edge_ref,
    ids_ref,
    weights_ref,
    vectors_ref,
    rcv_column,
    z_sent,
    rcv_local,
    out_ref,
    z_ref,
    message_ref,
    agg_near_ref,
    agg_far_ref,
    halo,
    rcv_table,
    w2_pair,
    total,
):
    nodes = rcv_local.shape[0]
    rim = near_ref.shape[0]
    half = rcv_table.shape[0]
    parity = parity_of_place()
    near_at = pl.multiple_of((1 - parity) * rim, rim)
    far_at = pl.multiple_of(parity * rim, rim)
    w1_rcv = weights_ref[2 * lane : 3 * lane]
    gain, shift = vector(vectors_ref, 2), vector(vectors_ref, 3)
    halo[pl.ds(near_at, rim), :] = dot(near_ref[...], w1_rcv).astype(bf16)
    halo[pl.ds(far_at, rim), :] = dot(far_ref[...], w1_rcv).astype(bf16)
    rcv_table[:, :lane] = rcv_local[:half, :]
    rcv_table[: nodes - half, lane:] = rcv_local[half:, :]
    rcv_table[nodes - half :, lane:] = halo[...]
    pair, b2 = centred_second(weights_ref[3 * lane : 4 * lane], vector(vectors_ref, 1))
    w2_pair[...] = pair
    total[...] = jnp.zeros_like(total)

    def tile(i, carry):
        rows = pl.ds(pl.multiple_of(i * edge_tile, edge_tile), edge_tile)
        x = edge_ref[rows, :]
        rcv = rcv_column[rows, :]
        z = z_sent[rows, :] + pick(rcv, rcv_table[...])
        z_ref[rows, :] = z
        act = (z * sigmoid(z)).astype(bf16)
        normed, unused = normed_of(act, w2_pair[...], b2)
        update = normed * gain + shift
        out_ref[rows, :] = (x.astype(f32) + update).astype(bf16)
        message = update.astype(bf16)
        message_ref[rows, :] = message
        first = (rcv_column.shape[0] + i * edge_tile) // lane
        parts = [
            hot_rows(ids_ref[pl.ds(first + k, 1), :] - nodes, 2 * rim)
            for k in range(edge_tile // lane)
        ]
        total[...] += dot(jnp.concatenate(parts, axis=1), message)
        return carry

    lax.fori_loop(0, edge_ref.shape[0] // edge_tile, tile, 0)
    agg_near_ref[...] = total[pl.ds(near_at, rim), :].astype(bf16)
    agg_far_ref[...] = total[pl.ds(far_at, rim), :].astype(bf16)


def collect_kernel(ids_ref, rcv_column, message_ref, agg_ref, total):
    half = total.shape[0]
    total[...] = jnp.zeros_like(total)

    def tile(i, carry):
        rows = pl.ds(pl.multiple_of(i * edge_tile, edge_tile), edge_tile)
        first = (rcv_column.shape[0] + i * edge_tile) // lane
        message = message_ref[rows, :].astype(f32)
        total[...] += spread(ids_ref, first, edge_tile // lane, half, rcv_column[rows, :], message)
        return carry

    lax.fori_loop(0, rcv_column.shape[0] // edge_tile, tile, 0)
    agg_ref[:half, :] = total[:, :lane]
    agg_ref[half:, :] = total[:, lane:]


def hot_lists(ids_ref, nodes):
    parity = parity_of_place()
    first = ids_ref.shape[0] - 2
    near = ids_ref[pl.ds(first + 1 - parity, 1), :]
    far = ids_ref[pl.ds(first + parity, 1), :]
    return jnp.concatenate([hot_rows(near, nodes), hot_rows(far, nodes)], axis=1)


def node_kernel(
    node_ref,
    agg_ref,
    near_ref,
    far_ref,
    ids_ref,
    weights_ref,
    vectors_ref,
    cot_ref,
    out_ref,
    base_ref,
    dagg_ref,
    rim_near_ref,
    rim_far_ref,
    grads_ref,
):
    nodes = node_ref.shape[0]
    node = node_ref[...]
    returned = jnp.concatenate([near_ref[...], far_ref[...]], axis=0)
    agg = (agg_ref[...] + dot(hot_lists(ids_ref, nodes), returned)).astype(bf16)
    x = jnp.concatenate([node, agg], axis=1)
    w1 = weights_ref[4 * lane : 6 * lane]
    w2 = weights_ref[6 * lane :]
    z = dot(x, w1) + vector(vectors_ref, 4)
    sig = sigmoid(z)
    act = (z * sig).astype(bf16)
    pair, b2 = centred_second(w2, vector(vectors_ref, 5))
    normed, scale_inv = normed_of(act, pair, b2)
    gain = vector(vectors_ref, 6)
    out_ref[...] = (node.astype(f32) + normed * gain + vector(vectors_ref, 7)).astype(bf16)
    upstream = cot_ref[...].astype(f32)
    dz2 = back_norm(upstream, normed, scale_inv, gain)
    dz2b = dz2.astype(bf16)
    da = dot_back(dz2b, w2)
    dz1 = da * sig * (1.0 + z * (1.0 - sig))
    dz1b = dz1.astype(bf16)
    dx = dot_back(dz1b, w1)
    base_ref[...] = upstream + dx[:, :lane]
    dagg = dx[:, lane:].astype(bf16)
    dagg_ref[...] = dagg
    parity = parity_of_place()
    first = ids_ref.shape[0] - 2
    for side, rim_ref in ((1 - parity, rim_near_ref), (parity, rim_far_ref)):
        picked = hot_columns(column_of(ids_ref[pl.ds(first + side, 1), :]), nodes)
        rim_ref[...] = dot(picked, dagg).astype(bf16)
    first = 2 * lane
    second = first + lane
    grads_ref[:first, :] = dot_rows(x, dz1b)
    grads_ref[first:second, :] = dot_rows(act, dz2b)
    sums = [column_sum(dz1), column_sum(dz2), column_sum(upstream * normed), column_sum(upstream)]
    sums.append(jnp.zeros((sum_rows - len(sums), lane), f32))
    grads_ref[second:, :] = jnp.concatenate(sums, axis=0)


def upstream_kernel(rcv_column, dagg_ref, cot_ref, up_ref, table):
    table[...] = side_by_side(dagg_ref[...])

    def tile(i, carry):
        rows = pl.ds(pl.multiple_of(i * edge_tile, edge_tile), edge_tile)
        up_ref[rows, :] = cot_ref[rows, :].astype(f32) + pick(rcv_column[rows, :], table[...])
        return carry

    lax.fori_loop(0, cot_ref.shape[0] // edge_tile, tile, 0)


def edge_backward_kernel(
    z_ref,
    up_ref,
    edge_ref,
    ids_ref,
    node_ref,
    near_ref,
    far_ref,
    dagg_near_ref,
    dagg_far_ref,
    weights_ref,
    vectors_ref,
    node_grads_ref,
    snd_column,
    rcv_column,
    dz_ref,
    snd_sum_ref,
    rcv_sum_ref,
    far_back_ref,
    kept_ref,
    sent_ref,
    halo,
    grads_ref,
    table,
    w2_pair,
    snd_total,
    rcv_total,
    squares,
    sums,
):
    nodes = node_ref.shape[0]
    rim = near_ref.shape[0]
    snd_half = snd_total.shape[0]
    rcv_half = rcv_total.shape[0]
    parity = parity_of_place()
    near_at = pl.multiple_of((1 - parity) * rim, rim)
    far_at = pl.multiple_of(parity * rim, rim)
    w2 = weights_ref[3 * lane : 4 * lane]
    gain = vector(vectors_ref, 2)
    table[pl.ds(near_at, rim), :] = dagg_near_ref[...]
    table[pl.ds(far_at, rim), :] = dagg_far_ref[...]
    halo[pl.ds(near_at, rim), :] = near_ref[...]
    halo[pl.ds(far_at, rim), :] = far_ref[...]
    pair, b2 = centred_second(w2, vector(vectors_ref, 1))
    w2_pair[...] = pair
    snd_total[...] = jnp.zeros_like(snd_total)
    rcv_total[...] = jnp.zeros_like(rcv_total)
    squares[...] = jnp.zeros_like(squares)
    sums[...] = jnp.zeros_like(sums)

    def tile(i, carry):
        rows = pl.ds(pl.multiple_of(i * edge_tile, edge_tile), edge_tile)
        chunk = edge_tile // lane
        rcv = rcv_column[rows, :]
        snd = snd_column[rows, :]
        x = edge_ref[rows, :]
        z = z_ref[rows, :]
        upstream = up_ref[rows, :] + dot(hot_columns(rcv - nodes, 2 * rim), table[...])
        sig = sigmoid(z)
        act = (z * sig).astype(bf16)
        normed, scale_inv = normed_of(act, w2_pair[...], b2)
        dz2 = back_norm(upstream, normed, scale_inv, gain)
        dz2b = dz2.astype(bf16)
        da = dot_back(dz2b, w2)
        dz1 = da * sig * (1.0 + z * (1.0 - sig))
        dz1b = dz1.astype(bf16)
        dz_ref[rows, :] = dz1b
        squares[:lane, :] += dot_rows(x, dz1b)
        squares[lane:, :] += dot_rows(act, dz2b)
        sums[0:1, :] += column_sum(dz1)
        sums[1:2, :] += column_sum(dz2)
        sums[2:3, :] += column_sum(upstream * normed)
        sums[3:4, :] += column_sum(upstream)
        first = rcv_column.shape[0] // lane + i * chunk
        snd_total[...] += spread(ids_ref, i * chunk, chunk, snd_half, snd, dz1)
        rcv_total[...] += spread(ids_ref, first, chunk, rcv_half, rcv, dz1)
        return carry

    lax.fori_loop(0, edge_ref.shape[0] // edge_tile, tile, 0)
    snd_sum = jnp.concatenate([snd_total[:, :lane], snd_total[:, lane:]], axis=0).astype(bf16)
    rcv_sum = jnp.concatenate([rcv_total[:, :lane], rcv_total[:, lane:]], axis=0).astype(bf16)
    snd_sum_ref[...] = snd_sum
    rcv_sum_ref[...] = rcv_sum[:nodes]
    w1_rcv = weights_ref[2 * lane : 3 * lane]
    kept = kept_ref.shape[0]
    for at, back_ref in ((near_at, sent_ref.at[kept:]), (far_at, far_back_ref)):
        returned = rcv_total[pl.ds(nodes - rcv_half + at, rim), lane:].astype(bf16)
        back_ref[...] = dot_back(returned, w1_rcv).astype(bf16)
    extended = jnp.concatenate([node_ref[...], halo[...]], axis=0)
    grads_ref[:lane, :] = squares[:lane, :]
    grads_ref[lane : 2 * lane, :] = dot_rows(node_ref[...], snd_sum)
    grads_ref[2 * lane : 3 * lane, :] = dot_rows(extended, rcv_sum)
    grads_ref[3 * lane : 4 * lane, :] = squares[lane:, :]
    node_rows = node_grads_ref.shape[0] - sum_rows
    last = 4 * lane + node_rows
    grads_ref[4 * lane : last, :] = node_grads_ref[:node_rows, :]
    grads_ref[last : last + sum_rows, :] = jnp.concatenate(
        [sums[0:4, :], node_grads_ref[node_rows : node_rows + 4, :], jnp.zeros((8, lane), f32)],
        axis=0,
    )
    if last + sum_rows < grads_ref.shape[0]:
        grads_ref[last + sum_rows :, :] = jnp.zeros(
            (grads_ref.shape[0] - last - sum_rows, lane), f32
        )
    own = lax.axis_index("sub")
    kept_ref[...] = grads_ref[pl.ds(pl.multiple_of(own * kept, sum_rows), kept), :]
    other = pl.multiple_of((1 - own) * kept, sum_rows)
    sent_ref[:kept, :] = grads_ref[pl.ds(other, kept), :].astype(bf16)


def edge_grad_kernel(dz_ref, cot_ref, weights_ref, out_ref):
    w1_edge = weights_ref[:lane]

    def tile(i, carry):
        rows = pl.ds(pl.multiple_of(i * edge_tile, edge_tile), edge_tile)
        cot = cot_ref[rows, :].astype(f32)
        out_ref[rows, :] = (cot + dot_back(dz_ref[rows, :], w1_edge)).astype(bf16)
        return carry

    lax.fori_loop(0, cot_ref.shape[0] // edge_tile, tile, 0)


def node_grad_kernel(
    base_ref, snd_sum_ref, rcv_sum_ref, weights_ref, near_ref, far_ref, ids_ref, out_ref
):
    rim = far_ref.shape[0]
    returned = jnp.concatenate([near_ref[near_ref.shape[0] - rim :, :], far_ref[...]], axis=0)
    total = base_ref[...] + dot_back(snd_sum_ref[...], weights_ref[lane : 2 * lane])
    total = total + dot_back(rcv_sum_ref[...], weights_ref[2 * lane : 3 * lane])
    hot = hot_lists(ids_ref, base_ref.shape[0])
    out_ref[...] = (total + dot(hot, returned)).astype(bf16)


def add_kernel(own_ref, other_ref, *refs):
    own = own_ref[...].astype(f32)
    refs[-1][...] = (own + other_ref[: own.shape[0], :].astype(f32)).astype(bf16)


def finish_kernel(own_ref, other_ref, *refs):
    out_refs, total_ref = refs[:-1], refs[-1]
    kept = own_ref.shape[0]
    own = lax.axis_index("sub")
    total_ref[pl.ds(pl.multiple_of(own * kept, sum_rows), kept), :] = own_ref[...].astype(f32)
    other = pl.multiple_of((1 - own) * kept, sum_rows)
    total_ref[pl.ds(other, kept), :] = other_ref[...].astype(f32)
    at = 0
    for out_ref in out_refs[:4]:
        out_ref[...] = total_ref[at : at + out_ref.shape[0], :]
        at += out_ref.shape[0]
    for k, out_ref in enumerate(out_refs[4:]):
        out_ref[...] = total_ref[at + k : at + k + 1, :]


def call(kernel, outs, scratch, *operands, anywhere=0, sems=0):
    moved = sum(x.size * x.dtype.itemsize for x in operands)
    held = operands[len(operands) - anywhere :]
    operands = operands[: len(operands) - anywhere]
    operands += tuple(pltpu.with_memory_space_constraint(x, pltpu.HBM) for x in held)
    inside = [pl.BlockSpec(memory_space=pltpu.VMEM)] * (len(operands) - anywhere)
    outside = [pl.BlockSpec(memory_space=pl.ANY)] * anywhere
    scratch_shapes = [pltpu.VMEM(shape, dtype) for shape, dtype in scratch]
    if sems:
        scratch_shapes.append(pltpu.SemaphoreType.DMA((sems,)))
    return pl.pallas_call(
        kernel,
        out_shape=[jax.ShapeDtypeStruct(shape, dtype) for shape, dtype in outs],
        in_specs=inside + outside,
        out_specs=[pl.BlockSpec(memory_space=pltpu.VMEM)] * len(outs),
        scratch_shapes=scratch_shapes,
        compiler_params=pltpu.CompilerParams(vmem_limit_bytes=vmem_limit),
        cost_estimate=pl.CostEstimate(flops=0, bytes_accessed=moved, transcendentals=0),
    )(*operands)


def swap(near, far):
    count = lax.axis_size("dom") * lax.axis_size("sub")
    outer = [(i, i + 1) for i in range(1, count - 1, 2)]
    inner = [(i, i + 1) for i in range(0, count - 1, 2)]
    outer += [(target, source) for source, target in outer]
    inner += [(target, source) for source, target in inner]
    far = lax.ppermute(far, chain, outer)
    return lax.ppermute(near, chain, inner), far


def sum_rounds():
    for axis in ("sample", "dom"):
        count = lax.axis_size(axis)
        step = 1
        while step < count:
            yield axis, [(i, i ^ step) for i in range(count)]
            step *= 2


def on_device(
    node_in,
    edge_in,
    senders,
    receivers,
    send_list,
    w_edge_first,
    b_edge_first,
    w_edge_second,
    b_edge_second,
    edge_gain,
    edge_shift,
    w_node_first,
    b_node_first,
    w_node_second,
    b_node_second,
    node_gain,
    node_shift,
    node_cotangent,
    edge_cotangent,
):
    node = node_in[0]
    edge = edge_in[0]
    nodes = node.shape[0]
    edges = edge.shape[0]
    rim = send_list.shape[2]
    rim_shape = ((rim, lane), bf16)
    snd_half = nodes // 2
    rcv_half = (nodes + 2 * rim) // 2
    kept = -(-(7 * lane + sum_rows) // (2 * sum_rows)) * sum_rows
    row = lambda x: x.reshape(1, lane)
    small = [w_edge_first, w_edge_second, w_node_first, w_node_second]
    small += [row(b_edge_first), row(b_edge_second), row(edge_gain), row(edge_shift)]
    small += [row(b_node_first), row(b_node_second), row(node_gain), row(node_shift)]
    chunks = edges // lane
    sources = [
        node,
        senders.reshape(chunks, lane),
        receivers.reshape(chunks, lane),
        send_list[0],
        edge,
        edge_cotangent[0],
        node_cotangent[0],
    ] + small
    node, ids, edge, edge_cot, node_cot, weights, vectors, rim_near, rim_far = call(
        first_kernel,
        [
            ((nodes, lane), bf16),
            ((2 * chunks + 2, lane), jnp.int32),
            ((edges, lane), bf16),
            ((edges, lane), bf16),
            ((nodes, lane), bf16),
            ((7 * lane, lane), bf16),
            ((8, lane), f32),
            rim_shape,
            rim_shape,
        ],
        [],
        *sources,
        anywhere=len(sources),
        sems=len(sources),
    )
    near, far = swap(rim_near, rim_far)
    snd_column, rcv_column, z_sent, rcv_local = call(
        prepare_kernel,
        [
            ((edges, lane), jnp.int32),
            ((edges, lane), jnp.int32),
            ((edges, lane), f32),
            ((nodes, lane), bf16),
        ],
        [((snd_half, 2 * lane), bf16)],
        ids,
        node,
        weights,
        vectors,
        edge,
    )
    edge_out, z, message, agg_near, agg_far = call(
        edge_forward_kernel,
        [((edges, lane), bf16), ((edges, lane), f32), ((edges, lane), bf16), rim_shape, rim_shape],
        [
            ((2 * rim, lane), bf16),
            ((rcv_half, 2 * lane), bf16),
            ((lane, 2 * lane), bf16),
            ((2 * rim, lane), f32),
        ],
        near,
        far,
        edge,
        ids,
        weights,
        vectors,
        rcv_column,
        z_sent,
        rcv_local,
    )
    back_near, back_far = swap(agg_near, agg_far)
    (agg,) = call(
        collect_kernel,
        [((nodes, lane), f32)],
        [((snd_half, 2 * lane), f32)],
        ids,
        rcv_column,
        message,
    )
    node_out, base, dagg, dagg_rim_near, dagg_rim_far, node_grads = call(
        node_kernel,
        [
            ((nodes, lane), bf16),
            ((nodes, lane), f32),
            ((nodes, lane), bf16),
            rim_shape,
            rim_shape,
            ((3 * lane + sum_rows, lane), f32),
        ],
        [],
        node,
        agg,
        back_near,
        back_far,
        ids,
        weights,
        vectors,
        node_cot,
    )
    dagg_near, dagg_far = swap(dagg_rim_near, dagg_rim_far)
    (upstream,) = call(
        upstream_kernel,
        [((edges, lane), f32)],
        [((snd_half, 2 * lane), bf16)],
        rcv_column,
        dagg,
        edge_cot,
    )
    dz, snd_sum, rcv_sum, grad_far, grads_kept, grads_sent = call(
        edge_backward_kernel,
        [
            ((edges, lane), bf16),
            ((nodes, lane), bf16),
            ((nodes, lane), bf16),
            rim_shape,
            ((kept, lane), f32),
            ((kept + rim, lane), bf16),
        ],
        [
            ((2 * rim, lane), bf16),
            ((2 * kept, lane), f32),
            ((2 * rim, lane), bf16),
            ((lane, 2 * lane), bf16),
            ((snd_half, 2 * lane), f32),
            ((rcv_half, 2 * lane), f32),
            ((2 * lane, lane), f32),
            ((8, lane), f32),
        ],
        z,
        upstream,
        edge,
        ids,
        node,
        near,
        far,
        dagg_near,
        dagg_far,
        weights,
        vectors,
        node_grads,
        snd_column,
        rcv_column,
    )
    returned_near, returned_far = swap(grads_sent, grad_far)
    (edge_grad,) = call(
        edge_grad_kernel, [((edges, lane), bf16)], [], dz, edge_cot, weights
    )
    (node_grad,) = call(
        node_grad_kernel,
        [((nodes, lane), bf16)],
        [],
        base,
        snd_sum,
        rcv_sum,
        weights,
        returned_near,
        returned_far,
        ids,
    )
    half_shape = ((kept, lane), bf16)
    (grads,) = call(add_kernel, [half_shape], [], grads_kept, returned_near)
    between = [[returned_far, edge_grad], [node_grad]]
    for number, (axis, pairs) in enumerate(sum_rounds()):
        other = lax.ppermute(grads, axis, pairs)
        early = between[number] if number < len(between) else []
        written = 1 if early else 0
        (grads,) = call(add_kernel, [half_shape], [], grads, other, *early, anywhere=written)
    others = lax.ppermute(grads, "sub", [(0, 1), (1, 0)])
    matrices = [3 * lane, lane, 2 * lane, lane]
    totals = call(
        finish_kernel,
        [((height, lane), f32) for height in matrices] + [((1, lane), f32)] * 8,
        [((2 * kept, lane), f32)],
        grads,
        others,
    )
    flat = [total.reshape(lane) for total in totals[4:]]
    return (
        node_out[None],
        edge_out[None],
        node_grad[None],
        edge_grad[None],
        totals[0],
        flat[0],
        totals[1],
        flat[1],
        flat[2],
        flat[3],
        totals[2],
        flat[4],
        totals[3],
        flat[5],
        flat[6],
        flat[7],
    )


def solution(mesh):
    node_spec = P(("groups", "sample"), ("dom", "sub"), None)
    ids_spec = P(("dom", "sub"))
    return jax.shard_map(
        on_device,
        mesh=mesh,
        in_specs=(
            (node_spec, node_spec, ids_spec, ids_spec, P(("dom", "sub"), None, None))
            + (P(),) * 12
            + (node_spec, node_spec)
        ),
        out_specs=(
            (node_spec,) * 4
            + (P("groups", None), P("groups"), P("groups", None), P("groups"), P("groups"), P("groups"))
            * 2
        ),
        check_vma=False,
    )
```

```python
import jax
import jax.numpy as jnp
from jax import lax
from jax.experimental import pallas as pl
from jax.experimental.pallas import tpu as pltpu
from jax.sharding import PartitionSpec as P

epsilon = 1e-05
rows_dims = (((0,), (0,)), ((), ()))
back_dims = (((1,), (1,)), ((), ()))
f32 = jnp.float32
bf16 = jnp.bfloat16
lane = 128
edge_tile = 512
vmem_limit = 32 * 1024 * 1024
sum_rows = 16
chain = ("dom", "sub")


def dot(left, right):
    return jnp.dot(left, right, preferred_element_type=f32)


def dot_rows(left, right):
    return lax.dot_general(left, right, rows_dims, preferred_element_type=f32)


def dot_back(left, right):
    return lax.dot_general(left, right, back_dims, preferred_element_type=f32)


def column_of(row):
    return jnp.broadcast_to(row, (lane, lane)).T


def hot_columns(low, *spans):
    targets = lax.broadcasted_iota(jnp.int16, low.shape, 1)
    one, zero = jnp.ones((), bf16), jnp.zeros((), bf16)
    parts = [
        jnp.where(low == targets + jnp.int16(at), one, zero)
        for start, stop in spans
        for at in range(start, stop, lane)
    ]
    return jnp.concatenate(parts, axis=1)


def hot_rows(row, height):
    low = jnp.broadcast_to(row, (16, lane)).astype(jnp.int16)
    targets = lax.broadcasted_iota(jnp.int16, (height, lane), 0).reshape(height // 16, 16, lane)
    one, zero = jnp.ones((), bf16), jnp.zeros((), bf16)
    return jnp.where(targets == low[None], one, zero).reshape(height, lane)


def folded(ids, half):
    return jnp.where((ids >= half) & (ids < 2 * half), ids - half, ids)


def side_by_side(rows):
    half = rows.shape[0] // 2
    return jnp.concatenate([rows[:half], rows[half:]], axis=1)


def pick(ids, low, half, table, *halo):
    both = dot(hot_columns(low, (0, half), *halo), table)
    return jnp.where(ids >= half, both[:, lane:], both[:, :lane])


def rows_of_ids(ids_ref, first, count, height, change):
    parts = [hot_rows(change(ids_ref[pl.ds(first + k, 1), :]), height) for k in range(count)]
    return jnp.concatenate(parts, axis=1)


def spread(ids_ref, first, count, half, ids, values):
    upper = ids >= half
    paired = jnp.concatenate(
        [jnp.where(upper, 0.0, values).astype(bf16), jnp.where(upper, values, 0.0).astype(bf16)],
        axis=1,
    )
    return dot(rows_of_ids(ids_ref, first, count, half, lambda row: folded(row, half)), paired)


def sigmoid(z):
    return 0.5 * jnp.tanh(0.5 * z) + 0.5


def vector(vectors_ref, k):
    return vectors_ref[k : k + 1, :]


def centred_second(w, b):
    w = w.astype(f32)
    w = w - jnp.mean(w, axis=1, keepdims=True)
    high = w.astype(bf16)
    low = (w - high.astype(f32)).astype(bf16)
    return jnp.concatenate([high, low], axis=1), b - jnp.mean(b, axis=1, keepdims=True)


def mean_weights():
    shape = (2 * lane, 2 * lane)
    left = lax.broadcasted_iota(jnp.int32, shape, 0) < lane
    right = lax.broadcasted_iota(jnp.int32, shape, 1) < lane
    return jnp.where(left == right, 1.0 / lane, 0.0).astype(bf16)


def normed_of(act, w_pair, b_centred, means):
    both = dot(act, w_pair)
    center = both[:, :lane] + both[:, lane:] + b_centred
    variance = dot((center * center).astype(bf16), means[:lane, :lane])
    scale_inv = lax.rsqrt(variance + epsilon)
    return center * scale_inv, scale_inv


def back_norm(upstream, normed, scale_inv, gain, means):
    d_normed = upstream * gain
    pair = jnp.concatenate([d_normed.astype(bf16), (d_normed * normed).astype(bf16)], axis=1)
    both = dot(pair, means)
    return scale_inv * (d_normed - both[:, :lane] - normed * both[:, lane:])


def column_sum(values):
    return jnp.sum(values, axis=0, keepdims=True)


def eight_sums(values):
    return jnp.sum(values.reshape(values.shape[0] // 8, 8, lane), axis=0)


def parity_of_place():
    return lax.axis_index(chain) % 2


def first_kernel(
    node_hbm,
    snd_hbm,
    rcv_hbm,
    list_hbm,
    edge_hbm,
    edge_cot_hbm,
    node_cot_hbm,
    *refs,
):
    small = refs[:12]
    node_ref, ids_ref, edge_ref, edge_cot_ref, node_cot_ref, weights_ref, vectors_ref = refs[12:19]
    near_ref, far_ref, sems = refs[19:]
    chunks = snd_hbm.shape[0]
    moves = [
        (node_hbm, node_ref),
        (list_hbm, ids_ref.at[2 * chunks : 2 * chunks + 2]),
        (snd_hbm, ids_ref.at[:chunks]),
        (rcv_hbm, ids_ref.at[chunks : 2 * chunks]),
    ]
    at = 0
    for source in small[:4]:
        moves.append((source, weights_ref.at[at : at + source.shape[0]]))
        at += source.shape[0]
    for k, source in enumerate(small[4:]):
        moves.append((source, vectors_ref.at[k : k + 1]))
    moves += [(edge_hbm, edge_ref), (edge_cot_hbm, edge_cot_ref), (node_cot_hbm, node_cot_ref)]
    copies = [
        pltpu.make_async_copy(source, target, sems.at[k])
        for k, (source, target) in enumerate(moves)
    ]
    for copy in copies:
        copy.start()
    for copy in copies[:2]:
        copy.wait()
    parity = parity_of_place()
    node = node_ref[...]
    for side, out_ref in ((1 - parity, near_ref), (parity, far_ref)):
        column = column_of(ids_ref[pl.ds(2 * chunks + side, 1), :]).astype(jnp.int16)
        hot = hot_columns(column, (0, node.shape[0]))
        out_ref[...] = dot(hot, node).astype(bf16)
    for copy in copies[2:]:
        copy.wait()


def prepare_kernel(
    ids_ref,
    node_ref,
    weights_ref,
    vectors_ref,
    edge_ref,
    snd_column,
    rcv_column,
    snd_low,
    rcv_low,
    z_ref,
    rcv_local,
    snd_table,
):
    chunks = snd_column.shape[0] // lane
    half = snd_table.shape[0]
    for k in range(chunks):
        at = slice(k * lane, (k + 1) * lane)
        snd = column_of(ids_ref[k : k + 1, :])
        rcv = column_of(ids_ref[chunks + k : chunks + k + 1, :])
        snd_column[at, :] = snd
        rcv_column[at, :] = rcv
        snd_low[at, :] = folded(snd, half).astype(jnp.int16)
        rcv_low[at, :] = folded(rcv, half).astype(jnp.int16)
    node = node_ref[...]
    snd_table[...] = side_by_side(dot(node, weights_ref[lane : 2 * lane]).astype(bf16))
    rcv_local[...] = side_by_side(dot(node, weights_ref[2 * lane : 3 * lane]).astype(bf16))
    w1_edge = weights_ref[:lane]
    b1 = vector(vectors_ref, 0)

    def tile(i, carry):
        rows = pl.ds(pl.multiple_of(i * edge_tile, edge_tile), edge_tile)
        z = dot(edge_ref[rows, :], w1_edge) + b1
        z_ref[rows, :] = z + pick(snd_column[rows, :], snd_low[rows, :], half, snd_table[...])
        return carry

    lax.fori_loop(0, edge_ref.shape[0] // edge_tile, tile, 0)


def edge_forward_kernel(
    near_ref,
    far_ref,
    edge_ref,
    ids_ref,
    weights_ref,
    vectors_ref,
    rcv_column,
    rcv_low,
    z_sent,
    rcv_local,
    out_ref,
    z_ref,
    normed_ref,
    scale_ref,
    message_ref,
    agg_near_ref,
    agg_far_ref,
    table,
    w2_pair,
    means,
    total,
):
    half = rcv_local.shape[0]
    nodes = 2 * half
    rim = near_ref.shape[0]
    parity = parity_of_place()
    near_at = pl.multiple_of((1 - parity) * rim, rim)
    far_at = pl.multiple_of(parity * rim, rim)
    w1_rcv = weights_ref[2 * lane : 3 * lane]
    gain, shift = vector(vectors_ref, 2), vector(vectors_ref, 3)
    table[:half, :] = rcv_local[...]
    table[half:, :lane] = jnp.zeros((2 * rim, lane), bf16)
    table[pl.ds(half + near_at, rim), lane:] = dot(near_ref[...], w1_rcv).astype(bf16)
    table[pl.ds(half + far_at, rim), lane:] = dot(far_ref[...], w1_rcv).astype(bf16)
    pair, b2 = centred_second(weights_ref[3 * lane : 4 * lane], vector(vectors_ref, 1))
    w2_pair[...] = pair
    means[...] = mean_weights()
    total[...] = jnp.zeros_like(total)

    def tile(i, carry):
        rows = pl.ds(pl.multiple_of(i * edge_tile, edge_tile), edge_tile)
        x = edge_ref[rows, :]
        slots = (nodes, nodes + 2 * rim)
        z = z_sent[rows, :]
        z = z + pick(rcv_column[rows, :], rcv_low[rows, :], half, table[...], slots)
        z_ref[rows, :] = z
        act = (z * sigmoid(z)).astype(bf16)
        normed, scale_inv = normed_of(act, w2_pair[...], b2, means[...])
        normed_ref[rows, :] = normed
        scale_ref[rows, :] = scale_inv
        update = normed * gain + shift
        out_ref[rows, :] = (x.astype(f32) + update).astype(bf16)
        message = update.astype(bf16)
        message_ref[rows, :] = message
        first = (rcv_column.shape[0] + i * edge_tile) // lane
        hot = rows_of_ids(ids_ref, first, edge_tile // lane, 2 * rim, lambda row: row - nodes)
        total[...] += dot(hot, message)
        return carry

    lax.fori_loop(0, edge_ref.shape[0] // edge_tile, tile, 0)
    agg_near_ref[...] = total[pl.ds(near_at, rim), :].astype(bf16)
    agg_far_ref[...] = total[pl.ds(far_at, rim), :].astype(bf16)


def collect_kernel(ids_ref, rcv_column, message_ref, edge_ref, agg_ref, turned_ref, total):
    half = total.shape[0]
    total[...] = jnp.zeros_like(total)

    def tile(i, carry):
        rows = pl.ds(pl.multiple_of(i * edge_tile, edge_tile), edge_tile)
        first = (rcv_column.shape[0] + i * edge_tile) // lane
        message = message_ref[rows, :].astype(f32)
        total[...] += spread(ids_ref, first, edge_tile // lane, half, rcv_column[rows, :], message)
        turned_ref[:, rows] = edge_ref[rows, :].T
        return carry

    lax.fori_loop(0, rcv_column.shape[0] // edge_tile, tile, 0)
    agg_ref[:half, :] = total[:, :lane]
    agg_ref[half:, :] = total[:, lane:]


def hot_lists(ids_ref, nodes):
    parity = parity_of_place()
    first = ids_ref.shape[0] - 2
    near = ids_ref[pl.ds(first + 1 - parity, 1), :]
    far = ids_ref[pl.ds(first + parity, 1), :]
    return jnp.concatenate([hot_rows(near, nodes), hot_rows(far, nodes)], axis=1)


def node_kernel(
    node_ref,
    agg_ref,
    near_ref,
    far_ref,
    ids_ref,
    weights_ref,
    vectors_ref,
    cot_ref,
    out_ref,
    base_ref,
    dagg_ref,
    rim_near_ref,
    rim_far_ref,
    grads_ref,
):
    nodes = node_ref.shape[0]
    node = node_ref[...]
    returned = jnp.concatenate([near_ref[...], far_ref[...]], axis=0)
    agg = (agg_ref[...] + dot(hot_lists(ids_ref, nodes), returned)).astype(bf16)
    x = jnp.concatenate([node, agg], axis=1)
    w1 = weights_ref[4 * lane : 6 * lane]
    w2 = weights_ref[6 * lane :]
    z = dot(x, w1) + vector(vectors_ref, 4)
    sig = sigmoid(z)
    act = (z * sig).astype(bf16)
    pair, b2 = centred_second(w2, vector(vectors_ref, 5))
    means = mean_weights()
    normed, scale_inv = normed_of(act, pair, b2, means)
    gain = vector(vectors_ref, 6)
    out_ref[...] = (node.astype(f32) + normed * gain + vector(vectors_ref, 7)).astype(bf16)
    upstream = cot_ref[...].astype(f32)
    dz2 = back_norm(upstream, normed, scale_inv, gain, means)
    dz2b = dz2.astype(bf16)
    da = dot_back(dz2b, w2)
    dz1 = da * sig * (1.0 + z * (1.0 - sig))
    dz1b = dz1.astype(bf16)
    dx = dot_back(dz1b, w1)
    base_ref[...] = upstream + dx[:, :lane]
    dagg = dx[:, lane:].astype(bf16)
    dagg_ref[...] = dagg
    parity = parity_of_place()
    first = ids_ref.shape[0] - 2
    for side, rim_ref in ((1 - parity, rim_near_ref), (parity, rim_far_ref)):
        column = column_of(ids_ref[pl.ds(first + side, 1), :]).astype(jnp.int16)
        picked = hot_columns(column, (0, nodes))
        rim_ref[...] = dot(picked, dagg).astype(bf16)
    first = 2 * lane
    second = first + lane
    grads_ref[:first, :] = dot_rows(x, dz1b)
    grads_ref[first:second, :] = dot_rows(act, dz2b)
    sums = [column_sum(dz1), column_sum(dz2), column_sum(upstream * normed), column_sum(upstream)]
    sums.append(jnp.zeros((sum_rows - len(sums), lane), f32))
    grads_ref[second:, :] = jnp.concatenate(sums, axis=0)


def upstream_kernel(
    rcv_column, rcv_low, dagg_ref, cot_ref, z_ref, up_ref, slope_ref, act_ref, table
):
    half = table.shape[0]
    table[...] = side_by_side(dagg_ref[...])

    def tile(i, carry):
        rows = pl.ds(pl.multiple_of(i * edge_tile, edge_tile), edge_tile)
        local = pick(rcv_column[rows, :], rcv_low[rows, :], half, table[...])
        up_ref[rows, :] = cot_ref[rows, :].astype(f32) + local
        z = z_ref[rows, :]
        sig = sigmoid(z)
        slope_ref[rows, :] = sig * (1.0 + z * (1.0 - sig))
        act_ref[:, rows] = (z * sig).astype(bf16).T
        return carry

    lax.fori_loop(0, cot_ref.shape[0] // edge_tile, tile, 0)


def edge_backward_kernel(
    up_ref,
    normed_ref,
    scale_ref,
    slope_ref,
    act_ref,
    turned_ref,
    ids_ref,
    node_ref,
    near_ref,
    far_ref,
    dagg_near_ref,
    dagg_far_ref,
    weights_ref,
    vectors_ref,
    node_grads_ref,
    snd_column,
    rcv_column,
    rcv_low,
    dz_ref,
    snd_sum_ref,
    rcv_sum_ref,
    far_back_ref,
    kept_ref,
    sent_ref,
    halo,
    grads_ref,
    table,
    means,
    snd_total,
    rcv_total,
    halo_total,
    squares,
    sums,
):
    nodes = node_ref.shape[0]
    rim = near_ref.shape[0]
    half = snd_total.shape[0]
    parity = parity_of_place()
    near_at = pl.multiple_of((1 - parity) * rim, rim)
    far_at = pl.multiple_of(parity * rim, rim)
    w2 = weights_ref[3 * lane : 4 * lane]
    gain = vector(vectors_ref, 2)
    table[pl.ds(near_at, rim), :] = dagg_near_ref[...]
    table[pl.ds(far_at, rim), :] = dagg_far_ref[...]
    halo[pl.ds(near_at, rim), :] = near_ref[...]
    halo[pl.ds(far_at, rim), :] = far_ref[...]
    means[...] = mean_weights()
    for total in (snd_total, rcv_total, halo_total, squares, sums):
        total[...] = jnp.zeros_like(total)

    def tile(i, carry):
        rows = pl.ds(pl.multiple_of(i * edge_tile, edge_tile), edge_tile)
        chunk = edge_tile // lane
        hot = hot_columns(rcv_low[rows, :], (nodes, nodes + 2 * rim))
        upstream = up_ref[rows, :] + dot(hot, table[...])
        normed = normed_ref[rows, :]
        dz2 = back_norm(upstream, normed, scale_ref[rows, :], gain, means[...])
        dz2b = dz2.astype(bf16)
        dz1 = dot_back(dz2b, w2) * slope_ref[rows, :]
        dz1b = dz1.astype(bf16)
        dz_ref[rows, :] = dz1b
        squares[:lane, :] += dot(turned_ref[:, rows], dz1b)
        squares[lane:, :] += dot(act_ref[:, rows], dz2b)
        sums[0:8, :] += eight_sums(dz1)
        sums[8:16, :] += eight_sums(dz2)
        sums[16:24, :] += eight_sums(upstream * normed)
        sums[24:32, :] += eight_sums(upstream)
        first = rcv_column.shape[0] // lane + i * chunk
        snd_total[...] += spread(ids_ref, i * chunk, chunk, half, snd_column[rows, :], dz1)
        rcv_total[...] += spread(ids_ref, first, chunk, half, rcv_column[rows, :], dz1)
        slots = rows_of_ids(ids_ref, first, chunk, 2 * rim, lambda row: row - nodes)
        halo_total[...] += dot(slots, dz1b)
        return carry

    lax.fori_loop(0, up_ref.shape[0] // edge_tile, tile, 0)
    snd_sum = jnp.concatenate([snd_total[:, :lane], snd_total[:, lane:]], axis=0).astype(bf16)
    rcv_sum = jnp.concatenate([rcv_total[:, :lane], rcv_total[:, lane:]], axis=0).astype(bf16)
    halo_sum = halo_total[...].astype(bf16)
    snd_sum_ref[...] = snd_sum
    rcv_sum_ref[...] = rcv_sum
    w1_rcv = weights_ref[2 * lane : 3 * lane]
    kept = kept_ref.shape[0]
    for at, back_ref in ((near_at, sent_ref.at[kept:]), (far_at, far_back_ref)):
        returned = halo_total[pl.ds(at, rim), :].astype(bf16)
        back_ref[...] = dot_back(returned, w1_rcv).astype(bf16)
    extended = jnp.concatenate([node_ref[...], halo[...]], axis=0)
    extended_sum = jnp.concatenate([rcv_sum, halo_sum], axis=0)
    grads_ref[:lane, :] = squares[:lane, :]
    grads_ref[lane : 2 * lane, :] = dot_rows(node_ref[...], snd_sum)
    grads_ref[2 * lane : 3 * lane, :] = dot_rows(extended, extended_sum)
    grads_ref[3 * lane : 4 * lane, :] = squares[lane:, :]
    node_rows = node_grads_ref.shape[0] - sum_rows
    last = 4 * lane + node_rows
    grads_ref[4 * lane : last, :] = node_grads_ref[:node_rows, :]
    grads_ref[last : last + sum_rows, :] = jnp.concatenate(
        [column_sum(sums[8 * k : 8 * k + 8, :]) for k in range(4)]
        + [node_grads_ref[node_rows : node_rows + 4, :], jnp.zeros((8, lane), f32)],
        axis=0,
    )
    if last + sum_rows < grads_ref.shape[0]:
        grads_ref[last + sum_rows :, :] = jnp.zeros(
            (grads_ref.shape[0] - last - sum_rows, lane), f32
        )
    own = lax.axis_index("sub")
    kept_ref[...] = grads_ref[pl.ds(pl.multiple_of(own * kept, sum_rows), kept), :]
    other = pl.multiple_of((1 - own) * kept, sum_rows)
    sent_ref[:kept, :] = grads_ref[pl.ds(other, kept), :].astype(bf16)


def edge_grad_kernel(dz_ref, cot_ref, weights_ref, out_ref):
    w1_edge = weights_ref[:lane]

    def tile(i, carry):
        rows = pl.ds(pl.multiple_of(i * edge_tile, edge_tile), edge_tile)
        cot = cot_ref[rows, :].astype(f32)
        out_ref[rows, :] = (cot + dot_back(dz_ref[rows, :], w1_edge)).astype(bf16)
        return carry

    lax.fori_loop(0, cot_ref.shape[0] // edge_tile, tile, 0)


def node_grad_kernel(
    base_ref, snd_sum_ref, rcv_sum_ref, weights_ref, near_ref, far_ref, ids_ref, out_ref
):
    rim = far_ref.shape[0]
    returned = jnp.concatenate([near_ref[near_ref.shape[0] - rim :, :], far_ref[...]], axis=0)
    total = base_ref[...] + dot_back(snd_sum_ref[...], weights_ref[lane : 2 * lane])
    total = total + dot_back(rcv_sum_ref[...], weights_ref[2 * lane : 3 * lane])
    hot = hot_lists(ids_ref, base_ref.shape[0])
    out_ref[...] = (total + dot(hot, returned)).astype(bf16)


def add_kernel(own_ref, other_ref, *refs):
    own = own_ref[...].astype(f32)
    refs[-1][...] = (own + other_ref[: own.shape[0], :].astype(f32)).astype(bf16)


def finish_kernel(own_ref, other_ref, *refs):
    out_refs, total_ref = refs[:-1], refs[-1]
    kept = own_ref.shape[0]
    own = lax.axis_index("sub")
    total_ref[pl.ds(pl.multiple_of(own * kept, sum_rows), kept), :] = own_ref[...].astype(f32)
    other = pl.multiple_of((1 - own) * kept, sum_rows)
    total_ref[pl.ds(other, kept), :] = other_ref[...].astype(f32)
    at = 0
    for out_ref in out_refs[:4]:
        out_ref[...] = total_ref[at : at + out_ref.shape[0], :]
        at += out_ref.shape[0]
    for k, out_ref in enumerate(out_refs[4:]):
        out_ref[...] = total_ref[at + k : at + k + 1, :]


def call(kernel, outs, scratch, *operands, anywhere=0, sems=0):
    moved = sum(x.size * x.dtype.itemsize for x in operands)
    held = operands[len(operands) - anywhere :]
    operands = operands[: len(operands) - anywhere]
    operands += tuple(pltpu.with_memory_space_constraint(x, pltpu.HBM) for x in held)
    inside = [pl.BlockSpec(memory_space=pltpu.VMEM)] * (len(operands) - anywhere)
    outside = [pl.BlockSpec(memory_space=pl.ANY)] * anywhere
    scratch_shapes = [pltpu.VMEM(shape, dtype) for shape, dtype in scratch]
    if sems:
        scratch_shapes.append(pltpu.SemaphoreType.DMA((sems,)))
    return pl.pallas_call(
        kernel,
        out_shape=[jax.ShapeDtypeStruct(shape, dtype) for shape, dtype in outs],
        in_specs=inside + outside,
        out_specs=[pl.BlockSpec(memory_space=pltpu.VMEM)] * len(outs),
        scratch_shapes=scratch_shapes,
        compiler_params=pltpu.CompilerParams(vmem_limit_bytes=vmem_limit),
        cost_estimate=pl.CostEstimate(flops=0, bytes_accessed=moved, transcendentals=0),
    )(*operands)


def swap(near, far):
    count = lax.axis_size("dom") * lax.axis_size("sub")
    outer = [(i, i + 1) for i in range(1, count - 1, 2)]
    inner = [(i, i + 1) for i in range(0, count - 1, 2)]
    outer += [(target, source) for source, target in outer]
    inner += [(target, source) for source, target in inner]
    far = lax.ppermute(far, chain, outer)
    return lax.ppermute(near, chain, inner), far


def sum_rounds():
    for axis in ("sample", "dom"):
        count = lax.axis_size(axis)
        step = 1
        while step < count:
            yield axis, [(i, i ^ step) for i in range(count)]
            step *= 2


def on_device(
    node_in,
    edge_in,
    senders,
    receivers,
    send_list,
    w_edge_first,
    b_edge_first,
    w_edge_second,
    b_edge_second,
    edge_gain,
    edge_shift,
    w_node_first,
    b_node_first,
    w_node_second,
    b_node_second,
    node_gain,
    node_shift,
    node_cotangent,
    edge_cotangent,
):
    node = node_in[0]
    edge = edge_in[0]
    nodes = node.shape[0]
    edges = edge.shape[0]
    rim = send_list.shape[2]
    rim_shape = ((rim, lane), bf16)
    snd_half = nodes // 2
    kept = -(-(7 * lane + sum_rows) // (2 * sum_rows)) * sum_rows
    row = lambda x: x.reshape(1, lane)
    small = [w_edge_first, w_edge_second, w_node_first, w_node_second]
    small += [row(b_edge_first), row(b_edge_second), row(edge_gain), row(edge_shift)]
    small += [row(b_node_first), row(b_node_second), row(node_gain), row(node_shift)]
    chunks = edges // lane
    sources = [
        node,
        senders.reshape(chunks, lane),
        receivers.reshape(chunks, lane),
        send_list[0],
        edge,
        edge_cotangent[0],
        node_cotangent[0],
    ] + small
    node, ids, edge, edge_cot, node_cot, weights, vectors, rim_near, rim_far = call(
        first_kernel,
        [
            ((nodes, lane), bf16),
            ((2 * chunks + 2, lane), jnp.int32),
            ((edges, lane), bf16),
            ((edges, lane), bf16),
            ((nodes, lane), bf16),
            ((7 * lane, lane), bf16),
            ((8, lane), f32),
            rim_shape,
            rim_shape,
        ],
        [],
        *sources,
        anywhere=len(sources),
        sems=len(sources),
    )
    near, far = swap(rim_near, rim_far)
    snd_column, rcv_column, snd_low, rcv_low, z_sent, rcv_local = call(
        prepare_kernel,
        [
            ((edges, lane), jnp.int32),
            ((edges, lane), jnp.int32),
            ((edges, lane), jnp.int16),
            ((edges, lane), jnp.int16),
            ((edges, lane), f32),
            ((snd_half, 2 * lane), bf16),
        ],
        [((snd_half, 2 * lane), bf16)],
        ids,
        node,
        weights,
        vectors,
        edge,
    )
    edge_out, z, normed, scale, message, agg_near, agg_far = call(
        edge_forward_kernel,
        [
            ((edges, lane), bf16),
            ((edges, lane), f32),
            ((edges, lane), f32),
            ((edges, lane), f32),
            ((edges, lane), bf16),
            rim_shape,
            rim_shape,
        ],
        [
            ((snd_half + 2 * rim, 2 * lane), bf16),
            ((lane, 2 * lane), bf16),
            ((2 * lane, 2 * lane), bf16),
            ((2 * rim, lane), f32),
        ],
        near,
        far,
        edge,
        ids,
        weights,
        vectors,
        rcv_column,
        rcv_low,
        z_sent,
        rcv_local,
    )
    back_near, back_far = swap(agg_near, agg_far)
    agg, turned = call(
        collect_kernel,
        [((nodes, lane), f32), ((lane, edges), bf16)],
        [((snd_half, 2 * lane), f32)],
        ids,
        rcv_column,
        message,
        edge,
    )
    node_out, base, dagg, dagg_rim_near, dagg_rim_far, node_grads = call(
        node_kernel,
        [
            ((nodes, lane), bf16),
            ((nodes, lane), f32),
            ((nodes, lane), bf16),
            rim_shape,
            rim_shape,
            ((3 * lane + sum_rows, lane), f32),
        ],
        [],
        node,
        agg,
        back_near,
        back_far,
        ids,
        weights,
        vectors,
        node_cot,
    )
    dagg_near, dagg_far = swap(dagg_rim_near, dagg_rim_far)
    upstream, slope, act = call(
        upstream_kernel,
        [((edges, lane), f32), ((edges, lane), f32), ((lane, edges), bf16)],
        [((snd_half, 2 * lane), bf16)],
        rcv_column,
        rcv_low,
        dagg,
        edge_cot,
        z,
    )
    dz, snd_sum, rcv_sum, grad_far, grads_kept, grads_sent = call(
        edge_backward_kernel,
        [
            ((edges, lane), bf16),
            ((nodes, lane), bf16),
            ((nodes, lane), bf16),
            rim_shape,
            ((kept, lane), f32),
            ((kept + rim, lane), bf16),
        ],
        [
            ((2 * rim, lane), bf16),
            ((2 * kept, lane), f32),
            ((2 * rim, lane), bf16),
            ((2 * lane, 2 * lane), bf16),
            ((snd_half, 2 * lane), f32),
            ((snd_half, 2 * lane), f32),
            ((2 * rim, lane), f32),
            ((2 * lane, lane), f32),
            ((32, lane), f32),
        ],
        upstream,
        normed,
        scale,
        slope,
        act,
        turned,
        ids,
        node,
        near,
        far,
        dagg_near,
        dagg_far,
        weights,
        vectors,
        node_grads,
        snd_column,
        rcv_column,
        rcv_low,
    )
    returned_near, returned_far = swap(grads_sent, grad_far)
    (edge_grad,) = call(
        edge_grad_kernel, [((edges, lane), bf16)], [], dz, edge_cot, weights
    )
    (node_grad,) = call(
        node_grad_kernel,
        [((nodes, lane), bf16)],
        [],
        base,
        snd_sum,
        rcv_sum,
        weights,
        returned_near,
        returned_far,
        ids,
    )
    half_shape = ((kept, lane), bf16)
    (grads,) = call(add_kernel, [half_shape], [], grads_kept, returned_near)
    between = [[returned_far, edge_grad], [node_grad]]
    for number, (axis, pairs) in enumerate(sum_rounds()):
        other = lax.ppermute(grads, axis, pairs)
        early = between[number] if number < len(between) else []
        written = 1 if early else 0
        (grads,) = call(add_kernel, [half_shape], [], grads, other, *early, anywhere=written)
    others = lax.ppermute(grads, "sub", [(0, 1), (1, 0)])
    matrices = [3 * lane, lane, 2 * lane, lane]
    totals = call(
        finish_kernel,
        [((height, lane), f32) for height in matrices] + [((1, lane), f32)] * 8,
        [((2 * kept, lane), f32)],
        grads,
        others,
    )
    flat = [total.reshape(lane) for total in totals[4:]]
    return (
        node_out[None],
        edge_out[None],
        node_grad[None],
        edge_grad[None],
        totals[0],
        flat[0],
        totals[1],
        flat[1],
        flat[2],
        flat[3],
        totals[2],
        flat[4],
        totals[3],
        flat[5],
        flat[6],
        flat[7],
    )


def solution(mesh):
    node_spec = P(("groups", "sample"), ("dom", "sub"), None)
    ids_spec = P(("dom", "sub"))
    return jax.shard_map(
        on_device,
        mesh=mesh,
        in_specs=(
            (node_spec, node_spec, ids_spec, ids_spec, P(("dom", "sub"), None, None))
            + (P(),) * 12
            + (node_spec, node_spec)
        ),
        out_specs=(
            (node_spec,) * 4
            + (P("groups", None), P("groups"), P("groups", None), P("groups"), P("groups"), P("groups"))
            * 2
        ),
        check_vma=False,
    )
```

```python
import math

import jax
import jax.numpy as jnp
from jax import lax
from jax.experimental import pallas as pl
from jax.experimental.pallas import tpu as pltpu
from jax.sharding import PartitionSpec as P

epsilon = 1e-05
rows_dims = (((0,), (0,)), ((), ()))
back_dims = (((1,), (1,)), ((), ()))
f32 = jnp.float32
bf16 = jnp.bfloat16
lane = 128
edge_tile = 512
tile_group = 3
vmem_limit = 32 * 1024 * 1024
sum_rows = 16
chain = ("dom", "sub")


def each_tile(rows, tile):
    count = rows // edge_tile
    group = math.gcd(count, tile_group)

    def several(i, carry):
        for k in range(group):
            tile(i * group + k)
        return carry

    lax.fori_loop(0, count // group, several, 0)


def dot(left, right):
    return jnp.dot(left, right, preferred_element_type=f32)


def dot_rows(left, right):
    return lax.dot_general(left, right, rows_dims, preferred_element_type=f32)


def dot_back(left, right):
    return lax.dot_general(left, right, back_dims, preferred_element_type=f32)


def column_of(row):
    return jnp.broadcast_to(row, (lane, lane)).T


def hot_columns(low, *spans):
    targets = lax.broadcasted_iota(jnp.int16, low.shape, 1)
    one, zero = jnp.ones((), bf16), jnp.zeros((), bf16)
    parts = [
        jnp.where(low == targets + jnp.int16(at), one, zero)
        for start, stop in spans
        for at in range(start, stop, lane)
    ]
    return jnp.concatenate(parts, axis=1)


def hot_rows(row, height):
    low = jnp.broadcast_to(row, (16, lane)).astype(jnp.int16)
    targets = lax.broadcasted_iota(jnp.int16, (height, lane), 0).reshape(height // 16, 16, lane)
    one, zero = jnp.ones((), bf16), jnp.zeros((), bf16)
    return jnp.where(targets == low[None], one, zero).reshape(height, lane)


def folded(ids, half):
    return jnp.where((ids >= half) & (ids < 2 * half), ids - half, ids)


def side_by_side(rows):
    half = rows.shape[0] // 2
    return jnp.concatenate([rows[:half], rows[half:]], axis=1)


def pick(ids, low, half, table, *halo):
    both = dot(hot_columns(low, (0, half), *halo), table)
    return jnp.where(ids >= half, both[:, lane:], both[:, :lane])


def rows_of_ids(ids_ref, first, count, height, change):
    parts = [hot_rows(change(ids_ref[pl.ds(first + k, 1), :]), height) for k in range(count)]
    return jnp.concatenate(parts, axis=1)


def spread(ids_ref, first, count, half, ids, values):
    upper = ids >= half
    paired = jnp.concatenate(
        [jnp.where(upper, 0.0, values).astype(bf16), jnp.where(upper, values, 0.0).astype(bf16)],
        axis=1,
    )
    return dot(rows_of_ids(ids_ref, first, count, half, lambda row: folded(row, half)), paired)


def sigmoid(z):
    return 0.5 * jnp.tanh(0.5 * z) + 0.5


def vector(vectors_ref, k):
    return vectors_ref[k : k + 1, :]


def centred_second(w, b):
    w = w.astype(f32)
    w = w - jnp.mean(w, axis=1, keepdims=True)
    high = w.astype(bf16)
    low = (w - high.astype(f32)).astype(bf16)
    return jnp.concatenate([high, low], axis=1), b - jnp.mean(b, axis=1, keepdims=True)


def mean_weights():
    shape = (2 * lane, 2 * lane)
    left = lax.broadcasted_iota(jnp.int32, shape, 0) < lane
    right = lax.broadcasted_iota(jnp.int32, shape, 1) < lane
    return jnp.where(left == right, 1.0 / lane, 0.0).astype(bf16)


def normed_of(act, w_pair, b_centred, means):
    both = dot(act, w_pair)
    center = both[:, :lane] + both[:, lane:] + b_centred
    variance = dot((center * center).astype(bf16), means[:lane, :lane])
    scale_inv = lax.rsqrt(variance + epsilon)
    return center * scale_inv, scale_inv


def back_norm(upstream, normed, scale_inv, gain, means):
    d_normed = upstream * gain
    pair = jnp.concatenate([d_normed.astype(bf16), (d_normed * normed).astype(bf16)], axis=1)
    both = dot(pair, means)
    return scale_inv * (d_normed - both[:, :lane] - normed * both[:, lane:])


def column_sum(values):
    return jnp.sum(values, axis=0, keepdims=True)


def eight_sums(values):
    return jnp.sum(values.reshape(values.shape[0] // 8, 8, lane), axis=0)


def parity_of_place():
    return lax.axis_index(chain) % 2


def first_kernel(
    node_hbm,
    snd_hbm,
    rcv_hbm,
    list_hbm,
    edge_hbm,
    edge_cot_hbm,
    node_cot_hbm,
    *refs,
):
    small = refs[:12]
    node_ref, ids_ref, edge_ref, edge_cot_ref, node_cot_ref, weights_ref, vectors_ref = refs[12:19]
    near_ref, far_ref, sems = refs[19:]
    chunks = snd_hbm.shape[0]
    moves = [
        (node_hbm, node_ref),
        (list_hbm, ids_ref.at[2 * chunks : 2 * chunks + 2]),
        (snd_hbm, ids_ref.at[:chunks]),
        (rcv_hbm, ids_ref.at[chunks : 2 * chunks]),
    ]
    at = 0
    for source in small[:4]:
        moves.append((source, weights_ref.at[at : at + source.shape[0]]))
        at += source.shape[0]
    for k, source in enumerate(small[4:]):
        moves.append((source, vectors_ref.at[k : k + 1]))
    moves += [(edge_hbm, edge_ref), (edge_cot_hbm, edge_cot_ref), (node_cot_hbm, node_cot_ref)]
    copies = [
        pltpu.make_async_copy(source, target, sems.at[k])
        for k, (source, target) in enumerate(moves)
    ]
    for copy in copies:
        copy.start()
    for copy in copies[:2]:
        copy.wait()
    parity = parity_of_place()
    node = node_ref[...]
    for side, out_ref in ((1 - parity, near_ref), (parity, far_ref)):
        column = column_of(ids_ref[pl.ds(2 * chunks + side, 1), :]).astype(jnp.int16)
        hot = hot_columns(column, (0, node.shape[0]))
        out_ref[...] = dot(hot, node).astype(bf16)
    for copy in copies[2:]:
        copy.wait()


def prepare_kernel(
    ids_ref,
    node_ref,
    weights_ref,
    vectors_ref,
    edge_ref,
    snd_column,
    rcv_column,
    snd_low,
    rcv_low,
    z_ref,
    rcv_local,
    snd_table,
):
    chunks = snd_column.shape[0] // lane
    half = snd_table.shape[0]
    for k in range(chunks):
        at = slice(k * lane, (k + 1) * lane)
        snd = column_of(ids_ref[k : k + 1, :])
        rcv = column_of(ids_ref[chunks + k : chunks + k + 1, :])
        snd_column[at, :] = snd
        rcv_column[at, :] = rcv
        snd_low[at, :] = folded(snd, half).astype(jnp.int16)
        rcv_low[at, :] = folded(rcv, half).astype(jnp.int16)
    node = node_ref[...]
    snd_table[...] = side_by_side(dot(node, weights_ref[lane : 2 * lane]).astype(bf16))
    rcv_local[...] = side_by_side(dot(node, weights_ref[2 * lane : 3 * lane]).astype(bf16))
    w1_edge = weights_ref[:lane]
    b1 = vector(vectors_ref, 0)

    def tile(i):
        rows = pl.ds(pl.multiple_of(i * edge_tile, edge_tile), edge_tile)
        z = dot(edge_ref[rows, :], w1_edge) + b1
        z_ref[rows, :] = z + pick(snd_column[rows, :], snd_low[rows, :], half, snd_table[...])

    each_tile(edge_ref.shape[0], tile)


def edge_forward_kernel(
    near_ref,
    far_ref,
    edge_ref,
    ids_ref,
    weights_ref,
    vectors_ref,
    rcv_column,
    rcv_low,
    z_sent,
    rcv_local,
    out_ref,
    z_ref,
    normed_ref,
    scale_ref,
    message_ref,
    agg_near_ref,
    agg_far_ref,
    table,
    w2_pair,
    means,
    total,
):
    half = rcv_local.shape[0]
    nodes = 2 * half
    rim = near_ref.shape[0]
    parity = parity_of_place()
    near_at = pl.multiple_of((1 - parity) * rim, rim)
    far_at = pl.multiple_of(parity * rim, rim)
    w1_rcv = weights_ref[2 * lane : 3 * lane]
    gain, shift = vector(vectors_ref, 2), vector(vectors_ref, 3)
    table[:half, :] = rcv_local[...]
    table[half:, :lane] = jnp.zeros((2 * rim, lane), bf16)
    table[pl.ds(half + near_at, rim), lane:] = dot(near_ref[...], w1_rcv).astype(bf16)
    table[pl.ds(half + far_at, rim), lane:] = dot(far_ref[...], w1_rcv).astype(bf16)
    pair, b2 = centred_second(weights_ref[3 * lane : 4 * lane], vector(vectors_ref, 1))
    w2_pair[...] = pair
    means[...] = mean_weights()
    total[...] = jnp.zeros_like(total)

    def tile(i):
        rows = pl.ds(pl.multiple_of(i * edge_tile, edge_tile), edge_tile)
        x = edge_ref[rows, :]
        slots = (nodes, nodes + 2 * rim)
        z = z_sent[rows, :]
        z = z + pick(rcv_column[rows, :], rcv_low[rows, :], half, table[...], slots)
        z_ref[rows, :] = z
        act = (z * sigmoid(z)).astype(bf16)
        normed, scale_inv = normed_of(act, w2_pair[...], b2, means[...])
        normed_ref[rows, :] = normed
        scale_ref[rows, :] = scale_inv
        update = normed * gain + shift
        out_ref[rows, :] = (x.astype(f32) + update).astype(bf16)
        message = update.astype(bf16)
        message_ref[rows, :] = message
        first = (rcv_column.shape[0] + i * edge_tile) // lane
        hot = rows_of_ids(ids_ref, first, edge_tile // lane, 2 * rim, lambda row: row - nodes)
        total[...] += dot(hot, message)

    each_tile(edge_ref.shape[0], tile)
    agg_near_ref[...] = total[pl.ds(near_at, rim), :].astype(bf16)
    agg_far_ref[...] = total[pl.ds(far_at, rim), :].astype(bf16)


def collect_kernel(ids_ref, rcv_column, message_ref, edge_ref, agg_ref, turned_ref, total):
    half = total.shape[0]
    total[...] = jnp.zeros_like(total)

    def tile(i):
        rows = pl.ds(pl.multiple_of(i * edge_tile, edge_tile), edge_tile)
        first = (rcv_column.shape[0] + i * edge_tile) // lane
        message = message_ref[rows, :].astype(f32)
        total[...] += spread(ids_ref, first, edge_tile // lane, half, rcv_column[rows, :], message)
        turned_ref[:, rows] = edge_ref[rows, :].T

    each_tile(rcv_column.shape[0], tile)
    agg_ref[:half, :] = total[:, :lane]
    agg_ref[half:, :] = total[:, lane:]


def hot_lists(ids_ref, nodes):
    parity = parity_of_place()
    first = ids_ref.shape[0] - 2
    near = ids_ref[pl.ds(first + 1 - parity, 1), :]
    far = ids_ref[pl.ds(first + parity, 1), :]
    return jnp.concatenate([hot_rows(near, nodes), hot_rows(far, nodes)], axis=1)


def node_kernel(
    node_ref,
    agg_ref,
    near_ref,
    far_ref,
    ids_ref,
    weights_ref,
    vectors_ref,
    cot_ref,
    out_ref,
    base_ref,
    dagg_ref,
    rim_near_ref,
    rim_far_ref,
    grads_ref,
):
    nodes = node_ref.shape[0]
    node = node_ref[...]
    returned = jnp.concatenate([near_ref[...], far_ref[...]], axis=0)
    agg = (agg_ref[...] + dot(hot_lists(ids_ref, nodes), returned)).astype(bf16)
    x = jnp.concatenate([node, agg], axis=1)
    w1 = weights_ref[4 * lane : 6 * lane]
    w2 = weights_ref[6 * lane :]
    z = dot(x, w1) + vector(vectors_ref, 4)
    sig = sigmoid(z)
    act = (z * sig).astype(bf16)
    pair, b2 = centred_second(w2, vector(vectors_ref, 5))
    means = mean_weights()
    normed, scale_inv = normed_of(act, pair, b2, means)
    gain = vector(vectors_ref, 6)
    out_ref[...] = (node.astype(f32) + normed * gain + vector(vectors_ref, 7)).astype(bf16)
    upstream = cot_ref[...].astype(f32)
    dz2 = back_norm(upstream, normed, scale_inv, gain, means)
    dz2b = dz2.astype(bf16)
    da = dot_back(dz2b, w2)
    dz1 = da * sig * (1.0 + z * (1.0 - sig))
    dz1b = dz1.astype(bf16)
    dx = dot_back(dz1b, w1)
    base_ref[...] = upstream + dx[:, :lane]
    dagg = dx[:, lane:].astype(bf16)
    dagg_ref[...] = dagg
    parity = parity_of_place()
    first = ids_ref.shape[0] - 2
    for side, rim_ref in ((1 - parity, rim_near_ref), (parity, rim_far_ref)):
        column = column_of(ids_ref[pl.ds(first + side, 1), :]).astype(jnp.int16)
        picked = hot_columns(column, (0, nodes))
        rim_ref[...] = dot(picked, dagg).astype(bf16)
    first = 2 * lane
    second = first + lane
    grads_ref[:first, :] = dot_rows(x, dz1b)
    grads_ref[first:second, :] = dot_rows(act, dz2b)
    sums = [column_sum(dz1), column_sum(dz2), column_sum(upstream * normed), column_sum(upstream)]
    sums.append(jnp.zeros((sum_rows - len(sums), lane), f32))
    grads_ref[second:, :] = jnp.concatenate(sums, axis=0)


def upstream_kernel(
    rcv_column, rcv_low, dagg_ref, cot_ref, z_ref, up_ref, slope_ref, act_ref, table
):
    half = table.shape[0]
    table[...] = side_by_side(dagg_ref[...])

    def tile(i):
        rows = pl.ds(pl.multiple_of(i * edge_tile, edge_tile), edge_tile)
        local = pick(rcv_column[rows, :], rcv_low[rows, :], half, table[...])
        up_ref[rows, :] = cot_ref[rows, :].astype(f32) + local
        z = z_ref[rows, :]
        sig = sigmoid(z)
        slope_ref[rows, :] = sig * (1.0 + z * (1.0 - sig))
        act_ref[:, rows] = (z * sig).astype(bf16).T

    each_tile(cot_ref.shape[0], tile)


def edge_backward_kernel(
    up_ref,
    normed_ref,
    scale_ref,
    slope_ref,
    act_ref,
    turned_ref,
    ids_ref,
    node_ref,
    near_ref,
    far_ref,
    dagg_near_ref,
    dagg_far_ref,
    weights_ref,
    vectors_ref,
    node_grads_ref,
    snd_column,
    rcv_column,
    rcv_low,
    dz_ref,
    snd_sum_ref,
    rcv_sum_ref,
    far_back_ref,
    kept_ref,
    sent_ref,
    halo,
    grads_ref,
    table,
    w2_turned,
    means,
    snd_total,
    rcv_total,
    halo_total,
    squares,
    sums,
):
    nodes = node_ref.shape[0]
    rim = near_ref.shape[0]
    half = snd_total.shape[0]
    parity = parity_of_place()
    near_at = pl.multiple_of((1 - parity) * rim, rim)
    far_at = pl.multiple_of(parity * rim, rim)
    w2_turned[...] = weights_ref[3 * lane : 4 * lane].T
    gain = vector(vectors_ref, 2)
    table[pl.ds(near_at, rim), :] = dagg_near_ref[...]
    table[pl.ds(far_at, rim), :] = dagg_far_ref[...]
    halo[pl.ds(near_at, rim), :] = near_ref[...]
    halo[pl.ds(far_at, rim), :] = far_ref[...]
    means[...] = mean_weights()
    for total in (snd_total, rcv_total, halo_total, squares, sums):
        total[...] = jnp.zeros_like(total)

    def tile(i):
        rows = pl.ds(pl.multiple_of(i * edge_tile, edge_tile), edge_tile)
        chunk = edge_tile // lane
        hot = hot_columns(rcv_low[rows, :], (nodes, nodes + 2 * rim))
        upstream = up_ref[rows, :] + dot(hot, table[...])
        normed = normed_ref[rows, :]
        dz2 = back_norm(upstream, normed, scale_ref[rows, :], gain, means[...])
        dz2b = dz2.astype(bf16)
        dz1 = dot(dz2b, w2_turned[...]) * slope_ref[rows, :]
        dz1b = dz1.astype(bf16)
        dz_ref[rows, :] = dz1b
        squares[:lane, :] += dot(turned_ref[:, rows], dz1b)
        squares[lane:, :] += dot(act_ref[:, rows], dz2b)
        sums[0:8, :] += eight_sums(dz1)
        sums[8:16, :] += eight_sums(dz2)
        sums[16:24, :] += eight_sums(upstream * normed)
        sums[24:32, :] += eight_sums(upstream)
        first = rcv_column.shape[0] // lane + i * chunk
        snd_total[...] += spread(ids_ref, i * chunk, chunk, half, snd_column[rows, :], dz1)
        rcv_total[...] += spread(ids_ref, first, chunk, half, rcv_column[rows, :], dz1)
        slots = rows_of_ids(ids_ref, first, chunk, 2 * rim, lambda row: row - nodes)
        halo_total[...] += dot(slots, dz1b)

    each_tile(up_ref.shape[0], tile)
    snd_sum = jnp.concatenate([snd_total[:, :lane], snd_total[:, lane:]], axis=0).astype(bf16)
    rcv_sum = jnp.concatenate([rcv_total[:, :lane], rcv_total[:, lane:]], axis=0).astype(bf16)
    halo_sum = halo_total[...].astype(bf16)
    snd_sum_ref[...] = snd_sum
    rcv_sum_ref[...] = rcv_sum
    w1_rcv = weights_ref[2 * lane : 3 * lane]
    kept = kept_ref.shape[0]
    for at, back_ref in ((near_at, sent_ref.at[kept:]), (far_at, far_back_ref)):
        returned = halo_total[pl.ds(at, rim), :].astype(bf16)
        back_ref[...] = dot_back(returned, w1_rcv).astype(bf16)
    extended = jnp.concatenate([node_ref[...], halo[...]], axis=0)
    extended_sum = jnp.concatenate([rcv_sum, halo_sum], axis=0)
    grads_ref[:lane, :] = squares[:lane, :]
    grads_ref[lane : 2 * lane, :] = dot_rows(node_ref[...], snd_sum)
    grads_ref[2 * lane : 3 * lane, :] = dot_rows(extended, extended_sum)
    grads_ref[3 * lane : 4 * lane, :] = squares[lane:, :]
    node_rows = node_grads_ref.shape[0] - sum_rows
    last = 4 * lane + node_rows
    grads_ref[4 * lane : last, :] = node_grads_ref[:node_rows, :]
    grads_ref[last : last + sum_rows, :] = jnp.concatenate(
        [column_sum(sums[8 * k : 8 * k + 8, :]) for k in range(4)]
        + [node_grads_ref[node_rows : node_rows + 4, :], jnp.zeros((8, lane), f32)],
        axis=0,
    )
    if last + sum_rows < grads_ref.shape[0]:
        grads_ref[last + sum_rows :, :] = jnp.zeros(
            (grads_ref.shape[0] - last - sum_rows, lane), f32
        )
    own = lax.axis_index("sub")
    kept_ref[...] = grads_ref[pl.ds(pl.multiple_of(own * kept, sum_rows), kept), :]
    other = pl.multiple_of((1 - own) * kept, sum_rows)
    sent_ref[:kept, :] = grads_ref[pl.ds(other, kept), :].astype(bf16)


def edge_grad_kernel(dz_ref, cot_ref, weights_ref, out_ref, w1_turned):
    w1_turned[...] = weights_ref[:lane].T

    def tile(i):
        rows = pl.ds(pl.multiple_of(i * edge_tile, edge_tile), edge_tile)
        cot = cot_ref[rows, :].astype(f32)
        out_ref[rows, :] = (cot + dot(dz_ref[rows, :], w1_turned[...])).astype(bf16)

    each_tile(cot_ref.shape[0], tile)


def node_grad_kernel(
    base_ref, snd_sum_ref, rcv_sum_ref, weights_ref, near_ref, far_ref, ids_ref, out_ref
):
    rim = far_ref.shape[0]
    returned = jnp.concatenate([near_ref[near_ref.shape[0] - rim :, :], far_ref[...]], axis=0)
    total = base_ref[...] + dot_back(snd_sum_ref[...], weights_ref[lane : 2 * lane])
    total = total + dot_back(rcv_sum_ref[...], weights_ref[2 * lane : 3 * lane])
    hot = hot_lists(ids_ref, base_ref.shape[0])
    out_ref[...] = (total + dot(hot, returned)).astype(bf16)


def add_kernel(own_ref, other_ref, *refs):
    own = own_ref[...].astype(f32)
    refs[-1][...] = (own + other_ref[: own.shape[0], :].astype(f32)).astype(bf16)


def finish_kernel(own_ref, other_ref, *refs):
    out_refs, total_ref = refs[:-1], refs[-1]
    kept = own_ref.shape[0]
    own = lax.axis_index("sub")
    total_ref[pl.ds(pl.multiple_of(own * kept, sum_rows), kept), :] = own_ref[...].astype(f32)
    other = pl.multiple_of((1 - own) * kept, sum_rows)
    total_ref[pl.ds(other, kept), :] = other_ref[...].astype(f32)
    at = 0
    for out_ref in out_refs[:4]:
        out_ref[...] = total_ref[at : at + out_ref.shape[0], :]
        at += out_ref.shape[0]
    for k, out_ref in enumerate(out_refs[4:]):
        out_ref[...] = total_ref[at + k : at + k + 1, :]


def call(kernel, outs, scratch, *operands, anywhere=0, sems=0):
    moved = sum(x.size * x.dtype.itemsize for x in operands)
    held = operands[len(operands) - anywhere :]
    operands = operands[: len(operands) - anywhere]
    operands += tuple(pltpu.with_memory_space_constraint(x, pltpu.HBM) for x in held)
    inside = [pl.BlockSpec(memory_space=pltpu.VMEM)] * (len(operands) - anywhere)
    outside = [pl.BlockSpec(memory_space=pl.ANY)] * anywhere
    scratch_shapes = [pltpu.VMEM(shape, dtype) for shape, dtype in scratch]
    if sems:
        scratch_shapes.append(pltpu.SemaphoreType.DMA((sems,)))
    return pl.pallas_call(
        kernel,
        out_shape=[jax.ShapeDtypeStruct(shape, dtype) for shape, dtype in outs],
        in_specs=inside + outside,
        out_specs=[pl.BlockSpec(memory_space=pltpu.VMEM)] * len(outs),
        scratch_shapes=scratch_shapes,
        compiler_params=pltpu.CompilerParams(vmem_limit_bytes=vmem_limit),
        cost_estimate=pl.CostEstimate(flops=0, bytes_accessed=moved, transcendentals=0),
    )(*operands)


def swap(near, far):
    count = lax.axis_size("dom") * lax.axis_size("sub")
    outer = [(i, i + 1) for i in range(1, count - 1, 2)]
    inner = [(i, i + 1) for i in range(0, count - 1, 2)]
    outer += [(target, source) for source, target in outer]
    inner += [(target, source) for source, target in inner]
    far = lax.ppermute(far, chain, outer)
    return lax.ppermute(near, chain, inner), far


def sum_rounds():
    for axis in ("sample", "dom"):
        count = lax.axis_size(axis)
        step = 1
        while step < count:
            yield axis, [(i, i ^ step) for i in range(count)]
            step *= 2


def on_device(
    node_in,
    edge_in,
    senders,
    receivers,
    send_list,
    w_edge_first,
    b_edge_first,
    w_edge_second,
    b_edge_second,
    edge_gain,
    edge_shift,
    w_node_first,
    b_node_first,
    w_node_second,
    b_node_second,
    node_gain,
    node_shift,
    node_cotangent,
    edge_cotangent,
):
    node = node_in[0]
    edge = edge_in[0]
    nodes = node.shape[0]
    edges = edge.shape[0]
    rim = send_list.shape[2]
    rim_shape = ((rim, lane), bf16)
    snd_half = nodes // 2
    kept = -(-(7 * lane + sum_rows) // (2 * sum_rows)) * sum_rows
    row = lambda x: x.reshape(1, lane)
    small = [w_edge_first, w_edge_second, w_node_first, w_node_second]
    small += [row(b_edge_first), row(b_edge_second), row(edge_gain), row(edge_shift)]
    small += [row(b_node_first), row(b_node_second), row(node_gain), row(node_shift)]
    chunks = edges // lane
    sources = [
        node,
        senders.reshape(chunks, lane),
        receivers.reshape(chunks, lane),
        send_list[0],
        edge,
        edge_cotangent[0],
        node_cotangent[0],
    ] + small
    node, ids, edge, edge_cot, node_cot, weights, vectors, rim_near, rim_far = call(
        first_kernel,
        [
            ((nodes, lane), bf16),
            ((2 * chunks + 2, lane), jnp.int32),
            ((edges, lane), bf16),
            ((edges, lane), bf16),
            ((nodes, lane), bf16),
            ((7 * lane, lane), bf16),
            ((8, lane), f32),
            rim_shape,
            rim_shape,
        ],
        [],
        *sources,
        anywhere=len(sources),
        sems=len(sources),
    )
    near, far = swap(rim_near, rim_far)
    snd_column, rcv_column, snd_low, rcv_low, z_sent, rcv_local = call(
        prepare_kernel,
        [
            ((edges, lane), jnp.int32),
            ((edges, lane), jnp.int32),
            ((edges, lane), jnp.int16),
            ((edges, lane), jnp.int16),
            ((edges, lane), f32),
            ((snd_half, 2 * lane), bf16),
        ],
        [((snd_half, 2 * lane), bf16)],
        ids,
        node,
        weights,
        vectors,
        edge,
    )
    edge_out, z, normed, scale, message, agg_near, agg_far = call(
        edge_forward_kernel,
        [
            ((edges, lane), bf16),
            ((edges, lane), f32),
            ((edges, lane), f32),
            ((edges, lane), f32),
            ((edges, lane), bf16),
            rim_shape,
            rim_shape,
        ],
        [
            ((snd_half + 2 * rim, 2 * lane), bf16),
            ((lane, 2 * lane), bf16),
            ((2 * lane, 2 * lane), bf16),
            ((2 * rim, lane), f32),
        ],
        near,
        far,
        edge,
        ids,
        weights,
        vectors,
        rcv_column,
        rcv_low,
        z_sent,
        rcv_local,
    )
    back_near, back_far = swap(agg_near, agg_far)
    agg, turned = call(
        collect_kernel,
        [((nodes, lane), f32), ((lane, edges), bf16)],
        [((snd_half, 2 * lane), f32)],
        ids,
        rcv_column,
        message,
        edge,
    )
    node_out, base, dagg, dagg_rim_near, dagg_rim_far, node_grads = call(
        node_kernel,
        [
            ((nodes, lane), bf16),
            ((nodes, lane), f32),
            ((nodes, lane), bf16),
            rim_shape,
            rim_shape,
            ((3 * lane + sum_rows, lane), f32),
        ],
        [],
        node,
        agg,
        back_near,
        back_far,
        ids,
        weights,
        vectors,
        node_cot,
    )
    dagg_near, dagg_far = swap(dagg_rim_near, dagg_rim_far)
    upstream, slope, act = call(
        upstream_kernel,
        [((edges, lane), f32), ((edges, lane), f32), ((lane, edges), bf16)],
        [((snd_half, 2 * lane), bf16)],
        rcv_column,
        rcv_low,
        dagg,
        edge_cot,
        z,
    )
    dz, snd_sum, rcv_sum, grad_far, grads_kept, grads_sent = call(
        edge_backward_kernel,
        [
            ((edges, lane), bf16),
            ((nodes, lane), bf16),
            ((nodes, lane), bf16),
            rim_shape,
            ((kept, lane), f32),
            ((kept + rim, lane), bf16),
        ],
        [
            ((2 * rim, lane), bf16),
            ((2 * kept, lane), f32),
            ((2 * rim, lane), bf16),
            ((lane, lane), bf16),
            ((2 * lane, 2 * lane), bf16),
            ((snd_half, 2 * lane), f32),
            ((snd_half, 2 * lane), f32),
            ((2 * rim, lane), f32),
            ((2 * lane, lane), f32),
            ((32, lane), f32),
        ],
        upstream,
        normed,
        scale,
        slope,
        act,
        turned,
        ids,
        node,
        near,
        far,
        dagg_near,
        dagg_far,
        weights,
        vectors,
        node_grads,
        snd_column,
        rcv_column,
        rcv_low,
    )
    returned_near, returned_far = swap(grads_sent, grad_far)
    (edge_grad,) = call(
        edge_grad_kernel,
        [((edges, lane), bf16)],
        [((lane, lane), bf16)],
        dz,
        edge_cot,
        weights,
    )
    (node_grad,) = call(
        node_grad_kernel,
        [((nodes, lane), bf16)],
        [],
        base,
        snd_sum,
        rcv_sum,
        weights,
        returned_near,
        returned_far,
        ids,
    )
    half_shape = ((kept, lane), bf16)
    (grads,) = call(add_kernel, [half_shape], [], grads_kept, returned_near)
    between = [[returned_far, edge_grad], [node_grad]]
    for number, (axis, pairs) in enumerate(sum_rounds()):
        other = lax.ppermute(grads, axis, pairs)
        early = between[number] if number < len(between) else []
        written = 1 if early else 0
        (grads,) = call(add_kernel, [half_shape], [], grads, other, *early, anywhere=written)
    others = lax.ppermute(grads, "sub", [(0, 1), (1, 0)])
    matrices = [3 * lane, lane, 2 * lane, lane]
    totals = call(
        finish_kernel,
        [((height, lane), f32) for height in matrices] + [((1, lane), f32)] * 8,
        [((2 * kept, lane), f32)],
        grads,
        others,
    )
    flat = [total.reshape(lane) for total in totals[4:]]
    return (
        node_out[None],
        edge_out[None],
        node_grad[None],
        edge_grad[None],
        totals[0],
        flat[0],
        totals[1],
        flat[1],
        flat[2],
        flat[3],
        totals[2],
        flat[4],
        totals[3],
        flat[5],
        flat[6],
        flat[7],
    )


def solution(mesh):
    node_spec = P(("groups", "sample"), ("dom", "sub"), None)
    ids_spec = P(("dom", "sub"))
    return jax.shard_map(
        on_device,
        mesh=mesh,
        in_specs=(
            (node_spec, node_spec, ids_spec, ids_spec, P(("dom", "sub"), None, None))
            + (P(),) * 12
            + (node_spec, node_spec)
        ),
        out_specs=(
            (node_spec,) * 4
            + (P("groups", None), P("groups"), P("groups", None), P("groups"), P("groups"), P("groups"))
            * 2
        ),
        check_vma=False,
    )
```

```python
import functools
import math

import jax
import jax.numpy as jnp
from jax import lax
from jax.experimental import pallas as pl
from jax.experimental.pallas import tpu as pltpu
from jax.sharding import PartitionSpec as P

epsilon = 1e-05
rows_dims = (((0,), (0,)), ((), ()))
back_dims = (((1,), (1,)), ((), ()))
f32 = jnp.float32
bf16 = jnp.bfloat16
lane = 128
edge_tile = 512
tile_group = 3
vmem_limit = 32 * 1024 * 1024
sum_rows = 16
chain = ("dom", "sub")


def each_tile(rows, tile):
    count = rows // edge_tile
    group = math.gcd(count, tile_group)

    def several(i, carry):
        for k in range(group):
            tile(i * group + k)
        return carry

    lax.fori_loop(0, count // group, several, 0)


def dot(left, right):
    return jnp.dot(left, right, preferred_element_type=f32)


def dot_rows(left, right):
    return lax.dot_general(left, right, rows_dims, preferred_element_type=f32)


def dot_back(left, right):
    return lax.dot_general(left, right, back_dims, preferred_element_type=f32)


def column_of(row):
    return jnp.broadcast_to(row, (lane, lane)).T


def hot_columns(low, *spans):
    targets = lax.broadcasted_iota(jnp.int16, low.shape, 1)
    one, zero = jnp.ones((), bf16), jnp.zeros((), bf16)
    parts = [
        jnp.where(low == targets + jnp.int16(at), one, zero)
        for start, stop in spans
        for at in range(start, stop, lane)
    ]
    return jnp.concatenate(parts, axis=1)


def hot_rows(row, height):
    low = jnp.broadcast_to(row, (16, lane)).astype(jnp.int16)
    targets = lax.broadcasted_iota(jnp.int16, (height, lane), 0).reshape(height // 16, 16, lane)
    one, zero = jnp.ones((), bf16), jnp.zeros((), bf16)
    return jnp.where(targets == low[None], one, zero).reshape(height, lane)


def folded(ids, half):
    return jnp.where((ids >= half) & (ids < 2 * half), ids - half, ids)


def side_by_side(rows):
    half = rows.shape[0] // 2
    return jnp.concatenate([rows[:half], rows[half:]], axis=1)


def pick(ids, low, half, table, *halo):
    both = dot(hot_columns(low, (0, half), *halo), table)
    return jnp.where(ids >= half, both[:, lane:], both[:, :lane])


def rows_of_ids(ids_ref, first, count, height, change):
    parts = [hot_rows(change(ids_ref[pl.ds(first + k, 1), :]), height) for k in range(count)]
    return jnp.concatenate(parts, axis=1)


def spread(ids_ref, first, count, half, ids, values):
    upper = ids >= half
    paired = jnp.concatenate(
        [jnp.where(upper, 0.0, values).astype(bf16), jnp.where(upper, values, 0.0).astype(bf16)],
        axis=1,
    )
    return dot(rows_of_ids(ids_ref, first, count, half, lambda row: folded(row, half)), paired)


def sigmoid(z):
    return 0.5 * jnp.tanh(0.5 * z) + 0.5


def vector(vectors_ref, k):
    return vectors_ref[k : k + 1, :]


def centred_second(w, b):
    w = w.astype(f32)
    w = w - jnp.mean(w, axis=1, keepdims=True)
    high = w.astype(bf16)
    low = (w - high.astype(f32)).astype(bf16)
    return jnp.concatenate([high, low], axis=1), b - jnp.mean(b, axis=1, keepdims=True)


def mean_weights():
    shape = (2 * lane, 2 * lane)
    left = lax.broadcasted_iota(jnp.int32, shape, 0) < lane
    right = lax.broadcasted_iota(jnp.int32, shape, 1) < lane
    return jnp.where(left == right, 1.0 / lane, 0.0).astype(bf16)


def normed_of(act, w_pair, b_centred, means):
    both = dot(act, w_pair)
    center = both[:, :lane] + both[:, lane:] + b_centred
    variance = dot((center * center).astype(bf16), means[:lane, :lane])
    scale_inv = lax.rsqrt(variance + epsilon)
    return center * scale_inv, scale_inv


def back_norm(upstream, normed, scale_inv, gain, means):
    d_normed = upstream * gain
    pair = jnp.concatenate([d_normed.astype(bf16), (d_normed * normed).astype(bf16)], axis=1)
    both = dot(pair, means)
    return scale_inv * (d_normed - both[:, :lane] - normed * both[:, lane:])


def column_sum(values):
    return jnp.sum(values, axis=0, keepdims=True)


def eight_sums(values):
    return jnp.sum(values.reshape(values.shape[0] // 8, 8, lane), axis=0)


def parity_of_place():
    return lax.axis_index(chain) % 2


def first_kernel(
    node_hbm,
    snd_hbm,
    rcv_hbm,
    list_hbm,
    edge_hbm,
    edge_cot_hbm,
    node_cot_hbm,
    *refs,
):
    small = refs[:12]
    node_ref, ids_ref, edge_ref, edge_cot_ref, node_cot_ref, weights_ref, vectors_ref = refs[12:19]
    near_ref, far_ref, sems = refs[19:]
    chunks = snd_hbm.shape[0]
    moves = [
        (node_hbm, node_ref),
        (list_hbm, ids_ref.at[2 * chunks : 2 * chunks + 2]),
        (snd_hbm, ids_ref.at[:chunks]),
        (rcv_hbm, ids_ref.at[chunks : 2 * chunks]),
    ]
    at = 0
    for source in small[:4]:
        moves.append((source, weights_ref.at[at : at + source.shape[0]]))
        at += source.shape[0]
    for k, source in enumerate(small[4:]):
        moves.append((source, vectors_ref.at[k : k + 1]))
    moves += [(edge_hbm, edge_ref), (edge_cot_hbm, edge_cot_ref), (node_cot_hbm, node_cot_ref)]
    copies = [
        pltpu.make_async_copy(source, target, sems.at[k])
        for k, (source, target) in enumerate(moves)
    ]
    for copy in copies:
        copy.start()
    for copy in copies[:2]:
        copy.wait()
    parity = parity_of_place()
    node = node_ref[...]
    for side, out_ref in ((1 - parity, near_ref), (parity, far_ref)):
        column = column_of(ids_ref[pl.ds(2 * chunks + side, 1), :]).astype(jnp.int16)
        hot = hot_columns(column, (0, node.shape[0]))
        out_ref[...] = dot(hot, node).astype(bf16)
    for copy in copies[2:]:
        copy.wait()


def prepare_kernel(
    ids_ref,
    node_ref,
    weights_ref,
    vectors_ref,
    edge_ref,
    snd_column,
    rcv_column,
    rcv_low,
    z_ref,
    rcv_local,
    turned_ref,
    snd_low,
    snd_table,
):
    chunks = snd_column.shape[0] // lane
    half = snd_table.shape[0]
    for k in range(chunks):
        at = slice(k * lane, (k + 1) * lane)
        snd = column_of(ids_ref[k : k + 1, :])
        rcv = column_of(ids_ref[chunks + k : chunks + k + 1, :])
        snd_column[at, :] = snd
        rcv_column[at, :] = rcv
        snd_low[at, :] = folded(snd, half).astype(jnp.int16)
        rcv_low[at, :] = folded(rcv, half).astype(jnp.int16)
    node = node_ref[...]
    snd_table[...] = side_by_side(node)
    rcv_local[...] = side_by_side(dot(node, weights_ref[2 * lane : 3 * lane]).astype(bf16))
    w1 = weights_ref[: 2 * lane]
    b1 = vector(vectors_ref, 0)

    def tile(i):
        rows = pl.ds(pl.multiple_of(i * edge_tile, edge_tile), edge_tile)
        x = edge_ref[rows, :]
        sent = pick(snd_column[rows, :], snd_low[rows, :], half, snd_table[...]).astype(bf16)
        z_ref[rows, :] = dot(jnp.concatenate([x, sent], axis=1), w1) + b1
        turned_ref[:lane, rows] = x.T
        turned_ref[lane:, rows] = sent.T

    each_tile(edge_ref.shape[0], tile)


def edge_forward_kernel(
    far_ref,
    near_ref,
    ids_ref,
    weights_ref,
    vectors_ref,
    rcv_column,
    rcv_low,
    z_sent,
    rcv_local,
    z_ref,
    normed_ref,
    scale_ref,
    message_ref,
    agg_near_ref,
    agg_far_ref,
    table,
    w2_pair,
    means,
    total,
):
    half = rcv_local.shape[0]
    nodes = 2 * half
    rim = near_ref.shape[0]
    parity = parity_of_place()
    near_at = pl.multiple_of((1 - parity) * rim, rim)
    far_at = pl.multiple_of(parity * rim, rim)
    w1_rcv = weights_ref[2 * lane : 3 * lane]
    gain, shift = vector(vectors_ref, 2), vector(vectors_ref, 3)
    table[:half, :] = rcv_local[...]
    table[half:, :lane] = jnp.zeros((2 * rim, lane), bf16)
    table[pl.ds(half + near_at, rim), lane:] = dot(near_ref[...], w1_rcv).astype(bf16)
    table[pl.ds(half + far_at, rim), lane:] = dot(far_ref[...], w1_rcv).astype(bf16)
    pair, b2 = centred_second(weights_ref[3 * lane : 4 * lane], vector(vectors_ref, 1))
    w2_pair[...] = pair
    means[...] = mean_weights()
    total[...] = jnp.zeros_like(total)

    def tile(i):
        rows = pl.ds(pl.multiple_of(i * edge_tile, edge_tile), edge_tile)
        slots = (nodes, nodes + 2 * rim)
        z = z_sent[rows, :]
        z = z + pick(rcv_column[rows, :], rcv_low[rows, :], half, table[...], slots)
        z_ref[rows, :] = z
        act = (z * sigmoid(z)).astype(bf16)
        normed, scale_inv = normed_of(act, w2_pair[...], b2, means[...])
        normed_ref[rows, :] = normed
        scale_ref[rows, :] = scale_inv
        message = (normed * gain + shift).astype(bf16)
        message_ref[rows, :] = message
        first = (rcv_column.shape[0] + i * edge_tile) // lane
        hot = rows_of_ids(ids_ref, first, edge_tile // lane, 2 * rim, lambda row: row - nodes)
        total[...] += dot(hot, message)

    each_tile(rcv_column.shape[0], tile)
    agg_near_ref[...] = total[pl.ds(near_at, rim), :].astype(bf16)
    agg_far_ref[...] = total[pl.ds(far_at, rim), :].astype(bf16)


def collect_kernel(
    ids_ref, rcv_column, message_ref, edge_ref, normed_ref, vectors_ref, agg_ref, out_ref, total
):
    half = total.shape[0]
    gain, shift = vector(vectors_ref, 2), vector(vectors_ref, 3)
    total[...] = jnp.zeros_like(total)

    def tile(i):
        rows = pl.ds(pl.multiple_of(i * edge_tile, edge_tile), edge_tile)
        first = (rcv_column.shape[0] + i * edge_tile) // lane
        message = message_ref[rows, :].astype(f32)
        total[...] += spread(ids_ref, first, edge_tile // lane, half, rcv_column[rows, :], message)
        update = normed_ref[rows, :] * gain + shift
        out_ref[rows, :] = (edge_ref[rows, :].astype(f32) + update).astype(bf16)

    each_tile(rcv_column.shape[0], tile)
    agg_ref[:half, :] = total[:, :lane]
    agg_ref[half:, :] = total[:, lane:]


def hot_lists(ids_ref, nodes):
    parity = parity_of_place()
    first = ids_ref.shape[0] - 2
    near = ids_ref[pl.ds(first + 1 - parity, 1), :]
    far = ids_ref[pl.ds(first + parity, 1), :]
    return jnp.concatenate([hot_rows(near, nodes), hot_rows(far, nodes)], axis=1)


def node_kernel(
    far_ref,
    near_ref,
    node_ref,
    agg_ref,
    ids_ref,
    weights_ref,
    vectors_ref,
    cot_ref,
    x_ref,
    act_ref,
    normed_ref,
    dz1_ref,
    dz2_ref,
    sums_ref,
    dagg_ref,
    rim_near_ref,
    rim_far_ref,
):
    nodes = node_ref.shape[0]
    returned = jnp.concatenate([near_ref[...], far_ref[...]], axis=0)
    agg = (agg_ref[...] + dot(hot_lists(ids_ref, nodes), returned)).astype(bf16)
    x = jnp.concatenate([node_ref[...], agg], axis=1)
    x_ref[...] = x
    w1 = weights_ref[4 * lane : 6 * lane]
    w2 = weights_ref[6 * lane :]
    z = dot(x, w1) + vector(vectors_ref, 4)
    sig = sigmoid(z)
    act = (z * sig).astype(bf16)
    act_ref[...] = act
    pair, b2 = centred_second(w2, vector(vectors_ref, 5))
    means = mean_weights()
    normed, scale_inv = normed_of(act, pair, b2, means)
    normed_ref[...] = normed
    upstream = cot_ref[...].astype(f32)
    dz2 = back_norm(upstream, normed, scale_inv, vector(vectors_ref, 6), means)
    dz2b = dz2.astype(bf16)
    dz2_ref[...] = dz2b
    dz1 = dot(dz2b, w2.T) * (sig * (1.0 + z * (1.0 - sig)))
    dz1b = dz1.astype(bf16)
    dz1_ref[...] = dz1b
    dagg = dot(dz1b, w1[lane:].T).astype(bf16)
    dagg_ref[...] = dagg
    parity = parity_of_place()
    first = ids_ref.shape[0] - 2
    for side, rim_ref in ((parity, rim_far_ref), (1 - parity, rim_near_ref)):
        column = column_of(ids_ref[pl.ds(first + side, 1), :]).astype(jnp.int16)
        picked = hot_columns(column, (0, nodes))
        rim_ref[...] = dot(picked, dagg).astype(bf16)
    sums_ref[0:8, :] = eight_sums(dz1)
    sums_ref[8:16, :] = eight_sums(dz2)


def node_rest_kernel(
    x_ref,
    act_ref,
    normed_ref,
    dz1_ref,
    dz2_ref,
    sums_ref,
    weights_ref,
    vectors_ref,
    cot_ref,
    out_ref,
    base_ref,
    grads_ref,
):
    x = x_ref[...]
    normed = normed_ref[...]
    dz1b = dz1_ref[...]
    update = normed * vector(vectors_ref, 6) + vector(vectors_ref, 7)
    out_ref[...] = (x[:, :lane].astype(f32) + update).astype(bf16)
    upstream = cot_ref[...].astype(f32)
    base_ref[...] = upstream + dot(dz1b, weights_ref[4 * lane : 5 * lane].T)
    first = 2 * lane
    second = first + lane
    grads_ref[:first, :] = dot_rows(x, dz1b)
    grads_ref[first:second, :] = dot_rows(act_ref[...], dz2_ref[...])
    sums = [column_sum(sums_ref[0:8, :]), column_sum(sums_ref[8:16, :])]
    sums += [column_sum(eight_sums(upstream * normed)), column_sum(eight_sums(upstream))]
    sums.append(jnp.zeros((sum_rows - len(sums), lane), f32))
    grads_ref[second:, :] = jnp.concatenate(sums, axis=0)


def upstream_kernel(
    rcv_column,
    rcv_low,
    node_ref,
    far_ref,
    near_ref,
    dagg_ref,
    cot_ref,
    z_ref,
    up_ref,
    slope_ref,
    turned_ref,
    table,
):
    rim = near_ref.shape[0]
    half = table.shape[0] - 2 * rim
    nodes = 2 * half
    parity = parity_of_place()
    near_at = pl.multiple_of((1 - parity) * rim, rim)
    far_at = pl.multiple_of(parity * rim, rim)
    table[:half, :] = jnp.concatenate(
        [side_by_side(node_ref[...]), side_by_side(dagg_ref[...])], axis=1
    )
    table[half:, :] = jnp.zeros((2 * rim, 4 * lane), bf16)
    table[pl.ds(half + near_at, rim), lane : 2 * lane] = near_ref[...]
    table[pl.ds(half + far_at, rim), lane : 2 * lane] = far_ref[...]

    def tile(i):
        rows = pl.ds(pl.multiple_of(i * edge_tile, edge_tile), edge_tile)
        hot = hot_columns(rcv_low[rows, :], (0, half), (nodes, nodes + 2 * rim))
        four = dot(hot, table[...])
        upper = rcv_column[rows, :] >= half
        received = jnp.where(upper, four[:, lane : 2 * lane], four[:, :lane])
        local = jnp.where(upper, four[:, 3 * lane :], four[:, 2 * lane : 3 * lane])
        up_ref[rows, :] = cot_ref[rows, :].astype(f32) + local
        z = z_ref[rows, :]
        sig = sigmoid(z)
        slope_ref[rows, :] = sig * (1.0 + z * (1.0 - sig))
        turned_ref[:lane, rows] = received.astype(bf16).T
        turned_ref[lane:, rows] = (z * sig).astype(bf16).T

    each_tile(cot_ref.shape[0], tile)


def edge_backward_kernel(
    nodes,
    dagg_far_ref,
    dagg_near_ref,
    up_ref,
    normed_ref,
    scale_ref,
    slope_ref,
    first_turned,
    second_turned,
    weights_ref,
    vectors_ref,
    node_grads_ref,
    rcv_low,
    dz_ref,
    kept_ref,
    sent_ref,
    grads_ref,
    table,
    w2_turned,
    means,
    sums,
):
    rim = dagg_near_ref.shape[0]
    parity = parity_of_place()
    w2_turned[...] = weights_ref[3 * lane : 4 * lane].T
    gain = vector(vectors_ref, 2)
    table[pl.ds(pl.multiple_of((1 - parity) * rim, rim), rim), :] = dagg_near_ref[...]
    table[pl.ds(pl.multiple_of(parity * rim, rim), rim), :] = dagg_far_ref[...]
    means[...] = mean_weights()
    grads_ref[: 4 * lane, :] = jnp.zeros((4 * lane, lane), f32)
    sums[...] = jnp.zeros_like(sums)

    def tile(i):
        rows = pl.ds(pl.multiple_of(i * edge_tile, edge_tile), edge_tile)
        hot = hot_columns(rcv_low[rows, :], (nodes, nodes + 2 * rim))
        upstream = up_ref[rows, :] + dot(hot, table[...])
        normed = normed_ref[rows, :]
        dz2 = back_norm(upstream, normed, scale_ref[rows, :], gain, means[...])
        dz2b = dz2.astype(bf16)
        dz1 = dot(dz2b, w2_turned[...]) * slope_ref[rows, :]
        dz1b = dz1.astype(bf16)
        dz_ref[rows, :] = dz1b
        grads_ref[: 2 * lane, :] += dot(first_turned[:, rows], dz1b)
        grads_ref[2 * lane : 3 * lane, :] += dot(second_turned[:lane, rows], dz1b)
        grads_ref[3 * lane : 4 * lane, :] += dot(second_turned[lane:, rows], dz2b)
        sums[0:8, :] += eight_sums(dz1)
        sums[8:16, :] += eight_sums(dz2)
        sums[16:24, :] += eight_sums(upstream * normed)
        sums[24:32, :] += eight_sums(upstream)

    each_tile(up_ref.shape[0], tile)
    kept = kept_ref.shape[0]
    node_rows = node_grads_ref.shape[0] - sum_rows
    last = 4 * lane + node_rows
    grads_ref[4 * lane : last, :] = node_grads_ref[:node_rows, :]
    grads_ref[last : last + sum_rows, :] = jnp.concatenate(
        [column_sum(sums[8 * k : 8 * k + 8, :]) for k in range(4)]
        + [node_grads_ref[node_rows : node_rows + 4, :], jnp.zeros((8, lane), f32)],
        axis=0,
    )
    if last + sum_rows < grads_ref.shape[0]:
        grads_ref[last + sum_rows :, :] = jnp.zeros(
            (grads_ref.shape[0] - last - sum_rows, lane), f32
        )
    own = lax.axis_index("sub")
    kept_ref[...] = grads_ref[pl.ds(pl.multiple_of(own * kept, sum_rows), kept), :]
    other = pl.multiple_of((1 - own) * kept, sum_rows)
    sent_ref[...] = grads_ref[pl.ds(other, kept), :].astype(bf16)


def scatter_kernel(
    ids_ref,
    dz_ref,
    snd_column,
    rcv_column,
    weights_ref,
    snd_sum_ref,
    rcv_sum_ref,
    far_back_ref,
    near_back_ref,
    snd_total,
    rcv_total,
    halo_total,
):
    half = snd_total.shape[0]
    nodes = 2 * half
    rim = near_back_ref.shape[0]
    parity = parity_of_place()
    for total in (snd_total, rcv_total, halo_total):
        total[...] = jnp.zeros_like(total)

    def tile(i):
        rows = pl.ds(pl.multiple_of(i * edge_tile, edge_tile), edge_tile)
        chunk = edge_tile // lane
        dz1b = dz_ref[rows, :]
        dz1 = dz1b.astype(f32)
        first = rcv_column.shape[0] // lane + i * chunk
        snd_total[...] += spread(ids_ref, i * chunk, chunk, half, snd_column[rows, :], dz1)
        rcv_total[...] += spread(ids_ref, first, chunk, half, rcv_column[rows, :], dz1)
        slots = rows_of_ids(ids_ref, first, chunk, 2 * rim, lambda row: row - nodes)
        halo_total[...] += dot(slots, dz1b)

    each_tile(dz_ref.shape[0], tile)
    for total, out_ref in ((snd_total, snd_sum_ref), (rcv_total, rcv_sum_ref)):
        out_ref[:half, :] = total[:, :lane].astype(bf16)
        out_ref[half:, :] = total[:, lane:].astype(bf16)
    w1_turned = weights_ref[2 * lane : 3 * lane].T
    for side, back_ref in ((parity, far_back_ref), (1 - parity, near_back_ref)):
        returned = halo_total[pl.ds(pl.multiple_of(side * rim, rim), rim), :].astype(bf16)
        back_ref[...] = dot(returned, w1_turned).astype(bf16)


def edge_grad_kernel(dz_ref, cot_ref, weights_ref, out_ref, w1_turned):
    w1_turned[...] = weights_ref[:lane].T

    def tile(i):
        rows = pl.ds(pl.multiple_of(i * edge_tile, edge_tile), edge_tile)
        cot = cot_ref[rows, :].astype(f32)
        out_ref[rows, :] = (cot + dot(dz_ref[rows, :], w1_turned[...])).astype(bf16)

    each_tile(cot_ref.shape[0], tile)


def node_grad_kernel(
    far_ref, near_ref, base_ref, snd_sum_ref, rcv_sum_ref, weights_ref, ids_ref, out_ref
):
    returned = jnp.concatenate([near_ref[...], far_ref[...]], axis=0)
    total = base_ref[...] + dot(snd_sum_ref[...], weights_ref[lane : 2 * lane].T)
    total = total + dot(rcv_sum_ref[...], weights_ref[2 * lane : 3 * lane].T)
    hot = hot_lists(ids_ref, base_ref.shape[0])
    out_ref[...] = (total + dot(hot, returned)).astype(bf16)


def add_kernel(passed, own_ref, other_ref, *refs):
    out_refs = refs[len(refs) - passed - 1 :]
    out_refs[0][...] = (own_ref[...].astype(f32) + other_ref[...].astype(f32)).astype(bf16)
    for source, target in zip(refs[:passed], out_refs[1:]):
        target[...] = source[...]


def finish_kernel(own_ref, other_ref, *refs):
    out_refs, total_ref = refs[:-1], refs[-1]
    kept = own_ref.shape[0]
    own = lax.axis_index("sub")
    total_ref[pl.ds(pl.multiple_of(own * kept, sum_rows), kept), :] = own_ref[...].astype(f32)
    other = pl.multiple_of((1 - own) * kept, sum_rows)
    total_ref[pl.ds(other, kept), :] = other_ref[...].astype(f32)
    at = 0
    for out_ref in out_refs[:4]:
        out_ref[...] = total_ref[at : at + out_ref.shape[0], :]
        at += out_ref.shape[0]
    for k, out_ref in enumerate(out_refs[4:]):
        out_ref[...] = total_ref[at + k : at + k + 1, :]


def call(kernel, outs, scratch, *operands, anywhere=0, sems=0):
    moved = sum(x.size * x.dtype.itemsize for x in operands)
    held = operands[len(operands) - anywhere :]
    operands = operands[: len(operands) - anywhere]
    operands += tuple(pltpu.with_memory_space_constraint(x, pltpu.HBM) for x in held)
    inside = [pl.BlockSpec(memory_space=pltpu.VMEM)] * (len(operands) - anywhere)
    outside = [pl.BlockSpec(memory_space=pl.ANY)] * anywhere
    scratch_shapes = [pltpu.VMEM(shape, dtype) for shape, dtype in scratch]
    if sems:
        scratch_shapes.append(pltpu.SemaphoreType.DMA((sems,)))
    return pl.pallas_call(
        kernel,
        out_shape=[jax.ShapeDtypeStruct(shape, dtype) for shape, dtype in outs],
        in_specs=inside + outside,
        out_specs=[pl.BlockSpec(memory_space=pltpu.VMEM)] * len(outs),
        scratch_shapes=scratch_shapes,
        compiler_params=pltpu.CompilerParams(vmem_limit_bytes=vmem_limit),
        cost_estimate=pl.CostEstimate(flops=0, bytes_accessed=moved, transcendentals=0),
    )(*operands)


def swap(near, far):
    count = lax.axis_size("dom") * lax.axis_size("sub")
    outer = [(i, i + 1) for i in range(1, count - 1, 2)]
    inner = [(i, i + 1) for i in range(0, count - 1, 2)]
    outer += [(target, source) for source, target in outer]
    inner += [(target, source) for source, target in inner]
    far = lax.ppermute(far, chain, outer)
    return lax.ppermute(near, chain, inner), far


def sum_rounds():
    for axis in ("sample", "dom"):
        count = lax.axis_size(axis)
        step = 1
        while step < count:
            yield axis, [(i, i ^ step) for i in range(count)]
            step *= 2


def on_device(
    node_in,
    edge_in,
    senders,
    receivers,
    send_list,
    w_edge_first,
    b_edge_first,
    w_edge_second,
    b_edge_second,
    edge_gain,
    edge_shift,
    w_node_first,
    b_node_first,
    w_node_second,
    b_node_second,
    node_gain,
    node_shift,
    node_cotangent,
    edge_cotangent,
):
    node = node_in[0]
    edge = edge_in[0]
    nodes = node.shape[0]
    edges = edge.shape[0]
    rim = send_list.shape[2]
    rim_shape = ((rim, lane), bf16)
    snd_half = nodes // 2
    kept = -(-(7 * lane + sum_rows) // (2 * sum_rows)) * sum_rows
    row = lambda x: x.reshape(1, lane)
    small = [w_edge_first, w_edge_second, w_node_first, w_node_second]
    small += [row(b_edge_first), row(b_edge_second), row(edge_gain), row(edge_shift)]
    small += [row(b_node_first), row(b_node_second), row(node_gain), row(node_shift)]
    chunks = edges // lane
    sources = [
        node,
        senders.reshape(chunks, lane),
        receivers.reshape(chunks, lane),
        send_list[0],
        edge,
        edge_cotangent[0],
        node_cotangent[0],
    ] + small
    node, ids, edge, edge_cot, node_cot, weights, vectors, rim_near, rim_far = call(
        first_kernel,
        [
            ((nodes, lane), bf16),
            ((2 * chunks + 2, lane), jnp.int32),
            ((edges, lane), bf16),
            ((edges, lane), bf16),
            ((nodes, lane), bf16),
            ((7 * lane, lane), bf16),
            ((8, lane), f32),
            rim_shape,
            rim_shape,
        ],
        [],
        *sources,
        anywhere=len(sources),
        sems=len(sources),
    )
    near, far = swap(rim_near, rim_far)
    edge_shape = ((edges, lane), bf16)
    wide_shape = ((edges, lane), f32)
    turned_shape = ((2 * lane, edges), bf16)
    node_shape = ((nodes, lane), bf16)
    snd_column, rcv_column, rcv_low, z_sent, rcv_local, first_turned = call(
        prepare_kernel,
        [
            ((edges, lane), jnp.int32),
            ((edges, lane), jnp.int32),
            ((edges, lane), jnp.int16),
            wide_shape,
            ((snd_half, 2 * lane), bf16),
            turned_shape,
        ],
        [((edges, lane), jnp.int16), ((snd_half, 2 * lane), bf16)],
        ids,
        node,
        weights,
        vectors,
        edge,
    )
    z, normed, scale, message, agg_near, agg_far = call(
        edge_forward_kernel,
        [wide_shape, wide_shape, wide_shape, edge_shape, rim_shape, rim_shape],
        [
            ((snd_half + 2 * rim, 2 * lane), bf16),
            ((lane, 2 * lane), bf16),
            ((2 * lane, 2 * lane), bf16),
            ((2 * rim, lane), f32),
        ],
        far,
        near,
        ids,
        weights,
        vectors,
        rcv_column,
        rcv_low,
        z_sent,
        rcv_local,
    )
    back_near, back_far = swap(agg_near, agg_far)
    agg, edge_out = call(
        collect_kernel,
        [((nodes, lane), f32), edge_shape],
        [((snd_half, 2 * lane), f32)],
        ids,
        rcv_column,
        message,
        edge,
        normed,
        vectors,
    )
    node_x, node_act, node_normed, node_dz1, node_dz2, node_sums, dagg, rim_near, rim_far = call(
        node_kernel,
        [
            ((nodes, 2 * lane), bf16),
            node_shape,
            ((nodes, lane), f32),
            node_shape,
            node_shape,
            ((16, lane), f32),
            node_shape,
            rim_shape,
            rim_shape,
        ],
        [],
        back_far,
        back_near,
        node,
        agg,
        ids,
        weights,
        vectors,
        node_cot,
    )
    dagg_near, dagg_far = swap(rim_near, rim_far)
    upstream, slope, second_turned = call(
        upstream_kernel,
        [wide_shape, wide_shape, turned_shape],
        [((snd_half + 2 * rim, 4 * lane), bf16)],
        rcv_column,
        rcv_low,
        node,
        far,
        near,
        dagg,
        edge_cot,
        z,
    )
    node_out, base, node_grads = call(
        node_rest_kernel,
        [node_shape, ((nodes, lane), f32), ((3 * lane + sum_rows, lane), f32)],
        [],
        node_x,
        node_act,
        node_normed,
        node_dz1,
        node_dz2,
        node_sums,
        weights,
        vectors,
        node_cot,
    )
    half_shape = ((kept, lane), bf16)
    dz, grads_kept, grads_sent = call(
        functools.partial(edge_backward_kernel, nodes),
        [edge_shape, ((kept, lane), f32), half_shape],
        [
            ((2 * kept, lane), f32),
            ((2 * rim, lane), bf16),
            ((lane, lane), bf16),
            ((2 * lane, 2 * lane), bf16),
            ((32, lane), f32),
        ],
        dagg_far,
        dagg_near,
        upstream,
        normed,
        scale,
        slope,
        first_turned,
        second_turned,
        weights,
        vectors,
        node_grads,
        rcv_low,
    )
    core_pairs = [(0, 1), (1, 0)]
    other = lax.ppermute(grads_sent, "sub", core_pairs)
    (grads,) = call(functools.partial(add_kernel, 0), [half_shape], [], grads_kept, other)
    snd_sum, rcv_sum, back_far, back_near = call(
        scatter_kernel,
        [node_shape, node_shape, rim_shape, rim_shape],
        [
            ((snd_half, 2 * lane), f32),
            ((snd_half, 2 * lane), f32),
            ((2 * rim, lane), f32),
        ],
        ids,
        dz,
        snd_column,
        rcv_column,
        weights,
    )
    (edge_grad,) = call(
        edge_grad_kernel,
        [edge_shape],
        [((lane, lane), bf16)],
        dz,
        edge_cot,
        weights,
    )
    node_grad = None
    for number, (axis, pairs) in enumerate(sum_rounds()):
        other = lax.ppermute(grads, axis, pairs)
        passed, written = [], []
        if number == 0:
            passed, written = [back_near, back_far], [edge_grad]
        elif number == 1:
            passed = list(swap(back_near, back_far))
        elif number == 2:
            (node_grad,) = call(
                node_grad_kernel,
                [node_shape],
                [],
                back_far,
                back_near,
                base,
                snd_sum,
                rcv_sum,
                weights,
                ids,
            )
            written = [node_grad]
        grads, *passed = call(
            functools.partial(add_kernel, len(passed)),
            [half_shape] + [rim_shape] * len(passed),
            [],
            grads,
            other,
            *passed,
            *written,
            anywhere=len(written),
        )
        if passed:
            back_near, back_far = passed
    others = lax.ppermute(grads, "sub", core_pairs)
    matrices = [3 * lane, lane, 2 * lane, lane]
    totals = call(
        finish_kernel,
        [((height, lane), f32) for height in matrices] + [((1, lane), f32)] * 8,
        [((2 * kept, lane), f32)],
        grads,
        others,
    )
    flat = [total.reshape(lane) for total in totals[4:]]
    return (
        node_out[None],
        edge_out[None],
        node_grad[None],
        edge_grad[None],
        totals[0],
        flat[0],
        totals[1],
        flat[1],
        flat[2],
        flat[3],
        totals[2],
        flat[4],
        totals[3],
        flat[5],
        flat[6],
        flat[7],
    )


def solution(mesh):
    node_spec = P(("groups", "sample"), ("dom", "sub"), None)
    ids_spec = P(("dom", "sub"))
    return jax.shard_map(
        on_device,
        mesh=mesh,
        in_specs=(
            (node_spec, node_spec, ids_spec, ids_spec, P(("dom", "sub"), None, None))
            + (P(),) * 12
            + (node_spec, node_spec)
        ),
        out_specs=(
            (node_spec,) * 4
            + (P("groups", None), P("groups"), P("groups", None), P("groups"), P("groups"), P("groups"))
            * 2
        ),
        check_vma=False,
    )
```

```python
import functools
import math

import jax
import jax.numpy as jnp
from jax import lax
from jax.experimental import pallas as pl
from jax.experimental.pallas import tpu as pltpu
from jax.sharding import PartitionSpec as P

epsilon = 1e-05
rows_dims = (((0,), (0,)), ((), ()))
back_dims = (((1,), (1,)), ((), ()))
f32 = jnp.float32
bf16 = jnp.bfloat16
lane = 128
edge_tile = 512
tile_group = 3
vmem_limit = 32 * 1024 * 1024
sum_rows = 16
chain = ("dom", "sub")


def each_tile(rows, tile):
    count = rows // edge_tile
    group = math.gcd(count, tile_group)

    def several(i, carry):
        for k in range(group):
            tile(i * group + k)
        return carry

    lax.fori_loop(0, count // group, several, 0)


def dot(left, right):
    return jnp.dot(left, right, preferred_element_type=f32)


def dot_rows(left, right):
    return lax.dot_general(left, right, rows_dims, preferred_element_type=f32)


def dot_back(left, right):
    return lax.dot_general(left, right, back_dims, preferred_element_type=f32)


def column_of(row):
    return jnp.broadcast_to(row, (lane, lane)).T


def hot_columns(low, *spans):
    targets = lax.broadcasted_iota(jnp.int16, low.shape, 1)
    one, zero = jnp.ones((), bf16), jnp.zeros((), bf16)
    parts = [
        jnp.where(low == targets + jnp.int16(at), one, zero)
        for start, stop in spans
        for at in range(start, stop, lane)
    ]
    return jnp.concatenate(parts, axis=1)


def hot_rows(row, height):
    low = jnp.broadcast_to(row, (16, lane)).astype(jnp.int16)
    targets = lax.broadcasted_iota(jnp.int16, (height, lane), 0).reshape(height // 16, 16, lane)
    one, zero = jnp.ones((), bf16), jnp.zeros((), bf16)
    return jnp.where(targets == low[None], one, zero).reshape(height, lane)


def folded(ids, half):
    return jnp.where((ids >= half) & (ids < 2 * half), ids - half, ids)


def side_by_side(rows):
    half = rows.shape[0] // 2
    return jnp.concatenate([rows[:half], rows[half:]], axis=1)


def pick(ids, low, half, table, *halo):
    both = dot(hot_columns(low, (0, half), *halo), table)
    return jnp.where(ids >= half, both[:, lane:], both[:, :lane])


def rows_of_ids(ids_ref, first, count, height, change):
    parts = [hot_rows(change(ids_ref[pl.ds(first + k, 1), :]), height) for k in range(count)]
    return jnp.concatenate(parts, axis=1)


def spread(ids_ref, first, count, half, ids, values):
    upper = ids >= half
    paired = jnp.concatenate(
        [jnp.where(upper, 0.0, values).astype(bf16), jnp.where(upper, values, 0.0).astype(bf16)],
        axis=1,
    )
    return dot(rows_of_ids(ids_ref, first, count, half, lambda row: folded(row, half)), paired)


def sigmoid(z):
    return 0.5 * jnp.tanh(0.5 * z) + 0.5


def vector(vectors_ref, k):
    return vectors_ref[k : k + 1, :]


def centred_second(w, b):
    w = w.astype(f32)
    w = w - jnp.mean(w, axis=1, keepdims=True)
    high = w.astype(bf16)
    low = (w - high.astype(f32)).astype(bf16)
    return jnp.concatenate([high, low], axis=1), b - jnp.mean(b, axis=1, keepdims=True)


def mean_weights():
    shape = (2 * lane, 2 * lane)
    left = lax.broadcasted_iota(jnp.int32, shape, 0) < lane
    right = lax.broadcasted_iota(jnp.int32, shape, 1) < lane
    return jnp.where(left == right, 1.0 / lane, 0.0).astype(bf16)


def normed_of(act, w_pair, b_centred, means):
    both = dot(act, w_pair)
    center = both[:, :lane] + both[:, lane:] + b_centred
    variance = dot((center * center).astype(bf16), means[:lane, :lane])
    scale_inv = lax.rsqrt(variance + epsilon)
    return center * scale_inv, scale_inv


def back_norm(upstream, normed, scale_inv, gain, means):
    d_normed = upstream * gain
    pair = jnp.concatenate([d_normed.astype(bf16), (d_normed * normed).astype(bf16)], axis=1)
    both = dot(pair, means)
    return scale_inv * (d_normed - both[:, :lane] - normed * both[:, lane:])


def column_sum(values):
    return jnp.sum(values, axis=0, keepdims=True)


def eight_sums(values):
    return jnp.sum(values.reshape(values.shape[0] // 8, 8, lane), axis=0)


def parity_of_place():
    return lax.axis_index(chain) % 2


def first_kernel(
    node_hbm,
    snd_hbm,
    rcv_hbm,
    list_hbm,
    edge_hbm,
    edge_cot_hbm,
    node_cot_hbm,
    *refs,
):
    small = refs[:12]
    node_ref, ids_ref, edge_ref, edge_cot_ref, node_cot_ref, weights_ref, vectors_ref = refs[12:19]
    near_ref, far_ref, sems = refs[19:]
    chunks = snd_hbm.shape[0]
    moves = [
        (node_hbm, node_ref),
        (list_hbm, ids_ref.at[2 * chunks : 2 * chunks + 2]),
        (snd_hbm, ids_ref.at[:chunks]),
        (rcv_hbm, ids_ref.at[chunks : 2 * chunks]),
    ]
    at = 0
    for source in small[:4]:
        moves.append((source, weights_ref.at[at : at + source.shape[0]]))
        at += source.shape[0]
    for k, source in enumerate(small[4:]):
        moves.append((source, vectors_ref.at[k : k + 1]))
    moves += [(edge_hbm, edge_ref), (edge_cot_hbm, edge_cot_ref), (node_cot_hbm, node_cot_ref)]
    copies = [
        pltpu.make_async_copy(source, target, sems.at[k])
        for k, (source, target) in enumerate(moves)
    ]
    for copy in copies:
        copy.start()
    for copy in copies[:2]:
        copy.wait()
    parity = parity_of_place()
    node = node_ref[...]
    for side, out_ref in ((1 - parity, near_ref), (parity, far_ref)):
        column = column_of(ids_ref[pl.ds(2 * chunks + side, 1), :]).astype(jnp.int16)
        hot = hot_columns(column, (0, node.shape[0]))
        out_ref[...] = dot(hot, node).astype(bf16)
    for copy in copies[2:]:
        copy.wait()


def prepare_kernel(
    ids_ref,
    node_ref,
    weights_ref,
    vectors_ref,
    edge_ref,
    snd_column,
    rcv_column,
    rcv_low,
    z_ref,
    rcv_local,
    turned_ref,
    snd_low,
    snd_table,
):
    chunks = snd_column.shape[0] // lane
    half = snd_table.shape[0]
    for k in range(chunks):
        at = slice(k * lane, (k + 1) * lane)
        snd = column_of(ids_ref[k : k + 1, :])
        rcv = column_of(ids_ref[chunks + k : chunks + k + 1, :])
        snd_column[at, :] = snd
        rcv_column[at, :] = rcv
        snd_low[at, :] = folded(snd, half).astype(jnp.int16)
        rcv_low[at, :] = folded(rcv, half).astype(jnp.int16)
    node = node_ref[...]
    snd_table[...] = side_by_side(node)
    rcv_local[...] = side_by_side(dot(node, weights_ref[2 * lane : 3 * lane]).astype(bf16))
    w1 = weights_ref[: 2 * lane]
    b1 = vector(vectors_ref, 0)

    def tile(i):
        rows = pl.ds(pl.multiple_of(i * edge_tile, edge_tile), edge_tile)
        x = edge_ref[rows, :]
        sent = pick(snd_column[rows, :], snd_low[rows, :], half, snd_table[...]).astype(bf16)
        z_ref[rows, :] = dot(jnp.concatenate([x, sent], axis=1), w1) + b1
        turned_ref[:, rows] = sent.T

    each_tile(edge_ref.shape[0], tile)


def edge_forward_kernel(
    near_ref,
    far_ref,
    ids_ref,
    weights_ref,
    vectors_ref,
    rcv_column,
    rcv_low,
    z_sent,
    rcv_local,
    z_ref,
    normed_ref,
    scale_ref,
    message_ref,
    agg_near_ref,
    agg_far_ref,
    table,
    w2_pair,
    means,
    total,
):
    half = rcv_local.shape[0]
    nodes = 2 * half
    rim = near_ref.shape[0]
    parity = parity_of_place()
    near_at = pl.multiple_of((1 - parity) * rim, rim)
    far_at = pl.multiple_of(parity * rim, rim)
    w1_rcv = weights_ref[2 * lane : 3 * lane]
    gain, shift = vector(vectors_ref, 2), vector(vectors_ref, 3)
    table[:half, :] = rcv_local[...]
    table[half:, :lane] = jnp.zeros((2 * rim, lane), bf16)
    table[pl.ds(half + near_at, rim), lane:] = dot(near_ref[...], w1_rcv).astype(bf16)
    table[pl.ds(half + far_at, rim), lane:] = dot(far_ref[...], w1_rcv).astype(bf16)
    pair, b2 = centred_second(weights_ref[3 * lane : 4 * lane], vector(vectors_ref, 1))
    w2_pair[...] = pair
    means[...] = mean_weights()
    total[...] = jnp.zeros_like(total)

    def tile(i):
        rows = pl.ds(pl.multiple_of(i * edge_tile, edge_tile), edge_tile)
        slots = (nodes, nodes + 2 * rim)
        z = z_sent[rows, :]
        z = z + pick(rcv_column[rows, :], rcv_low[rows, :], half, table[...], slots)
        z_ref[rows, :] = z
        act = (z * sigmoid(z)).astype(bf16)
        normed, scale_inv = normed_of(act, w2_pair[...], b2, means[...])
        normed_ref[rows, :] = normed
        scale_ref[rows, :] = scale_inv
        message = (normed * gain + shift).astype(bf16)
        message_ref[rows, :] = message
        first = (rcv_column.shape[0] + i * edge_tile) // lane
        hot = rows_of_ids(ids_ref, first, edge_tile // lane, 2 * rim, lambda row: row - nodes)
        total[...] += dot(hot, message)

    each_tile(rcv_column.shape[0], tile)
    agg_near_ref[...] = total[pl.ds(near_at, rim), :].astype(bf16)
    agg_far_ref[...] = total[pl.ds(far_at, rim), :].astype(bf16)


def collect_kernel(
    ids_ref,
    rcv_column,
    rcv_low,
    message_ref,
    node_ref,
    near_ref,
    far_ref,
    agg_ref,
    turned_ref,
    table,
    total,
):
    rim = near_ref.shape[0]
    half = total.shape[0]
    nodes = 2 * half
    parity = parity_of_place()
    near_at = pl.multiple_of((1 - parity) * rim, rim)
    far_at = pl.multiple_of(parity * rim, rim)
    table[:half, :] = side_by_side(node_ref[...])
    table[half:, :lane] = jnp.zeros((2 * rim, lane), bf16)
    table[pl.ds(half + near_at, rim), lane:] = near_ref[...]
    table[pl.ds(half + far_at, rim), lane:] = far_ref[...]
    total[...] = jnp.zeros_like(total)

    def tile(i):
        rows = pl.ds(pl.multiple_of(i * edge_tile, edge_tile), edge_tile)
        first = (rcv_column.shape[0] + i * edge_tile) // lane
        rcv = rcv_column[rows, :]
        message = message_ref[rows, :].astype(f32)
        total[...] += spread(ids_ref, first, edge_tile // lane, half, rcv, message)
        slots = (nodes, nodes + 2 * rim)
        turned_ref[:, rows] = pick(rcv, rcv_low[rows, :], half, table[...], slots).astype(bf16).T

    each_tile(rcv_column.shape[0], tile)
    agg_ref[:half, :] = total[:, :lane]
    agg_ref[half:, :] = total[:, lane:]


def hot_lists(ids_ref, nodes):
    parity = parity_of_place()
    first = ids_ref.shape[0] - 2
    near = ids_ref[pl.ds(first + 1 - parity, 1), :]
    far = ids_ref[pl.ds(first + parity, 1), :]
    return jnp.concatenate([hot_rows(near, nodes), hot_rows(far, nodes)], axis=1)


def node_kernel(
    near_ref,
    far_ref,
    node_ref,
    agg_ref,
    ids_ref,
    weights_ref,
    vectors_ref,
    cot_ref,
    x_ref,
    act_ref,
    normed_ref,
    dz1_ref,
    dz2_ref,
    sums_ref,
    dagg_ref,
    rim_near_ref,
    rim_far_ref,
):
    nodes = node_ref.shape[0]
    returned = jnp.concatenate([near_ref[...], far_ref[...]], axis=0)
    agg = (agg_ref[...] + dot(hot_lists(ids_ref, nodes), returned)).astype(bf16)
    x = jnp.concatenate([node_ref[...], agg], axis=1)
    x_ref[...] = x
    w1 = weights_ref[4 * lane : 6 * lane]
    w2 = weights_ref[6 * lane :]
    z = dot(x, w1) + vector(vectors_ref, 4)
    sig = sigmoid(z)
    act = (z * sig).astype(bf16)
    act_ref[...] = act
    pair, b2 = centred_second(w2, vector(vectors_ref, 5))
    means = mean_weights()
    normed, scale_inv = normed_of(act, pair, b2, means)
    normed_ref[...] = normed
    upstream = cot_ref[...].astype(f32)
    dz2 = back_norm(upstream, normed, scale_inv, vector(vectors_ref, 6), means)
    dz2b = dz2.astype(bf16)
    dz2_ref[...] = dz2b
    dz1 = dot(dz2b, w2.T) * (sig * (1.0 + z * (1.0 - sig)))
    dz1b = dz1.astype(bf16)
    dz1_ref[...] = dz1b
    dagg = dot(dz1b, w1[lane:].T).astype(bf16)
    dagg_ref[...] = dagg
    parity = parity_of_place()
    first = ids_ref.shape[0] - 2
    for side, rim_ref in ((parity, rim_far_ref), (1 - parity, rim_near_ref)):
        column = column_of(ids_ref[pl.ds(first + side, 1), :]).astype(jnp.int16)
        picked = hot_columns(column, (0, nodes))
        rim_ref[...] = dot(picked, dagg).astype(bf16)
    sums_ref[0:8, :] = eight_sums(dz1)
    sums_ref[8:16, :] = eight_sums(dz2)


def node_rest_kernel(
    x_ref,
    act_ref,
    normed_ref,
    dz1_ref,
    dz2_ref,
    sums_ref,
    weights_ref,
    vectors_ref,
    cot_ref,
    out_ref,
    base_ref,
    grads_ref,
):
    x = x_ref[...]
    normed = normed_ref[...]
    dz1b = dz1_ref[...]
    update = normed * vector(vectors_ref, 6) + vector(vectors_ref, 7)
    out_ref[...] = (x[:, :lane].astype(f32) + update).astype(bf16)
    upstream = cot_ref[...].astype(f32)
    base_ref[...] = upstream + dot(dz1b, weights_ref[4 * lane : 5 * lane].T)
    first = 2 * lane
    second = first + lane
    grads_ref[:first, :] = dot_rows(x, dz1b)
    grads_ref[first:second, :] = dot_rows(act_ref[...], dz2_ref[...])
    sums = [column_sum(sums_ref[0:8, :]), column_sum(sums_ref[8:16, :])]
    sums += [column_sum(eight_sums(upstream * normed)), column_sum(eight_sums(upstream))]
    sums.append(jnp.zeros((sum_rows - len(sums), lane), f32))
    grads_ref[second:, :] = jnp.concatenate(sums, axis=0)


def upstream_kernel(
    rcv_column, rcv_low, dagg_ref, cot_ref, z_ref, edge_ref, up_ref, slope_ref, turned_ref, table
):
    half = table.shape[0]
    table[...] = side_by_side(dagg_ref[...])

    def tile(i):
        rows = pl.ds(pl.multiple_of(i * edge_tile, edge_tile), edge_tile)
        local = pick(rcv_column[rows, :], rcv_low[rows, :], half, table[...])
        up_ref[rows, :] = cot_ref[rows, :].astype(f32) + local
        z = z_ref[rows, :]
        sig = sigmoid(z)
        slope_ref[rows, :] = sig * (1.0 + z * (1.0 - sig))
        turned_ref[:lane, rows] = edge_ref[rows, :].T
        turned_ref[lane:, rows] = (z * sig).astype(bf16).T

    each_tile(cot_ref.shape[0], tile)


def edge_backward_kernel(
    nodes,
    dagg_near_ref,
    dagg_far_ref,
    up_ref,
    normed_ref,
    scale_ref,
    slope_ref,
    sent_turned,
    received_turned,
    turned,
    weights_ref,
    vectors_ref,
    node_grads_ref,
    rcv_low,
    dz_ref,
    kept_ref,
    sent_ref,
    grads_ref,
    table,
    w2_turned,
    means,
    sums,
):
    rim = dagg_near_ref.shape[0]
    parity = parity_of_place()
    w2_turned[...] = weights_ref[3 * lane : 4 * lane].T
    gain = vector(vectors_ref, 2)
    table[pl.ds(pl.multiple_of((1 - parity) * rim, rim), rim), :] = dagg_near_ref[...]
    table[pl.ds(pl.multiple_of(parity * rim, rim), rim), :] = dagg_far_ref[...]
    means[...] = mean_weights()
    grads_ref[: 4 * lane, :] = jnp.zeros((4 * lane, lane), f32)
    sums[...] = jnp.zeros_like(sums)

    def tile(i):
        rows = pl.ds(pl.multiple_of(i * edge_tile, edge_tile), edge_tile)
        hot = hot_columns(rcv_low[rows, :], (nodes, nodes + 2 * rim))
        upstream = up_ref[rows, :] + dot(hot, table[...])
        normed = normed_ref[rows, :]
        dz2 = back_norm(upstream, normed, scale_ref[rows, :], gain, means[...])
        dz2b = dz2.astype(bf16)
        dz1 = dot(dz2b, w2_turned[...]) * slope_ref[rows, :]
        dz1b = dz1.astype(bf16)
        dz_ref[rows, :] = dz1b
        grads_ref[:lane, :] += dot(turned[:lane, rows], dz1b)
        grads_ref[lane : 2 * lane, :] += dot(sent_turned[:, rows], dz1b)
        grads_ref[2 * lane : 3 * lane, :] += dot(received_turned[:, rows], dz1b)
        grads_ref[3 * lane : 4 * lane, :] += dot(turned[lane:, rows], dz2b)
        sums[0:8, :] += eight_sums(dz1)
        sums[8:16, :] += eight_sums(dz2)
        sums[16:24, :] += eight_sums(upstream * normed)
        sums[24:32, :] += eight_sums(upstream)

    each_tile(up_ref.shape[0], tile)
    kept = kept_ref.shape[0]
    node_rows = node_grads_ref.shape[0] - sum_rows
    last = 4 * lane + node_rows
    grads_ref[4 * lane : last, :] = node_grads_ref[:node_rows, :]
    grads_ref[last : last + sum_rows, :] = jnp.concatenate(
        [column_sum(sums[8 * k : 8 * k + 8, :]) for k in range(4)]
        + [node_grads_ref[node_rows : node_rows + 4, :], jnp.zeros((8, lane), f32)],
        axis=0,
    )
    if last + sum_rows < grads_ref.shape[0]:
        grads_ref[last + sum_rows :, :] = jnp.zeros(
            (grads_ref.shape[0] - last - sum_rows, lane), f32
        )
    own = lax.axis_index("sub")
    kept_ref[...] = grads_ref[pl.ds(pl.multiple_of(own * kept, sum_rows), kept), :]
    other = pl.multiple_of((1 - own) * kept, sum_rows)
    sent_ref[...] = grads_ref[pl.ds(other, kept), :].astype(bf16)


def scatter_kernel(
    ids_ref,
    dz_ref,
    snd_column,
    rcv_column,
    weights_ref,
    snd_sum_ref,
    rcv_sum_ref,
    far_back_ref,
    near_back_ref,
    snd_total,
    rcv_total,
    halo_total,
):
    half = snd_total.shape[0]
    nodes = 2 * half
    rim = near_back_ref.shape[0]
    parity = parity_of_place()
    for total in (snd_total, rcv_total, halo_total):
        total[...] = jnp.zeros_like(total)

    def tile(i):
        rows = pl.ds(pl.multiple_of(i * edge_tile, edge_tile), edge_tile)
        chunk = edge_tile // lane
        dz1b = dz_ref[rows, :]
        dz1 = dz1b.astype(f32)
        first = rcv_column.shape[0] // lane + i * chunk
        snd_total[...] += spread(ids_ref, i * chunk, chunk, half, snd_column[rows, :], dz1)
        rcv_total[...] += spread(ids_ref, first, chunk, half, rcv_column[rows, :], dz1)
        slots = rows_of_ids(ids_ref, first, chunk, 2 * rim, lambda row: row - nodes)
        halo_total[...] += dot(slots, dz1b)

    each_tile(dz_ref.shape[0], tile)
    for total, out_ref in ((snd_total, snd_sum_ref), (rcv_total, rcv_sum_ref)):
        out_ref[:half, :] = total[:, :lane].astype(bf16)
        out_ref[half:, :] = total[:, lane:].astype(bf16)
    w1_turned = weights_ref[2 * lane : 3 * lane].T
    for side, back_ref in ((parity, far_back_ref), (1 - parity, near_back_ref)):
        returned = halo_total[pl.ds(pl.multiple_of(side * rim, rim), rim), :].astype(bf16)
        back_ref[...] = dot(returned, w1_turned).astype(bf16)


def edge_outputs_kernel(
    dz_ref, cot_ref, edge_ref, normed_ref, vectors_ref, w1_ref, out_ref, grad_ref, w1_turned
):
    w1_turned[...] = w1_ref[...].T
    gain, shift = vector(vectors_ref, 2), vector(vectors_ref, 3)

    def tile(i):
        rows = pl.ds(pl.multiple_of(i * edge_tile, edge_tile), edge_tile)
        cot = cot_ref[rows, :].astype(f32)
        grad_ref[rows, :] = (cot + dot(dz_ref[rows, :], w1_turned[...])).astype(bf16)
        update = normed_ref[rows, :] * gain + shift
        out_ref[rows, :] = (edge_ref[rows, :].astype(f32) + update).astype(bf16)

    each_tile(cot_ref.shape[0], tile)


def node_grad_kernel(
    near_ref, far_ref, base_ref, snd_sum_ref, rcv_sum_ref, weights_ref, ids_ref, out_ref
):
    returned = jnp.concatenate([near_ref[...], far_ref[...]], axis=0)
    total = base_ref[...] + dot(snd_sum_ref[...], weights_ref[lane : 2 * lane].T)
    total = total + dot(rcv_sum_ref[...], weights_ref[2 * lane : 3 * lane].T)
    hot = hot_lists(ids_ref, base_ref.shape[0])
    out_ref[...] = (total + dot(hot, returned)).astype(bf16)


def add_kernel(passed, own_ref, other_ref, *refs):
    out_refs = refs[len(refs) - passed - 1 :]
    out_refs[0][...] = (own_ref[...].astype(f32) + other_ref[...].astype(f32)).astype(bf16)
    for source, target in zip(refs[:passed], out_refs[1:]):
        target[...] = source[...]


def finish_kernel(own_ref, other_ref, *refs):
    out_refs, total_ref = refs[:-1], refs[-1]
    kept = own_ref.shape[0]
    own = lax.axis_index("sub")
    total_ref[pl.ds(pl.multiple_of(own * kept, sum_rows), kept), :] = own_ref[...].astype(f32)
    other = pl.multiple_of((1 - own) * kept, sum_rows)
    total_ref[pl.ds(other, kept), :] = other_ref[...].astype(f32)
    at = 0
    for out_ref in out_refs[:4]:
        out_ref[...] = total_ref[at : at + out_ref.shape[0], :]
        at += out_ref.shape[0]
    for k, out_ref in enumerate(out_refs[4:]):
        out_ref[...] = total_ref[at + k : at + k + 1, :]


def call(kernel, outs, scratch, *operands, anywhere=0, sems=0):
    moved = sum(x.size * x.dtype.itemsize for x in operands)
    held = operands[len(operands) - anywhere :]
    operands = operands[: len(operands) - anywhere]
    operands += tuple(pltpu.with_memory_space_constraint(x, pltpu.HBM) for x in held)
    inside = [pl.BlockSpec(memory_space=pltpu.VMEM)] * (len(operands) - anywhere)
    outside = [pl.BlockSpec(memory_space=pl.ANY)] * anywhere
    scratch_shapes = [pltpu.VMEM(shape, dtype) for shape, dtype in scratch]
    if sems:
        scratch_shapes.append(pltpu.SemaphoreType.DMA((sems,)))
    return pl.pallas_call(
        kernel,
        out_shape=[jax.ShapeDtypeStruct(shape, dtype) for shape, dtype in outs],
        in_specs=inside + outside,
        out_specs=[pl.BlockSpec(memory_space=pltpu.VMEM)] * len(outs),
        scratch_shapes=scratch_shapes,
        compiler_params=pltpu.CompilerParams(vmem_limit_bytes=vmem_limit),
        cost_estimate=pl.CostEstimate(flops=0, bytes_accessed=moved, transcendentals=0),
    )(*operands)


def swap(near, far):
    count = lax.axis_size("dom") * lax.axis_size("sub")
    outer = [(i, i + 1) for i in range(1, count - 1, 2)]
    inner = [(i, i + 1) for i in range(0, count - 1, 2)]
    outer += [(target, source) for source, target in outer]
    inner += [(target, source) for source, target in inner]
    far = lax.ppermute(far, chain, outer)
    return lax.ppermute(near, chain, inner), far


def sum_rounds():
    for axis in ("sample", "dom"):
        count = lax.axis_size(axis)
        step = count // 2
        while step > 0:
            yield axis, [(i, i ^ step) for i in range(count)]
            step //= 2


def on_device(
    node_in,
    edge_in,
    senders,
    receivers,
    send_list,
    w_edge_first,
    b_edge_first,
    w_edge_second,
    b_edge_second,
    edge_gain,
    edge_shift,
    w_node_first,
    b_node_first,
    w_node_second,
    b_node_second,
    node_gain,
    node_shift,
    node_cotangent,
    edge_cotangent,
):
    node = node_in[0]
    edge = edge_in[0]
    nodes = node.shape[0]
    edges = edge.shape[0]
    rim = send_list.shape[2]
    rim_shape = ((rim, lane), bf16)
    snd_half = nodes // 2
    kept = -(-(7 * lane + sum_rows) // (2 * sum_rows)) * sum_rows
    row = lambda x: x.reshape(1, lane)
    small = [w_edge_first, w_edge_second, w_node_first, w_node_second]
    small += [row(b_edge_first), row(b_edge_second), row(edge_gain), row(edge_shift)]
    small += [row(b_node_first), row(b_node_second), row(node_gain), row(node_shift)]
    chunks = edges // lane
    sources = [
        node,
        senders.reshape(chunks, lane),
        receivers.reshape(chunks, lane),
        send_list[0],
        edge,
        edge_cotangent[0],
        node_cotangent[0],
    ] + small
    node, ids, edge, edge_cot, node_cot, weights, vectors, rim_near, rim_far = call(
        first_kernel,
        [
            ((nodes, lane), bf16),
            ((2 * chunks + 2, lane), jnp.int32),
            ((edges, lane), bf16),
            ((edges, lane), bf16),
            ((nodes, lane), bf16),
            ((7 * lane, lane), bf16),
            ((8, lane), f32),
            rim_shape,
            rim_shape,
        ],
        [],
        *sources,
        anywhere=len(sources),
        sems=len(sources),
    )
    near, far = swap(rim_near, rim_far)
    edge_shape = ((edges, lane), bf16)
    wide_shape = ((edges, lane), f32)
    node_shape = ((nodes, lane), bf16)
    snd_column, rcv_column, rcv_low, z_sent, rcv_local, sent_turned = call(
        prepare_kernel,
        [
            ((edges, lane), jnp.int32),
            ((edges, lane), jnp.int32),
            ((edges, lane), jnp.int16),
            wide_shape,
            ((snd_half, 2 * lane), bf16),
            ((lane, edges), bf16),
        ],
        [((edges, lane), jnp.int16), ((snd_half, 2 * lane), bf16)],
        ids,
        node,
        weights,
        vectors,
        edge,
    )
    z, normed, scale, message, agg_near, agg_far = call(
        edge_forward_kernel,
        [wide_shape, wide_shape, wide_shape, edge_shape, rim_shape, rim_shape],
        [
            ((snd_half + 2 * rim, 2 * lane), bf16),
            ((lane, 2 * lane), bf16),
            ((2 * lane, 2 * lane), bf16),
            ((2 * rim, lane), f32),
        ],
        near,
        far,
        ids,
        weights,
        vectors,
        rcv_column,
        rcv_low,
        z_sent,
        rcv_local,
    )
    back_near, back_far = swap(agg_near, agg_far)
    agg, received_turned = call(
        collect_kernel,
        [((nodes, lane), f32), ((lane, edges), bf16)],
        [((snd_half + 2 * rim, 2 * lane), bf16), ((snd_half, 2 * lane), f32)],
        ids,
        rcv_column,
        rcv_low,
        message,
        node,
        near,
        far,
    )
    node_x, node_act, node_normed, node_dz1, node_dz2, node_sums, dagg, rim_near, rim_far = call(
        node_kernel,
        [
            ((nodes, 2 * lane), bf16),
            node_shape,
            ((nodes, lane), f32),
            node_shape,
            node_shape,
            ((16, lane), f32),
            node_shape,
            rim_shape,
            rim_shape,
        ],
        [],
        back_near,
        back_far,
        node,
        agg,
        ids,
        weights,
        vectors,
        node_cot,
    )
    dagg_near, dagg_far = swap(rim_near, rim_far)
    upstream, slope, turned = call(
        upstream_kernel,
        [wide_shape, wide_shape, ((2 * lane, edges), bf16)],
        [((snd_half, 2 * lane), bf16)],
        rcv_column,
        rcv_low,
        dagg,
        edge_cot,
        z,
        edge,
    )
    node_out, base, node_grads = call(
        node_rest_kernel,
        [node_shape, ((nodes, lane), f32), ((3 * lane + sum_rows, lane), f32)],
        [],
        node_x,
        node_act,
        node_normed,
        node_dz1,
        node_dz2,
        node_sums,
        weights,
        vectors,
        node_cot,
    )
    half_shape = ((kept, lane), bf16)
    dz, grads_kept, grads_sent = call(
        functools.partial(edge_backward_kernel, nodes),
        [edge_shape, ((kept, lane), f32), half_shape],
        [
            ((2 * kept, lane), f32),
            ((2 * rim, lane), bf16),
            ((lane, lane), bf16),
            ((2 * lane, 2 * lane), bf16),
            ((32, lane), f32),
        ],
        dagg_near,
        dagg_far,
        upstream,
        normed,
        scale,
        slope,
        sent_turned,
        received_turned,
        turned,
        weights,
        vectors,
        node_grads,
        rcv_low,
    )
    core_pairs = [(0, 1), (1, 0)]
    other = lax.ppermute(grads_sent, "sub", core_pairs)
    (grads,) = call(functools.partial(add_kernel, 0), [half_shape], [], grads_kept, other)
    snd_sum, rcv_sum, back_far, back_near = call(
        scatter_kernel,
        [node_shape, node_shape, rim_shape, rim_shape],
        [
            ((snd_half, 2 * lane), f32),
            ((snd_half, 2 * lane), f32),
            ((2 * rim, lane), f32),
        ],
        ids,
        dz,
        snd_column,
        rcv_column,
        weights,
    )
    w1_edge = weights[:lane]
    edge_out = edge_grad = node_grad = None
    for number, (axis, pairs) in enumerate(sum_rounds()):
        other = lax.ppermute(grads, axis, pairs)
        passed, written = [], []
        if number == 0:
            passed = [back_near, back_far]
        elif number == 1:
            passed = [*swap(back_near, back_far), vectors, w1_edge]
        elif number == 2:
            (node_grad,) = call(
                node_grad_kernel,
                [node_shape],
                [],
                back_near,
                back_far,
                base,
                snd_sum,
                rcv_sum,
                weights,
                ids,
            )
            edge_out, edge_grad = call(
                edge_outputs_kernel,
                [edge_shape, edge_shape],
                [((lane, lane), bf16)],
                dz,
                edge_cot,
                edge,
                normed,
                vectors,
                w1_edge,
            )
            written = [node_grad, edge_out, edge_grad]
        grads, *passed = call(
            functools.partial(add_kernel, len(passed)),
            [half_shape] + [(x.shape, x.dtype) for x in passed],
            [],
            grads,
            other,
            *passed,
            *written,
            anywhere=len(written),
        )
        if number == 0:
            back_near, back_far = passed
        elif number == 1:
            back_near, back_far, vectors, w1_edge = passed
    others = lax.ppermute(grads, "sub", core_pairs)
    matrices = [3 * lane, lane, 2 * lane, lane]
    totals = call(
        finish_kernel,
        [((height, lane), f32) for height in matrices] + [((1, lane), f32)] * 8,
        [((2 * kept, lane), f32)],
        grads,
        others,
    )
    flat = [total.reshape(lane) for total in totals[4:]]
    return (
        node_out[None],
        edge_out[None],
        node_grad[None],
        edge_grad[None],
        totals[0],
        flat[0],
        totals[1],
        flat[1],
        flat[2],
        flat[3],
        totals[2],
        flat[4],
        totals[3],
        flat[5],
        flat[6],
        flat[7],
    )


def solution(mesh):
    node_spec = P(("groups", "sample"), ("dom", "sub"), None)
    ids_spec = P(("dom", "sub"))
    return jax.shard_map(
        on_device,
        mesh=mesh,
        in_specs=(
            (node_spec, node_spec, ids_spec, ids_spec, P(("dom", "sub"), None, None))
            + (P(),) * 12
            + (node_spec, node_spec)
        ),
        out_specs=(
            (node_spec,) * 4
            + (P("groups", None), P("groups"), P("groups", None), P("groups"), P("groups"), P("groups"))
            * 2
        ),
        check_vma=False,
    )
```

```python
import functools
import math

import jax
import jax.numpy as jnp
from jax import lax
from jax.experimental import pallas as pl
from jax.experimental.pallas import tpu as pltpu
from jax.sharding import PartitionSpec as P

epsilon = 1e-05
rows_dims = (((0,), (0,)), ((), ()))
back_dims = (((1,), (1,)), ((), ()))
f32 = jnp.float32
bf16 = jnp.bfloat16
lane = 128
edge_tile = 512
tile_group = 6
vmem_limit = 32 * 1024 * 1024
sum_rows = 16
chain = ("dom", "sub")


def each_tile(rows, tile):
    count = rows // edge_tile
    group = math.gcd(count, tile_group)

    def several(i, carry):
        for k in range(group):
            tile(i * group + k)
        return carry

    lax.fori_loop(0, count // group, several, 0)


def dot(left, right):
    return jnp.dot(left, right, preferred_element_type=f32)


def dot_rows(left, right):
    return lax.dot_general(left, right, rows_dims, preferred_element_type=f32)


def dot_back(left, right):
    return lax.dot_general(left, right, back_dims, preferred_element_type=f32)


def column_of(row):
    return jnp.broadcast_to(row, (lane, lane)).T


def hot_columns(low, *spans):
    targets = lax.broadcasted_iota(jnp.int16, low.shape, 1)
    one, zero = jnp.ones((), bf16), jnp.zeros((), bf16)
    parts = [
        jnp.where(low == targets + jnp.int16(at), one, zero)
        for start, stop in spans
        for at in range(start, stop, lane)
    ]
    return jnp.concatenate(parts, axis=1)


def hot_rows(row, height):
    low = jnp.broadcast_to(row, (16, lane)).astype(jnp.int16)
    targets = lax.broadcasted_iota(jnp.int16, (height, lane), 0).reshape(height // 16, 16, lane)
    one, zero = jnp.ones((), bf16), jnp.zeros((), bf16)
    return jnp.where(targets == low[None], one, zero).reshape(height, lane)


def folded(ids, half):
    return jnp.where((ids >= half) & (ids < 2 * half), ids - half, ids)


def side_by_side(rows):
    half = rows.shape[0] // 2
    return jnp.concatenate([rows[:half], rows[half:]], axis=1)


def pick(ids, low, half, table, *halo):
    both = dot(hot_columns(low, (0, half), *halo), table)
    return jnp.where(ids >= half, both[:, lane:], both[:, :lane])


def rows_of_ids(ids_ref, first, count, height, change):
    parts = [hot_rows(change(ids_ref[pl.ds(first + k, 1), :]), height) for k in range(count)]
    return jnp.concatenate(parts, axis=1)


def spread(ids_ref, first, count, half, ids, values):
    upper = ids >= half
    paired = jnp.concatenate(
        [jnp.where(upper, 0.0, values).astype(bf16), jnp.where(upper, values, 0.0).astype(bf16)],
        axis=1,
    )
    return dot(rows_of_ids(ids_ref, first, count, half, lambda row: folded(row, half)), paired)


def sigmoid(z):
    return 0.5 * jnp.tanh(0.5 * z) + 0.5


def vector(vectors_ref, k):
    return vectors_ref[k : k + 1, :]


def centred_second(w, b):
    w = w.astype(f32)
    w = w - jnp.mean(w, axis=1, keepdims=True)
    high = w.astype(bf16)
    low = (w - high.astype(f32)).astype(bf16)
    return jnp.concatenate([high, low], axis=1), b - jnp.mean(b, axis=1, keepdims=True)


def mean_weights():
    shape = (2 * lane, 2 * lane)
    left = lax.broadcasted_iota(jnp.int32, shape, 0) < lane
    right = lax.broadcasted_iota(jnp.int32, shape, 1) < lane
    return jnp.where(left == right, 1.0 / lane, 0.0).astype(bf16)


def normed_of(act, w_pair, b_centred, means):
    both = dot(act, w_pair)
    center = both[:, :lane] + both[:, lane:] + b_centred
    variance = dot((center * center).astype(bf16), means[:lane, :lane])
    scale_inv = lax.rsqrt(variance + epsilon)
    return center * scale_inv, scale_inv


def back_norm(upstream, normed, scale_inv, gain, means):
    d_normed = upstream * gain
    pair = jnp.concatenate([d_normed.astype(bf16), (d_normed * normed).astype(bf16)], axis=1)
    both = dot(pair, means)
    return scale_inv * (d_normed - both[:, :lane] - normed * both[:, lane:])


def column_sum(values):
    return jnp.sum(values, axis=0, keepdims=True)


def eight_sums(values):
    return jnp.sum(values.reshape(values.shape[0] // 8, 8, lane), axis=0)


def parity_of_place():
    return lax.axis_index(chain) % 2


def started(moves, sems):
    copies = [
        pltpu.make_async_copy(source, target, sems.at[k])
        for k, (source, target) in enumerate(moves)
    ]
    for copy in copies:
        copy.start()
    return copies


def first_kernel(node_hbm, list_hbm, node_ref, message_ref, list_ref, sems):
    for copy in started([(node_hbm, node_ref), (list_hbm, list_ref)], sems):
        copy.wait()
    parity = parity_of_place()
    node = node_ref[...]
    rim = message_ref.shape[0] // 2
    for k, side in enumerate((1 - parity, parity)):
        column = column_of(list_ref[pl.ds(side, 1), :]).astype(jnp.int16)
        hot = hot_columns(column, (0, node.shape[0]))
        message_ref[k * rim : (k + 1) * rim, :] = dot(hot, node).astype(bf16)


def prepare_kernel(
    node_ref,
    unused_ref,
    snd_hbm,
    rcv_hbm,
    list_hbm,
    edge_hbm,
    edge_cot_hbm,
    node_cot_hbm,
    *refs,
):
    small = refs[:12]
    ids_ref, edge_ref, edge_cot_ref, node_cot_ref, weights_ref, vectors_ref = refs[12:18]
    snd_column, rcv_column, rcv_low, z_ref, rcv_local, turned_ref = refs[18:24]
    snd_low, snd_table, sems = refs[24:]
    chunks = snd_hbm.shape[0]
    moves = [
        (snd_hbm, ids_ref.at[:chunks]),
        (rcv_hbm, ids_ref.at[chunks : 2 * chunks]),
        (list_hbm, ids_ref.at[2 * chunks : 2 * chunks + 2]),
    ]
    at = 0
    for source in small[:4]:
        moves.append((source, weights_ref.at[at : at + source.shape[0]]))
        at += source.shape[0]
    for k, source in enumerate(small[4:]):
        moves.append((source, vectors_ref.at[k : k + 1]))
    moves += [(edge_hbm, edge_ref), (edge_cot_hbm, edge_cot_ref), (node_cot_hbm, node_cot_ref)]
    copies = started(moves, sems)
    half = snd_table.shape[0]
    node = node_ref[...]
    snd_table[...] = side_by_side(node)
    for copy in copies[:2]:
        copy.wait()
    for k in range(chunks):
        at = slice(k * lane, (k + 1) * lane)
        snd = column_of(ids_ref[k : k + 1, :])
        rcv = column_of(ids_ref[chunks + k : chunks + k + 1, :])
        snd_column[at, :] = snd
        rcv_column[at, :] = rcv
        snd_low[at, :] = folded(snd, half).astype(jnp.int16)
        rcv_low[at, :] = folded(rcv, half).astype(jnp.int16)
    for copy in copies[2:]:
        copy.wait()
    rcv_local[...] = side_by_side(dot(node, weights_ref[2 * lane : 3 * lane]).astype(bf16))
    w1 = weights_ref[: 2 * lane]
    b1 = vector(vectors_ref, 0)

    def tile(i):
        rows = pl.ds(pl.multiple_of(i * edge_tile, edge_tile), edge_tile)
        x = edge_ref[rows, :]
        sent = pick(snd_column[rows, :], snd_low[rows, :], half, snd_table[...]).astype(bf16)
        z_ref[rows, :] = dot(jnp.concatenate([x, sent], axis=1), w1) + b1
        turned_ref[:, rows] = sent.T

    each_tile(edge_ref.shape[0], tile)


def split_kernel(message_ref, near_ref, onward_ref):
    rim = near_ref.shape[0]
    near_ref[...] = message_ref[:rim, :]
    onward_ref[...] = message_ref[rim:, :]


def edge_forward_kernel(
    near_ref,
    far_ref,
    ids_ref,
    weights_ref,
    vectors_ref,
    rcv_column,
    rcv_low,
    z_sent,
    rcv_local,
    z_ref,
    normed_ref,
    scale_ref,
    message_ref,
    rims_ref,
    table,
    w2_pair,
    means,
    total,
):
    half = rcv_local.shape[0]
    nodes = 2 * half
    rim = near_ref.shape[0]
    parity = parity_of_place()
    near_at = pl.multiple_of((1 - parity) * rim, rim)
    far_at = pl.multiple_of(parity * rim, rim)
    w1_rcv = weights_ref[2 * lane : 3 * lane]
    gain, shift = vector(vectors_ref, 2), vector(vectors_ref, 3)
    table[:half, :] = rcv_local[...]
    table[half:, :lane] = jnp.zeros((2 * rim, lane), bf16)
    table[pl.ds(half + near_at, rim), lane:] = dot(near_ref[...], w1_rcv).astype(bf16)
    table[pl.ds(half + far_at, rim), lane:] = dot(far_ref[...], w1_rcv).astype(bf16)
    pair, b2 = centred_second(weights_ref[3 * lane : 4 * lane], vector(vectors_ref, 1))
    w2_pair[...] = pair
    means[...] = mean_weights()
    total[...] = jnp.zeros_like(total)

    def tile(i):
        rows = pl.ds(pl.multiple_of(i * edge_tile, edge_tile), edge_tile)
        slots = (nodes, nodes + 2 * rim)
        z = z_sent[rows, :]
        z = z + pick(rcv_column[rows, :], rcv_low[rows, :], half, table[...], slots)
        z_ref[rows, :] = z
        act = (z * sigmoid(z)).astype(bf16)
        normed, scale_inv = normed_of(act, w2_pair[...], b2, means[...])
        normed_ref[rows, :] = normed
        scale_ref[rows, :] = scale_inv
        message = (normed * gain + shift).astype(bf16)
        message_ref[rows, :] = message
        first = (rcv_column.shape[0] + i * edge_tile) // lane
        hot = rows_of_ids(ids_ref, first, edge_tile // lane, 2 * rim, lambda row: row - nodes)
        total[...] += dot(hot, message)

    each_tile(rcv_column.shape[0], tile)
    rims_ref[:rim, :] = total[pl.ds(near_at, rim), :].astype(bf16)
    rims_ref[rim:, :] = total[pl.ds(far_at, rim), :].astype(bf16)


def collect_kernel(
    ids_ref,
    rcv_column,
    rcv_low,
    message_ref,
    node_ref,
    near_ref,
    far_ref,
    unused_ref,
    agg_ref,
    turned_ref,
    table,
    total,
):
    rim = near_ref.shape[0]
    half = total.shape[0]
    nodes = 2 * half
    parity = parity_of_place()
    near_at = pl.multiple_of((1 - parity) * rim, rim)
    far_at = pl.multiple_of(parity * rim, rim)
    table[:half, :] = side_by_side(node_ref[...])
    table[half:, :lane] = jnp.zeros((2 * rim, lane), bf16)
    table[pl.ds(half + near_at, rim), lane:] = near_ref[...]
    table[pl.ds(half + far_at, rim), lane:] = far_ref[...]
    total[...] = jnp.zeros_like(total)

    def tile(i):
        rows = pl.ds(pl.multiple_of(i * edge_tile, edge_tile), edge_tile)
        first = (rcv_column.shape[0] + i * edge_tile) // lane
        rcv = rcv_column[rows, :]
        message = message_ref[rows, :].astype(f32)
        total[...] += spread(ids_ref, first, edge_tile // lane, half, rcv, message)
        slots = (nodes, nodes + 2 * rim)
        turned_ref[:, rows] = pick(rcv, rcv_low[rows, :], half, table[...], slots).astype(bf16).T

    each_tile(rcv_column.shape[0], tile)
    agg_ref[:half, :] = total[:, :lane]
    agg_ref[half:, :] = total[:, lane:]


def hot_lists(ids_ref, nodes):
    parity = parity_of_place()
    first = ids_ref.shape[0] - 2
    near = ids_ref[pl.ds(first + 1 - parity, 1), :]
    far = ids_ref[pl.ds(first + parity, 1), :]
    return jnp.concatenate([hot_rows(near, nodes), hot_rows(far, nodes)], axis=1)


def node_kernel(
    near_ref,
    far_ref,
    node_ref,
    agg_ref,
    ids_ref,
    weights_ref,
    vectors_ref,
    cot_ref,
    x_ref,
    act_ref,
    normed_ref,
    dz1_ref,
    dz2_ref,
    sums_ref,
    dagg_ref,
    rims_ref,
):
    nodes = node_ref.shape[0]
    returned = jnp.concatenate([near_ref[...], far_ref[...]], axis=0)
    agg = (agg_ref[...] + dot(hot_lists(ids_ref, nodes), returned)).astype(bf16)
    x = jnp.concatenate([node_ref[...], agg], axis=1)
    x_ref[...] = x
    w1 = weights_ref[4 * lane : 6 * lane]
    w2 = weights_ref[6 * lane :]
    z = dot(x, w1) + vector(vectors_ref, 4)
    sig = sigmoid(z)
    act = (z * sig).astype(bf16)
    act_ref[...] = act
    pair, b2 = centred_second(w2, vector(vectors_ref, 5))
    means = mean_weights()
    normed, scale_inv = normed_of(act, pair, b2, means)
    normed_ref[...] = normed
    upstream = cot_ref[...].astype(f32)
    dz2 = back_norm(upstream, normed, scale_inv, vector(vectors_ref, 6), means)
    dz2b = dz2.astype(bf16)
    dz2_ref[...] = dz2b
    dz1 = dot(dz2b, w2.T) * (sig * (1.0 + z * (1.0 - sig)))
    dz1b = dz1.astype(bf16)
    dz1_ref[...] = dz1b
    dagg = dot(dz1b, w1[lane:].T).astype(bf16)
    dagg_ref[...] = dagg
    parity = parity_of_place()
    first = ids_ref.shape[0] - 2
    rim = rims_ref.shape[0] // 2
    for k, side in enumerate((1 - parity, parity)):
        column = column_of(ids_ref[pl.ds(first + side, 1), :]).astype(jnp.int16)
        picked = hot_columns(column, (0, nodes))
        rims_ref[k * rim : (k + 1) * rim, :] = dot(picked, dagg).astype(bf16)
    sums_ref[0:8, :] = eight_sums(dz1)
    sums_ref[8:16, :] = eight_sums(dz2)


def node_rest_kernel(
    x_ref,
    act_ref,
    normed_ref,
    dz1_ref,
    dz2_ref,
    sums_ref,
    weights_ref,
    vectors_ref,
    cot_ref,
    unused_ref,
    out_ref,
    base_ref,
    grads_ref,
):
    x = x_ref[...]
    normed = normed_ref[...]
    dz1b = dz1_ref[...]
    update = normed * vector(vectors_ref, 6) + vector(vectors_ref, 7)
    out_ref[...] = (x[:, :lane].astype(f32) + update).astype(bf16)
    upstream = cot_ref[...].astype(f32)
    base_ref[...] = upstream + dot(dz1b, weights_ref[4 * lane : 5 * lane].T)
    first = 2 * lane
    second = first + lane
    grads_ref[:first, :] = dot_rows(x, dz1b)
    grads_ref[first:second, :] = dot_rows(act_ref[...], dz2_ref[...])
    sums = [column_sum(sums_ref[0:8, :]), column_sum(sums_ref[8:16, :])]
    sums += [column_sum(eight_sums(upstream * normed)), column_sum(eight_sums(upstream))]
    sums.append(jnp.zeros((sum_rows - len(sums), lane), f32))
    grads_ref[second:, :] = jnp.concatenate(sums, axis=0)


def upstream_kernel(
    rcv_column,
    rcv_low,
    dagg_ref,
    cot_ref,
    z_ref,
    edge_ref,
    unused_ref,
    up_ref,
    slope_ref,
    turned_ref,
    table,
):
    half = table.shape[0]
    table[...] = side_by_side(dagg_ref[...])

    def tile(i):
        rows = pl.ds(pl.multiple_of(i * edge_tile, edge_tile), edge_tile)
        local = pick(rcv_column[rows, :], rcv_low[rows, :], half, table[...])
        up_ref[rows, :] = cot_ref[rows, :].astype(f32) + local
        z = z_ref[rows, :]
        sig = sigmoid(z)
        slope_ref[rows, :] = sig * (1.0 + z * (1.0 - sig))
        turned_ref[:lane, rows] = edge_ref[rows, :].T
        turned_ref[lane:, rows] = (z * sig).astype(bf16).T

    each_tile(cot_ref.shape[0], tile)


def edge_backward_kernel(
    nodes,
    dagg_near_ref,
    dagg_far_ref,
    up_ref,
    normed_ref,
    scale_ref,
    slope_ref,
    sent_turned,
    received_turned,
    turned,
    weights_ref,
    vectors_ref,
    node_grads_ref,
    rcv_low,
    dz_ref,
    kept_ref,
    sent_ref,
    grads_ref,
    table,
    w2_turned,
    means,
    sums,
):
    rim = dagg_near_ref.shape[0]
    parity = parity_of_place()
    w2_turned[...] = weights_ref[3 * lane : 4 * lane].T
    gain = vector(vectors_ref, 2)
    table[pl.ds(pl.multiple_of((1 - parity) * rim, rim), rim), :] = dagg_near_ref[...]
    table[pl.ds(pl.multiple_of(parity * rim, rim), rim), :] = dagg_far_ref[...]
    means[...] = mean_weights()
    grads_ref[: 4 * lane, :] = jnp.zeros((4 * lane, lane), f32)
    sums[...] = jnp.zeros_like(sums)

    def tile(i):
        rows = pl.ds(pl.multiple_of(i * edge_tile, edge_tile), edge_tile)
        hot = hot_columns(rcv_low[rows, :], (nodes, nodes + 2 * rim))
        upstream = up_ref[rows, :] + dot(hot, table[...])
        normed = normed_ref[rows, :]
        dz2 = back_norm(upstream, normed, scale_ref[rows, :], gain, means[...])
        dz2b = dz2.astype(bf16)
        dz1 = dot(dz2b, w2_turned[...]) * slope_ref[rows, :]
        dz1b = dz1.astype(bf16)
        dz_ref[rows, :] = dz1b
        grads_ref[:lane, :] += dot(turned[:lane, rows], dz1b)
        grads_ref[lane : 2 * lane, :] += dot(sent_turned[:, rows], dz1b)
        grads_ref[2 * lane : 3 * lane, :] += dot(received_turned[:, rows], dz1b)
        grads_ref[3 * lane : 4 * lane, :] += dot(turned[lane:, rows], dz2b)
        sums[0:8, :] += eight_sums(dz1)
        sums[8:16, :] += eight_sums(dz2)
        sums[16:24, :] += eight_sums(upstream * normed)
        sums[24:32, :] += eight_sums(upstream)

    each_tile(up_ref.shape[0], tile)
    kept = kept_ref.shape[0]
    node_rows = node_grads_ref.shape[0] - sum_rows
    last = 4 * lane + node_rows
    grads_ref[4 * lane : last, :] = node_grads_ref[:node_rows, :]
    grads_ref[last : last + sum_rows, :] = jnp.concatenate(
        [column_sum(sums[8 * k : 8 * k + 8, :]) for k in range(4)]
        + [node_grads_ref[node_rows : node_rows + 4, :], jnp.zeros((8, lane), f32)],
        axis=0,
    )
    if last + sum_rows < grads_ref.shape[0]:
        grads_ref[last + sum_rows :, :] = jnp.zeros(
            (grads_ref.shape[0] - last - sum_rows, lane), f32
        )
    own = lax.axis_index("sub")
    kept_ref[...] = grads_ref[pl.ds(pl.multiple_of(own * kept, sum_rows), kept), :]
    other = pl.multiple_of((1 - own) * kept, sum_rows)
    sent_ref[...] = grads_ref[pl.ds(other, kept), :].astype(bf16)


def scatter_kernel(
    ids_ref,
    dz_ref,
    snd_column,
    rcv_column,
    weights_ref,
    snd_sum_ref,
    rcv_sum_ref,
    rims_ref,
    snd_total,
    rcv_total,
    halo_total,
):
    half = snd_total.shape[0]
    nodes = 2 * half
    rim = rims_ref.shape[0] // 2
    parity = parity_of_place()
    for total in (snd_total, rcv_total, halo_total):
        total[...] = jnp.zeros_like(total)

    def tile(i):
        rows = pl.ds(pl.multiple_of(i * edge_tile, edge_tile), edge_tile)
        chunk = edge_tile // lane
        dz1b = dz_ref[rows, :]
        dz1 = dz1b.astype(f32)
        first = rcv_column.shape[0] // lane + i * chunk
        snd_total[...] += spread(ids_ref, i * chunk, chunk, half, snd_column[rows, :], dz1)
        rcv_total[...] += spread(ids_ref, first, chunk, half, rcv_column[rows, :], dz1)
        slots = rows_of_ids(ids_ref, first, chunk, 2 * rim, lambda row: row - nodes)
        halo_total[...] += dot(slots, dz1b)

    each_tile(dz_ref.shape[0], tile)
    for total, out_ref in ((snd_total, snd_sum_ref), (rcv_total, rcv_sum_ref)):
        out_ref[:half, :] = total[:, :lane].astype(bf16)
        out_ref[half:, :] = total[:, lane:].astype(bf16)
    w1_turned = weights_ref[2 * lane : 3 * lane].T
    for k, side in enumerate((1 - parity, parity)):
        returned = halo_total[pl.ds(pl.multiple_of(side * rim, rim), rim), :].astype(bf16)
        rims_ref[k * rim : (k + 1) * rim, :] = dot(returned, w1_turned).astype(bf16)


def edge_outputs_kernel(
    dz_ref, cot_ref, edge_ref, normed_ref, vectors_ref, w1_ref, out_ref, grad_ref, w1_turned
):
    w1_turned[...] = w1_ref[...].T
    gain, shift = vector(vectors_ref, 2), vector(vectors_ref, 3)

    def tile(i):
        rows = pl.ds(pl.multiple_of(i * edge_tile, edge_tile), edge_tile)
        cot = cot_ref[rows, :].astype(f32)
        grad_ref[rows, :] = (cot + dot(dz_ref[rows, :], w1_turned[...])).astype(bf16)
        update = normed_ref[rows, :] * gain + shift
        out_ref[rows, :] = (edge_ref[rows, :].astype(f32) + update).astype(bf16)

    each_tile(cot_ref.shape[0], tile)


def node_grad_kernel(
    near_ref, far_ref, base_ref, snd_sum_ref, rcv_sum_ref, weights_ref, ids_ref, out_ref
):
    returned = jnp.concatenate([near_ref[...], far_ref[...]], axis=0)
    total = base_ref[...] + dot(snd_sum_ref[...], weights_ref[lane : 2 * lane].T)
    total = total + dot(rcv_sum_ref[...], weights_ref[2 * lane : 3 * lane].T)
    hot = hot_lists(ids_ref, base_ref.shape[0])
    out_ref[...] = (total + dot(hot, returned)).astype(bf16)


def add_kernel(passed, own_ref, other_ref, *refs):
    out_refs = refs[len(refs) - passed - 1 :]
    out_refs[0][...] = (own_ref[...].astype(f32) + other_ref[...].astype(f32)).astype(bf16)
    for source, target in zip(refs[:passed], out_refs[1:]):
        target[...] = source[...]


def finish_kernel(own_ref, other_ref, *refs):
    out_refs, total_ref = refs[:-1], refs[-1]
    kept = own_ref.shape[0]
    own = lax.axis_index("sub")
    total_ref[pl.ds(pl.multiple_of(own * kept, sum_rows), kept), :] = own_ref[...].astype(f32)
    other = pl.multiple_of((1 - own) * kept, sum_rows)
    total_ref[pl.ds(other, kept), :] = other_ref[...].astype(f32)
    at = 0
    for out_ref in out_refs[:4]:
        out_ref[...] = total_ref[at : at + out_ref.shape[0], :]
        at += out_ref.shape[0]
    for k, out_ref in enumerate(out_refs[4:]):
        out_ref[...] = total_ref[at + k : at + k + 1, :]


def call(kernel, outs, scratch, *operands, anywhere=0, sems=0):
    moved = sum(x.size * x.dtype.itemsize for x in operands)
    held = operands[len(operands) - anywhere :]
    operands = operands[: len(operands) - anywhere]
    operands += tuple(pltpu.with_memory_space_constraint(x, pltpu.HBM) for x in held)
    inside = [pl.BlockSpec(memory_space=pltpu.VMEM)] * (len(operands) - anywhere)
    outside = [pl.BlockSpec(memory_space=pl.ANY)] * anywhere
    scratch_shapes = [pltpu.VMEM(shape, dtype) for shape, dtype in scratch]
    if sems:
        scratch_shapes.append(pltpu.SemaphoreType.DMA((sems,)))
    return pl.pallas_call(
        kernel,
        out_shape=[jax.ShapeDtypeStruct(shape, dtype) for shape, dtype in outs],
        in_specs=inside + outside,
        out_specs=[pl.BlockSpec(memory_space=pltpu.VMEM)] * len(outs),
        scratch_shapes=scratch_shapes,
        compiler_params=pltpu.CompilerParams(vmem_limit_bytes=vmem_limit),
        cost_estimate=pl.CostEstimate(flops=0, bytes_accessed=moved, transcendentals=0),
    )(*operands)


def exchange(message):
    chips = lax.axis_size("dom")
    inner, outer = [], []
    for chip in range(chips):
        inner += [(2 * chip, 2 * chip + 1), (2 * chip + 1, 2 * chip)]
        if chip + 1 < chips:
            outer += [(2 * chip, 2 * chip + 2), (2 * chip + 3, 2 * chip + 1)]
    rim_shape = ((message.shape[0] // 2, lane), bf16)
    near, onward = call(
        split_kernel, [rim_shape, rim_shape], [], lax.ppermute(message, chain, inner)
    )
    return near, lax.ppermute(onward, chain, outer), onward


def sum_rounds():
    for axis in ("sample", "dom"):
        count = lax.axis_size(axis)
        step = count // 2
        while step > 0:
            yield axis, [(i, i ^ step) for i in range(count)]
            step //= 2


def on_device(
    node_in,
    edge_in,
    senders,
    receivers,
    send_list,
    w_edge_first,
    b_edge_first,
    w_edge_second,
    b_edge_second,
    edge_gain,
    edge_shift,
    w_node_first,
    b_node_first,
    w_node_second,
    b_node_second,
    node_gain,
    node_shift,
    node_cotangent,
    edge_cotangent,
):
    node = node_in[0]
    edge = edge_in[0]
    nodes = node.shape[0]
    edges = edge.shape[0]
    rim = send_list.shape[2]
    snd_half = nodes // 2
    kept = -(-(7 * lane + sum_rows) // (2 * sum_rows)) * sum_rows
    row = lambda x: x.reshape(1, lane)
    small = [w_edge_first, w_edge_second, w_node_first, w_node_second]
    small += [row(b_edge_first), row(b_edge_second), row(edge_gain), row(edge_shift)]
    small += [row(b_node_first), row(b_node_second), row(node_gain), row(node_shift)]
    chunks = edges // lane
    sources = [
        senders.reshape(chunks, lane),
        receivers.reshape(chunks, lane),
        send_list[0],
        edge,
        edge_cotangent[0],
        node_cotangent[0],
    ] + small
    rims_shape = ((2 * rim, lane), bf16)
    node, rims = call(
        first_kernel,
        [((nodes, lane), bf16), rims_shape],
        [((2, rim), jnp.int32)],
        node,
        send_list[0],
        anywhere=2,
        sems=2,
    )
    near, far, onward = exchange(rims)
    edge_shape = ((edges, lane), bf16)
    wide_shape = ((edges, lane), f32)
    node_shape = ((nodes, lane), bf16)
    prepared = call(
        prepare_kernel,
        [
            ((2 * chunks + 2, lane), jnp.int32),
            edge_shape,
            edge_shape,
            node_shape,
            ((7 * lane, lane), bf16),
            ((8, lane), f32),
            ((edges, lane), jnp.int32),
            ((edges, lane), jnp.int32),
            ((edges, lane), jnp.int16),
            wide_shape,
            ((snd_half, 2 * lane), bf16),
            ((lane, edges), bf16),
        ],
        [((edges, lane), jnp.int16), ((snd_half, 2 * lane), bf16)],
        node,
        onward,
        *sources,
        anywhere=len(sources),
        sems=len(sources),
    )
    ids, edge, edge_cot, node_cot, weights, vectors = prepared[:6]
    snd_column, rcv_column, rcv_low, z_sent, rcv_local, sent_turned = prepared[6:]
    z, normed, scale, message, rims = call(
        edge_forward_kernel,
        [wide_shape, wide_shape, wide_shape, edge_shape, rims_shape],
        [
            ((snd_half + 2 * rim, 2 * lane), bf16),
            ((lane, 2 * lane), bf16),
            ((2 * lane, 2 * lane), bf16),
            ((2 * rim, lane), f32),
        ],
        near,
        far,
        ids,
        weights,
        vectors,
        rcv_column,
        rcv_low,
        z_sent,
        rcv_local,
    )
    back_near, back_far, onward = exchange(rims)
    agg, received_turned = call(
        collect_kernel,
        [((nodes, lane), f32), ((lane, edges), bf16)],
        [((snd_half + 2 * rim, 2 * lane), bf16), ((snd_half, 2 * lane), f32)],
        ids,
        rcv_column,
        rcv_low,
        message,
        node,
        near,
        far,
        onward,
    )
    node_x, node_act, node_normed, node_dz1, node_dz2, node_sums, dagg, rims = call(
        node_kernel,
        [
            ((nodes, 2 * lane), bf16),
            node_shape,
            ((nodes, lane), f32),
            node_shape,
            node_shape,
            ((16, lane), f32),
            node_shape,
            rims_shape,
        ],
        [],
        back_near,
        back_far,
        node,
        agg,
        ids,
        weights,
        vectors,
        node_cot,
    )
    dagg_near, dagg_far, onward = exchange(rims)
    upstream, slope, turned = call(
        upstream_kernel,
        [wide_shape, wide_shape, ((2 * lane, edges), bf16)],
        [((snd_half, 2 * lane), bf16)],
        rcv_column,
        rcv_low,
        dagg,
        edge_cot,
        z,
        edge,
        onward,
    )
    node_out, base, node_grads = call(
        node_rest_kernel,
        [node_shape, ((nodes, lane), f32), ((3 * lane + sum_rows, lane), f32)],
        [],
        node_x,
        node_act,
        node_normed,
        node_dz1,
        node_dz2,
        node_sums,
        weights,
        vectors,
        node_cot,
        onward,
    )
    half_shape = ((kept, lane), bf16)
    dz, grads_kept, grads_sent = call(
        functools.partial(edge_backward_kernel, nodes),
        [edge_shape, ((kept, lane), f32), half_shape],
        [
            ((2 * kept, lane), f32),
            ((2 * rim, lane), bf16),
            ((lane, lane), bf16),
            ((2 * lane, 2 * lane), bf16),
            ((32, lane), f32),
        ],
        dagg_near,
        dagg_far,
        upstream,
        normed,
        scale,
        slope,
        sent_turned,
        received_turned,
        turned,
        weights,
        vectors,
        node_grads,
        rcv_low,
    )
    core_pairs = [(0, 1), (1, 0)]
    other = lax.ppermute(grads_sent, "sub", core_pairs)
    (grads,) = call(functools.partial(add_kernel, 0), [half_shape], [], grads_kept, other)
    snd_sum, rcv_sum, rims = call(
        scatter_kernel,
        [node_shape, node_shape, rims_shape],
        [
            ((snd_half, 2 * lane), f32),
            ((snd_half, 2 * lane), f32),
            ((2 * rim, lane), f32),
        ],
        ids,
        dz,
        snd_column,
        rcv_column,
        weights,
    )
    w1_edge = weights[:lane]
    edge_out = edge_grad = node_grad = None
    for number, (axis, pairs) in enumerate(sum_rounds()):
        other = lax.ppermute(grads, axis, pairs)
        passed, written = [], []
        if number == 0:
            passed = [rims]
        elif number == 1:
            back_near, back_far, unused = exchange(rims)
            passed = [back_near, back_far, vectors, w1_edge]
        elif number == 2:
            (node_grad,) = call(
                node_grad_kernel,
                [node_shape],
                [],
                back_near,
                back_far,
                base,
                snd_sum,
                rcv_sum,
                weights,
                ids,
            )
            edge_out, edge_grad = call(
                edge_outputs_kernel,
                [edge_shape, edge_shape],
                [((lane, lane), bf16)],
                dz,
                edge_cot,
                edge,
                normed,
                vectors,
                w1_edge,
            )
            written = [node_grad, edge_out, edge_grad]
        grads, *passed = call(
            functools.partial(add_kernel, len(passed)),
            [half_shape] + [(x.shape, x.dtype) for x in passed],
            [],
            grads,
            other,
            *passed,
            *written,
            anywhere=len(written),
        )
        if number == 0:
            (rims,) = passed
        elif number == 1:
            back_near, back_far, vectors, w1_edge = passed
    others = lax.ppermute(grads, "sub", core_pairs)
    matrices = [3 * lane, lane, 2 * lane, lane]
    totals = call(
        finish_kernel,
        [((height, lane), f32) for height in matrices] + [((1, lane), f32)] * 8,
        [((2 * kept, lane), f32)],
        grads,
        others,
    )
    flat = [total.reshape(lane) for total in totals[4:]]
    return (
        node_out[None],
        edge_out[None],
        node_grad[None],
        edge_grad[None],
        totals[0],
        flat[0],
        totals[1],
        flat[1],
        flat[2],
        flat[3],
        totals[2],
        flat[4],
        totals[3],
        flat[5],
        flat[6],
        flat[7],
    )


def solution(mesh):
    node_spec = P(("groups", "sample"), ("dom", "sub"), None)
    ids_spec = P(("dom", "sub"))
    return jax.shard_map(
        on_device,
        mesh=mesh,
        in_specs=(
            (node_spec, node_spec, ids_spec, ids_spec, P(("dom", "sub"), None, None))
            + (P(),) * 12
            + (node_spec, node_spec)
        ),
        out_specs=(
            (node_spec,) * 4
            + (P("groups", None), P("groups"), P("groups", None), P("groups"), P("groups"), P("groups"))
            * 2
        ),
        check_vma=False,
    )
```

```python
import functools
import math

import jax
import jax.numpy as jnp
from jax import lax
from jax.experimental import pallas as pl
from jax.experimental.pallas import tpu as pltpu
from jax.sharding import PartitionSpec as P

epsilon = 1e-05
rows_dims = (((0,), (0,)), ((), ()))
back_dims = (((1,), (1,)), ((), ()))
f32 = jnp.float32
bf16 = jnp.bfloat16
lane = 128
edge_tile = 512
vmem_limit = 32 * 1024 * 1024
sum_rows = 16
chain = ("dom", "sub")


def each_tile(rows, tile, tile_group=6):
    count = rows // edge_tile
    group = math.gcd(count, tile_group)

    def several(i, carry):
        for k in range(group):
            tile(i * group + k)
        return carry

    lax.fori_loop(0, count // group, several, 0)


def dot(left, right):
    return jnp.dot(left, right, preferred_element_type=f32)


def dot_rows(left, right):
    return lax.dot_general(left, right, rows_dims, preferred_element_type=f32)


def dot_back(left, right):
    return lax.dot_general(left, right, back_dims, preferred_element_type=f32)


def column_of(row):
    return jnp.broadcast_to(row, (lane, lane)).T


def hot_columns(low, *spans):
    targets = lax.broadcasted_iota(jnp.int16, low.shape, 1)
    one, zero = jnp.ones((), bf16), jnp.zeros((), bf16)
    parts = [
        jnp.where(low == targets + jnp.int16(at), one, zero)
        for start, stop in spans
        for at in range(start, stop, lane)
    ]
    return jnp.concatenate(parts, axis=1)


def hot_rows(row, height):
    low = jnp.broadcast_to(row, (16, lane)).astype(jnp.int16)
    targets = lax.broadcasted_iota(jnp.int16, (height, lane), 0).reshape(height // 16, 16, lane)
    one, zero = jnp.ones((), bf16), jnp.zeros((), bf16)
    return jnp.where(targets == low[None], one, zero).reshape(height, lane)


def folded(ids, half):
    return jnp.where((ids >= half) & (ids < 2 * half), ids - half, ids)


def side_by_side(rows):
    half = rows.shape[0] // 2
    return jnp.concatenate([rows[:half], rows[half:]], axis=1)


def pick(ids, low, half, table, *halo):
    both = dot(hot_columns(low, (0, half), *halo), table)
    return jnp.where(ids >= half, both[:, lane:], both[:, :lane])


def rows_of_ids(ids_ref, first, count, height, change):
    parts = [hot_rows(change(ids_ref[pl.ds(first + k, 1), :]), height) for k in range(count)]
    return jnp.concatenate(parts, axis=1)


def spread(ids_ref, first, count, half, ids, values):
    upper = ids >= half
    paired = jnp.concatenate(
        [jnp.where(upper, 0.0, values).astype(bf16), jnp.where(upper, values, 0.0).astype(bf16)],
        axis=1,
    )
    return dot(rows_of_ids(ids_ref, first, count, half, lambda row: folded(row, half)), paired)


def sigmoid(z):
    return 0.5 * jnp.tanh(0.5 * z) + 0.5


def vector(vectors_ref, k):
    return vectors_ref[k : k + 1, :]


def centred_second(w, b):
    w = w.astype(f32)
    w = w - jnp.mean(w, axis=1, keepdims=True)
    high = w.astype(bf16)
    low = (w - high.astype(f32)).astype(bf16)
    return jnp.concatenate([high, low], axis=1), b - jnp.mean(b, axis=1, keepdims=True)


def mean_weights():
    shape = (2 * lane, 2 * lane)
    left = lax.broadcasted_iota(jnp.int32, shape, 0) < lane
    right = lax.broadcasted_iota(jnp.int32, shape, 1) < lane
    return jnp.where(left == right, 1.0 / lane, 0.0).astype(bf16)


def normed_of(act, w_pair, b_centred, means):
    both = dot(act, w_pair)
    center = both[:, :lane] + both[:, lane:] + b_centred
    variance = dot((center * center).astype(bf16), means[:lane, :lane])
    scale_inv = lax.rsqrt(variance + epsilon)
    return center * scale_inv, scale_inv


def back_norm(upstream, normed, scale_inv, gain, means):
    d_normed = upstream * gain
    pair = jnp.concatenate([d_normed.astype(bf16), (d_normed * normed).astype(bf16)], axis=1)
    both = dot(pair, means)
    return scale_inv * (d_normed - both[:, :lane] - normed * both[:, lane:])


def column_sum(values):
    return jnp.sum(values, axis=0, keepdims=True)


def eight_sums(values):
    return jnp.sum(values.reshape(values.shape[0] // 8, 8, lane), axis=0)


def parity_of_place():
    return lax.axis_index(chain) % 2


def started(moves, sems):
    copies = [
        pltpu.make_async_copy(source, target, sems.at[k])
        for k, (source, target) in enumerate(moves)
    ]
    for copy in copies:
        copy.start()
    return copies


def first_kernel(node_hbm, list_hbm, snd_hbm, rcv_hbm, edge_hbm, *refs):
    small = refs[:12]
    node_ref, message_ref, ids_ref, edge_ref, weights_ref, vectors_ref, sems = refs[12:]
    chunks = snd_hbm.shape[0]
    moves = [
        (node_hbm, node_ref),
        (list_hbm, ids_ref.at[2 * chunks : 2 * chunks + 2]),
        (snd_hbm, ids_ref.at[:chunks]),
        (rcv_hbm, ids_ref.at[chunks : 2 * chunks]),
    ]
    at = 0
    for source in small[:4]:
        moves.append((source, weights_ref.at[at : at + source.shape[0]]))
        at += source.shape[0]
    for k, source in enumerate(small[4:]):
        moves.append((source, vectors_ref.at[k : k + 1]))
    moves.append((edge_hbm, edge_ref))
    copies = started(moves, sems)
    for copy in copies[:2]:
        copy.wait()
    parity = parity_of_place()
    node = node_ref[...]
    rim = message_ref.shape[0] // 2
    for k, side in enumerate((1 - parity, parity)):
        column = column_of(ids_ref[pl.ds(2 * chunks + side, 1), :]).astype(jnp.int16)
        hot = hot_columns(column, (0, node.shape[0]))
        message_ref[k * rim : (k + 1) * rim, :] = dot(hot, node).astype(bf16)
    for copy in copies[2:]:
        copy.wait()


def prepare_kernel(
    ids_ref,
    node_ref,
    weights_ref,
    vectors_ref,
    edge_ref,
    unused_ref,
    edge_cot_hbm,
    node_cot_hbm,
    edge_cot_ref,
    node_cot_ref,
    snd_column,
    rcv_column,
    rcv_low,
    z_ref,
    rcv_local,
    turned_ref,
    snd_low,
    snd_table,
    sems,
):
    copies = started([(edge_cot_hbm, edge_cot_ref), (node_cot_hbm, node_cot_ref)], sems)
    chunks = snd_column.shape[0] // lane
    half = snd_table.shape[0]
    for k in range(chunks):
        at = slice(k * lane, (k + 1) * lane)
        snd = column_of(ids_ref[k : k + 1, :])
        rcv = column_of(ids_ref[chunks + k : chunks + k + 1, :])
        snd_column[at, :] = snd
        rcv_column[at, :] = rcv
        snd_low[at, :] = folded(snd, half).astype(jnp.int16)
        rcv_low[at, :] = folded(rcv, half).astype(jnp.int16)
    node = node_ref[...]
    snd_table[...] = side_by_side(node)
    rcv_local[...] = side_by_side(dot(node, weights_ref[2 * lane : 3 * lane]).astype(bf16))
    w1 = weights_ref[: 2 * lane]
    b1 = vector(vectors_ref, 0)

    def tile(i):
        rows = pl.ds(pl.multiple_of(i * edge_tile, edge_tile), edge_tile)
        x = edge_ref[rows, :]
        sent = pick(snd_column[rows, :], snd_low[rows, :], half, snd_table[...]).astype(bf16)
        z_ref[rows, :] = dot(jnp.concatenate([x, sent], axis=1), w1) + b1
        turned_ref[:, rows] = sent.T

    each_tile(edge_ref.shape[0], tile)
    for copy in copies:
        copy.wait()


def split_kernel(message_ref, near_ref, far_ref):
    rim = near_ref.shape[0]
    near_ref[...] = message_ref[:rim, :]
    far_ref[...] = message_ref[rim:, :]


def edge_forward_kernel(
    near_ref,
    far_ref,
    ids_ref,
    weights_ref,
    vectors_ref,
    rcv_column,
    rcv_low,
    z_sent,
    rcv_local,
    z_ref,
    normed_ref,
    scale_ref,
    message_ref,
    rims_ref,
    table,
    w2_pair,
    means,
    total,
):
    half = rcv_local.shape[0]
    nodes = 2 * half
    rim = near_ref.shape[0]
    parity = parity_of_place()
    near_at = pl.multiple_of((1 - parity) * rim, rim)
    far_at = pl.multiple_of(parity * rim, rim)
    w1_rcv = weights_ref[2 * lane : 3 * lane]
    gain, shift = vector(vectors_ref, 2), vector(vectors_ref, 3)
    table[:half, :] = rcv_local[...]
    table[half:, :lane] = jnp.zeros((2 * rim, lane), bf16)
    table[pl.ds(half + near_at, rim), lane:] = dot(near_ref[...], w1_rcv).astype(bf16)
    table[pl.ds(half + far_at, rim), lane:] = dot(far_ref[...], w1_rcv).astype(bf16)
    pair, b2 = centred_second(weights_ref[3 * lane : 4 * lane], vector(vectors_ref, 1))
    w2_pair[...] = pair
    means[...] = mean_weights()
    total[...] = jnp.zeros_like(total)

    def tile(i):
        rows = pl.ds(pl.multiple_of(i * edge_tile, edge_tile), edge_tile)
        slots = (nodes, nodes + 2 * rim)
        z = z_sent[rows, :]
        z = z + pick(rcv_column[rows, :], rcv_low[rows, :], half, table[...], slots)
        z_ref[rows, :] = z
        act = (z * sigmoid(z)).astype(bf16)
        normed, scale_inv = normed_of(act, w2_pair[...], b2, means[...])
        normed_ref[rows, :] = normed
        scale_ref[rows, :] = scale_inv
        message = (normed * gain + shift).astype(bf16)
        message_ref[rows, :] = message
        first = (rcv_column.shape[0] + i * edge_tile) // lane
        hot = rows_of_ids(ids_ref, first, edge_tile // lane, 2 * rim, lambda row: row - nodes)
        total[...] += dot(hot, message)

    each_tile(rcv_column.shape[0], tile, 3)
    rims_ref[:rim, :] = total[pl.ds(near_at, rim), :].astype(bf16)
    rims_ref[rim:, :] = total[pl.ds(far_at, rim), :].astype(bf16)


def collect_kernel(
    ids_ref,
    rcv_column,
    rcv_low,
    message_ref,
    node_ref,
    near_ref,
    far_ref,
    unused_ref,
    agg_ref,
    turned_ref,
    table,
    total,
):
    rim = near_ref.shape[0]
    half = total.shape[0]
    nodes = 2 * half
    parity = parity_of_place()
    near_at = pl.multiple_of((1 - parity) * rim, rim)
    far_at = pl.multiple_of(parity * rim, rim)
    table[:half, :] = side_by_side(node_ref[...])
    table[half:, :lane] = jnp.zeros((2 * rim, lane), bf16)
    table[pl.ds(half + near_at, rim), lane:] = near_ref[...]
    table[pl.ds(half + far_at, rim), lane:] = far_ref[...]
    total[...] = jnp.zeros_like(total)

    def tile(i):
        rows = pl.ds(pl.multiple_of(i * edge_tile, edge_tile), edge_tile)
        first = (rcv_column.shape[0] + i * edge_tile) // lane
        rcv = rcv_column[rows, :]
        message = message_ref[rows, :].astype(f32)
        total[...] += spread(ids_ref, first, edge_tile // lane, half, rcv, message)
        slots = (nodes, nodes + 2 * rim)
        turned_ref[:, rows] = pick(rcv, rcv_low[rows, :], half, table[...], slots).astype(bf16).T

    each_tile(rcv_column.shape[0], tile)
    agg_ref[:half, :] = total[:, :lane]
    agg_ref[half:, :] = total[:, lane:]


def hot_lists(ids_ref, nodes):
    parity = parity_of_place()
    first = ids_ref.shape[0] - 2
    near = ids_ref[pl.ds(first + 1 - parity, 1), :]
    far = ids_ref[pl.ds(first + parity, 1), :]
    return jnp.concatenate([hot_rows(near, nodes), hot_rows(far, nodes)], axis=1)


def node_kernel(
    near_ref,
    far_ref,
    node_ref,
    agg_ref,
    ids_ref,
    weights_ref,
    vectors_ref,
    cot_ref,
    x_ref,
    act_ref,
    normed_ref,
    dz1_ref,
    dz2_ref,
    sums_ref,
    dagg_ref,
    rims_ref,
):
    nodes = node_ref.shape[0]
    returned = jnp.concatenate([near_ref[...], far_ref[...]], axis=0)
    agg = (agg_ref[...] + dot(hot_lists(ids_ref, nodes), returned)).astype(bf16)
    x = jnp.concatenate([node_ref[...], agg], axis=1)
    x_ref[...] = x
    w1 = weights_ref[4 * lane : 6 * lane]
    w2 = weights_ref[6 * lane :]
    z = dot(x, w1) + vector(vectors_ref, 4)
    sig = sigmoid(z)
    act = (z * sig).astype(bf16)
    act_ref[...] = act
    pair, b2 = centred_second(w2, vector(vectors_ref, 5))
    means = mean_weights()
    normed, scale_inv = normed_of(act, pair, b2, means)
    normed_ref[...] = normed
    upstream = cot_ref[...].astype(f32)
    dz2 = back_norm(upstream, normed, scale_inv, vector(vectors_ref, 6), means)
    dz2b = dz2.astype(bf16)
    dz2_ref[...] = dz2b
    dz1 = dot(dz2b, w2.T) * (sig * (1.0 + z * (1.0 - sig)))
    dz1b = dz1.astype(bf16)
    dz1_ref[...] = dz1b
    dagg = dot(dz1b, w1[lane:].T).astype(bf16)
    dagg_ref[...] = dagg
    parity = parity_of_place()
    first = ids_ref.shape[0] - 2
    rim = rims_ref.shape[0] // 2
    for k, side in enumerate((1 - parity, parity)):
        column = column_of(ids_ref[pl.ds(first + side, 1), :]).astype(jnp.int16)
        picked = hot_columns(column, (0, nodes))
        rims_ref[k * rim : (k + 1) * rim, :] = dot(picked, dagg).astype(bf16)
    sums_ref[0:8, :] = eight_sums(dz1)
    sums_ref[8:16, :] = eight_sums(dz2)


def node_rest_kernel(
    x_ref,
    act_ref,
    normed_ref,
    dz1_ref,
    dz2_ref,
    sums_ref,
    weights_ref,
    vectors_ref,
    cot_ref,
    unused_ref,
    out_ref,
    base_ref,
    grads_ref,
):
    x = x_ref[...]
    normed = normed_ref[...]
    dz1b = dz1_ref[...]
    update = normed * vector(vectors_ref, 6) + vector(vectors_ref, 7)
    out_ref[...] = (x[:, :lane].astype(f32) + update).astype(bf16)
    upstream = cot_ref[...].astype(f32)
    base_ref[...] = upstream + dot(dz1b, weights_ref[4 * lane : 5 * lane].T)
    first = 2 * lane
    second = first + lane
    grads_ref[:first, :] = dot_rows(x, dz1b)
    grads_ref[first:second, :] = dot_rows(act_ref[...], dz2_ref[...])
    sums = [column_sum(sums_ref[0:8, :]), column_sum(sums_ref[8:16, :])]
    sums += [column_sum(eight_sums(upstream * normed)), column_sum(eight_sums(upstream))]
    sums.append(jnp.zeros((sum_rows - len(sums), lane), f32))
    grads_ref[second:, :] = jnp.concatenate(sums, axis=0)


def upstream_kernel(
    rcv_column,
    rcv_low,
    dagg_ref,
    cot_ref,
    z_ref,
    edge_ref,
    unused_ref,
    up_ref,
    slope_ref,
    turned_ref,
    table,
):
    half = table.shape[0]
    table[...] = side_by_side(dagg_ref[...])

    def tile(i):
        rows = pl.ds(pl.multiple_of(i * edge_tile, edge_tile), edge_tile)
        local = pick(rcv_column[rows, :], rcv_low[rows, :], half, table[...])
        up_ref[rows, :] = cot_ref[rows, :].astype(f32) + local
        z = z_ref[rows, :]
        sig = sigmoid(z)
        slope_ref[rows, :] = sig * (1.0 + z * (1.0 - sig))
        turned_ref[:lane, rows] = edge_ref[rows, :].T
        turned_ref[lane:, rows] = (z * sig).astype(bf16).T

    each_tile(cot_ref.shape[0], tile)


def edge_backward_kernel(
    nodes,
    dagg_near_ref,
    dagg_far_ref,
    up_ref,
    normed_ref,
    scale_ref,
    slope_ref,
    sent_turned,
    received_turned,
    turned,
    weights_ref,
    vectors_ref,
    node_grads_ref,
    rcv_low,
    dz_ref,
    kept_ref,
    sent_ref,
    grads_ref,
    table,
    w2_turned,
    means,
    sums,
):
    rim = dagg_near_ref.shape[0]
    parity = parity_of_place()
    w2_turned[...] = weights_ref[3 * lane : 4 * lane].T
    gain = vector(vectors_ref, 2)
    table[pl.ds(pl.multiple_of((1 - parity) * rim, rim), rim), :] = dagg_near_ref[...]
    table[pl.ds(pl.multiple_of(parity * rim, rim), rim), :] = dagg_far_ref[...]
    means[...] = mean_weights()
    grads_ref[: 4 * lane, :] = jnp.zeros((4 * lane, lane), f32)
    sums[...] = jnp.zeros_like(sums)

    def tile(i):
        rows = pl.ds(pl.multiple_of(i * edge_tile, edge_tile), edge_tile)
        hot = hot_columns(rcv_low[rows, :], (nodes, nodes + 2 * rim))
        upstream = up_ref[rows, :] + dot(hot, table[...])
        normed = normed_ref[rows, :]
        dz2 = back_norm(upstream, normed, scale_ref[rows, :], gain, means[...])
        dz2b = dz2.astype(bf16)
        dz1 = dot(dz2b, w2_turned[...]) * slope_ref[rows, :]
        dz1b = dz1.astype(bf16)
        dz_ref[rows, :] = dz1b
        grads_ref[:lane, :] += dot(turned[:lane, rows], dz1b)
        grads_ref[lane : 2 * lane, :] += dot(sent_turned[:, rows], dz1b)
        grads_ref[2 * lane : 3 * lane, :] += dot(received_turned[:, rows], dz1b)
        grads_ref[3 * lane : 4 * lane, :] += dot(turned[lane:, rows], dz2b)
        sums[0:8, :] += eight_sums(dz1)
        sums[8:16, :] += eight_sums(dz2)
        sums[16:24, :] += eight_sums(upstream * normed)
        sums[24:32, :] += eight_sums(upstream)

    each_tile(up_ref.shape[0], tile)
    kept = kept_ref.shape[0]
    node_rows = node_grads_ref.shape[0] - sum_rows
    last = 4 * lane + node_rows
    grads_ref[4 * lane : last, :] = node_grads_ref[:node_rows, :]
    grads_ref[last : last + sum_rows, :] = jnp.concatenate(
        [column_sum(sums[8 * k : 8 * k + 8, :]) for k in range(4)]
        + [node_grads_ref[node_rows : node_rows + 4, :], jnp.zeros((8, lane), f32)],
        axis=0,
    )
    if last + sum_rows < grads_ref.shape[0]:
        grads_ref[last + sum_rows :, :] = jnp.zeros(
            (grads_ref.shape[0] - last - sum_rows, lane), f32
        )
    own = lax.axis_index("sub")
    kept_ref[...] = grads_ref[pl.ds(pl.multiple_of(own * kept, sum_rows), kept), :]
    other = pl.multiple_of((1 - own) * kept, sum_rows)
    sent_ref[...] = grads_ref[pl.ds(other, kept), :].astype(bf16)


def scatter_kernel(
    ids_ref,
    dz_ref,
    snd_column,
    rcv_column,
    weights_ref,
    snd_sum_ref,
    rcv_sum_ref,
    rims_ref,
    snd_total,
    rcv_total,
    halo_total,
):
    half = snd_total.shape[0]
    nodes = 2 * half
    rim = rims_ref.shape[0] // 2
    parity = parity_of_place()
    for total in (snd_total, rcv_total, halo_total):
        total[...] = jnp.zeros_like(total)

    def tile(i):
        rows = pl.ds(pl.multiple_of(i * edge_tile, edge_tile), edge_tile)
        chunk = edge_tile // lane
        dz1b = dz_ref[rows, :]
        dz1 = dz1b.astype(f32)
        first = rcv_column.shape[0] // lane + i * chunk
        snd_total[...] += spread(ids_ref, i * chunk, chunk, half, snd_column[rows, :], dz1)
        rcv_total[...] += spread(ids_ref, first, chunk, half, rcv_column[rows, :], dz1)
        slots = rows_of_ids(ids_ref, first, chunk, 2 * rim, lambda row: row - nodes)
        halo_total[...] += dot(slots, dz1b)

    each_tile(dz_ref.shape[0], tile)
    for total, out_ref in ((snd_total, snd_sum_ref), (rcv_total, rcv_sum_ref)):
        out_ref[:half, :] = total[:, :lane].astype(bf16)
        out_ref[half:, :] = total[:, lane:].astype(bf16)
    w1_turned = weights_ref[2 * lane : 3 * lane].T
    for k, side in enumerate((1 - parity, parity)):
        returned = halo_total[pl.ds(pl.multiple_of(side * rim, rim), rim), :].astype(bf16)
        rims_ref[k * rim : (k + 1) * rim, :] = dot(returned, w1_turned).astype(bf16)


def edge_outputs_kernel(
    dz_ref, cot_ref, edge_ref, normed_ref, vectors_ref, w1_ref, out_ref, grad_ref, w1_turned
):
    w1_turned[...] = w1_ref[...].T
    gain, shift = vector(vectors_ref, 2), vector(vectors_ref, 3)

    def tile(i):
        rows = pl.ds(pl.multiple_of(i * edge_tile, edge_tile), edge_tile)
        cot = cot_ref[rows, :].astype(f32)
        grad_ref[rows, :] = (cot + dot(dz_ref[rows, :], w1_turned[...])).astype(bf16)
        update = normed_ref[rows, :] * gain + shift
        out_ref[rows, :] = (edge_ref[rows, :].astype(f32) + update).astype(bf16)

    each_tile(cot_ref.shape[0], tile)


def node_grad_kernel(
    near_ref, far_ref, base_ref, snd_sum_ref, rcv_sum_ref, weights_ref, ids_ref, out_ref
):
    returned = jnp.concatenate([near_ref[...], far_ref[...]], axis=0)
    total = base_ref[...] + dot(snd_sum_ref[...], weights_ref[lane : 2 * lane].T)
    total = total + dot(rcv_sum_ref[...], weights_ref[2 * lane : 3 * lane].T)
    hot = hot_lists(ids_ref, base_ref.shape[0])
    out_ref[...] = (total + dot(hot, returned)).astype(bf16)


def add_kernel(passed, own_ref, other_ref, *refs):
    out_refs = refs[len(refs) - passed - 1 :]
    out_refs[0][...] = (own_ref[...].astype(f32) + other_ref[...].astype(f32)).astype(bf16)
    for source, target in zip(refs[:passed], out_refs[1:]):
        target[...] = source[...]


def finish_kernel(own_ref, other_ref, *refs):
    out_refs, total_ref = refs[:-1], refs[-1]
    kept = own_ref.shape[0]
    own = lax.axis_index("sub")
    total_ref[pl.ds(pl.multiple_of(own * kept, sum_rows), kept), :] = own_ref[...].astype(f32)
    other = pl.multiple_of((1 - own) * kept, sum_rows)
    total_ref[pl.ds(other, kept), :] = other_ref[...].astype(f32)
    at = 0
    for out_ref in out_refs[:4]:
        out_ref[...] = total_ref[at : at + out_ref.shape[0], :]
        at += out_ref.shape[0]
    for k, out_ref in enumerate(out_refs[4:]):
        out_ref[...] = total_ref[at + k : at + k + 1, :]


def call(kernel, outs, scratch, *operands, anywhere=0, sems=0):
    moved = sum(x.size * x.dtype.itemsize for x in operands)
    held = operands[len(operands) - anywhere :]
    operands = operands[: len(operands) - anywhere]
    operands += tuple(pltpu.with_memory_space_constraint(x, pltpu.HBM) for x in held)
    inside = [pl.BlockSpec(memory_space=pltpu.VMEM)] * (len(operands) - anywhere)
    outside = [pl.BlockSpec(memory_space=pl.ANY)] * anywhere
    scratch_shapes = [pltpu.VMEM(shape, dtype) for shape, dtype in scratch]
    if sems:
        scratch_shapes.append(pltpu.SemaphoreType.DMA((sems,)))
    return pl.pallas_call(
        kernel,
        out_shape=[jax.ShapeDtypeStruct(shape, dtype) for shape, dtype in outs],
        in_specs=inside + outside,
        out_specs=[pl.BlockSpec(memory_space=pltpu.VMEM)] * len(outs),
        scratch_shapes=scratch_shapes,
        compiler_params=pltpu.CompilerParams(vmem_limit_bytes=vmem_limit),
        cost_estimate=pl.CostEstimate(flops=0, bytes_accessed=moved, transcendentals=0),
    )(*operands)


def exchange(message):
    count = lax.axis_size("dom") * lax.axis_size("sub")
    inner = [(i, i ^ 1) for i in range(count)]
    outer = [(i, (((i - 1) % count ^ 1) + 1) % count) for i in range(count)]
    rim_shape = ((message.shape[0] // 2, lane), bf16)
    near, far = call(split_kernel, [rim_shape, rim_shape], [], message)
    return lax.ppermute(near, chain, inner), lax.ppermute(far, chain, outer), far


def sum_rounds():
    for axis in ("sample", "dom"):
        count = lax.axis_size(axis)
        step = count // 2
        while step > 0:
            yield axis, [(i, i ^ step) for i in range(count)]
            step //= 2


def on_device(
    node_in,
    edge_in,
    senders,
    receivers,
    send_list,
    w_edge_first,
    b_edge_first,
    w_edge_second,
    b_edge_second,
    edge_gain,
    edge_shift,
    w_node_first,
    b_node_first,
    w_node_second,
    b_node_second,
    node_gain,
    node_shift,
    node_cotangent,
    edge_cotangent,
):
    node = node_in[0]
    edge = edge_in[0]
    nodes = node.shape[0]
    edges = edge.shape[0]
    rim = send_list.shape[2]
    snd_half = nodes // 2
    kept = -(-(7 * lane + sum_rows) // (2 * sum_rows)) * sum_rows
    row = lambda x: x.reshape(1, lane)
    small = [w_edge_first, w_edge_second, w_node_first, w_node_second]
    small += [row(b_edge_first), row(b_edge_second), row(edge_gain), row(edge_shift)]
    small += [row(b_node_first), row(b_node_second), row(node_gain), row(node_shift)]
    chunks = edges // lane
    sources = [
        node,
        send_list[0],
        senders.reshape(chunks, lane),
        receivers.reshape(chunks, lane),
        edge,
    ] + small
    rims_shape = ((2 * rim, lane), bf16)
    edge_shape = ((edges, lane), bf16)
    wide_shape = ((edges, lane), f32)
    node_shape = ((nodes, lane), bf16)
    node, rims, ids, edge, weights, vectors = call(
        first_kernel,
        [
            node_shape,
            rims_shape,
            ((2 * chunks + 2, lane), jnp.int32),
            edge_shape,
            ((7 * lane, lane), bf16),
            ((8, lane), f32),
        ],
        [],
        *sources,
        anywhere=len(sources),
        sems=len(sources),
    )
    near, far, onward = exchange(rims)
    prepared = call(
        prepare_kernel,
        [
            edge_shape,
            node_shape,
            ((edges, lane), jnp.int32),
            ((edges, lane), jnp.int32),
            ((edges, lane), jnp.int16),
            wide_shape,
            ((snd_half, 2 * lane), bf16),
            ((lane, edges), bf16),
        ],
        [((edges, lane), jnp.int16), ((snd_half, 2 * lane), bf16)],
        ids,
        node,
        weights,
        vectors,
        edge,
        onward,
        edge_cotangent[0],
        node_cotangent[0],
        anywhere=2,
        sems=2,
    )
    edge_cot, node_cot, snd_column, rcv_column, rcv_low, z_sent, rcv_local, sent_turned = prepared
    z, normed, scale, message, rims = call(
        edge_forward_kernel,
        [wide_shape, wide_shape, wide_shape, edge_shape, rims_shape],
        [
            ((snd_half + 2 * rim, 2 * lane), bf16),
            ((lane, 2 * lane), bf16),
            ((2 * lane, 2 * lane), bf16),
            ((2 * rim, lane), f32),
        ],
        near,
        far,
        ids,
        weights,
        vectors,
        rcv_column,
        rcv_low,
        z_sent,
        rcv_local,
    )
    back_near, back_far, onward = exchange(rims)
    agg, received_turned = call(
        collect_kernel,
        [((nodes, lane), f32), ((lane, edges), bf16)],
        [((snd_half + 2 * rim, 2 * lane), bf16), ((snd_half, 2 * lane), f32)],
        ids,
        rcv_column,
        rcv_low,
        message,
        node,
        near,
        far,
        onward,
    )
    node_x, node_act, node_normed, node_dz1, node_dz2, node_sums, dagg, rims = call(
        node_kernel,
        [
            ((nodes, 2 * lane), bf16),
            node_shape,
            ((nodes, lane), f32),
            node_shape,
            node_shape,
            ((16, lane), f32),
            node_shape,
            rims_shape,
        ],
        [],
        back_near,
        back_far,
        node,
        agg,
        ids,
        weights,
        vectors,
        node_cot,
    )
    dagg_near, dagg_far, onward = exchange(rims)
    upstream, slope, turned = call(
        upstream_kernel,
        [wide_shape, wide_shape, ((2 * lane, edges), bf16)],
        [((snd_half, 2 * lane), bf16)],
        rcv_column,
        rcv_low,
        dagg,
        edge_cot,
        z,
        edge,
        onward,
    )
    node_out, base, node_grads = call(
        node_rest_kernel,
        [node_shape, ((nodes, lane), f32), ((3 * lane + sum_rows, lane), f32)],
        [],
        node_x,
        node_act,
        node_normed,
        node_dz1,
        node_dz2,
        node_sums,
        weights,
        vectors,
        node_cot,
        onward,
    )
    half_shape = ((kept, lane), bf16)
    dz, grads_kept, grads_sent = call(
        functools.partial(edge_backward_kernel, nodes),
        [edge_shape, ((kept, lane), f32), half_shape],
        [
            ((2 * kept, lane), f32),
            ((2 * rim, lane), bf16),
            ((lane, lane), bf16),
            ((2 * lane, 2 * lane), bf16),
            ((32, lane), f32),
        ],
        dagg_near,
        dagg_far,
        upstream,
        normed,
        scale,
        slope,
        sent_turned,
        received_turned,
        turned,
        weights,
        vectors,
        node_grads,
        rcv_low,
    )
    core_pairs = [(0, 1), (1, 0)]
    other = lax.ppermute(grads_sent, "sub", core_pairs)
    (grads,) = call(functools.partial(add_kernel, 0), [half_shape], [], grads_kept, other)
    snd_sum, rcv_sum, rims = call(
        scatter_kernel,
        [node_shape, node_shape, rims_shape],
        [
            ((snd_half, 2 * lane), f32),
            ((snd_half, 2 * lane), f32),
            ((2 * rim, lane), f32),
        ],
        ids,
        dz,
        snd_column,
        rcv_column,
        weights,
    )
    w1_edge = weights[:lane]
    edge_out = edge_grad = node_grad = None
    for number, (axis, pairs) in enumerate(sum_rounds()):
        other = lax.ppermute(grads, axis, pairs)
        passed, written = [], []
        if number == 0:
            passed = [rims]
        elif number == 1:
            back_near, back_far, unused = exchange(rims)
            passed = [back_near, back_far, vectors, w1_edge]
        elif number == 2:
            (node_grad,) = call(
                node_grad_kernel,
                [node_shape],
                [],
                back_near,
                back_far,
                base,
                snd_sum,
                rcv_sum,
                weights,
                ids,
            )
            edge_out, edge_grad = call(
                edge_outputs_kernel,
                [edge_shape, edge_shape],
                [((lane, lane), bf16)],
                dz,
                edge_cot,
                edge,
                normed,
                vectors,
                w1_edge,
            )
            written = [node_grad, edge_out, edge_grad]
        grads, *passed = call(
            functools.partial(add_kernel, len(passed)),
            [half_shape] + [(x.shape, x.dtype) for x in passed],
            [],
            grads,
            other,
            *passed,
            *written,
            anywhere=len(written),
        )
        if number == 0:
            (rims,) = passed
        elif number == 1:
            back_near, back_far, vectors, w1_edge = passed
    others = lax.ppermute(grads, "sub", core_pairs)
    matrices = [3 * lane, lane, 2 * lane, lane]
    totals = call(
        finish_kernel,
        [((height, lane), f32) for height in matrices] + [((1, lane), f32)] * 8,
        [((2 * kept, lane), f32)],
        grads,
        others,
    )
    flat = [total.reshape(lane) for total in totals[4:]]
    return (
        node_out[None],
        edge_out[None],
        node_grad[None],
        edge_grad[None],
        totals[0],
        flat[0],
        totals[1],
        flat[1],
        flat[2],
        flat[3],
        totals[2],
        flat[4],
        totals[3],
        flat[5],
        flat[6],
        flat[7],
    )


def solution(mesh):
    node_spec = P(("groups", "sample"), ("dom", "sub"), None)
    ids_spec = P(("dom", "sub"))
    return jax.shard_map(
        on_device,
        mesh=mesh,
        in_specs=(
            (node_spec, node_spec, ids_spec, ids_spec, P(("dom", "sub"), None, None))
            + (P(),) * 12
            + (node_spec, node_spec)
        ),
        out_specs=(
            (node_spec,) * 4
            + (P("groups", None), P("groups"), P("groups", None), P("groups"), P("groups"), P("groups"))
            * 2
        ),
        check_vma=False,
    )
```

```python
import functools
import math

import jax
import jax.numpy as jnp
from jax import lax
from jax.experimental import pallas as pl
from jax.experimental.pallas import tpu as pltpu
from jax.sharding import PartitionSpec as P

epsilon = 1e-05
rows_dims = (((0,), (0,)), ((), ()))
back_dims = (((1,), (1,)), ((), ()))
f32 = jnp.float32
bf16 = jnp.bfloat16
lane = 128
edge_tile = 512
vmem_limit = 32 * 1024 * 1024
sum_rows = 16
chain = ("dom", "sub")


def each_tile(rows, tile, tile_group=6):
    count = rows // edge_tile
    group = math.gcd(count, tile_group)

    def several(i, carry):
        for k in range(group):
            tile(i * group + k)
        return carry

    lax.fori_loop(0, count // group, several, 0)


def dot(left, right):
    return jnp.dot(left, right, preferred_element_type=f32)


def dot_rows(left, right):
    return lax.dot_general(left, right, rows_dims, preferred_element_type=f32)


def dot_back(left, right):
    return lax.dot_general(left, right, back_dims, preferred_element_type=f32)


def column_of(row):
    return jnp.broadcast_to(row, (lane, lane)).T


def hot_columns(low, *spans):
    targets = lax.broadcasted_iota(jnp.int16, low.shape, 1)
    one, zero = jnp.ones((), bf16), jnp.zeros((), bf16)
    parts = [
        jnp.where(low == targets + jnp.int16(at), one, zero)
        for start, stop in spans
        for at in range(start, stop, lane)
    ]
    return jnp.concatenate(parts, axis=1)


def hot_rows(row, height):
    low = jnp.broadcast_to(row, (16, lane)).astype(jnp.int16)
    targets = lax.broadcasted_iota(jnp.int16, (height, lane), 0).reshape(height // 16, 16, lane)
    one, zero = jnp.ones((), bf16), jnp.zeros((), bf16)
    return jnp.where(targets == low[None], one, zero).reshape(height, lane)


def folded(ids, half):
    return jnp.where((ids >= half) & (ids < 2 * half), ids - half, ids)


def side_by_side(rows):
    half = rows.shape[0] // 2
    return jnp.concatenate([rows[:half], rows[half:]], axis=1)


def pick(ids, low, half, table, *halo):
    both = dot(hot_columns(low, (0, half), *halo), table)
    return jnp.where(ids >= half, both[:, lane:], both[:, :lane])


def rows_of_ids(ids_ref, first, count, height, change):
    parts = [hot_rows(change(ids_ref[pl.ds(first + k, 1), :]), height) for k in range(count)]
    return jnp.concatenate(parts, axis=1)


def spread(ids_ref, first, count, half, ids, values):
    upper = ids >= half
    paired = jnp.concatenate(
        [jnp.where(upper, 0.0, values).astype(bf16), jnp.where(upper, values, 0.0).astype(bf16)],
        axis=1,
    )
    return dot(rows_of_ids(ids_ref, first, count, half, lambda row: folded(row, half)), paired)


def sigmoid(z):
    return 0.5 * jnp.tanh(0.5 * z) + 0.5


def vector(vectors_ref, k):
    return vectors_ref[k : k + 1, :]


def centred_pair(w):
    w = w.astype(f32)
    w = w - jnp.mean(w, axis=1, keepdims=True)
    high = w.astype(bf16)
    low = (w - high.astype(f32)).astype(bf16)
    return jnp.concatenate([high, low], axis=1)


def centred(b):
    return b - jnp.mean(b, axis=1, keepdims=True)


def mean_weights():
    shape = (2 * lane, 2 * lane)
    left = lax.broadcasted_iota(jnp.int32, shape, 0) < lane
    right = lax.broadcasted_iota(jnp.int32, shape, 1) < lane
    return jnp.where(left == right, 1.0 / lane, 0.0).astype(bf16)


def normed_of(act, w_pair, b_centred, means):
    both = dot(act, w_pair)
    center = both[:, :lane] + both[:, lane:] + b_centred
    variance = dot((center * center).astype(bf16), means[:lane, :lane])
    scale_inv = lax.rsqrt(variance + epsilon)
    return center * scale_inv, scale_inv


def back_norm(upstream, normed, scale_inv, gain, means):
    d_normed = upstream * gain
    pair = jnp.concatenate([d_normed.astype(bf16), (d_normed * normed).astype(bf16)], axis=1)
    both = dot(pair, means)
    return scale_inv * (d_normed - both[:, :lane] - normed * both[:, lane:])


def column_sum(values):
    return jnp.sum(values, axis=0, keepdims=True)


def eight_sums(values):
    return jnp.sum(values.reshape(values.shape[0] // 8, 8, lane), axis=0)


def parity_of_place():
    return lax.axis_index(chain) % 2


def started(moves, sems):
    copies = [
        pltpu.make_async_copy(source, target, sems.at[k])
        for k, (source, target) in enumerate(moves)
    ]
    for copy in copies:
        copy.start()
    return copies


def first_kernel(node_hbm, list_hbm, snd_hbm, rcv_hbm, edge_hbm, *refs):
    small = refs[:12]
    node_ref, message_ref, ids_ref, edge_ref, weights_ref, vectors_ref, sems = refs[12:]
    chunks = snd_hbm.shape[0]
    moves = [
        (node_hbm, node_ref),
        (list_hbm, ids_ref.at[2 * chunks : 2 * chunks + 2]),
        (snd_hbm, ids_ref.at[:chunks]),
        (rcv_hbm, ids_ref.at[chunks : 2 * chunks]),
    ]
    at = 0
    for source in small[:4]:
        moves.append((source, weights_ref.at[at : at + source.shape[0]]))
        at += source.shape[0]
    for k, source in enumerate(small[4:]):
        moves.append((source, vectors_ref.at[k : k + 1]))
    moves.append((edge_hbm, edge_ref))
    copies = started(moves, sems)
    for copy in copies[:2]:
        copy.wait()
    parity = parity_of_place()
    node = node_ref[...]
    rim = message_ref.shape[0] // 2
    for k, side in enumerate((1 - parity, parity)):
        column = column_of(ids_ref[pl.ds(2 * chunks + side, 1), :]).astype(jnp.int16)
        hot = hot_columns(column, (0, node.shape[0]))
        message_ref[k * rim : (k + 1) * rim, :] = dot(hot, node).astype(bf16)
    for copy in copies[2:]:
        copy.wait()


def prepare_kernel(
    ids_ref,
    node_ref,
    weights_ref,
    vectors_ref,
    edge_ref,
    unused_ref,
    edge_cot_hbm,
    node_cot_hbm,
    edge_cot_ref,
    node_cot_ref,
    snd_column,
    rcv_column,
    rcv_low,
    z_ref,
    rcv_local,
    turned_ref,
    pairs_ref,
    means_ref,
    turned_weights,
    snd_low,
    snd_table,
    sems,
):
    copies = started([(edge_cot_hbm, edge_cot_ref), (node_cot_hbm, node_cot_ref)], sems)
    means_ref[...] = mean_weights()
    for k, at in enumerate((3 * lane, 6 * lane)):
        w = weights_ref[at : at + lane]
        pairs_ref[k * lane : (k + 1) * lane, :] = centred_pair(w)
    for k in range(7):
        at = slice(k * lane, (k + 1) * lane)
        turned_weights[at, :] = weights_ref[at, :].T
    chunks = snd_column.shape[0] // lane
    half = snd_table.shape[0]
    for k in range(chunks):
        at = slice(k * lane, (k + 1) * lane)
        snd = column_of(ids_ref[k : k + 1, :])
        rcv = column_of(ids_ref[chunks + k : chunks + k + 1, :])
        snd_column[at, :] = snd
        rcv_column[at, :] = rcv
        snd_low[at, :] = folded(snd, half).astype(jnp.int16)
        rcv_low[at, :] = folded(rcv, half).astype(jnp.int16)
    node = node_ref[...]
    snd_table[...] = side_by_side(node)
    rcv_local[...] = side_by_side(dot(node, weights_ref[2 * lane : 3 * lane]).astype(bf16))
    w1 = weights_ref[: 2 * lane]
    b1 = vector(vectors_ref, 0)

    def tile(i):
        rows = pl.ds(pl.multiple_of(i * edge_tile, edge_tile), edge_tile)
        x = edge_ref[rows, :]
        sent = pick(snd_column[rows, :], snd_low[rows, :], half, snd_table[...]).astype(bf16)
        z_ref[rows, :] = dot(jnp.concatenate([x, sent], axis=1), w1) + b1
        turned_ref[:, rows] = sent.T

    each_tile(edge_ref.shape[0], tile)
    for copy in copies:
        copy.wait()


def split_kernel(message_ref, near_ref, far_ref):
    rim = near_ref.shape[0]
    near_ref[...] = message_ref[:rim, :]
    far_ref[...] = message_ref[rim:, :]


def edge_forward_kernel(
    near_ref,
    far_ref,
    ids_ref,
    weights_ref,
    vectors_ref,
    rcv_column,
    rcv_low,
    z_sent,
    rcv_local,
    pairs_ref,
    means,
    z_ref,
    normed_ref,
    scale_ref,
    message_ref,
    rims_ref,
    table,
    total,
):
    half = rcv_local.shape[0]
    nodes = 2 * half
    rim = near_ref.shape[0]
    parity = parity_of_place()
    near_at = pl.multiple_of((1 - parity) * rim, rim)
    far_at = pl.multiple_of(parity * rim, rim)
    w1_rcv = weights_ref[2 * lane : 3 * lane]
    gain, shift = vector(vectors_ref, 2), vector(vectors_ref, 3)
    table[:half, :] = rcv_local[...]
    table[half:, :lane] = jnp.zeros((2 * rim, lane), bf16)
    table[pl.ds(half + near_at, rim), lane:] = dot(near_ref[...], w1_rcv).astype(bf16)
    table[pl.ds(half + far_at, rim), lane:] = dot(far_ref[...], w1_rcv).astype(bf16)
    b2 = centred(vector(vectors_ref, 1))
    total[...] = jnp.zeros_like(total)

    def tile(i):
        rows = pl.ds(pl.multiple_of(i * edge_tile, edge_tile), edge_tile)
        slots = (nodes, nodes + 2 * rim)
        z = z_sent[rows, :]
        z = z + pick(rcv_column[rows, :], rcv_low[rows, :], half, table[...], slots)
        z_ref[rows, :] = z
        act = (z * sigmoid(z)).astype(bf16)
        normed, scale_inv = normed_of(act, pairs_ref[:lane, :], b2, means[...])
        normed_ref[rows, :] = normed
        scale_ref[rows, :] = scale_inv
        message = (normed * gain + shift).astype(bf16)
        message_ref[rows, :] = message
        first = (rcv_column.shape[0] + i * edge_tile) // lane
        hot = rows_of_ids(ids_ref, first, edge_tile // lane, 2 * rim, lambda row: row - nodes)
        total[...] += dot(hot, message)

    each_tile(rcv_column.shape[0], tile, 3)
    rims_ref[:rim, :] = total[pl.ds(near_at, rim), :].astype(bf16)
    rims_ref[rim:, :] = total[pl.ds(far_at, rim), :].astype(bf16)


def collect_kernel(
    ids_ref,
    rcv_column,
    rcv_low,
    message_ref,
    node_ref,
    near_ref,
    far_ref,
    unused_ref,
    agg_ref,
    turned_ref,
    table,
    total,
):
    rim = near_ref.shape[0]
    half = total.shape[0]
    nodes = 2 * half
    parity = parity_of_place()
    near_at = pl.multiple_of((1 - parity) * rim, rim)
    far_at = pl.multiple_of(parity * rim, rim)
    table[:half, :] = side_by_side(node_ref[...])
    table[half:, :lane] = jnp.zeros((2 * rim, lane), bf16)
    table[pl.ds(half + near_at, rim), lane:] = near_ref[...]
    table[pl.ds(half + far_at, rim), lane:] = far_ref[...]
    total[...] = jnp.zeros_like(total)

    def tile(i):
        rows = pl.ds(pl.multiple_of(i * edge_tile, edge_tile), edge_tile)
        first = (rcv_column.shape[0] + i * edge_tile) // lane
        rcv = rcv_column[rows, :]
        message = message_ref[rows, :].astype(f32)
        total[...] += spread(ids_ref, first, edge_tile // lane, half, rcv, message)
        slots = (nodes, nodes + 2 * rim)
        turned_ref[:, rows] = pick(rcv, rcv_low[rows, :], half, table[...], slots).astype(bf16).T

    each_tile(rcv_column.shape[0], tile)
    agg_ref[:half, :] = total[:, :lane]
    agg_ref[half:, :] = total[:, lane:]


def hot_lists(ids_ref, nodes):
    parity = parity_of_place()
    first = ids_ref.shape[0] - 2
    near = ids_ref[pl.ds(first + 1 - parity, 1), :]
    far = ids_ref[pl.ds(first + parity, 1), :]
    return jnp.concatenate([hot_rows(near, nodes), hot_rows(far, nodes)], axis=1)


def node_kernel(
    near_ref,
    far_ref,
    node_ref,
    agg_ref,
    ids_ref,
    weights_ref,
    vectors_ref,
    cot_ref,
    pairs_ref,
    means,
    turned_weights,
    x_ref,
    act_ref,
    normed_ref,
    dz1_ref,
    dz2_ref,
    sums_ref,
    dagg_ref,
    rims_ref,
):
    nodes = node_ref.shape[0]
    returned = jnp.concatenate([near_ref[...], far_ref[...]], axis=0)
    agg = (agg_ref[...] + dot(hot_lists(ids_ref, nodes), returned)).astype(bf16)
    x = jnp.concatenate([node_ref[...], agg], axis=1)
    x_ref[...] = x
    w1 = weights_ref[4 * lane : 6 * lane]
    z = dot(x, w1) + vector(vectors_ref, 4)
    sig = sigmoid(z)
    act = (z * sig).astype(bf16)
    act_ref[...] = act
    b2 = centred(vector(vectors_ref, 5))
    normed, scale_inv = normed_of(act, pairs_ref[lane:, :], b2, means[...])
    normed_ref[...] = normed
    upstream = cot_ref[...].astype(f32)
    dz2 = back_norm(upstream, normed, scale_inv, vector(vectors_ref, 6), means[...])
    dz2b = dz2.astype(bf16)
    dz2_ref[...] = dz2b
    dz1 = dot(dz2b, turned_weights[6 * lane :]) * (sig * (1.0 + z * (1.0 - sig)))
    dz1b = dz1.astype(bf16)
    dz1_ref[...] = dz1b
    dagg = dot(dz1b, turned_weights[5 * lane : 6 * lane]).astype(bf16)
    dagg_ref[...] = dagg
    parity = parity_of_place()
    first = ids_ref.shape[0] - 2
    rim = rims_ref.shape[0] // 2
    for k, side in enumerate((1 - parity, parity)):
        column = column_of(ids_ref[pl.ds(first + side, 1), :]).astype(jnp.int16)
        picked = hot_columns(column, (0, nodes))
        rims_ref[k * rim : (k + 1) * rim, :] = dot(picked, dagg).astype(bf16)
    sums_ref[0:8, :] = eight_sums(dz1)
    sums_ref[8:16, :] = eight_sums(dz2)


def node_rest_kernel(
    x_ref,
    act_ref,
    normed_ref,
    dz1_ref,
    dz2_ref,
    sums_ref,
    turned_weights,
    vectors_ref,
    cot_ref,
    unused_ref,
    out_ref,
    base_ref,
    grads_ref,
):
    x = x_ref[...]
    normed = normed_ref[...]
    dz1b = dz1_ref[...]
    update = normed * vector(vectors_ref, 6) + vector(vectors_ref, 7)
    out_ref[...] = (x[:, :lane].astype(f32) + update).astype(bf16)
    upstream = cot_ref[...].astype(f32)
    base_ref[...] = upstream + dot(dz1b, turned_weights[4 * lane : 5 * lane])
    first = 2 * lane
    second = first + lane
    grads_ref[:first, :] = dot_rows(x, dz1b)
    grads_ref[first:second, :] = dot_rows(act_ref[...], dz2_ref[...])
    sums = [column_sum(sums_ref[0:8, :]), column_sum(sums_ref[8:16, :])]
    sums += [column_sum(eight_sums(upstream * normed)), column_sum(eight_sums(upstream))]
    sums.append(jnp.zeros((sum_rows - len(sums), lane), f32))
    grads_ref[second:, :] = jnp.concatenate(sums, axis=0)


def upstream_kernel(
    rcv_column,
    rcv_low,
    dagg_ref,
    cot_ref,
    z_ref,
    edge_ref,
    unused_ref,
    up_ref,
    slope_ref,
    turned_ref,
    table,
):
    half = table.shape[0]
    table[...] = side_by_side(dagg_ref[...])

    def tile(i):
        rows = pl.ds(pl.multiple_of(i * edge_tile, edge_tile), edge_tile)
        local = pick(rcv_column[rows, :], rcv_low[rows, :], half, table[...])
        up_ref[rows, :] = cot_ref[rows, :].astype(f32) + local
        z = z_ref[rows, :]
        sig = sigmoid(z)
        slope_ref[rows, :] = sig * (1.0 + z * (1.0 - sig))
        turned_ref[:lane, rows] = edge_ref[rows, :].T
        turned_ref[lane:, rows] = (z * sig).astype(bf16).T

    each_tile(cot_ref.shape[0], tile)


def edge_backward_kernel(
    nodes,
    dagg_near_ref,
    dagg_far_ref,
    up_ref,
    normed_ref,
    scale_ref,
    slope_ref,
    sent_turned,
    received_turned,
    turned,
    turned_weights,
    means,
    vectors_ref,
    node_grads_ref,
    rcv_low,
    dz_ref,
    kept_ref,
    sent_ref,
    grads_ref,
    table,
    sums,
):
    rim = dagg_near_ref.shape[0]
    parity = parity_of_place()
    w2_turned = turned_weights[3 * lane : 4 * lane]
    gain = vector(vectors_ref, 2)
    table[pl.ds(pl.multiple_of((1 - parity) * rim, rim), rim), :] = dagg_near_ref[...]
    table[pl.ds(pl.multiple_of(parity * rim, rim), rim), :] = dagg_far_ref[...]
    grads_ref[: 4 * lane, :] = jnp.zeros((4 * lane, lane), f32)
    sums[...] = jnp.zeros_like(sums)

    def tile(i):
        rows = pl.ds(pl.multiple_of(i * edge_tile, edge_tile), edge_tile)
        hot = hot_columns(rcv_low[rows, :], (nodes, nodes + 2 * rim))
        upstream = up_ref[rows, :] + dot(hot, table[...])
        normed = normed_ref[rows, :]
        dz2 = back_norm(upstream, normed, scale_ref[rows, :], gain, means[...])
        dz2b = dz2.astype(bf16)
        dz1 = dot(dz2b, w2_turned) * slope_ref[rows, :]
        dz1b = dz1.astype(bf16)
        dz_ref[rows, :] = dz1b
        grads_ref[:lane, :] += dot(turned[:lane, rows], dz1b)
        grads_ref[lane : 2 * lane, :] += dot(sent_turned[:, rows], dz1b)
        grads_ref[2 * lane : 3 * lane, :] += dot(received_turned[:, rows], dz1b)
        grads_ref[3 * lane : 4 * lane, :] += dot(turned[lane:, rows], dz2b)
        sums[0:8, :] += eight_sums(dz1)
        sums[8:16, :] += eight_sums(dz2)
        sums[16:24, :] += eight_sums(upstream * normed)
        sums[24:32, :] += eight_sums(upstream)

    each_tile(up_ref.shape[0], tile)
    kept = kept_ref.shape[0]
    node_rows = node_grads_ref.shape[0] - sum_rows
    last = 4 * lane + node_rows
    grads_ref[4 * lane : last, :] = node_grads_ref[:node_rows, :]
    grads_ref[last : last + sum_rows, :] = jnp.concatenate(
        [column_sum(sums[8 * k : 8 * k + 8, :]) for k in range(4)]
        + [node_grads_ref[node_rows : node_rows + 4, :], jnp.zeros((8, lane), f32)],
        axis=0,
    )
    if last + sum_rows < grads_ref.shape[0]:
        grads_ref[last + sum_rows :, :] = jnp.zeros(
            (grads_ref.shape[0] - last - sum_rows, lane), f32
        )
    own = lax.axis_index("sub")
    kept_ref[...] = grads_ref[pl.ds(pl.multiple_of(own * kept, sum_rows), kept), :]
    other = pl.multiple_of((1 - own) * kept, sum_rows)
    sent_ref[...] = grads_ref[pl.ds(other, kept), :].astype(bf16)


def scatter_kernel(
    ids_ref,
    dz_ref,
    snd_column,
    rcv_column,
    turned_weights,
    snd_sum_ref,
    rcv_sum_ref,
    rims_ref,
    snd_total,
    rcv_total,
    halo_total,
):
    half = snd_total.shape[0]
    nodes = 2 * half
    rim = rims_ref.shape[0] // 2
    parity = parity_of_place()
    for total in (snd_total, rcv_total, halo_total):
        total[...] = jnp.zeros_like(total)

    def tile(i):
        rows = pl.ds(pl.multiple_of(i * edge_tile, edge_tile), edge_tile)
        chunk = edge_tile // lane
        dz1b = dz_ref[rows, :]
        dz1 = dz1b.astype(f32)
        first = rcv_column.shape[0] // lane + i * chunk
        snd_total[...] += spread(ids_ref, i * chunk, chunk, half, snd_column[rows, :], dz1)
        rcv_total[...] += spread(ids_ref, first, chunk, half, rcv_column[rows, :], dz1)
        slots = rows_of_ids(ids_ref, first, chunk, 2 * rim, lambda row: row - nodes)
        halo_total[...] += dot(slots, dz1b)

    each_tile(dz_ref.shape[0], tile)
    for total, out_ref in ((snd_total, snd_sum_ref), (rcv_total, rcv_sum_ref)):
        out_ref[:half, :] = total[:, :lane].astype(bf16)
        out_ref[half:, :] = total[:, lane:].astype(bf16)
    w1_turned = turned_weights[2 * lane : 3 * lane]
    for k, side in enumerate((1 - parity, parity)):
        returned = halo_total[pl.ds(pl.multiple_of(side * rim, rim), rim), :].astype(bf16)
        rims_ref[k * rim : (k + 1) * rim, :] = dot(returned, w1_turned).astype(bf16)


def edge_outputs_kernel(
    dz_ref, cot_ref, edge_ref, normed_ref, vectors_ref, turned_weights, out_ref, grad_ref
):
    w1_turned = turned_weights[:lane]
    gain, shift = vector(vectors_ref, 2), vector(vectors_ref, 3)

    def tile(i):
        rows = pl.ds(pl.multiple_of(i * edge_tile, edge_tile), edge_tile)
        cot = cot_ref[rows, :].astype(f32)
        grad_ref[rows, :] = (cot + dot(dz_ref[rows, :], w1_turned)).astype(bf16)
        update = normed_ref[rows, :] * gain + shift
        out_ref[rows, :] = (edge_ref[rows, :].astype(f32) + update).astype(bf16)

    each_tile(cot_ref.shape[0], tile)


def node_grad_kernel(
    near_ref, far_ref, base_ref, snd_sum_ref, rcv_sum_ref, turned_weights, ids_ref, out_ref
):
    returned = jnp.concatenate([near_ref[...], far_ref[...]], axis=0)
    total = base_ref[...] + dot(snd_sum_ref[...], turned_weights[lane : 2 * lane])
    total = total + dot(rcv_sum_ref[...], turned_weights[2 * lane : 3 * lane])
    hot = hot_lists(ids_ref, base_ref.shape[0])
    out_ref[...] = (total + dot(hot, returned)).astype(bf16)


def add_kernel(passed, own_ref, other_ref, *refs):
    out_refs = refs[len(refs) - passed - 1 :]
    out_refs[0][...] = (own_ref[...].astype(f32) + other_ref[...].astype(f32)).astype(bf16)
    for source, target in zip(refs[:passed], out_refs[1:]):
        target[...] = source[...]


def finish_kernel(own_ref, other_ref, *refs):
    out_refs, total_ref = refs[:-1], refs[-1]
    kept = own_ref.shape[0]
    own = lax.axis_index("sub")
    total_ref[pl.ds(pl.multiple_of(own * kept, sum_rows), kept), :] = own_ref[...].astype(f32)
    other = pl.multiple_of((1 - own) * kept, sum_rows)
    total_ref[pl.ds(other, kept), :] = other_ref[...].astype(f32)
    at = 0
    for out_ref in out_refs[:4]:
        out_ref[...] = total_ref[at : at + out_ref.shape[0], :]
        at += out_ref.shape[0]
    for k, out_ref in enumerate(out_refs[4:]):
        out_ref[...] = total_ref[at + k : at + k + 1, :]


def call(kernel, outs, scratch, *operands, anywhere=0, sems=0):
    moved = sum(x.size * x.dtype.itemsize for x in operands)
    held = operands[len(operands) - anywhere :]
    operands = operands[: len(operands) - anywhere]
    operands += tuple(pltpu.with_memory_space_constraint(x, pltpu.HBM) for x in held)
    inside = [pl.BlockSpec(memory_space=pltpu.VMEM)] * (len(operands) - anywhere)
    outside = [pl.BlockSpec(memory_space=pl.ANY)] * anywhere
    scratch_shapes = [pltpu.VMEM(shape, dtype) for shape, dtype in scratch]
    if sems:
        scratch_shapes.append(pltpu.SemaphoreType.DMA((sems,)))
    return pl.pallas_call(
        kernel,
        out_shape=[jax.ShapeDtypeStruct(shape, dtype) for shape, dtype in outs],
        in_specs=inside + outside,
        out_specs=[pl.BlockSpec(memory_space=pltpu.VMEM)] * len(outs),
        scratch_shapes=scratch_shapes,
        compiler_params=pltpu.CompilerParams(vmem_limit_bytes=vmem_limit),
        cost_estimate=pl.CostEstimate(flops=0, bytes_accessed=moved, transcendentals=0),
    )(*operands)


def exchange(message):
    chips, samples = lax.axis_size("dom"), lax.axis_size("sample")
    place = lambda chip, sample, core: (chip * samples + sample) * 2 + core
    inner = [(i, i ^ 1) for i in range(2 * chips)]
    outer = []
    for sample in range(samples):
        for chip in range(chips - 1):
            ends = place(chip, sample, 1), place(chip + 1, sample, 0)
            outer += [ends, ends[::-1]]
        for chip, core in ((0, 0), (chips - 1, 1)):
            outer.append((place(chip, sample, core), place(chip, sample ^ 1, core)))
    rim_shape = ((message.shape[0] // 2, lane), bf16)
    near, far = call(split_kernel, [rim_shape, rim_shape], [], message)
    near = lax.ppermute(near, chain, inner)
    return near, lax.ppermute(far, ("dom", "sample", "sub"), outer), far


def sum_rounds():
    for axis in ("sample", "dom"):
        count = lax.axis_size(axis)
        step = count // 2
        while step > 0:
            yield axis, [(i, i ^ step) for i in range(count)]
            step //= 2


def on_device(
    node_in,
    edge_in,
    senders,
    receivers,
    send_list,
    w_edge_first,
    b_edge_first,
    w_edge_second,
    b_edge_second,
    edge_gain,
    edge_shift,
    w_node_first,
    b_node_first,
    w_node_second,
    b_node_second,
    node_gain,
    node_shift,
    node_cotangent,
    edge_cotangent,
):
    node = node_in[0]
    edge = edge_in[0]
    nodes = node.shape[0]
    edges = edge.shape[0]
    rim = send_list.shape[2]
    snd_half = nodes // 2
    kept = -(-(7 * lane + sum_rows) // (2 * sum_rows)) * sum_rows
    row = lambda x: x.reshape(1, lane)
    small = [w_edge_first, w_edge_second, w_node_first, w_node_second]
    small += [row(b_edge_first), row(b_edge_second), row(edge_gain), row(edge_shift)]
    small += [row(b_node_first), row(b_node_second), row(node_gain), row(node_shift)]
    chunks = edges // lane
    sources = [
        node,
        send_list[0],
        senders.reshape(chunks, lane),
        receivers.reshape(chunks, lane),
        edge,
    ] + small
    rims_shape = ((2 * rim, lane), bf16)
    edge_shape = ((edges, lane), bf16)
    wide_shape = ((edges, lane), f32)
    node_shape = ((nodes, lane), bf16)
    node, rims, ids, edge, weights, vectors = call(
        first_kernel,
        [
            node_shape,
            rims_shape,
            ((2 * chunks + 2, lane), jnp.int32),
            edge_shape,
            ((7 * lane, lane), bf16),
            ((8, lane), f32),
        ],
        [],
        *sources,
        anywhere=len(sources),
        sems=len(sources),
    )
    near, far, onward = exchange(rims)
    prepared = call(
        prepare_kernel,
        [
            edge_shape,
            node_shape,
            ((edges, lane), jnp.int32),
            ((edges, lane), jnp.int32),
            ((edges, lane), jnp.int16),
            wide_shape,
            ((snd_half, 2 * lane), bf16),
            ((lane, edges), bf16),
            ((2 * lane, 2 * lane), bf16),
            ((2 * lane, 2 * lane), bf16),
            ((7 * lane, lane), bf16),
        ],
        [((edges, lane), jnp.int16), ((snd_half, 2 * lane), bf16)],
        ids,
        node,
        weights,
        vectors,
        edge,
        onward,
        edge_cotangent[0],
        node_cotangent[0],
        anywhere=2,
        sems=2,
    )
    edge_cot, node_cot, snd_column, rcv_column, rcv_low = prepared[:5]
    z_sent, rcv_local, sent_turned, pairs, means, turned_weights = prepared[5:]
    z, normed, scale, message, rims = call(
        edge_forward_kernel,
        [wide_shape, wide_shape, wide_shape, edge_shape, rims_shape],
        [
            ((snd_half + 2 * rim, 2 * lane), bf16),
            ((2 * rim, lane), f32),
        ],
        near,
        far,
        ids,
        weights,
        vectors,
        rcv_column,
        rcv_low,
        z_sent,
        rcv_local,
        pairs,
        means,
    )
    back_near, back_far, onward = exchange(rims)
    agg, received_turned = call(
        collect_kernel,
        [((nodes, lane), f32), ((lane, edges), bf16)],
        [((snd_half + 2 * rim, 2 * lane), bf16), ((snd_half, 2 * lane), f32)],
        ids,
        rcv_column,
        rcv_low,
        message,
        node,
        near,
        far,
        onward,
    )
    node_x, node_act, node_normed, node_dz1, node_dz2, node_sums, dagg, rims = call(
        node_kernel,
        [
            ((nodes, 2 * lane), bf16),
            node_shape,
            ((nodes, lane), f32),
            node_shape,
            node_shape,
            ((16, lane), f32),
            node_shape,
            rims_shape,
        ],
        [],
        back_near,
        back_far,
        node,
        agg,
        ids,
        weights,
        vectors,
        node_cot,
        pairs,
        means,
        turned_weights,
    )
    dagg_near, dagg_far, onward = exchange(rims)
    upstream, slope, turned = call(
        upstream_kernel,
        [wide_shape, wide_shape, ((2 * lane, edges), bf16)],
        [((snd_half, 2 * lane), bf16)],
        rcv_column,
        rcv_low,
        dagg,
        edge_cot,
        z,
        edge,
        onward,
    )
    node_out, base, node_grads = call(
        node_rest_kernel,
        [node_shape, ((nodes, lane), f32), ((3 * lane + sum_rows, lane), f32)],
        [],
        node_x,
        node_act,
        node_normed,
        node_dz1,
        node_dz2,
        node_sums,
        turned_weights,
        vectors,
        node_cot,
        onward,
    )
    half_shape = ((kept, lane), bf16)
    dz, grads_kept, grads_sent = call(
        functools.partial(edge_backward_kernel, nodes),
        [edge_shape, ((kept, lane), f32), half_shape],
        [
            ((2 * kept, lane), f32),
            ((2 * rim, lane), bf16),
            ((32, lane), f32),
        ],
        dagg_near,
        dagg_far,
        upstream,
        normed,
        scale,
        slope,
        sent_turned,
        received_turned,
        turned,
        turned_weights,
        means,
        vectors,
        node_grads,
        rcv_low,
    )
    core_pairs = [(0, 1), (1, 0)]
    other = lax.ppermute(grads_sent, "sub", core_pairs)
    (grads,) = call(functools.partial(add_kernel, 0), [half_shape], [], grads_kept, other)
    snd_sum, rcv_sum, rims = call(
        scatter_kernel,
        [node_shape, node_shape, rims_shape],
        [
            ((snd_half, 2 * lane), f32),
            ((snd_half, 2 * lane), f32),
            ((2 * rim, lane), f32),
        ],
        ids,
        dz,
        snd_column,
        rcv_column,
        turned_weights,
    )
    node_grad = edge_out = edge_grad = None
    early_vectors = vectors
    for number, (axis, partners) in enumerate(sum_rounds()):
        other = lax.ppermute(grads, axis, partners)
        passed, written = [], []
        if number == 0:
            passed = [rims, vectors]
        elif number == 1:
            edge_out, edge_grad = call(
                edge_outputs_kernel,
                [edge_shape, edge_shape],
                [],
                dz,
                edge_cot,
                edge,
                normed,
                early_vectors,
                turned_weights,
            )
            passed, written = [rims], [edge_out, edge_grad]
        elif number == 2:
            passed = exchange(rims)[:2]
        grads, *passed = call(
            functools.partial(add_kernel, len(passed)),
            [half_shape] + [(x.shape, x.dtype) for x in passed],
            [],
            grads,
            other,
            *passed,
            *written,
            anywhere=len(written),
        )
        if number == 0:
            rims, early_vectors = passed
        elif number == 1:
            (rims,) = passed
        elif number == 2:
            back_near, back_far = passed
    others = lax.ppermute(grads, "sub", core_pairs)
    (node_grad,) = call(
        node_grad_kernel,
        [node_shape],
        [],
        back_near,
        back_far,
        base,
        snd_sum,
        rcv_sum,
        turned_weights,
        ids,
    )
    matrices = [3 * lane, lane, 2 * lane, lane]
    totals = call(
        finish_kernel,
        [((height, lane), f32) for height in matrices] + [((1, lane), f32)] * 8,
        [((2 * kept, lane), f32)],
        grads,
        others,
    )
    flat = [total.reshape(lane) for total in totals[4:]]
    return (
        node_out[None],
        edge_out[None],
        node_grad[None],
        edge_grad[None],
        totals[0],
        flat[0],
        totals[1],
        flat[1],
        flat[2],
        flat[3],
        totals[2],
        flat[4],
        totals[3],
        flat[5],
        flat[6],
        flat[7],
    )


def solution(mesh):
    node_spec = P(("groups", "sample"), ("dom", "sub"), None)
    ids_spec = P(("dom", "sub"))
    return jax.shard_map(
        on_device,
        mesh=mesh,
        in_specs=(
            (node_spec, node_spec, ids_spec, ids_spec, P(("dom", "sub"), None, None))
            + (P(),) * 12
            + (node_spec, node_spec)
        ),
        out_specs=(
            (node_spec,) * 4
            + (P("groups", None), P("groups"), P("groups", None), P("groups"), P("groups"), P("groups"))
            * 2
        ),
        check_vma=False,
    )
```

```python
import functools
import math

import jax
import jax.numpy as jnp
from jax import lax
from jax.experimental import pallas as pl
from jax.experimental.pallas import tpu as pltpu
from jax.sharding import PartitionSpec as P

epsilon = 1e-05
rows_dims = (((0,), (0,)), ((), ()))
back_dims = (((1,), (1,)), ((), ()))
f32 = jnp.float32
bf16 = jnp.bfloat16
lane = 128
edge_tile = 512
vmem_limit = 32 * 1024 * 1024
sum_rows = 16
chain = ("dom", "sub")


def each_tile(rows, tile, tile_group=6):
    count = rows // edge_tile
    group = math.gcd(count, tile_group)

    def several(i, carry):
        for k in range(group):
            tile(i * group + k)
        return carry

    lax.fori_loop(0, count // group, several, 0)


def dot(left, right):
    return jnp.dot(left, right, preferred_element_type=f32)


def dot_rows(left, right):
    return lax.dot_general(left, right, rows_dims, preferred_element_type=f32)


def dot_back(left, right):
    return lax.dot_general(left, right, back_dims, preferred_element_type=f32)


def column_of(row):
    return jnp.broadcast_to(row, (lane, lane)).T


def hot_columns(low, *spans):
    targets = lax.broadcasted_iota(jnp.int16, low.shape, 1)
    one, zero = jnp.ones((), bf16), jnp.zeros((), bf16)
    parts = [
        jnp.where(low == targets + jnp.int16(at), one, zero)
        for start, stop in spans
        for at in range(start, stop, lane)
    ]
    return jnp.concatenate(parts, axis=1)


def hot_rows(row, height):
    low = jnp.broadcast_to(row, (16, lane)).astype(jnp.int16)
    targets = lax.broadcasted_iota(jnp.int16, (height, lane), 0).reshape(height // 16, 16, lane)
    one, zero = jnp.ones((), bf16), jnp.zeros((), bf16)
    return jnp.where(targets == low[None], one, zero).reshape(height, lane)


def folded(ids, half):
    return jnp.where((ids >= half) & (ids < 2 * half), ids - half, ids)


def side_by_side(rows):
    half = rows.shape[0] // 2
    return jnp.concatenate([rows[:half], rows[half:]], axis=1)


def pick(ids, low, half, table, *halo):
    both = dot(hot_columns(low, (0, half), *halo), table)
    return jnp.where(ids >= half, both[:, lane:], both[:, :lane])


def rows_of_ids(ids_ref, first, count, height, change):
    parts = [hot_rows(change(ids_ref[pl.ds(first + k, 1), :]), height) for k in range(count)]
    return jnp.concatenate(parts, axis=1)


def spread(ids_ref, first, count, half, ids, values):
    upper = ids >= half
    paired = jnp.concatenate(
        [jnp.where(upper, 0.0, values).astype(bf16), jnp.where(upper, values, 0.0).astype(bf16)],
        axis=1,
    )
    return dot(rows_of_ids(ids_ref, first, count, half, lambda row: folded(row, half)), paired)


def sigmoid(z):
    return 0.5 * jnp.tanh(0.5 * z) + 0.5


def vector(vectors_ref, k):
    return vectors_ref[k : k + 1, :]


def centred_pair(w):
    w = w.astype(f32)
    w = w - jnp.mean(w, axis=1, keepdims=True)
    high = w.astype(bf16)
    low = (w - high.astype(f32)).astype(bf16)
    return jnp.concatenate([high, low], axis=1)


def centred(b):
    return b - jnp.mean(b, axis=1, keepdims=True)


def mean_weights():
    shape = (2 * lane, 2 * lane)
    left = lax.broadcasted_iota(jnp.int32, shape, 0) < lane
    right = lax.broadcasted_iota(jnp.int32, shape, 1) < lane
    return jnp.where(left == right, 1.0 / lane, 0.0).astype(bf16)


def normed_of(act, w_pair, b_centred, means):
    both = dot(act, w_pair)
    center = both[:, :lane] + both[:, lane:] + b_centred
    variance = dot((center * center).astype(bf16), means[:lane, :lane])
    scale_inv = lax.rsqrt(variance + epsilon)
    return center * scale_inv, scale_inv


def back_norm(upstream, normed, scale_inv, gain, means):
    d_normed = upstream * gain
    pair = jnp.concatenate([d_normed.astype(bf16), (d_normed * normed).astype(bf16)], axis=1)
    both = dot(pair, means)
    return scale_inv * (d_normed - both[:, :lane] - normed * both[:, lane:])


def column_sum(values):
    return jnp.sum(values, axis=0, keepdims=True)


def eight_sums(values):
    return jnp.sum(values.reshape(values.shape[0] // 8, 8, lane), axis=0)


def parity_of_place():
    return lax.axis_index(chain) % 2


def started(moves, sems):
    copies = [
        pltpu.make_async_copy(source, target, sems.at[k])
        for k, (source, target) in enumerate(moves)
    ]
    for copy in copies:
        copy.start()
    return copies


def first_kernel(node_hbm, list_hbm, snd_hbm, rcv_hbm, edge_hbm, *refs):
    small = refs[:12]
    node_ref, message_ref, ids_ref, edge_ref, weights_ref, vectors_ref, sems = refs[12:]
    chunks = snd_hbm.shape[0]
    moves = [
        (node_hbm, node_ref),
        (list_hbm, ids_ref.at[2 * chunks : 2 * chunks + 2]),
        (snd_hbm, ids_ref.at[:chunks]),
        (rcv_hbm, ids_ref.at[chunks : 2 * chunks]),
    ]
    at = 0
    for source in small[:4]:
        moves.append((source, weights_ref.at[at : at + source.shape[0]]))
        at += source.shape[0]
    for k, source in enumerate(small[4:]):
        moves.append((source, vectors_ref.at[k : k + 1]))
    moves.append((edge_hbm, edge_ref))
    copies = started(moves, sems)
    for copy in copies[:2]:
        copy.wait()
    parity = parity_of_place()
    node = node_ref[...]
    rim = message_ref.shape[0] // 2
    for k, side in enumerate((1 - parity, parity)):
        column = column_of(ids_ref[pl.ds(2 * chunks + side, 1), :]).astype(jnp.int16)
        hot = hot_columns(column, (0, node.shape[0]))
        message_ref[k * rim : (k + 1) * rim, :] = dot(hot, node).astype(bf16)
    for copy in copies[2:]:
        copy.wait()


def prepare_kernel(
    ids_ref,
    node_ref,
    weights_ref,
    vectors_ref,
    edge_ref,
    unused_ref,
    edge_cot_hbm,
    node_cot_hbm,
    edge_cot_ref,
    node_cot_ref,
    snd_column,
    rcv_column,
    rcv_low,
    z_ref,
    rcv_local,
    turned_ref,
    pairs_ref,
    means_ref,
    turned_weights,
    snd_low,
    snd_table,
    sems,
):
    copies = started([(edge_cot_hbm, edge_cot_ref), (node_cot_hbm, node_cot_ref)], sems)
    means_ref[...] = mean_weights()
    for k, at in enumerate((3 * lane, 6 * lane)):
        w = weights_ref[at : at + lane]
        pairs_ref[k * lane : (k + 1) * lane, :] = centred_pair(w)
    for k in range(7):
        at = slice(k * lane, (k + 1) * lane)
        turned_weights[at, :] = weights_ref[at, :].T
    chunks = snd_column.shape[0] // lane
    half = snd_table.shape[0]
    for k in range(chunks):
        at = slice(k * lane, (k + 1) * lane)
        snd = column_of(ids_ref[k : k + 1, :])
        rcv = column_of(ids_ref[chunks + k : chunks + k + 1, :])
        snd_column[at, :] = snd
        rcv_column[at, :] = rcv
        snd_low[at, :] = folded(snd, half).astype(jnp.int16)
        rcv_low[at, :] = folded(rcv, half).astype(jnp.int16)
    node = node_ref[...]
    snd_table[...] = side_by_side(node)
    rcv_local[...] = side_by_side(dot(node, weights_ref[2 * lane : 3 * lane]).astype(bf16))
    w1 = weights_ref[: 2 * lane]
    b1 = vector(vectors_ref, 0)

    def tile(i):
        rows = pl.ds(pl.multiple_of(i * edge_tile, edge_tile), edge_tile)
        x = edge_ref[rows, :]
        sent = pick(snd_column[rows, :], snd_low[rows, :], half, snd_table[...]).astype(bf16)
        z_ref[rows, :] = dot(jnp.concatenate([x, sent], axis=1), w1) + b1
        turned_ref[:, rows] = sent.T

    each_tile(edge_ref.shape[0], tile)
    for copy in copies:
        copy.wait()


def split_kernel(message_ref, near_ref, far_ref):
    rim = near_ref.shape[0]
    near_ref[...] = message_ref[:rim, :]
    far_ref[...] = message_ref[rim:, :]


def edge_forward_kernel(
    near_ref,
    far_ref,
    ids_ref,
    weights_ref,
    vectors_ref,
    rcv_column,
    rcv_low,
    z_sent,
    rcv_local,
    pairs_ref,
    means,
    z_ref,
    normed_ref,
    scale_ref,
    message_ref,
    rims_ref,
    table,
    total,
):
    half = rcv_local.shape[0]
    nodes = 2 * half
    rim = near_ref.shape[0]
    parity = parity_of_place()
    near_at = pl.multiple_of((1 - parity) * rim, rim)
    far_at = pl.multiple_of(parity * rim, rim)
    w1_rcv = weights_ref[2 * lane : 3 * lane]
    gain, shift = vector(vectors_ref, 2), vector(vectors_ref, 3)
    table[:half, :] = rcv_local[...]
    table[half:, :lane] = jnp.zeros((2 * rim, lane), bf16)
    table[pl.ds(half + near_at, rim), lane:] = dot(near_ref[...], w1_rcv).astype(bf16)
    table[pl.ds(half + far_at, rim), lane:] = dot(far_ref[...], w1_rcv).astype(bf16)
    b2 = centred(vector(vectors_ref, 1))
    total[...] = jnp.zeros_like(total)

    def tile(i):
        rows = pl.ds(pl.multiple_of(i * edge_tile, edge_tile), edge_tile)
        slots = (nodes, nodes + 2 * rim)
        z = z_sent[rows, :]
        z = z + pick(rcv_column[rows, :], rcv_low[rows, :], half, table[...], slots)
        z_ref[rows, :] = z

    def rest(i):
        rows = pl.ds(pl.multiple_of(i * edge_tile, edge_tile), edge_tile)
        z = z_ref[rows, :]
        act = (z * sigmoid(z)).astype(bf16)
        normed, scale_inv = normed_of(act, pairs_ref[:lane, :], b2, means[...])
        normed_ref[rows, :] = normed
        scale_ref[rows, :] = scale_inv
        message = (normed * gain + shift).astype(bf16)
        message_ref[rows, :] = message
        first = (rcv_column.shape[0] + i * edge_tile) // lane
        hot = rows_of_ids(ids_ref, first, edge_tile // lane, 2 * rim, lambda row: row - nodes)
        total[...] += dot(hot, message)

    each_tile(rcv_column.shape[0], tile)
    each_tile(rcv_column.shape[0], rest)
    rims_ref[:rim, :] = total[pl.ds(near_at, rim), :].astype(bf16)
    rims_ref[rim:, :] = total[pl.ds(far_at, rim), :].astype(bf16)


def collect_kernel(
    ids_ref,
    rcv_column,
    rcv_low,
    message_ref,
    node_ref,
    near_ref,
    far_ref,
    unused_ref,
    agg_ref,
    turned_ref,
    table,
    total,
):
    rim = near_ref.shape[0]
    half = total.shape[0]
    nodes = 2 * half
    parity = parity_of_place()
    near_at = pl.multiple_of((1 - parity) * rim, rim)
    far_at = pl.multiple_of(parity * rim, rim)
    table[:half, :] = side_by_side(node_ref[...])
    table[half:, :lane] = jnp.zeros((2 * rim, lane), bf16)
    table[pl.ds(half + near_at, rim), lane:] = near_ref[...]
    table[pl.ds(half + far_at, rim), lane:] = far_ref[...]
    total[...] = jnp.zeros_like(total)

    def tile(i):
        rows = pl.ds(pl.multiple_of(i * edge_tile, edge_tile), edge_tile)
        first = (rcv_column.shape[0] + i * edge_tile) // lane
        rcv = rcv_column[rows, :]
        message = message_ref[rows, :].astype(f32)
        total[...] += spread(ids_ref, first, edge_tile // lane, half, rcv, message)
        slots = (nodes, nodes + 2 * rim)
        turned_ref[:, rows] = pick(rcv, rcv_low[rows, :], half, table[...], slots).astype(bf16).T

    each_tile(rcv_column.shape[0], tile)
    agg_ref[:half, :] = total[:, :lane]
    agg_ref[half:, :] = total[:, lane:]


def hot_lists(ids_ref, nodes):
    parity = parity_of_place()
    first = ids_ref.shape[0] - 2
    near = ids_ref[pl.ds(first + 1 - parity, 1), :]
    far = ids_ref[pl.ds(first + parity, 1), :]
    return jnp.concatenate([hot_rows(near, nodes), hot_rows(far, nodes)], axis=1)


def node_kernel(
    near_ref,
    far_ref,
    node_ref,
    agg_ref,
    ids_ref,
    weights_ref,
    vectors_ref,
    cot_ref,
    pairs_ref,
    means,
    turned_weights,
    x_ref,
    act_ref,
    normed_ref,
    dz1_ref,
    dz2_ref,
    sums_ref,
    dagg_ref,
    rims_ref,
):
    nodes = node_ref.shape[0]
    returned = jnp.concatenate([near_ref[...], far_ref[...]], axis=0)
    agg = (agg_ref[...] + dot(hot_lists(ids_ref, nodes), returned)).astype(bf16)
    x = jnp.concatenate([node_ref[...], agg], axis=1)
    x_ref[...] = x
    w1 = weights_ref[4 * lane : 6 * lane]
    z = dot(x, w1) + vector(vectors_ref, 4)
    sig = sigmoid(z)
    act = (z * sig).astype(bf16)
    act_ref[...] = act
    b2 = centred(vector(vectors_ref, 5))
    normed, scale_inv = normed_of(act, pairs_ref[lane:, :], b2, means[...])
    normed_ref[...] = normed
    upstream = cot_ref[...].astype(f32)
    dz2 = back_norm(upstream, normed, scale_inv, vector(vectors_ref, 6), means[...])
    dz2b = dz2.astype(bf16)
    dz2_ref[...] = dz2b
    dz1 = dot(dz2b, turned_weights[6 * lane :]) * (sig * (1.0 + z * (1.0 - sig)))
    dz1b = dz1.astype(bf16)
    dz1_ref[...] = dz1b
    dagg = dot(dz1b, turned_weights[5 * lane : 6 * lane]).astype(bf16)
    dagg_ref[...] = dagg
    parity = parity_of_place()
    first = ids_ref.shape[0] - 2
    rim = rims_ref.shape[0] // 2
    for k, side in enumerate((1 - parity, parity)):
        column = column_of(ids_ref[pl.ds(first + side, 1), :]).astype(jnp.int16)
        picked = hot_columns(column, (0, nodes))
        rims_ref[k * rim : (k + 1) * rim, :] = dot(picked, dagg).astype(bf16)
    sums_ref[0:8, :] = eight_sums(dz1)
    sums_ref[8:16, :] = eight_sums(dz2)


def node_rest_kernel(
    x_ref,
    act_ref,
    normed_ref,
    dz1_ref,
    dz2_ref,
    sums_ref,
    turned_weights,
    vectors_ref,
    cot_ref,
    unused_ref,
    out_ref,
    base_ref,
    grads_ref,
):
    x = x_ref[...]
    normed = normed_ref[...]
    dz1b = dz1_ref[...]
    update = normed * vector(vectors_ref, 6) + vector(vectors_ref, 7)
    out_ref[...] = (x[:, :lane].astype(f32) + update).astype(bf16)
    upstream = cot_ref[...].astype(f32)
    base_ref[...] = upstream + dot(dz1b, turned_weights[4 * lane : 5 * lane])
    first = 2 * lane
    second = first + lane
    grads_ref[:first, :] = dot_rows(x, dz1b)
    grads_ref[first:second, :] = dot_rows(act_ref[...], dz2_ref[...])
    sums = [column_sum(sums_ref[0:8, :]), column_sum(sums_ref[8:16, :])]
    sums += [column_sum(eight_sums(upstream * normed)), column_sum(eight_sums(upstream))]
    sums.append(jnp.zeros((sum_rows - len(sums), lane), f32))
    grads_ref[second:, :] = jnp.concatenate(sums, axis=0)


def upstream_kernel(
    rcv_column,
    rcv_low,
    dagg_ref,
    cot_ref,
    z_ref,
    edge_ref,
    unused_ref,
    up_ref,
    slope_ref,
    turned_ref,
    table,
):
    half = table.shape[0]
    table[...] = side_by_side(dagg_ref[...])

    def tile(i):
        rows = pl.ds(pl.multiple_of(i * edge_tile, edge_tile), edge_tile)
        local = pick(rcv_column[rows, :], rcv_low[rows, :], half, table[...])
        up_ref[rows, :] = cot_ref[rows, :].astype(f32) + local
        z = z_ref[rows, :]
        sig = sigmoid(z)
        slope_ref[rows, :] = sig * (1.0 + z * (1.0 - sig))
        turned_ref[:lane, rows] = edge_ref[rows, :].T
        turned_ref[lane:, rows] = (z * sig).astype(bf16).T

    each_tile(cot_ref.shape[0], tile)


def edge_backward_kernel(
    nodes,
    dagg_near_ref,
    dagg_far_ref,
    up_ref,
    normed_ref,
    scale_ref,
    slope_ref,
    sent_turned,
    received_turned,
    turned,
    turned_weights,
    means,
    vectors_ref,
    node_grads_ref,
    rcv_low,
    dz_ref,
    kept_ref,
    sent_ref,
    grads_ref,
    table,
    sums,
):
    rim = dagg_near_ref.shape[0]
    parity = parity_of_place()
    w2_turned = turned_weights[3 * lane : 4 * lane]
    gain = vector(vectors_ref, 2)
    table[pl.ds(pl.multiple_of((1 - parity) * rim, rim), rim), :] = dagg_near_ref[...]
    table[pl.ds(pl.multiple_of(parity * rim, rim), rim), :] = dagg_far_ref[...]
    grads_ref[: 4 * lane, :] = jnp.zeros((4 * lane, lane), f32)
    sums[...] = jnp.zeros_like(sums)

    def tile(i):
        rows = pl.ds(pl.multiple_of(i * edge_tile, edge_tile), edge_tile)
        hot = hot_columns(rcv_low[rows, :], (nodes, nodes + 2 * rim))
        upstream = up_ref[rows, :] + dot(hot, table[...])
        normed = normed_ref[rows, :]
        dz2 = back_norm(upstream, normed, scale_ref[rows, :], gain, means[...])
        dz2b = dz2.astype(bf16)
        dz1 = dot(dz2b, w2_turned) * slope_ref[rows, :]
        dz1b = dz1.astype(bf16)
        dz_ref[rows, :] = dz1b
        grads_ref[:lane, :] += dot(turned[:lane, rows], dz1b)
        grads_ref[lane : 2 * lane, :] += dot(sent_turned[:, rows], dz1b)
        grads_ref[2 * lane : 3 * lane, :] += dot(received_turned[:, rows], dz1b)
        grads_ref[3 * lane : 4 * lane, :] += dot(turned[lane:, rows], dz2b)
        sums[0:8, :] += eight_sums(dz1)
        sums[8:16, :] += eight_sums(dz2)
        sums[16:24, :] += eight_sums(upstream * normed)
        sums[24:32, :] += eight_sums(upstream)

    each_tile(up_ref.shape[0], tile)
    kept = kept_ref.shape[0]
    node_rows = node_grads_ref.shape[0] - sum_rows
    last = 4 * lane + node_rows
    grads_ref[4 * lane : last, :] = node_grads_ref[:node_rows, :]
    grads_ref[last : last + sum_rows, :] = jnp.concatenate(
        [column_sum(sums[8 * k : 8 * k + 8, :]) for k in range(4)]
        + [node_grads_ref[node_rows : node_rows + 4, :], jnp.zeros((8, lane), f32)],
        axis=0,
    )
    if last + sum_rows < grads_ref.shape[0]:
        grads_ref[last + sum_rows :, :] = jnp.zeros(
            (grads_ref.shape[0] - last - sum_rows, lane), f32
        )
    own = lax.axis_index("sub")
    kept_ref[...] = grads_ref[pl.ds(pl.multiple_of(own * kept, sum_rows), kept), :]
    other = pl.multiple_of((1 - own) * kept, sum_rows)
    sent_ref[...] = grads_ref[pl.ds(other, kept), :].astype(bf16)


def halo_kernel(nodes, ids_ref, dz_ref, turned_weights, rims_ref, total):
    rim = rims_ref.shape[0] // 2
    edges = dz_ref.shape[0]
    parity = parity_of_place()
    total[...] = jnp.zeros_like(total)

    def tile(i):
        rows = pl.ds(pl.multiple_of(i * edge_tile, edge_tile), edge_tile)
        first = (edges + i * edge_tile) // lane
        slots = rows_of_ids(ids_ref, first, edge_tile // lane, 2 * rim, lambda row: row - nodes)
        total[...] += dot(slots, dz_ref[rows, :])

    each_tile(edges, tile)
    w1_turned = turned_weights[2 * lane : 3 * lane]
    for k, side in enumerate((1 - parity, parity)):
        returned = total[pl.ds(pl.multiple_of(side * rim, rim), rim), :].astype(bf16)
        rims_ref[k * rim : (k + 1) * rim, :] = dot(returned, w1_turned).astype(bf16)


def scatter_kernel(
    ids_ref,
    dz_ref,
    snd_column,
    rcv_column,
    unused_ref,
    snd_sum_ref,
    rcv_sum_ref,
    snd_total,
    rcv_total,
):
    half = snd_total.shape[0]
    for total in (snd_total, rcv_total):
        total[...] = jnp.zeros_like(total)

    def tile(i):
        rows = pl.ds(pl.multiple_of(i * edge_tile, edge_tile), edge_tile)
        chunk = edge_tile // lane
        dz1 = dz_ref[rows, :].astype(f32)
        first = rcv_column.shape[0] // lane + i * chunk
        snd_total[...] += spread(ids_ref, i * chunk, chunk, half, snd_column[rows, :], dz1)
        rcv_total[...] += spread(ids_ref, first, chunk, half, rcv_column[rows, :], dz1)

    each_tile(dz_ref.shape[0], tile)
    for total, out_ref in ((snd_total, snd_sum_ref), (rcv_total, rcv_sum_ref)):
        out_ref[:half, :] = total[:, :lane].astype(bf16)
        out_ref[half:, :] = total[:, lane:].astype(bf16)


def edge_outputs_kernel(
    dz_ref, cot_ref, edge_ref, normed_ref, vectors_ref, turned_weights, out_ref, grad_ref
):
    w1_turned = turned_weights[:lane]
    gain, shift = vector(vectors_ref, 2), vector(vectors_ref, 3)

    def tile(i):
        rows = pl.ds(pl.multiple_of(i * edge_tile, edge_tile), edge_tile)
        cot = cot_ref[rows, :].astype(f32)
        grad_ref[rows, :] = (cot + dot(dz_ref[rows, :], w1_turned)).astype(bf16)
        update = normed_ref[rows, :] * gain + shift
        out_ref[rows, :] = (edge_ref[rows, :].astype(f32) + update).astype(bf16)

    each_tile(cot_ref.shape[0], tile)


def node_grad_kernel(
    near_ref, far_ref, base_ref, snd_sum_ref, rcv_sum_ref, turned_weights, ids_ref, out_ref
):
    returned = jnp.concatenate([near_ref[...], far_ref[...]], axis=0)
    total = base_ref[...] + dot(snd_sum_ref[...], turned_weights[lane : 2 * lane])
    total = total + dot(rcv_sum_ref[...], turned_weights[2 * lane : 3 * lane])
    hot = hot_lists(ids_ref, base_ref.shape[0])
    out_ref[...] = (total + dot(hot, returned)).astype(bf16)


def add_kernel(passed, own_ref, other_ref, *refs):
    out_refs = refs[len(refs) - passed - 1 :]
    out_refs[0][...] = (own_ref[...].astype(f32) + other_ref[...].astype(f32)).astype(bf16)
    for source, target in zip(refs[:passed], out_refs[1:]):
        target[...] = source[...]


def finish_kernel(own_ref, other_ref, *refs):
    out_refs, total_ref = refs[:-1], refs[-1]
    kept = own_ref.shape[0]
    own = lax.axis_index("sub")
    total_ref[pl.ds(pl.multiple_of(own * kept, sum_rows), kept), :] = own_ref[...].astype(f32)
    other = pl.multiple_of((1 - own) * kept, sum_rows)
    total_ref[pl.ds(other, kept), :] = other_ref[...].astype(f32)
    at = 0
    for out_ref in out_refs[:4]:
        out_ref[...] = total_ref[at : at + out_ref.shape[0], :]
        at += out_ref.shape[0]
    for k, out_ref in enumerate(out_refs[4:]):
        out_ref[...] = total_ref[at + k : at + k + 1, :]


def call(kernel, outs, scratch, *operands, anywhere=0, sems=0):
    moved = sum(x.size * x.dtype.itemsize for x in operands)
    held = operands[len(operands) - anywhere :]
    operands = operands[: len(operands) - anywhere]
    operands += tuple(pltpu.with_memory_space_constraint(x, pltpu.HBM) for x in held)
    inside = [pl.BlockSpec(memory_space=pltpu.VMEM)] * (len(operands) - anywhere)
    outside = [pl.BlockSpec(memory_space=pl.ANY)] * anywhere
    scratch_shapes = [pltpu.VMEM(shape, dtype) for shape, dtype in scratch]
    if sems:
        scratch_shapes.append(pltpu.SemaphoreType.DMA((sems,)))
    return pl.pallas_call(
        kernel,
        out_shape=[jax.ShapeDtypeStruct(shape, dtype) for shape, dtype in outs],
        in_specs=inside + outside,
        out_specs=[pl.BlockSpec(memory_space=pltpu.VMEM)] * len(outs),
        scratch_shapes=scratch_shapes,
        compiler_params=pltpu.CompilerParams(vmem_limit_bytes=vmem_limit),
        cost_estimate=pl.CostEstimate(flops=0, bytes_accessed=moved, transcendentals=0),
    )(*operands)


def exchange(message):
    chips, samples = lax.axis_size("dom"), lax.axis_size("sample")
    place = lambda chip, sample, core: (chip * samples + sample) * 2 + core
    inner = [(i, i ^ 1) for i in range(2 * chips)]
    outer = []
    for sample in range(samples):
        for chip in range(chips - 1):
            ends = place(chip, sample, 1), place(chip + 1, sample, 0)
            outer += [ends, ends[::-1]]
        for chip, core in ((0, 0), (chips - 1, 1)):
            outer.append((place(chip, sample, core), place(chip, sample ^ 1, core)))
    rim_shape = ((message.shape[0] // 2, lane), bf16)
    near, far = call(split_kernel, [rim_shape, rim_shape], [], message)
    near = lax.ppermute(near, chain, inner)
    return near, lax.ppermute(far, ("dom", "sample", "sub"), outer), far


def sum_rounds():
    for axis in ("sample", "dom"):
        count = lax.axis_size(axis)
        step = count // 2
        while step > 0:
            yield axis, [(i, i ^ step) for i in range(count)]
            step //= 2


def on_device(
    node_in,
    edge_in,
    senders,
    receivers,
    send_list,
    w_edge_first,
    b_edge_first,
    w_edge_second,
    b_edge_second,
    edge_gain,
    edge_shift,
    w_node_first,
    b_node_first,
    w_node_second,
    b_node_second,
    node_gain,
    node_shift,
    node_cotangent,
    edge_cotangent,
):
    node = node_in[0]
    edge = edge_in[0]
    nodes = node.shape[0]
    edges = edge.shape[0]
    rim = send_list.shape[2]
    snd_half = nodes // 2
    kept = -(-(7 * lane + sum_rows) // (2 * sum_rows)) * sum_rows
    row = lambda x: x.reshape(1, lane)
    small = [w_edge_first, w_edge_second, w_node_first, w_node_second]
    small += [row(b_edge_first), row(b_edge_second), row(edge_gain), row(edge_shift)]
    small += [row(b_node_first), row(b_node_second), row(node_gain), row(node_shift)]
    chunks = edges // lane
    sources = [
        node,
        send_list[0],
        senders.reshape(chunks, lane),
        receivers.reshape(chunks, lane),
        edge,
    ] + small
    rims_shape = ((2 * rim, lane), bf16)
    edge_shape = ((edges, lane), bf16)
    wide_shape = ((edges, lane), f32)
    node_shape = ((nodes, lane), bf16)
    node, rims, ids, edge, weights, vectors = call(
        first_kernel,
        [
            node_shape,
            rims_shape,
            ((2 * chunks + 2, lane), jnp.int32),
            edge_shape,
            ((7 * lane, lane), bf16),
            ((8, lane), f32),
        ],
        [],
        *sources,
        anywhere=len(sources),
        sems=len(sources),
    )
    near, far, onward = exchange(rims)
    prepared = call(
        prepare_kernel,
        [
            edge_shape,
            node_shape,
            ((edges, lane), jnp.int32),
            ((edges, lane), jnp.int32),
            ((edges, lane), jnp.int16),
            wide_shape,
            ((snd_half, 2 * lane), bf16),
            ((lane, edges), bf16),
            ((2 * lane, 2 * lane), bf16),
            ((2 * lane, 2 * lane), bf16),
            ((7 * lane, lane), bf16),
        ],
        [((edges, lane), jnp.int16), ((snd_half, 2 * lane), bf16)],
        ids,
        node,
        weights,
        vectors,
        edge,
        onward,
        edge_cotangent[0],
        node_cotangent[0],
        anywhere=2,
        sems=2,
    )
    edge_cot, node_cot, snd_column, rcv_column, rcv_low = prepared[:5]
    z_sent, rcv_local, sent_turned, pairs, means, turned_weights = prepared[5:]
    z, normed, scale, message, rims = call(
        edge_forward_kernel,
        [wide_shape, wide_shape, wide_shape, edge_shape, rims_shape],
        [
            ((snd_half + 2 * rim, 2 * lane), bf16),
            ((2 * rim, lane), f32),
        ],
        near,
        far,
        ids,
        weights,
        vectors,
        rcv_column,
        rcv_low,
        z_sent,
        rcv_local,
        pairs,
        means,
    )
    back_near, back_far, onward = exchange(rims)
    agg, received_turned = call(
        collect_kernel,
        [((nodes, lane), f32), ((lane, edges), bf16)],
        [((snd_half + 2 * rim, 2 * lane), bf16), ((snd_half, 2 * lane), f32)],
        ids,
        rcv_column,
        rcv_low,
        message,
        node,
        near,
        far,
        onward,
    )
    node_x, node_act, node_normed, node_dz1, node_dz2, node_sums, dagg, rims = call(
        node_kernel,
        [
            ((nodes, 2 * lane), bf16),
            node_shape,
            ((nodes, lane), f32),
            node_shape,
            node_shape,
            ((16, lane), f32),
            node_shape,
            rims_shape,
        ],
        [],
        back_near,
        back_far,
        node,
        agg,
        ids,
        weights,
        vectors,
        node_cot,
        pairs,
        means,
        turned_weights,
    )
    dagg_near, dagg_far, onward = exchange(rims)
    upstream, slope, turned = call(
        upstream_kernel,
        [wide_shape, wide_shape, ((2 * lane, edges), bf16)],
        [((snd_half, 2 * lane), bf16)],
        rcv_column,
        rcv_low,
        dagg,
        edge_cot,
        z,
        edge,
        onward,
    )
    node_out, base, node_grads = call(
        node_rest_kernel,
        [node_shape, ((nodes, lane), f32), ((3 * lane + sum_rows, lane), f32)],
        [],
        node_x,
        node_act,
        node_normed,
        node_dz1,
        node_dz2,
        node_sums,
        turned_weights,
        vectors,
        node_cot,
        onward,
    )
    half_shape = ((kept, lane), bf16)
    dz, grads_kept, grads_sent = call(
        functools.partial(edge_backward_kernel, nodes),
        [edge_shape, ((kept, lane), f32), half_shape],
        [
            ((2 * kept, lane), f32),
            ((2 * rim, lane), bf16),
            ((32, lane), f32),
        ],
        dagg_near,
        dagg_far,
        upstream,
        normed,
        scale,
        slope,
        sent_turned,
        received_turned,
        turned,
        turned_weights,
        means,
        vectors,
        node_grads,
        rcv_low,
    )
    core_pairs = [(0, 1), (1, 0)]
    other = lax.ppermute(grads_sent, "sub", core_pairs)
    (grads,) = call(functools.partial(add_kernel, 0), [half_shape], [], grads_kept, other)
    (rims,) = call(
        functools.partial(halo_kernel, nodes),
        [rims_shape],
        [((2 * rim, lane), f32)],
        ids,
        dz,
        turned_weights,
    )
    back_near, back_far, onward = exchange(rims)
    snd_sum, rcv_sum = call(
        scatter_kernel,
        [node_shape, node_shape],
        [((snd_half, 2 * lane), f32), ((snd_half, 2 * lane), f32)],
        ids,
        dz,
        snd_column,
        rcv_column,
        onward,
    )
    node_grad = edge_out = edge_grad = None
    early_vectors, early_ids = vectors, ids
    for number, (axis, partners) in enumerate(sum_rounds()):
        other = lax.ppermute(grads, axis, partners)
        passed, before, written = [], [], []
        if number == 0:
            passed, before = [vectors], [back_near, back_far, snd_sum, rcv_sum]
        elif number == 1:
            edge_out, edge_grad = call(
                edge_outputs_kernel,
                [edge_shape, edge_shape],
                [],
                dz,
                edge_cot,
                edge,
                normed,
                early_vectors,
                turned_weights,
            )
            passed, written = [ids], [edge_out, edge_grad]
        elif number == 2:
            (node_grad,) = call(
                node_grad_kernel,
                [node_shape],
                [],
                back_near,
                back_far,
                base,
                snd_sum,
                rcv_sum,
                turned_weights,
                early_ids,
            )
            written = [node_grad]
        grads, *passed = call(
            functools.partial(add_kernel, len(passed)),
            [half_shape] + [(x.shape, x.dtype) for x in passed],
            [],
            grads,
            other,
            *passed,
            *before,
            *written,
            anywhere=len(written),
        )
        if number == 0:
            (early_vectors,) = passed
        elif number == 1:
            (early_ids,) = passed
    others = lax.ppermute(grads, "sub", core_pairs)
    matrices = [3 * lane, lane, 2 * lane, lane]
    totals = call(
        finish_kernel,
        [((height, lane), f32) for height in matrices] + [((1, lane), f32)] * 8,
        [((2 * kept, lane), f32)],
        grads,
        others,
    )
    flat = [total.reshape(lane) for total in totals[4:]]
    return (
        node_out[None],
        edge_out[None],
        node_grad[None],
        edge_grad[None],
        totals[0],
        flat[0],
        totals[1],
        flat[1],
        flat[2],
        flat[3],
        totals[2],
        flat[4],
        totals[3],
        flat[5],
        flat[6],
        flat[7],
    )


def solution(mesh):
    node_spec = P(("groups", "sample"), ("dom", "sub"), None)
    ids_spec = P(("dom", "sub"))
    return jax.shard_map(
        on_device,
        mesh=mesh,
        in_specs=(
            (node_spec, node_spec, ids_spec, ids_spec, P(("dom", "sub"), None, None))
            + (P(),) * 12
            + (node_spec, node_spec)
        ),
        out_specs=(
            (node_spec,) * 4
            + (P("groups", None), P("groups"), P("groups", None), P("groups"), P("groups"), P("groups"))
            * 2
        ),
        check_vma=False,
    )
```

```python
import functools
import math

import jax
import jax.numpy as jnp
from jax import lax
from jax.experimental import pallas as pl
from jax.experimental.pallas import tpu as pltpu
from jax.sharding import PartitionSpec as P

epsilon = 1e-05
rows_dims = (((0,), (0,)), ((), ()))
back_dims = (((1,), (1,)), ((), ()))
f32 = jnp.float32
bf16 = jnp.bfloat16
lane = 128
edge_tile = 512
vmem_limit = 32 * 1024 * 1024
sum_rows = 16
chain = ("dom", "sub")


def each_tile(rows, tile, tile_group=6):
    count = rows // edge_tile
    group = math.gcd(count, tile_group)

    def several(i, carry):
        for k in range(group):
            tile(i * group + k)
        return carry

    lax.fori_loop(0, count // group, several, 0)


def dot(left, right):
    return jnp.dot(left, right, preferred_element_type=f32)


def dot_rows(left, right):
    return lax.dot_general(left, right, rows_dims, preferred_element_type=f32)


def dot_back(left, right):
    return lax.dot_general(left, right, back_dims, preferred_element_type=f32)


def column_of(row):
    return jnp.broadcast_to(row, (lane, lane)).T


def hot_columns(low, *spans):
    targets = lax.broadcasted_iota(jnp.int16, low.shape, 1)
    one, zero = jnp.ones((), bf16), jnp.zeros((), bf16)
    parts = [
        jnp.where(low == targets + jnp.int16(at), one, zero)
        for start, stop in spans
        for at in range(start, stop, lane)
    ]
    return jnp.concatenate(parts, axis=1)


def hot_rows(row, height):
    low = jnp.broadcast_to(row, (16, lane)).astype(jnp.int16)
    targets = lax.broadcasted_iota(jnp.int16, (height, lane), 0).reshape(height // 16, 16, lane)
    one, zero = jnp.ones((), bf16), jnp.zeros((), bf16)
    return jnp.where(targets == low[None], one, zero).reshape(height, lane)


def folded(ids, half):
    return jnp.where((ids >= half) & (ids < 2 * half), ids - half, ids)


def side_by_side(rows):
    half = rows.shape[0] // 2
    return jnp.concatenate([rows[:half], rows[half:]], axis=1)


def pick(ids, low, half, table, *halo):
    both = dot(hot_columns(low, (0, half), *halo), table)
    return jnp.where(ids >= half, both[:, lane:], both[:, :lane])


def rows_of_ids(ids_ref, first, count, height, change):
    parts = [hot_rows(change(ids_ref[pl.ds(first + k, 1), :]), height) for k in range(count)]
    return jnp.concatenate(parts, axis=1)


def spread(ids_ref, first, count, half, ids, values):
    upper = ids >= half
    paired = jnp.concatenate(
        [jnp.where(upper, 0.0, values).astype(bf16), jnp.where(upper, values, 0.0).astype(bf16)],
        axis=1,
    )
    return dot(rows_of_ids(ids_ref, first, count, half, lambda row: folded(row, half)), paired)


def sigmoid(z):
    return 0.5 * jnp.tanh(0.5 * z) + 0.5


def vector(vectors_ref, k):
    return vectors_ref[k : k + 1, :]


def centred_pair(w):
    w = w.astype(f32)
    w = w - jnp.mean(w, axis=1, keepdims=True)
    high = w.astype(bf16)
    low = (w - high.astype(f32)).astype(bf16)
    return jnp.concatenate([high, low], axis=1)


def centred(b):
    return b - jnp.mean(b, axis=1, keepdims=True)


def mean_weights():
    shape = (2 * lane, 2 * lane)
    left = lax.broadcasted_iota(jnp.int32, shape, 0) < lane
    right = lax.broadcasted_iota(jnp.int32, shape, 1) < lane
    return jnp.where(left == right, 1.0 / lane, 0.0).astype(bf16)


def normed_of(act, w_pair, b_centred, means):
    both = dot(act, w_pair)
    center = both[:, :lane] + both[:, lane:] + b_centred
    variance = dot((center * center).astype(bf16), means[:lane, :lane])
    scale_inv = lax.rsqrt(variance + epsilon)
    return center * scale_inv, scale_inv


def back_norm(upstream, normed, scale_inv, gain, means):
    d_normed = upstream * gain
    pair = jnp.concatenate([d_normed.astype(bf16), (d_normed * normed).astype(bf16)], axis=1)
    both = dot(pair, means)
    return scale_inv * (d_normed - both[:, :lane] - normed * both[:, lane:])


def column_sum(values):
    return jnp.sum(values, axis=0, keepdims=True)


def eight_sums(values):
    return jnp.sum(values.reshape(values.shape[0] // 8, 8, lane), axis=0)


def parity_of_place():
    return lax.axis_index(chain) % 2


def started(moves, sems):
    copies = [
        pltpu.make_async_copy(source, target, sems.at[k])
        for k, (source, target) in enumerate(moves)
    ]
    for copy in copies:
        copy.start()
    return copies


def first_kernel(node_hbm, list_hbm, snd_hbm, rcv_hbm, edge_hbm, *refs):
    small = refs[:12]
    node_ref, message_ref, ids_ref, edge_ref, weights_ref, vectors_ref, sems = refs[12:]
    chunks = snd_hbm.shape[0]
    moves = [
        (node_hbm, node_ref),
        (list_hbm, ids_ref.at[2 * chunks : 2 * chunks + 2]),
        (snd_hbm, ids_ref.at[:chunks]),
        (rcv_hbm, ids_ref.at[chunks : 2 * chunks]),
    ]
    at = 0
    for source in small[:4]:
        moves.append((source, weights_ref.at[at : at + source.shape[0]]))
        at += source.shape[0]
    for k, source in enumerate(small[4:]):
        moves.append((source, vectors_ref.at[k : k + 1]))
    moves.append((edge_hbm, edge_ref))
    copies = started(moves, sems)
    for copy in copies[:2]:
        copy.wait()
    parity = parity_of_place()
    node = node_ref[...]
    rim = message_ref.shape[0] // 2
    for k, side in enumerate((1 - parity, parity)):
        column = column_of(ids_ref[pl.ds(2 * chunks + side, 1), :]).astype(jnp.int16)
        hot = hot_columns(column, (0, node.shape[0]))
        message_ref[k * rim : (k + 1) * rim, :] = dot(hot, node).astype(bf16)
    for copy in copies[2:]:
        copy.wait()


def prepare_kernel(
    ids_ref,
    node_ref,
    weights_ref,
    vectors_ref,
    edge_ref,
    unused_ref,
    edge_cot_hbm,
    node_cot_hbm,
    edge_cot_ref,
    node_cot_ref,
    snd_column,
    rcv_column,
    rcv_low,
    z_ref,
    rcv_local,
    turned_ref,
    pairs_ref,
    means_ref,
    turned_weights,
    snd_low,
    snd_table,
    sems,
):
    copies = started([(edge_cot_hbm, edge_cot_ref), (node_cot_hbm, node_cot_ref)], sems)
    means_ref[...] = mean_weights()
    for k, at in enumerate((3 * lane, 6 * lane)):
        w = weights_ref[at : at + lane]
        pairs_ref[k * lane : (k + 1) * lane, :] = centred_pair(w)
    for k in range(7):
        at = slice(k * lane, (k + 1) * lane)
        turned_weights[at, :] = weights_ref[at, :].T
    chunks = snd_column.shape[0] // lane
    half = snd_table.shape[0]
    for k in range(chunks):
        at = slice(k * lane, (k + 1) * lane)
        snd = column_of(ids_ref[k : k + 1, :])
        rcv = column_of(ids_ref[chunks + k : chunks + k + 1, :])
        snd_column[at, :] = snd
        rcv_column[at, :] = rcv
        snd_low[at, :] = folded(snd, half).astype(jnp.int16)
        rcv_low[at, :] = folded(rcv, half).astype(jnp.int16)
    node = node_ref[...]
    snd_table[...] = side_by_side(node)
    rcv_local[...] = side_by_side(dot(node, weights_ref[2 * lane : 3 * lane]).astype(bf16))
    w1 = weights_ref[: 2 * lane]
    b1 = vector(vectors_ref, 0)

    def tile(i):
        rows = pl.ds(pl.multiple_of(i * edge_tile, edge_tile), edge_tile)
        x = edge_ref[rows, :]
        sent = pick(snd_column[rows, :], snd_low[rows, :], half, snd_table[...]).astype(bf16)
        z_ref[rows, :] = dot(jnp.concatenate([x, sent], axis=1), w1) + b1
        turned_ref[:, rows] = sent.T

    each_tile(edge_ref.shape[0], tile)
    for copy in copies:
        copy.wait()


def split_kernel(message_ref, near_ref, far_ref):
    rim = near_ref.shape[0]
    near_ref[...] = message_ref[:rim, :]
    far_ref[...] = message_ref[rim:, :]


def edge_forward_kernel(
    near_ref,
    far_ref,
    ids_ref,
    weights_ref,
    vectors_ref,
    rcv_column,
    rcv_low,
    z_sent,
    rcv_local,
    pairs_ref,
    means,
    z_ref,
    normed_ref,
    scale_ref,
    message_ref,
    rims_ref,
    table,
    total,
):
    half = rcv_local.shape[0]
    nodes = 2 * half
    rim = near_ref.shape[0]
    parity = parity_of_place()
    near_at = pl.multiple_of((1 - parity) * rim, rim)
    far_at = pl.multiple_of(parity * rim, rim)
    w1_rcv = weights_ref[2 * lane : 3 * lane]
    gain, shift = vector(vectors_ref, 2), vector(vectors_ref, 3)
    table[:half, :] = rcv_local[...]
    table[half:, :lane] = jnp.zeros((2 * rim, lane), bf16)
    table[pl.ds(half + near_at, rim), lane:] = dot(near_ref[...], w1_rcv).astype(bf16)
    table[pl.ds(half + far_at, rim), lane:] = dot(far_ref[...], w1_rcv).astype(bf16)
    b2 = centred(vector(vectors_ref, 1))
    total[...] = jnp.zeros_like(total)

    def tile(i):
        rows = pl.ds(pl.multiple_of(i * edge_tile, edge_tile), edge_tile)
        slots = (nodes, nodes + 2 * rim)
        z = z_sent[rows, :]
        z = z + pick(rcv_column[rows, :], rcv_low[rows, :], half, table[...], slots)
        z_ref[rows, :] = z

    def rest(i):
        rows = pl.ds(pl.multiple_of(i * edge_tile, edge_tile), edge_tile)
        z = z_ref[rows, :]
        act = (z * sigmoid(z)).astype(bf16)
        normed, scale_inv = normed_of(act, pairs_ref[:lane, :], b2, means[...])
        normed_ref[rows, :] = normed
        scale_ref[rows, :] = scale_inv
        message = (normed * gain + shift).astype(bf16)
        message_ref[rows, :] = message
        first = (rcv_column.shape[0] + i * edge_tile) // lane
        hot = rows_of_ids(ids_ref, first, edge_tile // lane, 2 * rim, lambda row: row - nodes)
        total[...] += dot(hot, message)

    each_tile(rcv_column.shape[0], tile)
    each_tile(rcv_column.shape[0], rest)
    rims_ref[:rim, :] = total[pl.ds(near_at, rim), :].astype(bf16)
    rims_ref[rim:, :] = total[pl.ds(far_at, rim), :].astype(bf16)


def collect_kernel(
    ids_ref,
    rcv_column,
    rcv_low,
    message_ref,
    node_ref,
    near_ref,
    far_ref,
    unused_ref,
    agg_ref,
    turned_ref,
    table,
    total,
):
    rim = near_ref.shape[0]
    half = total.shape[0]
    nodes = 2 * half
    parity = parity_of_place()
    near_at = pl.multiple_of((1 - parity) * rim, rim)
    far_at = pl.multiple_of(parity * rim, rim)
    table[:half, :] = side_by_side(node_ref[...])
    table[half:, :lane] = jnp.zeros((2 * rim, lane), bf16)
    table[pl.ds(half + near_at, rim), lane:] = near_ref[...]
    table[pl.ds(half + far_at, rim), lane:] = far_ref[...]
    total[...] = jnp.zeros_like(total)

    def tile(i):
        rows = pl.ds(pl.multiple_of(i * edge_tile, edge_tile), edge_tile)
        first = (rcv_column.shape[0] + i * edge_tile) // lane
        rcv = rcv_column[rows, :]
        message = message_ref[rows, :].astype(f32)
        total[...] += spread(ids_ref, first, edge_tile // lane, half, rcv, message)

    def receivers(i):
        rows = pl.ds(pl.multiple_of(i * edge_tile, edge_tile), edge_tile)
        rcv = rcv_column[rows, :]
        slots = (nodes, nodes + 2 * rim)
        turned_ref[:, rows] = pick(rcv, rcv_low[rows, :], half, table[...], slots).astype(bf16).T

    each_tile(rcv_column.shape[0], tile)
    each_tile(rcv_column.shape[0], receivers)
    agg_ref[:half, :] = total[:, :lane]
    agg_ref[half:, :] = total[:, lane:]


def hot_lists(ids_ref, nodes):
    parity = parity_of_place()
    first = ids_ref.shape[0] - 2
    near = ids_ref[pl.ds(first + 1 - parity, 1), :]
    far = ids_ref[pl.ds(first + parity, 1), :]
    return jnp.concatenate([hot_rows(near, nodes), hot_rows(far, nodes)], axis=1)


def node_kernel(
    near_ref,
    far_ref,
    node_ref,
    agg_ref,
    ids_ref,
    weights_ref,
    vectors_ref,
    cot_ref,
    pairs_ref,
    means,
    turned_weights,
    x_ref,
    act_ref,
    normed_ref,
    dz1_ref,
    dz2_ref,
    sums_ref,
    dagg_ref,
    rims_ref,
):
    nodes = node_ref.shape[0]
    returned = jnp.concatenate([near_ref[...], far_ref[...]], axis=0)
    agg = (agg_ref[...] + dot(hot_lists(ids_ref, nodes), returned)).astype(bf16)
    x = jnp.concatenate([node_ref[...], agg], axis=1)
    x_ref[...] = x
    w1 = weights_ref[4 * lane : 6 * lane]
    z = dot(x, w1) + vector(vectors_ref, 4)
    sig = sigmoid(z)
    act = (z * sig).astype(bf16)
    act_ref[...] = act
    b2 = centred(vector(vectors_ref, 5))
    normed, scale_inv = normed_of(act, pairs_ref[lane:, :], b2, means[...])
    normed_ref[...] = normed
    upstream = cot_ref[...].astype(f32)
    dz2 = back_norm(upstream, normed, scale_inv, vector(vectors_ref, 6), means[...])
    dz2b = dz2.astype(bf16)
    dz2_ref[...] = dz2b
    dz1 = dot(dz2b, turned_weights[6 * lane :]) * (sig * (1.0 + z * (1.0 - sig)))
    dz1b = dz1.astype(bf16)
    dz1_ref[...] = dz1b
    dagg = dot(dz1b, turned_weights[5 * lane : 6 * lane]).astype(bf16)
    dagg_ref[...] = dagg
    parity = parity_of_place()
    first = ids_ref.shape[0] - 2
    rim = rims_ref.shape[0] // 2
    for k, side in enumerate((1 - parity, parity)):
        column = column_of(ids_ref[pl.ds(first + side, 1), :]).astype(jnp.int16)
        picked = hot_columns(column, (0, nodes))
        rims_ref[k * rim : (k + 1) * rim, :] = dot(picked, dagg).astype(bf16)
    sums_ref[0:8, :] = eight_sums(dz1)
    sums_ref[8:16, :] = eight_sums(dz2)


def node_rest_kernel(
    x_ref,
    act_ref,
    normed_ref,
    dz1_ref,
    dz2_ref,
    sums_ref,
    turned_weights,
    vectors_ref,
    cot_ref,
    unused_ref,
    out_ref,
    base_ref,
    grads_ref,
):
    x = x_ref[...]
    normed = normed_ref[...]
    dz1b = dz1_ref[...]
    update = normed * vector(vectors_ref, 6) + vector(vectors_ref, 7)
    out_ref[...] = (x[:, :lane].astype(f32) + update).astype(bf16)
    upstream = cot_ref[...].astype(f32)
    base_ref[...] = upstream + dot(dz1b, turned_weights[4 * lane : 5 * lane])
    first = 2 * lane
    second = first + lane
    grads_ref[:first, :] = dot_rows(x, dz1b)
    grads_ref[first:second, :] = dot_rows(act_ref[...], dz2_ref[...])
    sums = [column_sum(sums_ref[0:8, :]), column_sum(sums_ref[8:16, :])]
    sums += [column_sum(eight_sums(upstream * normed)), column_sum(eight_sums(upstream))]
    sums.append(jnp.zeros((sum_rows - len(sums), lane), f32))
    grads_ref[second:, :] = jnp.concatenate(sums, axis=0)


def upstream_kernel(
    rcv_column,
    rcv_low,
    dagg_ref,
    cot_ref,
    z_ref,
    edge_ref,
    unused_ref,
    up_ref,
    slope_ref,
    turned_ref,
    table,
):
    half = table.shape[0]
    table[...] = side_by_side(dagg_ref[...])

    def tile(i):
        rows = pl.ds(pl.multiple_of(i * edge_tile, edge_tile), edge_tile)
        local = pick(rcv_column[rows, :], rcv_low[rows, :], half, table[...])
        up_ref[rows, :] = cot_ref[rows, :].astype(f32) + local
        z = z_ref[rows, :]
        sig = sigmoid(z)
        slope_ref[rows, :] = sig * (1.0 + z * (1.0 - sig))
        turned_ref[:lane, rows] = edge_ref[rows, :].T
        turned_ref[lane:, rows] = (z * sig).astype(bf16).T

    each_tile(cot_ref.shape[0], tile)


def edge_backward_kernel(
    nodes,
    dagg_near_ref,
    dagg_far_ref,
    up_ref,
    normed_ref,
    scale_ref,
    slope_ref,
    sent_turned,
    received_turned,
    turned,
    turned_weights,
    means,
    vectors_ref,
    node_grads_ref,
    rcv_low,
    dz_ref,
    kept_ref,
    sent_ref,
    grads_ref,
    table,
    sums,
    upstream_ref,
    dz2_ref,
):
    rim = dagg_near_ref.shape[0]
    parity = parity_of_place()
    w2_turned = turned_weights[3 * lane : 4 * lane]
    gain = vector(vectors_ref, 2)
    table[pl.ds(pl.multiple_of((1 - parity) * rim, rim), rim), :] = dagg_near_ref[...]
    table[pl.ds(pl.multiple_of(parity * rim, rim), rim), :] = dagg_far_ref[...]
    sums[...] = jnp.zeros_like(sums)

    def tile(i):
        rows = pl.ds(pl.multiple_of(i * edge_tile, edge_tile), edge_tile)
        hot = hot_columns(rcv_low[rows, :], (nodes, nodes + 2 * rim))
        upstream_ref[rows, :] = up_ref[rows, :] + dot(hot, table[...])

    def chain_of(i):
        rows = pl.ds(pl.multiple_of(i * edge_tile, edge_tile), edge_tile)
        upstream = upstream_ref[rows, :]
        normed = normed_ref[rows, :]
        dz2 = back_norm(upstream, normed, scale_ref[rows, :], gain, means[...])
        dz2b = dz2.astype(bf16)
        dz1 = dot(dz2b, w2_turned) * slope_ref[rows, :]
        dz1b = dz1.astype(bf16)
        dz_ref[rows, :] = dz1b
        dz2_ref[rows, :] = dz2b
        sums[0:8, :] += eight_sums(dz1)
        sums[8:16, :] += eight_sums(dz2)
        sums[16:24, :] += eight_sums(upstream * normed)
        sums[24:32, :] += eight_sums(upstream)

    each_tile(up_ref.shape[0], tile)
    each_tile(up_ref.shape[0], chain_of)
    dz1_all = dz_ref[...]
    grads_ref[:lane, :] = dot(turned[:lane, :], dz1_all)
    grads_ref[lane : 2 * lane, :] = dot(sent_turned[...], dz1_all)
    grads_ref[2 * lane : 3 * lane, :] = dot(received_turned[...], dz1_all)
    grads_ref[3 * lane : 4 * lane, :] = dot(turned[lane:, :], dz2_ref[...])
    kept = kept_ref.shape[0]
    node_rows = node_grads_ref.shape[0] - sum_rows
    last = 4 * lane + node_rows
    grads_ref[4 * lane : last, :] = node_grads_ref[:node_rows, :]
    grads_ref[last : last + sum_rows, :] = jnp.concatenate(
        [column_sum(sums[8 * k : 8 * k + 8, :]) for k in range(4)]
        + [node_grads_ref[node_rows : node_rows + 4, :], jnp.zeros((8, lane), f32)],
        axis=0,
    )
    if last + sum_rows < grads_ref.shape[0]:
        grads_ref[last + sum_rows :, :] = jnp.zeros(
            (grads_ref.shape[0] - last - sum_rows, lane), f32
        )
    own = lax.axis_index("sub")
    kept_ref[...] = grads_ref[pl.ds(pl.multiple_of(own * kept, sum_rows), kept), :]
    other = pl.multiple_of((1 - own) * kept, sum_rows)
    sent_ref[...] = grads_ref[pl.ds(other, kept), :].astype(bf16)


def halo_kernel(nodes, ids_ref, dz_ref, turned_weights, rims_ref, total):
    rim = rims_ref.shape[0] // 2
    edges = dz_ref.shape[0]
    parity = parity_of_place()
    total[...] = jnp.zeros_like(total)

    def tile(i):
        rows = pl.ds(pl.multiple_of(i * edge_tile, edge_tile), edge_tile)
        first = (edges + i * edge_tile) // lane
        slots = rows_of_ids(ids_ref, first, edge_tile // lane, 2 * rim, lambda row: row - nodes)
        total[...] += dot(slots, dz_ref[rows, :])

    each_tile(edges, tile)
    w1_turned = turned_weights[2 * lane : 3 * lane]
    for k, side in enumerate((1 - parity, parity)):
        returned = total[pl.ds(pl.multiple_of(side * rim, rim), rim), :].astype(bf16)
        rims_ref[k * rim : (k + 1) * rim, :] = dot(returned, w1_turned).astype(bf16)


def scatter_kernel(
    ids_ref,
    dz_ref,
    snd_column,
    rcv_column,
    unused_ref,
    snd_sum_ref,
    rcv_sum_ref,
    snd_total,
    rcv_total,
):
    half = snd_total.shape[0]
    for total in (snd_total, rcv_total):
        total[...] = jnp.zeros_like(total)

    def tile(i):
        rows = pl.ds(pl.multiple_of(i * edge_tile, edge_tile), edge_tile)
        chunk = edge_tile // lane
        dz1 = dz_ref[rows, :].astype(f32)
        first = rcv_column.shape[0] // lane + i * chunk
        snd_total[...] += spread(ids_ref, i * chunk, chunk, half, snd_column[rows, :], dz1)
        rcv_total[...] += spread(ids_ref, first, chunk, half, rcv_column[rows, :], dz1)

    each_tile(dz_ref.shape[0], tile)
    for total, out_ref in ((snd_total, snd_sum_ref), (rcv_total, rcv_sum_ref)):
        out_ref[:half, :] = total[:, :lane].astype(bf16)
        out_ref[half:, :] = total[:, lane:].astype(bf16)


def edge_outputs_kernel(
    dz_ref, cot_ref, edge_ref, normed_ref, vectors_ref, turned_weights, out_ref, grad_ref
):
    w1_turned = turned_weights[:lane]
    gain, shift = vector(vectors_ref, 2), vector(vectors_ref, 3)

    def tile(i):
        rows = pl.ds(pl.multiple_of(i * edge_tile, edge_tile), edge_tile)
        cot = cot_ref[rows, :].astype(f32)
        grad_ref[rows, :] = (cot + dot(dz_ref[rows, :], w1_turned)).astype(bf16)
        update = normed_ref[rows, :] * gain + shift
        out_ref[rows, :] = (edge_ref[rows, :].astype(f32) + update).astype(bf16)

    each_tile(cot_ref.shape[0], tile)


def node_grad_kernel(
    near_ref, far_ref, base_ref, snd_sum_ref, rcv_sum_ref, turned_weights, ids_ref, out_ref
):
    returned = jnp.concatenate([near_ref[...], far_ref[...]], axis=0)
    total = base_ref[...] + dot(snd_sum_ref[...], turned_weights[lane : 2 * lane])
    total = total + dot(rcv_sum_ref[...], turned_weights[2 * lane : 3 * lane])
    hot = hot_lists(ids_ref, base_ref.shape[0])
    out_ref[...] = (total + dot(hot, returned)).astype(bf16)


def add_kernel(passed, own_ref, other_ref, *refs):
    out_refs = refs[len(refs) - passed - 1 :]
    out_refs[0][...] = (own_ref[...].astype(f32) + other_ref[...].astype(f32)).astype(bf16)
    for source, target in zip(refs[:passed], out_refs[1:]):
        target[...] = source[...]


def finish_kernel(own_ref, other_ref, *refs):
    out_refs, total_ref = refs[:-1], refs[-1]
    kept = own_ref.shape[0]
    own = lax.axis_index("sub")
    total_ref[pl.ds(pl.multiple_of(own * kept, sum_rows), kept), :] = own_ref[...].astype(f32)
    other = pl.multiple_of((1 - own) * kept, sum_rows)
    total_ref[pl.ds(other, kept), :] = other_ref[...].astype(f32)
    at = 0
    for out_ref in out_refs[:4]:
        out_ref[...] = total_ref[at : at + out_ref.shape[0], :]
        at += out_ref.shape[0]
    for k, out_ref in enumerate(out_refs[4:]):
        out_ref[...] = total_ref[at + k : at + k + 1, :]


def call(kernel, outs, scratch, *operands, anywhere=0, sems=0):
    moved = sum(x.size * x.dtype.itemsize for x in operands)
    held = operands[len(operands) - anywhere :]
    operands = operands[: len(operands) - anywhere]
    operands += tuple(pltpu.with_memory_space_constraint(x, pltpu.HBM) for x in held)
    inside = [pl.BlockSpec(memory_space=pltpu.VMEM)] * (len(operands) - anywhere)
    outside = [pl.BlockSpec(memory_space=pl.ANY)] * anywhere
    scratch_shapes = [pltpu.VMEM(shape, dtype) for shape, dtype in scratch]
    if sems:
        scratch_shapes.append(pltpu.SemaphoreType.DMA((sems,)))
    return pl.pallas_call(
        kernel,
        out_shape=[jax.ShapeDtypeStruct(shape, dtype) for shape, dtype in outs],
        in_specs=inside + outside,
        out_specs=[pl.BlockSpec(memory_space=pltpu.VMEM)] * len(outs),
        scratch_shapes=scratch_shapes,
        compiler_params=pltpu.CompilerParams(vmem_limit_bytes=vmem_limit),
        cost_estimate=pl.CostEstimate(flops=0, bytes_accessed=moved, transcendentals=0),
    )(*operands)


def exchange(message):
    chips, samples = lax.axis_size("dom"), lax.axis_size("sample")
    place = lambda chip, sample, core: (chip * samples + sample) * 2 + core
    inner = [(i, i ^ 1) for i in range(2 * chips)]
    outer = []
    for sample in range(samples):
        for chip in range(chips - 1):
            ends = place(chip, sample, 1), place(chip + 1, sample, 0)
            outer += [ends, ends[::-1]]
        for chip, core in ((0, 0), (chips - 1, 1)):
            outer.append((place(chip, sample, core), place(chip, sample ^ 1, core)))
    rim_shape = ((message.shape[0] // 2, lane), bf16)
    near, far = call(split_kernel, [rim_shape, rim_shape], [], message)
    near = lax.ppermute(near, chain, inner)
    return near, lax.ppermute(far, ("dom", "sample", "sub"), outer), far


def sum_rounds():
    for axis in ("sample", "dom"):
        count = lax.axis_size(axis)
        step = count // 2
        while step > 0:
            yield axis, [(i, i ^ step) for i in range(count)]
            step //= 2


def on_device(
    node_in,
    edge_in,
    senders,
    receivers,
    send_list,
    w_edge_first,
    b_edge_first,
    w_edge_second,
    b_edge_second,
    edge_gain,
    edge_shift,
    w_node_first,
    b_node_first,
    w_node_second,
    b_node_second,
    node_gain,
    node_shift,
    node_cotangent,
    edge_cotangent,
):
    node = node_in[0]
    edge = edge_in[0]
    nodes = node.shape[0]
    edges = edge.shape[0]
    rim = send_list.shape[2]
    snd_half = nodes // 2
    kept = -(-(7 * lane + sum_rows) // (2 * sum_rows)) * sum_rows
    row = lambda x: x.reshape(1, lane)
    small = [w_edge_first, w_edge_second, w_node_first, w_node_second]
    small += [row(b_edge_first), row(b_edge_second), row(edge_gain), row(edge_shift)]
    small += [row(b_node_first), row(b_node_second), row(node_gain), row(node_shift)]
    chunks = edges // lane
    sources = [
        node,
        send_list[0],
        senders.reshape(chunks, lane),
        receivers.reshape(chunks, lane),
        edge,
    ] + small
    rims_shape = ((2 * rim, lane), bf16)
    edge_shape = ((edges, lane), bf16)
    wide_shape = ((edges, lane), f32)
    node_shape = ((nodes, lane), bf16)
    node, rims, ids, edge, weights, vectors = call(
        first_kernel,
        [
            node_shape,
            rims_shape,
            ((2 * chunks + 2, lane), jnp.int32),
            edge_shape,
            ((7 * lane, lane), bf16),
            ((8, lane), f32),
        ],
        [],
        *sources,
        anywhere=len(sources),
        sems=len(sources),
    )
    near, far, onward = exchange(rims)
    prepared = call(
        prepare_kernel,
        [
            edge_shape,
            node_shape,
            ((edges, lane), jnp.int32),
            ((edges, lane), jnp.int32),
            ((edges, lane), jnp.int16),
            wide_shape,
            ((snd_half, 2 * lane), bf16),
            ((lane, edges), bf16),
            ((2 * lane, 2 * lane), bf16),
            ((2 * lane, 2 * lane), bf16),
            ((7 * lane, lane), bf16),
        ],
        [((edges, lane), jnp.int16), ((snd_half, 2 * lane), bf16)],
        ids,
        node,
        weights,
        vectors,
        edge,
        onward,
        edge_cotangent[0],
        node_cotangent[0],
        anywhere=2,
        sems=2,
    )
    edge_cot, node_cot, snd_column, rcv_column, rcv_low = prepared[:5]
    z_sent, rcv_local, sent_turned, pairs, means, turned_weights = prepared[5:]
    z, normed, scale, message, rims = call(
        edge_forward_kernel,
        [wide_shape, wide_shape, wide_shape, edge_shape, rims_shape],
        [
            ((snd_half + 2 * rim, 2 * lane), bf16),
            ((2 * rim, lane), f32),
        ],
        near,
        far,
        ids,
        weights,
        vectors,
        rcv_column,
        rcv_low,
        z_sent,
        rcv_local,
        pairs,
        means,
    )
    back_near, back_far, onward = exchange(rims)
    agg, received_turned = call(
        collect_kernel,
        [((nodes, lane), f32), ((lane, edges), bf16)],
        [((snd_half + 2 * rim, 2 * lane), bf16), ((snd_half, 2 * lane), f32)],
        ids,
        rcv_column,
        rcv_low,
        message,
        node,
        near,
        far,
        onward,
    )
    node_x, node_act, node_normed, node_dz1, node_dz2, node_sums, dagg, rims = call(
        node_kernel,
        [
            ((nodes, 2 * lane), bf16),
            node_shape,
            ((nodes, lane), f32),
            node_shape,
            node_shape,
            ((16, lane), f32),
            node_shape,
            rims_shape,
        ],
        [],
        back_near,
        back_far,
        node,
        agg,
        ids,
        weights,
        vectors,
        node_cot,
        pairs,
        means,
        turned_weights,
    )
    dagg_near, dagg_far, onward = exchange(rims)
    upstream, slope, turned = call(
        upstream_kernel,
        [wide_shape, wide_shape, ((2 * lane, edges), bf16)],
        [((snd_half, 2 * lane), bf16)],
        rcv_column,
        rcv_low,
        dagg,
        edge_cot,
        z,
        edge,
        onward,
    )
    node_out, base, node_grads = call(
        node_rest_kernel,
        [node_shape, ((nodes, lane), f32), ((3 * lane + sum_rows, lane), f32)],
        [],
        node_x,
        node_act,
        node_normed,
        node_dz1,
        node_dz2,
        node_sums,
        turned_weights,
        vectors,
        node_cot,
        onward,
    )
    half_shape = ((kept, lane), bf16)
    dz, grads_kept, grads_sent = call(
        functools.partial(edge_backward_kernel, nodes),
        [edge_shape, ((kept, lane), f32), half_shape],
        [
            ((2 * kept, lane), f32),
            ((2 * rim, lane), bf16),
            ((32, lane), f32),
            wide_shape,
            edge_shape,
        ],
        dagg_near,
        dagg_far,
        upstream,
        normed,
        scale,
        slope,
        sent_turned,
        received_turned,
        turned,
        turned_weights,
        means,
        vectors,
        node_grads,
        rcv_low,
    )
    core_pairs = [(0, 1), (1, 0)]
    other = lax.ppermute(grads_sent, "sub", core_pairs)
    (grads,) = call(functools.partial(add_kernel, 0), [half_shape], [], grads_kept, other)
    (rims,) = call(
        functools.partial(halo_kernel, nodes),
        [rims_shape],
        [((2 * rim, lane), f32)],
        ids,
        dz,
        turned_weights,
    )
    back_near, back_far, unused = exchange(rims)
    node_grad = edge_out = edge_grad = None
    early_vectors, early_ids = vectors, ids
    for number, (axis, partners) in enumerate(sum_rounds()):
        other = lax.ppermute(grads, axis, partners)
        passed, before, written = [], [], []
        if number == 0:
            passed, before = [vectors], [back_near, back_far]
        elif number == 1:
            snd_sum, rcv_sum = call(
                scatter_kernel,
                [node_shape, node_shape],
                [((snd_half, 2 * lane), f32), ((snd_half, 2 * lane), f32)],
                ids,
                dz,
                snd_column,
                rcv_column,
                early_vectors,
            )
            edge_out, edge_grad = call(
                edge_outputs_kernel,
                [edge_shape, edge_shape],
                [],
                dz,
                edge_cot,
                edge,
                normed,
                early_vectors,
                turned_weights,
            )
            passed, before, written = [ids], [snd_sum, rcv_sum], [edge_out, edge_grad]
        elif number == 2:
            (node_grad,) = call(
                node_grad_kernel,
                [node_shape],
                [],
                back_near,
                back_far,
                base,
                snd_sum,
                rcv_sum,
                turned_weights,
                early_ids,
            )
            written = [node_grad]
        grads, *passed = call(
            functools.partial(add_kernel, len(passed)),
            [half_shape] + [(x.shape, x.dtype) for x in passed],
            [],
            grads,
            other,
            *passed,
            *before,
            *written,
            anywhere=len(written),
        )
        if number == 0:
            (early_vectors,) = passed
        elif number == 1:
            (early_ids,) = passed
    others = lax.ppermute(grads, "sub", core_pairs)
    matrices = [3 * lane, lane, 2 * lane, lane]
    totals = call(
        finish_kernel,
        [((height, lane), f32) for height in matrices] + [((1, lane), f32)] * 8,
        [((2 * kept, lane), f32)],
        grads,
        others,
    )
    flat = [total.reshape(lane) for total in totals[4:]]
    return (
        node_out[None],
        edge_out[None],
        node_grad[None],
        edge_grad[None],
        totals[0],
        flat[0],
        totals[1],
        flat[1],
        flat[2],
        flat[3],
        totals[2],
        flat[4],
        totals[3],
        flat[5],
        flat[6],
        flat[7],
    )


def solution(mesh):
    node_spec = P(("groups", "sample"), ("dom", "sub"), None)
    ids_spec = P(("dom", "sub"))
    return jax.shard_map(
        on_device,
        mesh=mesh,
        in_specs=(
            (node_spec, node_spec, ids_spec, ids_spec, P(("dom", "sub"), None, None))
            + (P(),) * 12
            + (node_spec, node_spec)
        ),
        out_specs=(
            (node_spec,) * 4
            + (P("groups", None), P("groups"), P("groups", None), P("groups"), P("groups"), P("groups"))
            * 2
        ),
        check_vma=False,
    )
```

```python
import functools
import math

import jax
import jax.numpy as jnp
from jax import lax
from jax.experimental import pallas as pl
from jax.experimental.pallas import tpu as pltpu
from jax.sharding import PartitionSpec as P

epsilon = 1e-05
rows_dims = (((0,), (0,)), ((), ()))
back_dims = (((1,), (1,)), ((), ()))
f32 = jnp.float32
bf16 = jnp.bfloat16
lane = 128
edge_tile = 512
vmem_limit = 32 * 1024 * 1024
sum_rows = 16
chain = ("dom", "sub")


def each_tile(rows, tile, tile_group=6):
    count = rows // edge_tile
    group = math.gcd(count, tile_group)

    def several(i, carry):
        for k in range(group):
            tile(i * group + k)
        return carry

    lax.fori_loop(0, count // group, several, 0)


def dot(left, right):
    return jnp.dot(left, right, preferred_element_type=f32)


def dot_rows(left, right):
    return lax.dot_general(left, right, rows_dims, preferred_element_type=f32)


def dot_back(left, right):
    return lax.dot_general(left, right, back_dims, preferred_element_type=f32)


def column_of(row):
    return jnp.broadcast_to(row, (lane, lane)).T


def hot_columns(low, *spans):
    targets = lax.broadcasted_iota(jnp.int16, low.shape, 1)
    one, zero = jnp.ones((), bf16), jnp.zeros((), bf16)
    parts = [
        jnp.where(low == targets + jnp.int16(at), one, zero)
        for start, stop in spans
        for at in range(start, stop, lane)
    ]
    return jnp.concatenate(parts, axis=1)


def hot_rows(row, height):
    low = jnp.broadcast_to(row, (16, lane)).astype(jnp.int16)
    targets = lax.broadcasted_iota(jnp.int16, (height, lane), 0).reshape(height // 16, 16, lane)
    one, zero = jnp.ones((), bf16), jnp.zeros((), bf16)
    return jnp.where(targets == low[None], one, zero).reshape(height, lane)


def folded(ids, half):
    return jnp.where((ids >= half) & (ids < 2 * half), ids - half, ids)


def side_by_side(rows):
    half = rows.shape[0] // 2
    return jnp.concatenate([rows[:half], rows[half:]], axis=1)


def pick(ids, low, half, table, *halo):
    both = dot(hot_columns(low, (0, half), *halo), table)
    return jnp.where(ids >= half, both[:, lane:], both[:, :lane])


def rows_of_ids(ids_ref, first, count, height, change):
    parts = [hot_rows(change(ids_ref[pl.ds(first + k, 1), :]), height) for k in range(count)]
    return jnp.concatenate(parts, axis=1)


def spread(ids_ref, first, count, half, ids, values):
    upper = ids >= half
    paired = jnp.concatenate(
        [jnp.where(upper, 0.0, values).astype(bf16), jnp.where(upper, values, 0.0).astype(bf16)],
        axis=1,
    )
    return dot(rows_of_ids(ids_ref, first, count, half, lambda row: folded(row, half)), paired)


def sigmoid(z):
    return 0.5 * jnp.tanh(0.5 * z) + 0.5


def vector(vectors_ref, k):
    return vectors_ref[k : k + 1, :]


def centred_pair(w):
    w = w.astype(f32)
    w = w - jnp.mean(w, axis=1, keepdims=True)
    high = w.astype(bf16)
    low = (w - high.astype(f32)).astype(bf16)
    return jnp.concatenate([high, low], axis=1)


def centred(b):
    return b - jnp.mean(b, axis=1, keepdims=True)


def mean_weights():
    shape = (2 * lane, 2 * lane)
    left = lax.broadcasted_iota(jnp.int32, shape, 0) < lane
    right = lax.broadcasted_iota(jnp.int32, shape, 1) < lane
    return jnp.where(left == right, 1.0 / lane, 0.0).astype(bf16)


def normed_of(act, w_pair, b_centred, means):
    both = dot(act, w_pair)
    center = both[:, :lane] + both[:, lane:] + b_centred
    variance = dot((center * center).astype(bf16), means[:lane, :lane])
    scale_inv = lax.rsqrt(variance + epsilon)
    return center * scale_inv, scale_inv


def back_norm(upstream, normed, scale_inv, gain, means):
    d_normed = upstream * gain
    pair = jnp.concatenate([d_normed.astype(bf16), (d_normed * normed).astype(bf16)], axis=1)
    both = dot(pair, means)
    return scale_inv * (d_normed - both[:, :lane] - normed * both[:, lane:])


def column_sum(values):
    return jnp.sum(values, axis=0, keepdims=True)


def eight_sums(values):
    return jnp.sum(values.reshape(values.shape[0] // 8, 8, lane), axis=0)


def parity_of_place():
    return lax.axis_index(chain) % 2


def started(moves, sems):
    copies = [
        pltpu.make_async_copy(source, target, sems.at[k])
        for k, (source, target) in enumerate(moves)
    ]
    for copy in copies:
        copy.start()
    return copies


def first_kernel(node_hbm, list_hbm, snd_hbm, rcv_hbm, edge_hbm, *refs):
    small = refs[:12]
    node_ref, message_ref, ids_ref, edge_ref, weights_ref, vectors_ref, sems = refs[12:]
    chunks = snd_hbm.shape[0]
    moves = [
        (node_hbm, node_ref),
        (list_hbm, ids_ref.at[2 * chunks : 2 * chunks + 2]),
        (snd_hbm, ids_ref.at[:chunks]),
        (rcv_hbm, ids_ref.at[chunks : 2 * chunks]),
    ]
    at = 0
    for source in small[:4]:
        moves.append((source, weights_ref.at[at : at + source.shape[0]]))
        at += source.shape[0]
    for k, source in enumerate(small[4:]):
        moves.append((source, vectors_ref.at[k : k + 1]))
    moves.append((edge_hbm, edge_ref))
    copies = started(moves, sems)
    for copy in copies[:2]:
        copy.wait()
    parity = parity_of_place()
    node = node_ref[...]
    rim = message_ref.shape[0] // 2
    for k, side in enumerate((1 - parity, parity)):
        column = column_of(ids_ref[pl.ds(2 * chunks + side, 1), :]).astype(jnp.int16)
        hot = hot_columns(column, (0, node.shape[0]))
        message_ref[k * rim : (k + 1) * rim, :] = dot(hot, node).astype(bf16)
    for copy in copies[2:]:
        copy.wait()


def prepare_kernel(
    ids_ref,
    node_ref,
    weights_ref,
    vectors_ref,
    edge_ref,
    unused_ref,
    edge_cot_hbm,
    node_cot_hbm,
    edge_cot_ref,
    node_cot_ref,
    snd_column,
    rcv_column,
    rcv_low,
    z_ref,
    rcv_local,
    turned_ref,
    pairs_ref,
    means_ref,
    turned_weights,
    snd_low,
    snd_table,
    sent_rows,
    sems,
):
    copies = started([(edge_cot_hbm, edge_cot_ref), (node_cot_hbm, node_cot_ref)], sems)
    means_ref[...] = mean_weights()
    for k, at in enumerate((3 * lane, 6 * lane)):
        w = weights_ref[at : at + lane]
        pairs_ref[k * lane : (k + 1) * lane, :] = centred_pair(w)
    for k in range(7):
        at = slice(k * lane, (k + 1) * lane)
        turned_weights[at, :] = weights_ref[at, :].T
    chunks = snd_column.shape[0] // lane
    half = snd_table.shape[0]
    for k in range(chunks):
        at = slice(k * lane, (k + 1) * lane)
        snd = column_of(ids_ref[k : k + 1, :])
        rcv = column_of(ids_ref[chunks + k : chunks + k + 1, :])
        snd_column[at, :] = snd
        rcv_column[at, :] = rcv
        snd_low[at, :] = folded(snd, half).astype(jnp.int16)
        rcv_low[at, :] = folded(rcv, half).astype(jnp.int16)
    node = node_ref[...]
    snd_table[...] = side_by_side(node)
    rcv_local[...] = side_by_side(dot(node, weights_ref[2 * lane : 3 * lane]).astype(bf16))
    w1 = weights_ref[: 2 * lane]
    b1 = vector(vectors_ref, 0)

    def tile(i):
        rows = pl.ds(pl.multiple_of(i * edge_tile, edge_tile), edge_tile)
        sent = pick(snd_column[rows, :], snd_low[rows, :], half, snd_table[...])
        sent_rows[rows, :] = sent.astype(bf16)

    def rest(i):
        rows = pl.ds(pl.multiple_of(i * edge_tile, edge_tile), edge_tile)
        sent = sent_rows[rows, :]
        z_ref[rows, :] = dot(jnp.concatenate([edge_ref[rows, :], sent], axis=1), w1) + b1
        turned_ref[:, rows] = sent.T

    each_tile(edge_ref.shape[0], tile)
    each_tile(edge_ref.shape[0], rest)
    for copy in copies:
        copy.wait()


def split_kernel(message_ref, near_ref, far_ref):
    rim = near_ref.shape[0]
    near_ref[...] = message_ref[:rim, :]
    far_ref[...] = message_ref[rim:, :]


def edge_forward_kernel(
    near_ref,
    far_ref,
    ids_ref,
    weights_ref,
    vectors_ref,
    rcv_column,
    rcv_low,
    z_sent,
    rcv_local,
    pairs_ref,
    means,
    z_ref,
    normed_ref,
    scale_ref,
    message_ref,
    rims_ref,
    table,
    total,
):
    half = rcv_local.shape[0]
    nodes = 2 * half
    rim = near_ref.shape[0]
    parity = parity_of_place()
    near_at = pl.multiple_of((1 - parity) * rim, rim)
    far_at = pl.multiple_of(parity * rim, rim)
    w1_rcv = weights_ref[2 * lane : 3 * lane]
    gain, shift = vector(vectors_ref, 2), vector(vectors_ref, 3)
    table[:half, :] = rcv_local[...]
    table[half:, :lane] = jnp.zeros((2 * rim, lane), bf16)
    table[pl.ds(half + near_at, rim), lane:] = dot(near_ref[...], w1_rcv).astype(bf16)
    table[pl.ds(half + far_at, rim), lane:] = dot(far_ref[...], w1_rcv).astype(bf16)
    b2 = centred(vector(vectors_ref, 1))
    total[...] = jnp.zeros_like(total)

    def tile(i):
        rows = pl.ds(pl.multiple_of(i * edge_tile, edge_tile), edge_tile)
        slots = (nodes, nodes + 2 * rim)
        z = z_sent[rows, :]
        z = z + pick(rcv_column[rows, :], rcv_low[rows, :], half, table[...], slots)
        z_ref[rows, :] = z

    def rest(i):
        rows = pl.ds(pl.multiple_of(i * edge_tile, edge_tile), edge_tile)
        z = z_ref[rows, :]
        act = (z * sigmoid(z)).astype(bf16)
        normed, scale_inv = normed_of(act, pairs_ref[:lane, :], b2, means[...])
        normed_ref[rows, :] = normed
        scale_ref[rows, :] = scale_inv
        message = (normed * gain + shift).astype(bf16)
        message_ref[rows, :] = message
        first = (rcv_column.shape[0] + i * edge_tile) // lane
        hot = rows_of_ids(ids_ref, first, edge_tile // lane, 2 * rim, lambda row: row - nodes)
        total[...] += dot(hot, message)

    each_tile(rcv_column.shape[0], tile)
    each_tile(rcv_column.shape[0], rest)
    rims_ref[:rim, :] = total[pl.ds(near_at, rim), :].astype(bf16)
    rims_ref[rim:, :] = total[pl.ds(far_at, rim), :].astype(bf16)


def collect_kernel(
    ids_ref,
    rcv_column,
    rcv_low,
    message_ref,
    node_ref,
    near_ref,
    far_ref,
    unused_ref,
    agg_ref,
    turned_ref,
    table,
    total,
):
    rim = near_ref.shape[0]
    half = total.shape[0]
    nodes = 2 * half
    parity = parity_of_place()
    near_at = pl.multiple_of((1 - parity) * rim, rim)
    far_at = pl.multiple_of(parity * rim, rim)
    table[:half, :] = side_by_side(node_ref[...])
    table[half:, :lane] = jnp.zeros((2 * rim, lane), bf16)
    table[pl.ds(half + near_at, rim), lane:] = near_ref[...]
    table[pl.ds(half + far_at, rim), lane:] = far_ref[...]
    total[...] = jnp.zeros_like(total)

    def tile(i):
        rows = pl.ds(pl.multiple_of(i * edge_tile, edge_tile), edge_tile)
        first = (rcv_column.shape[0] + i * edge_tile) // lane
        rcv = rcv_column[rows, :]
        message = message_ref[rows, :].astype(f32)
        total[...] += spread(ids_ref, first, edge_tile // lane, half, rcv, message)

    def receivers(i):
        rows = pl.ds(pl.multiple_of(i * edge_tile, edge_tile), edge_tile)
        rcv = rcv_column[rows, :]
        slots = (nodes, nodes + 2 * rim)
        turned_ref[:, rows] = pick(rcv, rcv_low[rows, :], half, table[...], slots).astype(bf16).T

    each_tile(rcv_column.shape[0], tile)
    each_tile(rcv_column.shape[0], receivers)
    agg_ref[:half, :] = total[:, :lane]
    agg_ref[half:, :] = total[:, lane:]


def hot_lists(ids_ref, nodes):
    parity = parity_of_place()
    first = ids_ref.shape[0] - 2
    near = ids_ref[pl.ds(first + 1 - parity, 1), :]
    far = ids_ref[pl.ds(first + parity, 1), :]
    return jnp.concatenate([hot_rows(near, nodes), hot_rows(far, nodes)], axis=1)


def node_kernel(
    near_ref,
    far_ref,
    node_ref,
    agg_ref,
    ids_ref,
    weights_ref,
    vectors_ref,
    cot_ref,
    pairs_ref,
    means,
    turned_weights,
    x_ref,
    act_ref,
    normed_ref,
    dz1_ref,
    dz2_ref,
    sums_ref,
    dagg_ref,
    rims_ref,
):
    nodes = node_ref.shape[0]
    returned = jnp.concatenate([near_ref[...], far_ref[...]], axis=0)
    agg = (agg_ref[...] + dot(hot_lists(ids_ref, nodes), returned)).astype(bf16)
    x = jnp.concatenate([node_ref[...], agg], axis=1)
    x_ref[...] = x
    w1 = weights_ref[4 * lane : 6 * lane]
    z = dot(x, w1) + vector(vectors_ref, 4)
    sig = sigmoid(z)
    act = (z * sig).astype(bf16)
    act_ref[...] = act
    b2 = centred(vector(vectors_ref, 5))
    normed, scale_inv = normed_of(act, pairs_ref[lane:, :], b2, means[...])
    normed_ref[...] = normed
    upstream = cot_ref[...].astype(f32)
    dz2 = back_norm(upstream, normed, scale_inv, vector(vectors_ref, 6), means[...])
    dz2b = dz2.astype(bf16)
    dz2_ref[...] = dz2b
    dz1 = dot(dz2b, turned_weights[6 * lane :]) * (sig * (1.0 + z * (1.0 - sig)))
    dz1b = dz1.astype(bf16)
    dz1_ref[...] = dz1b
    dagg = dot(dz1b, turned_weights[5 * lane : 6 * lane]).astype(bf16)
    dagg_ref[...] = dagg
    parity = parity_of_place()
    first = ids_ref.shape[0] - 2
    rim = rims_ref.shape[0] // 2
    for k, side in enumerate((1 - parity, parity)):
        column = column_of(ids_ref[pl.ds(first + side, 1), :]).astype(jnp.int16)
        picked = hot_columns(column, (0, nodes))
        rims_ref[k * rim : (k + 1) * rim, :] = dot(picked, dagg).astype(bf16)
    sums_ref[0:8, :] = eight_sums(dz1)
    sums_ref[8:16, :] = eight_sums(dz2)


def node_rest_kernel(
    x_ref,
    act_ref,
    normed_ref,
    dz1_ref,
    dz2_ref,
    sums_ref,
    turned_weights,
    vectors_ref,
    cot_ref,
    unused_ref,
    out_ref,
    base_ref,
    grads_ref,
):
    x = x_ref[...]
    normed = normed_ref[...]
    dz1b = dz1_ref[...]
    update = normed * vector(vectors_ref, 6) + vector(vectors_ref, 7)
    out_ref[...] = (x[:, :lane].astype(f32) + update).astype(bf16)
    upstream = cot_ref[...].astype(f32)
    base_ref[...] = upstream + dot(dz1b, turned_weights[4 * lane : 5 * lane])
    first = 2 * lane
    second = first + lane
    grads_ref[:first, :] = dot_rows(x, dz1b)
    grads_ref[first:second, :] = dot_rows(act_ref[...], dz2_ref[...])
    sums = [column_sum(sums_ref[0:8, :]), column_sum(sums_ref[8:16, :])]
    sums += [column_sum(eight_sums(upstream * normed)), column_sum(eight_sums(upstream))]
    sums.append(jnp.zeros((sum_rows - len(sums), lane), f32))
    grads_ref[second:, :] = jnp.concatenate(sums, axis=0)


def upstream_kernel(
    rcv_column,
    rcv_low,
    dagg_ref,
    cot_ref,
    z_ref,
    edge_ref,
    unused_ref,
    up_ref,
    slope_ref,
    turned_ref,
    table,
):
    half = table.shape[0]
    table[...] = side_by_side(dagg_ref[...])

    def tile(i):
        rows = pl.ds(pl.multiple_of(i * edge_tile, edge_tile), edge_tile)
        local = pick(rcv_column[rows, :], rcv_low[rows, :], half, table[...])
        up_ref[rows, :] = cot_ref[rows, :].astype(f32) + local

    def rest(i):
        rows = pl.ds(pl.multiple_of(i * edge_tile, edge_tile), edge_tile)
        z = z_ref[rows, :]
        sig = sigmoid(z)
        slope_ref[rows, :] = sig * (1.0 + z * (1.0 - sig))
        turned_ref[:lane, rows] = edge_ref[rows, :].T
        turned_ref[lane:, rows] = (z * sig).astype(bf16).T

    each_tile(cot_ref.shape[0], tile)
    each_tile(cot_ref.shape[0], rest)


def edge_backward_kernel(
    nodes,
    dagg_near_ref,
    dagg_far_ref,
    up_ref,
    normed_ref,
    scale_ref,
    slope_ref,
    sent_turned,
    received_turned,
    turned,
    turned_weights,
    means,
    vectors_ref,
    node_grads_ref,
    rcv_low,
    dz_ref,
    kept_ref,
    sent_ref,
    grads_ref,
    table,
    sums,
    upstream_ref,
    dz2_ref,
):
    rim = dagg_near_ref.shape[0]
    parity = parity_of_place()
    w2_turned = turned_weights[3 * lane : 4 * lane]
    gain = vector(vectors_ref, 2)
    table[pl.ds(pl.multiple_of((1 - parity) * rim, rim), rim), :] = dagg_near_ref[...]
    table[pl.ds(pl.multiple_of(parity * rim, rim), rim), :] = dagg_far_ref[...]
    sums[...] = jnp.zeros_like(sums)

    def tile(i):
        rows = pl.ds(pl.multiple_of(i * edge_tile, edge_tile), edge_tile)
        hot = hot_columns(rcv_low[rows, :], (nodes, nodes + 2 * rim))
        upstream_ref[rows, :] = up_ref[rows, :] + dot(hot, table[...])

    def chain_of(i):
        rows = pl.ds(pl.multiple_of(i * edge_tile, edge_tile), edge_tile)
        upstream = upstream_ref[rows, :]
        normed = normed_ref[rows, :]
        dz2 = back_norm(upstream, normed, scale_ref[rows, :], gain, means[...])
        dz2b = dz2.astype(bf16)
        dz1 = dot(dz2b, w2_turned) * slope_ref[rows, :]
        dz1b = dz1.astype(bf16)
        dz_ref[rows, :] = dz1b
        dz2_ref[rows, :] = dz2b
        sums[0:8, :] += eight_sums(dz1)
        sums[8:16, :] += eight_sums(dz2)
        sums[16:24, :] += eight_sums(upstream * normed)
        sums[24:32, :] += eight_sums(upstream)

    each_tile(up_ref.shape[0], tile)
    each_tile(up_ref.shape[0], chain_of)
    dz1_all = dz_ref[...]
    grads_ref[:lane, :] = dot(turned[:lane, :], dz1_all)
    grads_ref[lane : 2 * lane, :] = dot(sent_turned[...], dz1_all)
    grads_ref[2 * lane : 3 * lane, :] = dot(received_turned[...], dz1_all)
    grads_ref[3 * lane : 4 * lane, :] = dot(turned[lane:, :], dz2_ref[...])
    kept = kept_ref.shape[0]
    node_rows = node_grads_ref.shape[0] - sum_rows
    last = 4 * lane + node_rows
    grads_ref[4 * lane : last, :] = node_grads_ref[:node_rows, :]
    grads_ref[last : last + sum_rows, :] = jnp.concatenate(
        [column_sum(sums[8 * k : 8 * k + 8, :]) for k in range(4)]
        + [node_grads_ref[node_rows : node_rows + 4, :], jnp.zeros((8, lane), f32)],
        axis=0,
    )
    if last + sum_rows < grads_ref.shape[0]:
        grads_ref[last + sum_rows :, :] = jnp.zeros(
            (grads_ref.shape[0] - last - sum_rows, lane), f32
        )
    own = lax.axis_index("sub")
    kept_ref[...] = grads_ref[pl.ds(pl.multiple_of(own * kept, sum_rows), kept), :]
    other = pl.multiple_of((1 - own) * kept, sum_rows)
    sent_ref[...] = grads_ref[pl.ds(other, kept), :].astype(bf16)


def halo_kernel(nodes, ids_ref, dz_ref, turned_weights, rims_ref, total):
    rim = rims_ref.shape[0] // 2
    edges = dz_ref.shape[0]
    parity = parity_of_place()
    total[...] = jnp.zeros_like(total)

    def tile(i):
        rows = pl.ds(pl.multiple_of(i * edge_tile, edge_tile), edge_tile)
        first = (edges + i * edge_tile) // lane
        slots = rows_of_ids(ids_ref, first, edge_tile // lane, 2 * rim, lambda row: row - nodes)
        total[...] += dot(slots, dz_ref[rows, :])

    each_tile(edges, tile)
    w1_turned = turned_weights[2 * lane : 3 * lane]
    for k, side in enumerate((1 - parity, parity)):
        returned = total[pl.ds(pl.multiple_of(side * rim, rim), rim), :].astype(bf16)
        rims_ref[k * rim : (k + 1) * rim, :] = dot(returned, w1_turned).astype(bf16)


def scatter_kernel(
    ids_ref,
    dz_ref,
    snd_column,
    rcv_column,
    unused_ref,
    snd_sum_ref,
    rcv_sum_ref,
    snd_total,
    rcv_total,
):
    half = snd_total.shape[0]
    for total in (snd_total, rcv_total):
        total[...] = jnp.zeros_like(total)

    def tile(i):
        rows = pl.ds(pl.multiple_of(i * edge_tile, edge_tile), edge_tile)
        chunk = edge_tile // lane
        dz1 = dz_ref[rows, :].astype(f32)
        first = rcv_column.shape[0] // lane + i * chunk
        snd_total[...] += spread(ids_ref, i * chunk, chunk, half, snd_column[rows, :], dz1)
        rcv_total[...] += spread(ids_ref, first, chunk, half, rcv_column[rows, :], dz1)

    each_tile(dz_ref.shape[0], tile)
    for total, out_ref in ((snd_total, snd_sum_ref), (rcv_total, rcv_sum_ref)):
        out_ref[:half, :] = total[:, :lane].astype(bf16)
        out_ref[half:, :] = total[:, lane:].astype(bf16)


def edge_outputs_kernel(
    dz_ref, cot_ref, edge_ref, normed_ref, vectors_ref, turned_weights, out_ref, grad_ref
):
    w1_turned = turned_weights[:lane]
    gain, shift = vector(vectors_ref, 2), vector(vectors_ref, 3)

    def tile(i):
        rows = pl.ds(pl.multiple_of(i * edge_tile, edge_tile), edge_tile)
        cot = cot_ref[rows, :].astype(f32)
        grad_ref[rows, :] = (cot + dot(dz_ref[rows, :], w1_turned)).astype(bf16)
        update = normed_ref[rows, :] * gain + shift
        out_ref[rows, :] = (edge_ref[rows, :].astype(f32) + update).astype(bf16)

    each_tile(cot_ref.shape[0], tile)


def node_grad_kernel(
    near_ref, far_ref, base_ref, snd_sum_ref, rcv_sum_ref, turned_weights, ids_ref, out_ref
):
    returned = jnp.concatenate([near_ref[...], far_ref[...]], axis=0)
    total = base_ref[...] + dot(snd_sum_ref[...], turned_weights[lane : 2 * lane])
    total = total + dot(rcv_sum_ref[...], turned_weights[2 * lane : 3 * lane])
    hot = hot_lists(ids_ref, base_ref.shape[0])
    out_ref[...] = (total + dot(hot, returned)).astype(bf16)


def add_kernel(passed, own_ref, other_ref, *refs):
    out_refs = refs[len(refs) - passed - 1 :]
    out_refs[0][...] = (own_ref[...].astype(f32) + other_ref[...].astype(f32)).astype(bf16)
    for source, target in zip(refs[:passed], out_refs[1:]):
        target[...] = source[...]


def finish_kernel(own_ref, other_ref, *refs):
    out_refs, total_ref = refs[:-1], refs[-1]
    kept = own_ref.shape[0]
    own = lax.axis_index("sub")
    total_ref[pl.ds(pl.multiple_of(own * kept, sum_rows), kept), :] = own_ref[...].astype(f32)
    other = pl.multiple_of((1 - own) * kept, sum_rows)
    total_ref[pl.ds(other, kept), :] = other_ref[...].astype(f32)
    at = 0
    for out_ref in out_refs[:4]:
        out_ref[...] = total_ref[at : at + out_ref.shape[0], :]
        at += out_ref.shape[0]
    for k, out_ref in enumerate(out_refs[4:]):
        out_ref[...] = total_ref[at + k : at + k + 1, :]


def call(kernel, outs, scratch, *operands, anywhere=0, sems=0):
    moved = sum(x.size * x.dtype.itemsize for x in operands)
    held = operands[len(operands) - anywhere :]
    operands = operands[: len(operands) - anywhere]
    operands += tuple(pltpu.with_memory_space_constraint(x, pltpu.HBM) for x in held)
    inside = [pl.BlockSpec(memory_space=pltpu.VMEM)] * (len(operands) - anywhere)
    outside = [pl.BlockSpec(memory_space=pl.ANY)] * anywhere
    scratch_shapes = [pltpu.VMEM(shape, dtype) for shape, dtype in scratch]
    if sems:
        scratch_shapes.append(pltpu.SemaphoreType.DMA((sems,)))
    return pl.pallas_call(
        kernel,
        out_shape=[jax.ShapeDtypeStruct(shape, dtype) for shape, dtype in outs],
        in_specs=inside + outside,
        out_specs=[pl.BlockSpec(memory_space=pltpu.VMEM)] * len(outs),
        scratch_shapes=scratch_shapes,
        compiler_params=pltpu.CompilerParams(vmem_limit_bytes=vmem_limit),
        cost_estimate=pl.CostEstimate(flops=0, bytes_accessed=moved, transcendentals=0),
    )(*operands)


def exchange(message):
    chips, samples = lax.axis_size("dom"), lax.axis_size("sample")
    place = lambda chip, sample, core: (chip * samples + sample) * 2 + core
    inner = [(i, i ^ 1) for i in range(2 * chips)]
    outer = []
    for sample in range(samples):
        for chip in range(chips - 1):
            ends = place(chip, sample, 1), place(chip + 1, sample, 0)
            outer += [ends, ends[::-1]]
        for chip, core in ((0, 0), (chips - 1, 1)):
            outer.append((place(chip, sample, core), place(chip, sample ^ 1, core)))
    rim_shape = ((message.shape[0] // 2, lane), bf16)
    near, far = call(split_kernel, [rim_shape, rim_shape], [], message)
    near = lax.ppermute(near, chain, inner)
    return near, lax.ppermute(far, ("dom", "sample", "sub"), outer), far


def sum_rounds():
    for axis in ("sample", "dom"):
        count = lax.axis_size(axis)
        step = count // 2
        while step > 0:
            yield axis, [(i, i ^ step) for i in range(count)]
            step //= 2


def on_device(
    node_in,
    edge_in,
    senders,
    receivers,
    send_list,
    w_edge_first,
    b_edge_first,
    w_edge_second,
    b_edge_second,
    edge_gain,
    edge_shift,
    w_node_first,
    b_node_first,
    w_node_second,
    b_node_second,
    node_gain,
    node_shift,
    node_cotangent,
    edge_cotangent,
):
    node = node_in[0]
    edge = edge_in[0]
    nodes = node.shape[0]
    edges = edge.shape[0]
    rim = send_list.shape[2]
    snd_half = nodes // 2
    kept = -(-(7 * lane + sum_rows) // (2 * sum_rows)) * sum_rows
    row = lambda x: x.reshape(1, lane)
    small = [w_edge_first, w_edge_second, w_node_first, w_node_second]
    small += [row(b_edge_first), row(b_edge_second), row(edge_gain), row(edge_shift)]
    small += [row(b_node_first), row(b_node_second), row(node_gain), row(node_shift)]
    chunks = edges // lane
    sources = [
        node,
        send_list[0],
        senders.reshape(chunks, lane),
        receivers.reshape(chunks, lane),
        edge,
    ] + small
    rims_shape = ((2 * rim, lane), bf16)
    edge_shape = ((edges, lane), bf16)
    wide_shape = ((edges, lane), f32)
    node_shape = ((nodes, lane), bf16)
    node, rims, ids, edge, weights, vectors = call(
        first_kernel,
        [
            node_shape,
            rims_shape,
            ((2 * chunks + 2, lane), jnp.int32),
            edge_shape,
            ((7 * lane, lane), bf16),
            ((8, lane), f32),
        ],
        [],
        *sources,
        anywhere=len(sources),
        sems=len(sources),
    )
    near, far, onward = exchange(rims)
    prepared = call(
        prepare_kernel,
        [
            edge_shape,
            node_shape,
            ((edges, lane), jnp.int32),
            ((edges, lane), jnp.int32),
            ((edges, lane), jnp.int16),
            wide_shape,
            ((snd_half, 2 * lane), bf16),
            ((lane, edges), bf16),
            ((2 * lane, 2 * lane), bf16),
            ((2 * lane, 2 * lane), bf16),
            ((7 * lane, lane), bf16),
        ],
        [((edges, lane), jnp.int16), ((snd_half, 2 * lane), bf16), edge_shape],
        ids,
        node,
        weights,
        vectors,
        edge,
        onward,
        edge_cotangent[0],
        node_cotangent[0],
        anywhere=2,
        sems=2,
    )
    edge_cot, node_cot, snd_column, rcv_column, rcv_low = prepared[:5]
    z_sent, rcv_local, sent_turned, pairs, means, turned_weights = prepared[5:]
    z, normed, scale, message, rims = call(
        edge_forward_kernel,
        [wide_shape, wide_shape, wide_shape, edge_shape, rims_shape],
        [
            ((snd_half + 2 * rim, 2 * lane), bf16),
            ((2 * rim, lane), f32),
        ],
        near,
        far,
        ids,
        weights,
        vectors,
        rcv_column,
        rcv_low,
        z_sent,
        rcv_local,
        pairs,
        means,
    )
    back_near, back_far, onward = exchange(rims)
    agg, received_turned = call(
        collect_kernel,
        [((nodes, lane), f32), ((lane, edges), bf16)],
        [((snd_half + 2 * rim, 2 * lane), bf16), ((snd_half, 2 * lane), f32)],
        ids,
        rcv_column,
        rcv_low,
        message,
        node,
        near,
        far,
        onward,
    )
    node_x, node_act, node_normed, node_dz1, node_dz2, node_sums, dagg, rims = call(
        node_kernel,
        [
            ((nodes, 2 * lane), bf16),
            node_shape,
            ((nodes, lane), f32),
            node_shape,
            node_shape,
            ((16, lane), f32),
            node_shape,
            rims_shape,
        ],
        [],
        back_near,
        back_far,
        node,
        agg,
        ids,
        weights,
        vectors,
        node_cot,
        pairs,
        means,
        turned_weights,
    )
    dagg_near, dagg_far, onward = exchange(rims)
    upstream, slope, turned = call(
        upstream_kernel,
        [wide_shape, wide_shape, ((2 * lane, edges), bf16)],
        [((snd_half, 2 * lane), bf16)],
        rcv_column,
        rcv_low,
        dagg,
        edge_cot,
        z,
        edge,
        onward,
    )
    node_out, base, node_grads = call(
        node_rest_kernel,
        [node_shape, ((nodes, lane), f32), ((3 * lane + sum_rows, lane), f32)],
        [],
        node_x,
        node_act,
        node_normed,
        node_dz1,
        node_dz2,
        node_sums,
        turned_weights,
        vectors,
        node_cot,
        onward,
    )
    half_shape = ((kept, lane), bf16)
    dz, grads_kept, grads_sent = call(
        functools.partial(edge_backward_kernel, nodes),
        [edge_shape, ((kept, lane), f32), half_shape],
        [
            ((2 * kept, lane), f32),
            ((2 * rim, lane), bf16),
            ((32, lane), f32),
            wide_shape,
            edge_shape,
        ],
        dagg_near,
        dagg_far,
        upstream,
        normed,
        scale,
        slope,
        sent_turned,
        received_turned,
        turned,
        turned_weights,
        means,
        vectors,
        node_grads,
        rcv_low,
    )
    core_pairs = [(0, 1), (1, 0)]
    other = lax.ppermute(grads_sent, "sub", core_pairs)
    (grads,) = call(functools.partial(add_kernel, 0), [half_shape], [], grads_kept, other)
    (rims,) = call(
        functools.partial(halo_kernel, nodes),
        [rims_shape],
        [((2 * rim, lane), f32)],
        ids,
        dz,
        turned_weights,
    )
    back_near, back_far, unused = exchange(rims)
    node_grad = edge_out = edge_grad = None
    early_vectors, early_ids = vectors, ids
    for number, (axis, partners) in enumerate(sum_rounds()):
        other = lax.ppermute(grads, axis, partners)
        passed, before, written = [], [], []
        if number == 0:
            passed, before = [vectors], [back_near, back_far]
        elif number == 1:
            snd_sum, rcv_sum = call(
                scatter_kernel,
                [node_shape, node_shape],
                [((snd_half, 2 * lane), f32), ((snd_half, 2 * lane), f32)],
                ids,
                dz,
                snd_column,
                rcv_column,
                early_vectors,
            )
            edge_out, edge_grad = call(
                edge_outputs_kernel,
                [edge_shape, edge_shape],
                [],
                dz,
                edge_cot,
                edge,
                normed,
                early_vectors,
                turned_weights,
            )
            passed, before, written = [ids], [snd_sum, rcv_sum], [edge_out, edge_grad]
        elif number == 2:
            (node_grad,) = call(
                node_grad_kernel,
                [node_shape],
                [],
                back_near,
                back_far,
                base,
                snd_sum,
                rcv_sum,
                turned_weights,
                early_ids,
            )
            written = [node_grad]
        grads, *passed = call(
            functools.partial(add_kernel, len(passed)),
            [half_shape] + [(x.shape, x.dtype) for x in passed],
            [],
            grads,
            other,
            *passed,
            *before,
            *written,
            anywhere=len(written),
        )
        if number == 0:
            (early_vectors,) = passed
        elif number == 1:
            (early_ids,) = passed
    others = lax.ppermute(grads, "sub", core_pairs)
    matrices = [3 * lane, lane, 2 * lane, lane]
    totals = call(
        finish_kernel,
        [((height, lane), f32) for height in matrices] + [((1, lane), f32)] * 8,
        [((2 * kept, lane), f32)],
        grads,
        others,
    )
    flat = [total.reshape(lane) for total in totals[4:]]
    return (
        node_out[None],
        edge_out[None],
        node_grad[None],
        edge_grad[None],
        totals[0],
        flat[0],
        totals[1],
        flat[1],
        flat[2],
        flat[3],
        totals[2],
        flat[4],
        totals[3],
        flat[5],
        flat[6],
        flat[7],
    )


def solution(mesh):
    node_spec = P(("groups", "sample"), ("dom", "sub"), None)
    ids_spec = P(("dom", "sub"))
    return jax.shard_map(
        on_device,
        mesh=mesh,
        in_specs=(
            (node_spec, node_spec, ids_spec, ids_spec, P(("dom", "sub"), None, None))
            + (P(),) * 12
            + (node_spec, node_spec)
        ),
        out_specs=(
            (node_spec,) * 4
            + (P("groups", None), P("groups"), P("groups", None), P("groups"), P("groups"), P("groups"))
            * 2
        ),
        check_vma=False,
    )
```
